32 devices in a mesh: ctx: 16 (over z, x, core), fsdp: 2 (over y).
Axes of the slice: x: 2, y: 2, z: 4, core: 2. Of those that a mesh axis runs over, the one named last changes fastest.
Arguments:
- tokens: bfloat16 [4, 2048, 2304], P('fsdp', 'ctx'), may hold values from -6 to 6
- cotangent: bfloat16 [4, 2048, 2304], P('fsdp', 'ctx'), may hold values from -6 to 6
- segment: int32 [4, 2048], P('fsdp', 'ctx'), may hold values from 0 to 3, as said below
- position: int32 [4, 2048], P('fsdp', 'ctx'), may hold values from 0 to 2047, as said below
- gain_attn: bfloat16 [2304], P(('ctx', 'fsdp')), may hold values from 0.5 to 1.5
- w_query: bfloat16 [2304, 2304], P(('ctx', 'fsdp')), may hold values from -0.125 to 0.125
- w_key: bfloat16 [2304, 2304], P(('ctx', 'fsdp')), may hold values from -0.125 to 0.125
- w_value: bfloat16 [2304, 2304], P(('ctx', 'fsdp')), may hold values from -0.125 to 0.125
- w_output: bfloat16 [2304, 2304], P(('ctx', 'fsdp')), may hold values from -3 to 3
- gain_mlp: bfloat16 [2304], P(('ctx', 'fsdp')), may hold values from 0.5 to 1.5
- w_gate: bfloat16 [2304, 5760], P(('ctx', 'fsdp')), may hold values from -0.125 to 0.125
- w_up: bfloat16 [2304, 5760], P(('ctx', 'fsdp')), may hold values from -0.125 to 0.125
- w_down: bfloat16 [5760, 2304], P(('ctx', 'fsdp')), may hold values from -0.59765625 to 0.59765625
Outputs:
- layer_out: bfloat16 [4, 2048, 2304], P('fsdp', 'ctx')
- grad_tokens: bfloat16 [4, 2048, 2304], P('fsdp', 'ctx')
- grad_gain_attn: float32 [2304], P(('ctx', 'fsdp'))
- grad_query: float32 [2304, 2304], P(('ctx', 'fsdp'))
- grad_key: float32 [2304, 2304], P(('ctx', 'fsdp'))
- grad_value: float32 [2304, 2304], P(('ctx', 'fsdp'))
- grad_output: float32 [2304, 2304], P(('ctx', 'fsdp'))
- grad_gain_mlp: float32 [2304], P(('ctx', 'fsdp'))
- grad_gate: float32 [2304, 5760], P(('ctx', 'fsdp'))
- grad_up: float32 [2304, 5760], P(('ctx', 'fsdp'))
- grad_down: float32 [5760, 2304], P(('ctx', 'fsdp'))
The draws below stay inside these ranges and needn't reach their ends.
Inputs may be any that keep to these rules, and one draw needn't show every extreme that they name: `segment`: A sequence is 32 blocks of 64 tokens in the order of its text; index i of ctx holds blocks i and 31 - i, in this order. In the blocks' order documents are consecutive and numbered from 0 upwards; on every index of fsdp one of its 2 sequences is a single document, each other sequence holds 4 documents. `position`: A token's place in its document, counted from 0 in the blocks' order of its sequence.
All inputs are finite; a program needn't handle non-finite values.
Results may differ from the reference program's by a relative error of at most 0.033.
Values may be sent and summed in bfloat16 or wider, within the bound.
A program may use at most 960 MiB of HBM per device.

```python
import math
from functools import partial
import jax
import jax.numpy as jnp
from jax import lax

D = 2304
HEADS = 36
HEAD_DIM = 64
FF = 5760
WINDOW = 1024
DOCS = 4
SEQ_GRP = 2
SEQ_LEN = 2048
BLK = 128
HALF = 64
SEQS = 4


def layout(key):
    cut_key, pick_key = jax.random.split(key)
    lines = SEQS
    line_keys = jax.random.split(cut_key, lines)
    orders = jax.vmap(lambda line_key: jax.random.permutation(line_key, SEQ_LEN - 1))(line_keys)
    cuts = orders[:, :DOCS - 1].astype(jnp.int32) + 1
    single = jax.random.randint(pick_key, (lines // SEQ_GRP,), 0, SEQ_GRP)
    line_index = jnp.arange(lines, dtype=jnp.int32)
    chosen = line_index % SEQ_GRP == single[line_index // SEQ_GRP]
    cuts = jnp.where(chosen[:, None], SEQ_LEN, cuts)
    places = jnp.arange(SEQ_LEN, dtype=jnp.int32)
    passed = cuts[:, None, :] <= places[None, :, None]
    segments = jnp.sum(passed.astype(jnp.int32), -1)
    starts = jnp.max(jnp.where(passed, cuts[:, None, :], 0), -1)
    inside = places[None, :] - starts
    stored = jnp.arange(SEQ_LEN, dtype=jnp.int32)
    device_index = stored // BLK
    within = stored % BLK
    slot = within // HALF
    offset_in = within % HALF
    blocks_all = SEQ_LEN // HALF
    source = jnp.where(slot == 0, device_index, blocks_all - 1 - device_index) * HALF + offset_in
    return (segments[:, source].astype(jnp.int32), inside[:, source].astype(jnp.int32))


def draw_segment(key, part):
    segments, inside = layout(key)
    return segments


def draw_position(key, part):
    segments, inside = layout(key)
    return inside


def block_levels(stream_key, dims, cuts, low, high):
    def one(dim, shards_of):
        heights = jax.random.uniform(jax.random.fold_in(jax.random.fold_in(stream_key, 6), dim), (shards_of,), jnp.float32, low / len(cuts), high / len(cuts))
        return jnp.repeat(jnp.exp(heights), dims[dim] // shards_of).reshape((-1,) + (1,) * (len(dims) - dim - 1))

    loudness = one(*cuts[0])
    for cut in cuts[1:]:
        loudness = loudness * one(*cut)
    return loudness


def gaussian(stream_key, extent, width, reach, cuts=(), kind=jnp.bfloat16):
    entries = width * jax.random.normal(stream_key, extent, jnp.float32)
    if cuts:
        entries = entries * block_levels(stream_key, extent, cuts, -0.22, 0.18)
    return jnp.clip(entries, -reach, reach).astype(kind)


def setup_inputs(seed: int = 0) -> dict:
    seeds = jax.random.split(jax.random.key(seed), 14)
    return {
        "tokens": gaussian(seeds[0], (SEQS, SEQ_LEN, D), 1.0, 6.0, ((0, 2), (1, 16))),
        "cotangent": gaussian(seeds[1], (SEQS, SEQ_LEN, D), 1.0, 6.0, ((0, 2), (1, 16))),
        "segment": draw_segment(jax.random.fold_in(seeds[13], 71), 0),
        "position": draw_position(jax.random.fold_in(seeds[13], 71), 0),
        "gain_attn": jnp.clip(1.0 + 0.1 * jax.random.normal(seeds[4], (D,), jnp.float32), 0.5, 1.5).astype(jnp.bfloat16),
        "w_query": gaussian(seeds[5], (D, D), D ** -0.5, 0.125, ((0, 32),)),
        "w_key": gaussian(seeds[6], (D, D), D ** -0.5, 0.125, ((0, 32),)),
        "w_value": gaussian(seeds[7], (D, D), D ** -0.5, 0.125, ((0, 32),)),
        "w_output": gaussian(seeds[8], (D, D), 0.5, 3.0, ((0, 32),)),
        "gain_mlp": jnp.clip(1.0 + 0.1 * jax.random.normal(seeds[9], (D,), jnp.float32), 0.5, 1.5).astype(jnp.bfloat16),
        "w_gate": gaussian(seeds[10], (D, FF), D ** -0.5, 0.125, ((0, 32),)),
        "w_up": gaussian(seeds[11], (D, FF), D ** -0.5, 0.125, ((0, 32),)),
        "w_down": gaussian(seeds[12], (FF, D), 0.1, 0.59765625, ((0, 32),)),
    }


@jax.custom_vjp
def low(v):
    return lax.optimization_barrier(v.astype(jnp.bfloat16)).astype(jnp.float32)

@jax.custom_vjp
def low_back(v):
    return v

def low_keep(v):
    return (low(v), None)

def low_pass(kept, grad):
    return (grad,)

def back_keep(v):
    return (v, None)

def back_low(kept, grad):
    return (low(grad),)
low.defvjp(low_keep, low_pass)
low_back.defvjp(back_keep, back_low)
EPSILON = 1e-05
BRANCH_SCALE = 1.4 / math.sqrt(40.0)
NEG_LARGE = -1e+30
BLOCK_QUERIES = 512

def product(left, right):
    return jnp.dot(left, right, precision=lax.Precision.HIGHEST, preferred_element_type=jnp.float32)

def rope_tables(places):
    halfway = HEAD_DIM // 2
    rate_table = jnp.exp(jnp.arange(halfway, dtype=jnp.float32) * (-math.log(10000.0) / halfway))
    angles = places.astype(jnp.float32)[:, None] * rate_table[None, :]
    return (jnp.cos(angles)[:, None, :], jnp.sin(angles)[:, None, :])

def rotate(tensor, cosine, sine_table):
    halfway = HEAD_DIM // 2
    first_half, second_half = (tensor[..., :halfway], tensor[..., halfway:])
    return jnp.concatenate([first_half * cosine - second_half * sine_table, second_half * cosine + first_half * sine_table], -1)

def normalize(inputs, gains):
    inverse = lax.rsqrt(lax.optimization_barrier(jnp.mean(inputs * inputs, -1, keepdims=True)) + EPSILON)
    return low(inputs * inverse * gains)

def attend_block(query_all, key_all, value_all, segments, places, index):
    query_rows = min(BLOCK_QUERIES, SEQ_LEN)
    per_line = SEQ_LEN // query_rows
    line = index // per_line
    first_row = index % per_line * query_rows
    key_line = lax.dynamic_index_in_dim(key_all, line, 0, keepdims=False)
    value_line = lax.dynamic_index_in_dim(value_all, line, 0, keepdims=False)
    segment_line = lax.dynamic_index_in_dim(segments, line, 0, keepdims=False)
    place_line = lax.dynamic_index_in_dim(places, line, 0, keepdims=False)
    query_line = lax.dynamic_index_in_dim(query_all, line, 0, keepdims=False)
    query_block = lax.dynamic_slice_in_dim(query_line, first_row, query_rows, 0)
    segment_query = lax.dynamic_slice_in_dim(segment_line, first_row, query_rows, 0)
    place_query = lax.dynamic_slice_in_dim(place_line, first_row, query_rows, 0)
    spread = place_query[:, None] - place_line[None, :]
    permitted = (segment_query[:, None] == segment_line[None, :]) & (spread >= 0) & (spread < WINDOW)
    scores = low_back(jnp.einsum('qhd,khd->hqk', query_block, key_line, precision=lax.Precision.HIGHEST) * 0.125)
    scores = jnp.where(permitted[None], scores, NEG_LARGE)
    highest = lax.optimization_barrier(jnp.max(scores, -1, keepdims=True))
    weights = jnp.exp(scores - highest)
    probabilities = low(weights / lax.optimization_barrier(jnp.sum(weights, -1, keepdims=True)))
    return jnp.einsum('hqk,khd->qhd', probabilities, value_line, precision=lax.Precision.HIGHEST)

def layer(tokens, gain_attn, w_query, w_key, w_value, w_output, gain_mlp, w_gate, w_up, w_down, segment, position, cosine, sine_table):
    lines = tokens.shape[0]
    inputs = tokens.reshape(-1, D)
    held_one = normalize(inputs, gain_attn)
    query_raw = low_back(product(held_one, w_query))
    key_raw = low_back(product(held_one, w_key))
    value_raw = low_back(product(held_one, w_value))
    heads_shape = (-1, HEADS, HEAD_DIM)
    four_shape = (lines, SEQ_LEN, HEADS, HEAD_DIM)
    query_rot = low(rotate(query_raw.reshape(heads_shape), cosine, sine_table)).reshape(four_shape)
    key_rot = low(rotate(key_raw.reshape(heads_shape), cosine, sine_table)).reshape(four_shape)
    value_low = low(value_raw).reshape(four_shape)
    blocks = lines * (SEQ_LEN // min(BLOCK_QUERIES, SEQ_LEN))
    block_step = jax.checkpoint(attend_block)
    attended = lax.map(lambda index: block_step(query_rot, key_rot, value_low, segment, position, index), jnp.arange(blocks, dtype=jnp.int32))
    attn_low = low(low_back(attended.reshape(-1, D)))
    branch_attn = low_back(product(attn_low, w_output))
    middle = inputs + BRANCH_SCALE * branch_attn
    held_two = normalize(middle, gain_mlp)
    gate_proj = low_back(product(held_two, w_gate))
    up_proj = low_back(product(held_two, w_up))
    activated = low(jax.nn.silu(gate_proj) * up_proj)
    branch_mlp = low_back(product(activated, w_down))
    return (middle + BRANCH_SCALE * branch_mlp).reshape(tokens.shape)

def reference(tokens, cotangent, segment, position, gain_attn, w_query, w_key, w_value, w_output, gain_mlp, w_gate, w_up, w_down):
    floats = [array.astype(jnp.float32) for array in (tokens, gain_attn, w_query, w_key, w_value, w_output, gain_mlp, w_gate, w_up, w_down)]
    cosine, sine_table = rope_tables(position.reshape(-1))
    bound = partial(layer, segment=segment, position=position, cosine=cosine, sine_table=sine_table)
    result, pullback = jax.vjp(bound, *floats)
    grads = pullback(cotangent.astype(jnp.float32))
    return (result.astype(jnp.bfloat16), grads[0].astype(jnp.bfloat16), grads[1], grads[2], grads[3], grads[4], grads[5], grads[6], grads[7], grads[8], grads[9])
```

```python
import functools
import math

import jax
import jax.numpy as jnp
from jax import lax
from jax.experimental import pallas as pl
from jax.experimental.pallas import tpu as pltpu
from jax.sharding import Mesh, PartitionSpec as P

HEADS = 36
HEAD_DIM = 64
WINDOW = 1024
EPSILON = 1e-05
BRANCH_SCALE = 1.4 / math.sqrt(40.0)
NEG_LARGE = -1e30
LANES = 128
PAIRS = 5
KEY_TILE = 256
QUERY_BLOCKS = 2
MIB = 1024 * 1024

f32, bf16 = jnp.float32, jnp.bfloat16


def matmul(left, right):
    return jnp.dot(left, right, preferred_element_type=f32)


def times_transposed(left, right):
    return lax.dot_general(left, right, (((1,), (1,)), ((), ())), preferred_element_type=f32)


def transposed_times(left, right):
    return lax.dot_general(left, right, (((0,), (0,)), ((), ())), preferred_element_type=f32)


def rms_back(upstream, normed, inverse):
    return inverse * (upstream - normed * jnp.mean(upstream * normed, -1, keepdims=True))


HBM = pl.BlockSpec(memory_space=pl.ANY)


def ignoring(kernel, args, extra):
    return lambda *refs: kernel(*refs[:args], *refs[args + extra :])


def lasting(micros):
    return pl.CostEstimate(flops=0, bytes_accessed=micros * 3_600_000, transcendentals=0)


MESH_IDS = pl.DeviceIdType.MESH
ALL = ("u", "w", "v", "core", "f")
KEYS = ("w", "v", "core")
HEAD_SUM = ("w", "v", "core", "f")
HIDDEN = ("v", "f")
HIDDEN_SUM = ("u", "w", "core")


def coords():
    return {axis: lax.axis_index(axis) for axis in ALL}


def device(place, **moved):
    return tuple(moved.get(axis, place[axis]) for axis in ALL)


def remote(src, dst, send, recv, where):
    return pltpu.make_async_remote_copy(
        src_ref=src, dst_ref=dst, send_sem=send, recv_sem=recv, device_id=where, device_id_type=MESH_IDS
    )


def ride_out(kind, x):
    shape = {
        "gather_u": (8,) + x.shape[1:],
        "scatter_u": (3, 2) + x.shape[1:],
        "gather_hidden": (4,) + x.shape,
        "scatter_hidden": (3,) + x.shape[1:],
        "gather_keys": (3,) + x.shape,
    }
    return jax.ShapeDtypeStruct(shape[kind], x.dtype)


def partner(kind, place, step):
    if kind in ("gather_u", "scatter_u"):
        k = place["u"] ^ step
        return k, device(place, u=k)
    if kind == "gather_keys":
        k = (2 * place["v"] + place["core"]) ^ step
        return k, device(place, v=k // 2, core=k % 2)
    k = (2 * place["v"] + place["f"]) ^ step
    return k, device(place, v=k // 2, f=k % 2)


def ride_slices(kind, src, dst, place, step):
    k, _ = partner(kind, place, step)
    u, t = place["u"], 2 * place["v"] + place["f"]
    if kind == "gather_u":
        return [(src.at[s], dst.at[7 - u if s else u], dst.at[7 - k if s else k]) for s in range(2)]
    if kind == "scatter_u":
        return [(src.at[7 - k if s else k], dst.at[step - 1, s], dst.at[step - 1, s]) for s in range(2)]
    if kind == "gather_hidden":
        return [(src, dst.at[t], dst.at[k])]
    if kind == "scatter_hidden":
        return [(src.at[k], dst.at[step - 1], dst.at[step - 1])]
    return [(src, dst.at[step - 1], dst.at[step - 1])]


def ride_copies(kind, src, dst, send, recv, keep, place, part):
    u, t = place["u"], 2 * place["v"] + place["f"]
    if part == "own":
        if kind == "gather_u":
            return [pltpu.make_async_copy(src.at[s], dst.at[7 - u if s else u], keep.at[s]) for s in range(2)]
        return [pltpu.make_async_copy(src, dst.at[t], keep.at[0])] if kind == "gather_hidden" else []
    copies = []
    for step in (3, 2, 1):
        _, to = partner(kind, place, step)
        for i, (here, there, landing) in enumerate(ride_slices(kind, src, dst, place, step)):
            at = 2 * step - 2 + i
            if part == "away":
                copies.append(remote(here, there, send.at[at], recv.at[at], to))
            else:
                copies.append(remote(landing, landing, send.at[at], recv.at[at], to))
    return copies


def ride_greet(kinds, place):
    barrier = pltpu.get_barrier_semaphore()
    for kind in kinds:
        for step in range(1, 4):
            _, to = partner(kind, place, step)
            pl.semaphore_signal(barrier, inc=1, device_id=to, device_id_type=MESH_IDS)


def ride_start(kinds, rides, arrived, sems, place):
    for a, kind in enumerate(kinds):
        for part in ("away", "own"):
            for copy in ride_copies(kind, rides[a], arrived[a], *(sem.at[a] for sem in sems), place, part):
                copy.start()


def ride_end(kinds, rides, arrived, sems, place):
    for a, kind in enumerate(kinds):
        for part in ("away", "own", "back"):
            for copy in ride_copies(kind, rides[a], arrived[a], *(sem.at[a] for sem in sems), place, part):
                copy.wait_send() if part == "away" else copy.wait() if part == "own" else copy.wait_recv()


def ride_scratch(n):
    return [pltpu.SemaphoreType.DMA((n, 6)), pltpu.SemaphoreType.DMA((n, 6)), pltpu.SemaphoreType.DMA((n, 2))]


def riding(kernel, args, extra, outs, kinds, grid):
    n = len(kinds)

    def whole(*refs):
        ins, rides = refs[:args], refs[args : args + n]
        rest = refs[args + n + extra :]
        results, arrived, scratch = rest[:outs], rest[outs : outs + n], rest[outs + n : len(rest) - 3]
        sems = rest[len(rest) - 3 :]
        place = coords()
        ids = [pl.program_id(i) for i in range(len(grid))]
        first, last = ids[0] == 0, ids[0] == grid[0] - 1
        for i in range(1, len(grid)):
            first, last = first & (ids[i] == 0), last & (ids[i] == grid[i] - 1)

        @pl.when(first)
        def _():
            ride_greet(kinds, place)
            pl.semaphore_wait(pltpu.get_barrier_semaphore(), 3 * n)
            ride_start(kinds, rides, arrived, sems, place)

        kernel(*ins, *results, *scratch)

        @pl.when(last)
        def _():
            ride_end(kinds, rides, arrived, sems, place)

    return whole


def grid_call(kernel, grid, args, in_specs, out_specs, out_shape, scratch, name, micros, after=(), rides=(), ident=None):
    limit = 56 * MIB
    if not rides:
        return pl.pallas_call(
            ignoring(kernel, len(args), len(after)),
            grid=grid,
            in_specs=in_specs + [HBM] * len(after),
            out_specs=out_specs,
            out_shape=out_shape,
            scratch_shapes=scratch,
            compiler_params=pltpu.CompilerParams(vmem_limit_bytes=limit),
            cost_estimate=lasting(micros),
            name=name,
        )(*args, *after)
    kinds = [kind for kind, _ in rides]
    n = len(rides)
    return pl.pallas_call(
        riding(kernel, len(args), len(after), len(out_shape), kinds, grid),
        grid=grid,
        in_specs=in_specs + [HBM] * (n + len(after)),
        out_specs=out_specs + [HBM] * n,
        out_shape=out_shape + [ride_out(kind, x) for kind, x in rides],
        scratch_shapes=scratch + ride_scratch(n),
        compiler_params=pltpu.CompilerParams(vmem_limit_bytes=limit, collective_id=ident, has_side_effects=True),
        cost_estimate=lasting(max(micros, 50)),
        name=name + "_riding",
    )(*args, *[x for _, x in rides], *after)


def swap_halves(x):
    lane = lax.broadcasted_iota(jnp.int32, x.shape, 1)
    return jnp.where(lane % 64 < 32, pltpu.roll(x, LANES - 32, 1), pltpu.roll(x, 32, 1))


def rope_kernel(raw_ref, cos_ref, sin_ref, kv_ref, q_ref):
    cos, sin = cos_ref[...], sin_ref[...]

    def turn(x):
        return x * cos + swap_halves(x) * sin

    for p in range(4):
        kv_ref[:, 256 * p : 256 * p + 128] = turn(raw_ref[:, 256 * p : 256 * p + 128]).astype(bf16)
        kv_ref[:, 256 * p + 128 : 256 * p + 256] = raw_ref[:, 256 * p + 128 : 256 * p + 256].astype(bf16)
    last = raw_ref[:, 1024:1152]
    lane = lax.broadcasted_iota(jnp.int32, last.shape, 1)
    kv_ref[:, 1024:1152] = jnp.where(lane < 64, turn(last), last).astype(bf16)
    for p in range(5):
        q_ref[:, 128 * p : 128 * p + 128] = turn(raw_ref[:, 1152 + 128 * p : 1280 + 128 * p]).astype(bf16)


def rope(raw, cos, sin):
    rows = raw.shape[0]
    tile = min(256, rows)
    row = lambda cols: pl.BlockSpec((tile, cols), lambda i: (i, 0))
    return pl.pallas_call(
        rope_kernel,
        grid=(rows // tile,),
        in_specs=[row(1792), row(LANES), row(LANES)],
        out_specs=[row(1152), row(640)],
        out_shape=[jax.ShapeDtypeStruct((rows, 1152), bf16), jax.ShapeDtypeStruct((rows, 640), bf16)],
        compiler_params=pltpu.CompilerParams(vmem_limit_bytes=40 * MIB),
        name="rope",
    )(raw, cos, sin)


def unrope_kernel(dkv_ref, dq_ref, cos_ref, sin_ref, out_ref):
    cos, sin = cos_ref[...], sin_ref[...]

    def turn(x):
        return x * cos - swap_halves(x) * sin

    for p in range(4):
        a = 256 * p
        out_ref[:, a : a + 128] = turn(dkv_ref[:, a : a + 128].astype(f32)).astype(bf16)
        out_ref[:, a + 128 : a + 256] = dkv_ref[:, a + 128 : a + 256].astype(bf16)
    last = dkv_ref[:, 1024:1152].astype(f32)
    lane = lax.broadcasted_iota(jnp.int32, last.shape, 1)
    out_ref[:, 1024:1152] = jnp.where(lane < 64, turn(last), last).astype(bf16)
    for p in range(5):
        out_ref[:, 1152 + 128 * p : 1280 + 128 * p] = turn(
            dq_ref[:, 128 * p : 128 * p + 128].astype(f32)
        ).astype(bf16)


def unrope(dkv, dq, cos, sin, after=()):
    rows = dkv.shape[0]
    tile = min(256, rows)
    row = lambda cols: pl.BlockSpec((tile, cols), lambda i: (i, 0))
    return pl.pallas_call(
        ignoring(unrope_kernel, 4, len(after)),
        grid=(rows // tile,),
        in_specs=[row(1152), row(640), row(LANES), row(LANES)] + [HBM] * len(after),
        out_specs=row(1792),
        out_shape=jax.ShapeDtypeStruct((rows, 1792), bf16),
        compiler_params=pltpu.CompilerParams(vmem_limit_bytes=40 * MIB),
        name="unrope",
    )(dkv, dq, cos, sin, *after)


def stack_heads(x, first, second):
    return jnp.concatenate([jnp.where(first, x, 0), jnp.where(second, x, 0)], 0)


def text_rows(source, ring, j, half, many):
    v, core = lax.axis_index("v"), lax.axis_index("core")
    v = 1 - v if source // 2 else v
    core = 1 - core if source % 2 else core
    at = (ring * 2 + v) * 2 + core
    block = many * j + (at if j < 4 else many - 1 - at)
    return pl.multiple_of(block * half, half)


def assemble(kv_refs, kv_s):
    rings, _, half, _ = kv_refs[0].shape
    for source, ref in enumerate(kv_refs):
        for ring in range(rings):
            for j in range(8):
                kv_s[pl.ds(text_rows(source, ring, j, half, 4 * rings), half), :] = ref[ring, j]


def flash_forward_kernel(
    bounds, q_ref, kv0, kv1, kv2, kv3, lim_ref, o_ref, lse_ref, kv_s, s_ref, vt_ref
):
    p, t = pl.program_id(0), pl.program_id(1)
    nq = q_ref.shape[0]
    tail = p == 4
    voff = pl.multiple_of(jnp.where(tail, 0, LANES), LANES)
    tiles = s_ref.shape[0]

    @pl.when(t == 0)
    def _():
        assemble((kv0, kv1, kv2, kv3), kv_s)
        for k in range(tiles):
            vt_ref[k] = kv_s[k * KEY_TILE : (k + 1) * KEY_TILE, pl.ds(voff, LANES)].T

    lane = lax.broadcasted_iota(jnp.int32, (nq, LANES), 1)
    qm = stack_heads(q_ref[...] * bf16(0.125), lane < 64, lane >= 64)
    lo, hi = lim_ref[0, 0:1, :], lim_ref[0, 1:2, :]
    row = lax.broadcasted_iota(jnp.int32, (KEY_TILE, 2 * nq), 0)
    klo, khi = bounds(t)

    def scores(k, high):
        base = pl.multiple_of(k * KEY_TILE, KEY_TILE)
        s = times_transposed(kv_s[pl.ds(base, KEY_TILE), 0:LANES], qm)
        s = jnp.where((row >= lo - base) & (row <= hi - base), s, NEG_LARGE)
        s_ref[k] = s
        return jnp.maximum(high, jnp.max(s.reshape(KEY_TILE // 8, 8, 2 * nq), 0))

    high = lax.fori_loop(klo, khi, scores, jnp.full((8, 2 * nq), NEG_LARGE, f32))
    high = jnp.max(high, 0, keepdims=True)

    def mix(k, carry):
        total, acc = carry
        w = jnp.exp(s_ref[k] - high)
        total = total + jnp.sum(w.reshape(KEY_TILE // 8, 8, 2 * nq), 0)
        acc = acc + matmul(vt_ref[k], w.astype(bf16))
        return total, acc

    total, acc = lax.fori_loop(
        klo, khi, mix, (jnp.zeros((8, 2 * nq), f32), jnp.zeros((LANES, 2 * nq), f32))
    )
    total = jnp.sum(total, 0, keepdims=True)
    out = (acc / total).T
    first, second = out[:nq], out[nq:]
    low = jnp.where(tail, 0.0, first)
    up = jnp.where(tail, first, second)
    o_ref[...] = jnp.where(lane < 64, low, up).astype(bf16)
    lse_ref[0, 0] = jnp.broadcast_to(high + jnp.log(total), (8, 2 * nq))


def flash_specs(rows, tiles, kv):
    nq = rows // tiles
    _, rings, _, half, _ = kv[0].shape
    part = pl.BlockSpec((nq, LANES), lambda p, t, *_: (t, p))
    keys = [
        pl.BlockSpec((None, rings, 8, half, 2 * LANES), lambda p, t, *_, i=i: (i, 0, 0, 0, p)) for i in (0, 0, 1, 2)
    ]
    lim = pl.BlockSpec((1, 8, 2 * nq), lambda p, t, *_: (t, 0, 0))
    lse = pl.BlockSpec((1, 1, 8, 2 * nq), lambda p, t, *_: (p, t, 0, 0))
    return nq, 32 * rings * half, part, keys, lim, lse


def window_bounds(rows, tiles, rings):
    half, many = rows // 8, 4 * rings

    def bounds(t):
        at = (lax.axis_index("w") * 2 + lax.axis_index("v")) * 2 + lax.axis_index("core")

        def first_row(j):
            return (many * j + jnp.where(j < 4, at, many - 1 - at)) * half

        low = jnp.maximum(first_row(t * QUERY_BLOCKS) - (WINDOW - 1), 0)
        high = first_row(t * QUERY_BLOCKS + QUERY_BLOCKS - 1) + half - 1
        return low // KEY_TILE, high // KEY_TILE + 1

    return bounds


def flash_call(kernel, name, args, klo, khi, in_specs, out_specs, out_shape, scratch, micros, after, rides, ident):
    tiles = klo.shape[0]
    grid = (PAIRS, tiles)
    if rides:
        bounds = window_bounds(args[0].shape[0], tiles, args[-3 if name == "flash_backward" else -2].shape[1])
        return grid_call(
            functools.partial(kernel, bounds), grid, args, in_specs, out_specs, out_shape, scratch, name, micros,
            after, rides, ident,
        )

    def bounded(klo_ref, khi_ref, *refs):
        kernel(lambda t: (klo_ref[t], khi_ref[t]), *refs)

    return pl.pallas_call(
        ignoring(bounded, 2 + len(args), len(after)),
        grid_spec=pltpu.PrefetchScalarGridSpec(
            num_scalar_prefetch=2,
            grid=grid,
            in_specs=in_specs + [HBM] * len(after),
            out_specs=out_specs,
            scratch_shapes=scratch,
        ),
        out_shape=out_shape,
        compiler_params=pltpu.CompilerParams(vmem_limit_bytes=56 * MIB),
        cost_estimate=lasting(micros),
        name=name,
    )(klo, khi, *args, *after)


def flash_forward(q, kv, lim, klo, khi, after=(), rides=(), ident=None):
    rows, tiles = q.shape[0], klo.shape[0]
    nq, keys, part, whole, limits, lses = flash_specs(rows, tiles, kv)
    return flash_call(
        flash_forward_kernel,
        "flash_forward",
        [q, kv[0], kv[1], kv[1], kv[1], lim],
        klo,
        khi,
        [part, *whole, limits],
        [part, lses],
        [jax.ShapeDtypeStruct((rows, 640), bf16), jax.ShapeDtypeStruct((PAIRS, tiles, 8, 2 * nq), f32)],
        [
            pltpu.VMEM((keys, 2 * LANES), bf16),
            pltpu.VMEM((keys // KEY_TILE, KEY_TILE, 2 * nq), f32),
            pltpu.VMEM((keys // KEY_TILE, LANES, KEY_TILE), bf16),
        ],
        40,
        after,
        rides,
        ident,
    )


def flash_backward_kernel(
    bounds, q_ref, do_ref, o_ref, kv0, kv1, kv2, kv3, lim_ref, lse_ref,
    dq_ref, dkv0, dkv1, dkv2, dkv3, kv_s, kt_ref, dk_ref, dv_ref,
):
    p, t = pl.program_id(0), pl.program_id(1)
    nq = q_ref.shape[0]
    tail = p == 4
    voff = pl.multiple_of(jnp.where(tail, 0, LANES), LANES)
    tiles = kt_ref.shape[0]

    @pl.when(t == 0)
    def _():
        assemble((kv0, kv1, kv2, kv3), kv_s)
        for k in range(tiles):
            kt_ref[k] = kv_s[k * KEY_TILE : (k + 1) * KEY_TILE, 0:LANES].T
        dk_ref[...] = jnp.zeros_like(dk_ref)
        dv_ref[...] = jnp.zeros_like(dv_ref)

    lane = lax.broadcasted_iota(jnp.int32, (nq, LANES), 1)
    qm = stack_heads(q_ref[...] * bf16(0.125), lane < 64, lane >= 64)
    side = jnp.where(tail, 1, 0)
    head = lane // 64
    dom = stack_heads(do_ref[...], head == side, head == 1 + side)
    back = do_ref[...].astype(f32) * o_ref[...].astype(f32)
    back = stack_heads(back, head == side, head == 1 + side)
    delta = jnp.sum(back.T, 0, keepdims=True)
    lo, hi = lim_ref[0, 0:1, :], lim_ref[0, 1:2, :]
    lse = lse_ref[0, 0, 0:1, :]
    row = lax.broadcasted_iota(jnp.int32, (KEY_TILE, 2 * nq), 0)

    def step(k, acc):
        base = pl.multiple_of(k * KEY_TILE, KEY_TILE)
        s = times_transposed(kv_s[pl.ds(base, KEY_TILE), 0:LANES], qm)
        w = jnp.exp(jnp.where((row >= lo - base) & (row <= hi - base), s - lse, NEG_LARGE))
        dp = times_transposed(kv_s[pl.ds(base, KEY_TILE), pl.ds(voff, LANES)], dom)
        ds = (w * (dp - delta)).astype(bf16)
        dv_ref[pl.ds(base, KEY_TILE), :] += matmul(w.astype(bf16), dom)
        dk_ref[pl.ds(base, KEY_TILE), :] += matmul(ds, qm)
        return acc + matmul(kt_ref[k], ds)

    acc = lax.fori_loop(*bounds(t), step, jnp.zeros((LANES, 2 * nq), f32))
    out = acc.T * 0.125
    dq_ref[...] = jnp.where(lane < 64, out[:nq], jnp.where(tail, 0.0, out[nq:]))

    @pl.when(t == pl.num_programs(1) - 1)
    def _():
        rings, _, half, _ = dkv0.shape
        for source, ref in enumerate((dkv0, dkv1, dkv2, dkv3)):
            for ring in range(rings):
                for j in range(8):
                    at = pl.ds(text_rows(source, ring, j, half, 4 * rings), half)
                    dk, dv = dk_ref[at, :], dv_ref[at, :]
                    ref[ring, j, :, 0:LANES] = jnp.where(tail, dk + dv, dk).astype(bf16)
                    ref[ring, j, :, LANES : 2 * LANES] = dv.astype(bf16)


def flash_backward(q, do, o, kv, lim, lse, klo, khi, after=(), rides=(), ident=None):
    rows, tiles = q.shape[0], klo.shape[0]
    nq, keys, part, whole, limits, lses = flash_specs(rows, tiles, kv)
    return flash_call(
        flash_backward_kernel,
        "flash_backward",
        [q, do, o, kv[0], kv[1], kv[1], kv[1], lim, lse],
        klo,
        khi,
        [part, part, part, *whole, limits, lses],
        [part] + [whole[0]] * 4,
        [jax.ShapeDtypeStruct((rows, 640), f32)] + [jax.ShapeDtypeStruct(kv[0].shape, bf16)] * 4,
        [
            pltpu.VMEM((keys, 2 * LANES), bf16),
            pltpu.VMEM((keys // KEY_TILE, LANES, KEY_TILE), bf16),
            pltpu.VMEM((keys, LANES), f32),
            pltpu.VMEM((keys, LANES), f32),
        ],
        48,
        after,
        rides,
        ident,
    )


def feed_forward_kernel(
    held_ref, back_ref, wg_ref, wu_ref, wd_ref, act_ref, bg_ref, bu_ref, bh_ref, br_ref, bh_acc, br_acc
):
    t = pl.program_id(0)
    held = held_ref[...]
    width = held.shape[1]
    wg, wu = wg_ref[...].reshape(width, wg_ref.shape[2]), wu_ref[...].reshape(width, wu_ref.shape[2])
    gate, up = matmul(held, wg), matmul(held, wu)
    back_act = times_transposed(back_ref[...], wd_ref[...])
    sig = jax.nn.sigmoid(gate)
    gs = gate * sig
    act = (gs * up).astype(bf16)
    bg = (back_act * up * sig * (1.0 + gate * (1.0 - sig))).astype(bf16)
    bu = (back_act * gs).astype(bf16)
    act_ref[...], bg_ref[...], bu_ref[...] = act, bg, bu
    bh = times_transposed(bg, wg) + times_transposed(bu, wu)
    br = matmul(act, wd_ref[...])

    @pl.when(t == 0)
    def _():
        bh_acc[...] = bh
        br_acc[...] = br

    @pl.when(t > 0)
    def _():
        bh_acc[...] += bh
        br_acc[...] += br

    @pl.when(t == pl.num_programs(0) - 1)
    def _():
        bh_ref[...] = bh_acc[...].astype(bf16)
        br_ref[...] = br_acc[...].astype(bf16)


def feed_forward(held, back, packed, down_whole, after=(), rides=(), ident=None):
    rows, width = held.shape
    wide = down_whole.shape[0]
    tile = 256
    tiles = wide // tile
    whole = pl.BlockSpec((rows, width), lambda t: (0, 0))
    part = pl.BlockSpec((rows, tile), lambda t: (0, t))
    many, per = packed.shape[0], packed.shape[2] // tile
    cols = lambda off: pl.BlockSpec((many, width // many, tile), lambda t: (0, (t + off) // per, (t + off) % per))
    return grid_call(
        feed_forward_kernel,
        (tiles,),
        [held, back, packed, packed, down_whole],
        [whole, whole, cols(0), cols(tiles), pl.BlockSpec((tile, width), lambda t: (t, 0))],
        [part, part, part, whole, whole],
        [jax.ShapeDtypeStruct((rows, wide), bf16)] * 3 + [jax.ShapeDtypeStruct((rows, width), bf16)] * 2,
        [pltpu.VMEM((rows, width), f32)] * 2,
        "feed_forward",
        42,
        after,
        rides,
        ident,
    )


def weight_gradient(lefts, rights, tile=256, after=(), rides=(), ident=None):
    many, per = len(lefts), len(rights[0])
    flat = [x for group in rights for x in group]
    rows, high = lefts[0].shape
    widths = [x.shape[1] for x in rights[0]]

    def kernel(*refs):
        ls, rs, out = refs[:many], refs[many : many + len(flat)], refs[many + len(flat)]
        start = 0
        for i, cols in enumerate(widths):
            total = transposed_times(ls[0][...], rs[i][...])
            for g in range(1, many):
                total = total + transposed_times(ls[g][...], rs[g * per + i][...])
            out[:, start : start + cols] = total.astype(bf16)
            start += cols

    return grid_call(
        kernel,
        (high // tile,),
        [*lefts, *flat],
        [pl.BlockSpec((rows, tile), lambda i: (0, i))] * many + [pl.BlockSpec(x.shape, lambda i: (0, 0)) for x in flat],
        [pl.BlockSpec((tile, sum(widths)), lambda i: (i, 0))],
        [jax.ShapeDtypeStruct((high, sum(widths)), bf16)],
        [],
        "weight_gradient",
        max(4, 2 * many * rows * high * sum(widths) // 10**9),
        after,
        rides,
        ident,
    )


def greet(places):
    barrier = pltpu.get_barrier_semaphore()
    for place in places:
        pl.semaphore_signal(barrier, inc=1, device_id=place, device_id_type=MESH_IDS)
    pl.semaphore_wait(barrier, len(places))


def greet_line(me, place, more=0):
    barrier = pltpu.get_barrier_semaphore()

    @pl.when(me > 0)
    def _():
        pl.semaphore_signal(barrier, inc=1, device_id=device(place, u=me - 1), device_id_type=MESH_IDS)

    @pl.when(me < 3)
    def _():
        pl.semaphore_signal(barrier, inc=1, device_id=device(place, u=me + 1), device_id_type=MESH_IDS)

    pl.semaphore_wait(barrier, 2 + more - jnp.where(me == 0, 1, 0) - jnp.where(me == 3, 1, 0))


def communicating(kernel, out, args, scratch, collective_id, name, vmem=40, after=(), micros=50):
    return pl.pallas_call(
        ignoring(kernel, len(args), len(after)),
        out_shape=out,
        in_specs=[HBM] * (len(args) + len(after)),
        out_specs=[HBM] * len(out) if isinstance(out, list) else HBM,
        scratch_shapes=scratch,
        compiler_params=pltpu.CompilerParams(
            collective_id=collective_id, has_side_effects=True, vmem_limit_bytes=vmem * MIB
        ),
        cost_estimate=lasting(micros),
        name=name,
    )(*args, *after)


def gather_u_kernel(n, kinds, *refs):
    r = len(kinds)
    ins, rides, outs, arrived = refs[:n], refs[n : n + r], refs[n + r : 2 * n + r], refs[2 * n + r : 2 * n + 2 * r]
    keep, send_r, send_l, recv_r, recv_l, *ride_sems = refs[2 * n + 2 * r :]
    place = coords()
    me = place["u"]
    if kinds:
        ride_greet(kinds, place)
    greet_line(me, place, 3 * r)
    right, left = device(place, u=jnp.minimum(me + 1, 3)), device(place, u=jnp.maximum(me - 1, 0))

    def spot(owner, slot, a):
        return outs[a].at[:, owner if slot == 0 else 7 - owner]

    def going(step, slot, a, rightward):
        owner = me - step if rightward else me + step
        owner = jnp.clip(owner, 0, 3)
        src = ins[a].at[:, slot] if step == 0 else spot(owner, slot, a)
        send, recv, to = (send_r, recv_l, right) if rightward else (send_l, recv_r, left)
        return remote(src, spot(owner, slot, a), send.at[step, slot, a], recv.at[step, slot, a], to)

    def coming(step, slot, a, from_left):
        owner = jnp.clip(me - 1 - step if from_left else me + 1 + step, 0, 3)
        send, recv, to = (send_r, recv_l, right) if from_left else (send_l, recv_r, left)
        there = spot(owner, slot, a)
        return remote(there, there, send.at[step, slot, a], recv.at[step, slot, a], to)

    parts = [(slot, a) for slot in range(2) for a in range(n)]
    own = [pltpu.make_async_copy(ins[a].at[:, s], spot(me, s, a), keep.at[s, a]) for s, a in parts]
    for step in range(3):
        for part in parts:
            if step > 0:

                @pl.when(me >= step)
                def _():
                    coming(step - 1, *part, True).wait_recv()

            @pl.when((me < 3) & (me >= step))
            def _():
                going(step, *part, True).start()

            if step > 0:

                @pl.when(me <= 3 - step)
                def _():
                    coming(step - 1, *part, False).wait_recv()

            @pl.when((me > 0) & (me <= 3 - step))
            def _():
                going(step, *part, False).start()

        if step == 0:
            for copy in own:
                copy.start()
            ride_start(kinds, rides, arrived, ride_sems, place)
    for part in parts:

        @pl.when(me == 3)
        def _():
            coming(2, *part, True).wait_recv()

        @pl.when(me == 0)
        def _():
            coming(2, *part, False).wait_recv()

    for step in range(3):
        for part in parts:

            @pl.when((me < 3) & (me >= step))
            def _():
                going(step, *part, True).wait_send()

            @pl.when((me > 0) & (me <= 3 - step))
            def _():
                going(step, *part, False).wait_send()

    for copy in own:
        copy.wait()
    ride_end(kinds, rides, arrived, ride_sems, place)


def gather_u(arrays, collective_id, after=(), rides=()):
    n = len(arrays)
    sems = pltpu.SemaphoreType.DMA((3, 2, n))
    return communicating(
        functools.partial(gather_u_kernel, n, [kind for kind, _ in rides]),
        [jax.ShapeDtypeStruct((x.shape[0], 8) + x.shape[2:], x.dtype) for x in arrays]
        + [ride_out(kind, x) for kind, x in rides],
        arrays + [x for _, x in rides],
        [pltpu.SemaphoreType.DMA((2, n)), sems, sems, sems, sems] + (ride_scratch(len(rides)) if rides else []),
        collective_id,
        "gather_u",
        after=after,
    )


def scatter_u_kernel(kinds, *refs):
    r = len(kinds)
    p_ref, *rides = refs[: 1 + r]
    out_ref, *arrived = refs[1 + r : 2 + 2 * r]
    own, from_l, from_r, total, load, send_r, send_l, recv_l, recv_r, store, *ride_sems = refs[2 + 2 * r :]
    place = coords()
    me = place["u"]
    if kinds:
        ride_greet(kinds, place)
    greet_line(me, place, 3 * r)
    ride_start(kinds, rides, arrived, ride_sems, place)
    right, left = device(place, u=jnp.minimum(me + 1, 3)), device(place, u=jnp.maximum(me - 1, 0))

    def mine(owner, slot):
        return p_ref.at[:, owner if slot == 0 else 7 - owner]

    loads = [
        pltpu.make_async_copy(mine(k, s), own.at[k, s], load.at[k, s]) for k in range(4) for s in range(2)
    ]
    order = [3, 0, 2, 1]

    def fetch(k, s):
        return loads[2 * k + s]

    for k in order:
        for s in range(2):
            fetch(k, s).start()

    def rightward(e, s):
        src = from_l.at[e, s]
        return remote(src, from_l.at[e, s], send_r.at[e, s], recv_l.at[e, s], right)

    def rightward_first(e, s):
        return remote(own.at[3 - e, s], from_l.at[e, s], send_r.at[e, s], recv_l.at[e, s], right)

    def leftward(k, s):
        return remote(from_r.at[k, s], from_r.at[k, s], send_l.at[k, s], recv_r.at[k, s], left)

    def leftward_first(k, s):
        return remote(own.at[k, s], from_r.at[k, s], send_l.at[k, s], recv_r.at[k, s], left)

    def add(into, other):
        into[...] = (into[...].astype(f32) + other[...].astype(f32)).astype(into.dtype)

    for s in range(2):
        for k in order:
            fetch(k, s).wait()
        for e in range(3):

            @pl.when(me == 0)
            def _():
                rightward_first(e, s).start()

            @pl.when(me == 3)
            def _():
                leftward_first(e, s).start()

    for e in range(3):
        for s in range(2):

            @pl.when((me > 0) & (me < 3 - e))
            def _():
                rightward(e, s).wait_recv()
                add(from_l.at[e, s], own.at[3 - e, s])
                rightward(e, s).start()

            @pl.when((me < 3) & (me > e))
            def _():
                leftward(e, s).wait_recv()
                add(from_r.at[e, s], own.at[e, s])
                leftward(e, s).start()

    stores = [pltpu.make_async_copy(total.at[s], out_ref.at[:, s], store.at[s]) for s in range(2)]
    for s in range(2):
        total[s] = own[me, s].astype(f32)

        @pl.when(me > 0)
        def _():
            e = jnp.minimum(3 - me, 2)
            rightward(e, s).wait_recv()
            total[s] += from_l[e, s].astype(f32)

        @pl.when(me < 3)
        def _():
            e = jnp.minimum(me, 2)
            leftward(e, s).wait_recv()
            total[s] += from_r[e, s].astype(f32)

        stores[s].start()
    for e in range(3):
        for s in range(2):

            @pl.when(me < 3 - e)
            def _():
                rightward(e, s).wait_send()

            @pl.when(me > e)
            def _():
                leftward(e, s).wait_send()

    for copy in stores:
        copy.wait()
    ride_end(kinds, rides, arrived, ride_sems, place)


def scatter_u(x, rides=(), after=()):
    groups, _, half, cols = x.shape
    piece = (groups, half, cols)
    sems = pltpu.SemaphoreType.DMA((3, 2))
    return communicating(
        functools.partial(scatter_u_kernel, [kind for kind, _ in rides]),
        [jax.ShapeDtypeStruct((groups, 2, half, cols), f32)] + [ride_out(kind, x) for kind, x in rides],
        [x] + [x for _, x in rides],
        [
            pltpu.VMEM((4, 2) + piece, x.dtype),
            pltpu.VMEM((3, 2) + piece, x.dtype),
            pltpu.VMEM((3, 2) + piece, x.dtype),
            pltpu.VMEM((2,) + piece, f32),
            pltpu.SemaphoreType.DMA((4, 2)),
            sems,
            sems,
            sems,
            sems,
            pltpu.SemaphoreType.DMA((2,)),
        ]
        + (ride_scratch(len(rides)) if rides else []),
        1,
        "scatter_u",
        after=after,
    )


def gather_hidden_kernel(x_ref, out_ref, keep, send_x, send_y, recv_x, recv_y):
    place = coords()
    v, f = place["v"], place["f"]
    x_to, y_to = device(place, v=1 - v), device(place, f=1 - f)
    greet([x_to, y_to])
    half = x_ref.shape[0] // 2

    def spot(row, col, h):
        start = pl.multiple_of((row * 2 + col) * 2 * half + h * half, half)
        return out_ref.at[pl.ds(start, half)]

    def own(h):
        return x_ref.at[pl.ds(h * half, half)]

    def via_x(src, dst, i):
        return remote(src, dst, send_x.at[i], recv_x.at[i], x_to)

    def via_y(src, dst, i):
        return remote(src, dst, send_y.at[i], recv_y.at[i], y_to)

    x_own = [via_x(own(h), spot(v, f, h), h) for h in range(2)]
    y_own = [via_y(own(h), spot(v, f, h), h) for h in range(2)]
    x_own[0].start()
    y_own[1].start()
    x_own[1].start()
    y_own[0].start()
    keeps = [pltpu.make_async_copy(own(h), spot(v, f, h), keep.at[h]) for h in range(2)]
    for copy in keeps:
        copy.start()
    via_x(own(0), spot(1 - v, f, 0), 0).wait_recv()
    y_on = via_y(spot(1 - v, f, 0), spot(1 - v, f, 0), 2)
    y_on.start()
    via_y(own(1), spot(v, 1 - f, 1), 1).wait_recv()
    x_on = via_x(spot(v, 1 - f, 1), spot(v, 1 - f, 1), 2)
    x_on.start()
    via_x(own(1), spot(1 - v, f, 1), 1).wait_recv()
    via_y(own(0), spot(v, 1 - f, 0), 0).wait_recv()
    via_x(own(1), spot(1 - v, 1 - f, 1), 2).wait_recv()
    via_y(own(0), spot(1 - v, 1 - f, 0), 2).wait_recv()
    for copy in x_own + y_own + [x_on, y_on]:
        copy.wait_send()
    for copy in keeps:
        copy.wait()


def gather_hidden(x, after=()):
    rows, cols = x.shape
    sems = pltpu.SemaphoreType.DMA((3,))
    return communicating(
        gather_hidden_kernel,
        jax.ShapeDtypeStruct((4 * rows, cols), x.dtype),
        [x],
        [pltpu.SemaphoreType.DMA((2,)), sems, sems, sems, sems],
        2,
        "gather_hidden",
        after=after,
        micros=20,
    )


def scatter_hidden_kernel(p_ref, out_ref, own, got_x, got_y, total, load, send_x, send_y, recv_x, recv_y, store):
    place = coords()
    v, f = place["v"], place["f"]
    x_to, y_to = device(place, v=1 - v), device(place, f=1 - f)
    greet([x_to, y_to])
    half = total.shape[1]

    def mine(row, col, h):
        start = pl.multiple_of((row * 2 + col) * 2 * half + h * half, half)
        return p_ref.at[pl.ds(start, half)]

    corners = [(v, f), (1 - v, f), (v, 1 - f), (1 - v, 1 - f)]
    loads = [
        [pltpu.make_async_copy(mine(*corners[i], h), own.at[i, h], load.at[i, h]) for h in range(2)]
        for i in range(4)
    ]
    for i in (3, 1, 2, 0):
        for h in range(2):
            loads[i][h].start()

    def via_x(src, i):
        return remote(src, got_x.at[i], send_x.at[i], recv_x.at[i], x_to)

    def via_y(src, i):
        return remote(src, got_y.at[i], send_y.at[i], recv_y.at[i], y_to)

    loads[3][0].wait()
    x_far = via_x(own.at[3, 0], 0)
    x_far.start()
    loads[3][1].wait()
    y_far = via_y(own.at[3, 1], 0)
    y_far.start()
    loads[1][0].wait()
    x_near = via_x(own.at[1, 0], 1)
    x_near.start()
    loads[2][1].wait()
    y_near = via_y(own.at[2, 1], 2)
    y_near.start()

    def add(into, other):
        into[...] = (into[...].astype(f32) + other[...].astype(f32)).astype(into.dtype)

    loads[2][0].wait()
    x_far.wait_recv()
    add(own.at[2, 0], got_x.at[0])
    y_sum = via_y(own.at[2, 0], 1)
    y_sum.start()
    loads[1][1].wait()
    y_far.wait_recv()
    add(own.at[1, 1], got_y.at[0])
    x_sum = via_x(own.at[1, 1], 2)
    x_sum.start()
    stores = [
        pltpu.make_async_copy(total.at[h], out_ref.at[pl.ds(h * half, half)], store.at[h]) for h in range(2)
    ]
    loads[0][0].wait()
    loads[0][1].wait()
    x_near.wait_recv()
    y_near.wait_recv()
    total[0] = own[0, 0].astype(f32) + got_x[1].astype(f32)
    total[1] = own[0, 1].astype(f32) + got_y[2].astype(f32)
    y_sum.wait_recv()
    total[0] += got_y[1].astype(f32)
    stores[0].start()
    x_sum.wait_recv()
    total[1] += got_x[2].astype(f32)
    stores[1].start()
    for copy in (x_far, y_far, x_near, y_near, x_sum, y_sum):
        copy.wait_send()
    for copy in stores:
        copy.wait()


def scatter_hidden(x):
    rows, cols = x.shape[0] // 4, x.shape[1]
    half = (rows // 2, cols)
    sems = pltpu.SemaphoreType.DMA((3,))
    return communicating(
        scatter_hidden_kernel,
        jax.ShapeDtypeStruct((rows, cols), f32),
        [x],
        [
            pltpu.VMEM((4, 2) + half, x.dtype),
            pltpu.VMEM((3,) + half, x.dtype),
            pltpu.VMEM((3,) + half, x.dtype),
            pltpu.VMEM((2,) + half, f32),
            pltpu.SemaphoreType.DMA((4, 2)),
            sems,
            sems,
            sems,
            sems,
            pltpu.SemaphoreType.DMA((2,)),
        ],
        3,
        "scatter_hidden",
    )


FLIP = [(0, 1), (1, 0)]


def head_sum_start(x, sizes):
    _, many, nv, nc, nf = sizes
    x = x.reshape(many, nv, nc, nf, x.shape[0] // (many * nv * nc * nf), x.shape[1])
    x = lax.psum_scatter(x, "w", scatter_dimension=0, tiled=False) if many > 1 else x[0]
    core = lax.axis_index("core")
    mine, other = (lax.dynamic_index_in_dim(x, k, 1, False) for k in (core, 1 - core))
    x = mine.astype(f32) + lax.ppermute(other, "core", FLIP).astype(f32)
    return x.astype(bf16).reshape((nv * nf,) + x.shape[2:])


def with_rings(x, many):
    return lax.all_gather(x, "w", axis=1) if many > 1 else x[:, None]


def scatter_keys_start(parts, many):
    parts = [x[0] for x in parts]
    if many > 1:
        parts = [lax.psum_scatter(x, "w", scatter_dimension=0, tiled=True) for x in parts]
    along = parts[2][0].astype(f32) + lax.ppermute(parts[3][0], "core", FLIP).astype(f32)
    own = parts[0][0].astype(f32) + lax.ppermute(parts[1][0], "core", FLIP).astype(f32)
    return own, along.astype(bf16)


def scatter_keys_end(own, along):
    return own + lax.ppermute(along, "v", FLIP).astype(f32)


def pieces_of(part, axes):
    me = lax.axis_index(axes)
    return [part(me ^ step) for step in (0, 3, 2, 1)]


def tied(xs, after):
    return lax.optimization_barrier((tuple(xs), tuple(after)))[0]


def scatter_pieces(pieces, axes, after=()):
    got = [
        lax.ppermute(piece, axes, [(i, i ^ step) for i in range(4)])
        for step, piece in zip((3, 2, 1), pieces[1:])
    ]
    total = pieces[0].astype(f32)
    for part in tied(got, after):
        total = total + part.astype(f32)
    return total


def pieces_u(x):
    def part(k):
        return jnp.stack(
            [lax.dynamic_index_in_dim(x, k, 0, False), lax.dynamic_index_in_dim(x, 7 - k, 0, False)], 0
        )

    return pieces_of(part, "u")


def pieces_hidden(x):
    blocks = x.reshape(4, x.shape[0] // 4, x.shape[1])
    return pieces_of(lambda k: lax.dynamic_index_in_dim(blocks, k, 0, False), HIDDEN)


def gather_hidden_async(x):
    me = lax.axis_index(HIDDEN)
    out = jnp.zeros((4,) + x.shape, x.dtype)
    for step in range(4):
        part = x if step == 0 else lax.ppermute(x, HIDDEN, [(i, i ^ step) for i in range(4)])
        out = lax.dynamic_update_index_in_dim(out, part, me ^ step, 0)
    return out.reshape(4 * x.shape[0], x.shape[1])


def gather_u_start(x):
    return [x] + [lax.ppermute(x, "u", [(i, i ^ step) for i in range(4)]) for step in (3, 2, 1)]


def gather_u_end(parts, after):
    me = lax.axis_index("u")
    out = jnp.zeros((8,) + parts[0].shape[1:], parts[0].dtype)
    for step, part in zip((0, 3, 2, 1), tied(parts, after)):
        k = me ^ step
        out = lax.dynamic_update_slice_in_dim(out, part[0:1], k, 0)
        out = lax.dynamic_update_slice_in_dim(out, part[1:2], 7 - k, 0)
    return out


def exchange_kernel(sizes, kinds, back, *refs):
    n = len(kinds)
    ins, outs = refs[:n], refs[n : 2 * n]
    send, recv, keep = refs[2 * n :]
    nu, nw, nv, nc, nf = sizes
    place = coords()
    u, w, v, core, f = (place[axis] for axis in ALL)

    def holder(kind, block):
        if kind == "heads":
            at = (u * nw + w) * nv + v
            return (block, at // (nf * nc * nv), at // (nf * nc) % nv, at // nf % nc, at % nf)
        return (u, w, block // nf, v, block % nf)

    def owner(kind, slot):
        if kind == "heads":
            at = ((w * nv + v) * nc + core) * nf + f
            return (at // (nv * nw), at // nv % nw, at % nv, slot // nf, slot % nf)
        return (u, w, core, slot // nf, slot % nf)

    def same(other):
        equal = other[0] == u
        for a, b in zip(other[1:], (w, v, core, f)):
            equal = equal & (a == b)
        return equal

    def landing(kind):
        slot = core * nf + f
        block = u if kind == "heads" else v * nf + f
        return block if back else slot

    to, frm = (owner, holder) if back else (holder, owner)
    barrier = pltpu.get_barrier_semaphore()
    waits = jnp.int32(0)
    for kind in kinds:
        for i in range(4):
            other = frm(kind, i)

            @pl.when(jnp.logical_not(same(other)))
            def _():
                pl.semaphore_signal(barrier, inc=1, device_id=other, device_id_type=MESH_IDS)

            waits = waits + jnp.where(same(to(kind, i)), 0, 1)
    pl.semaphore_wait(barrier, waits)

    def copy(a, i):
        at = landing(kinds[a])
        return remote(ins[a].at[i], outs[a].at[at], send.at[a, i], recv.at[a, at], to(kinds[a], i))

    def local(a, i):
        return pltpu.make_async_copy(ins[a].at[i], outs[a].at[landing(kinds[a])], keep.at[a])

    for stage in range(3):
        for a in range(n):
            for i in range(4):
                here = same(to(kinds[a], i))

                @pl.when(here)
                def _():
                    local(a, i).start() if stage == 0 else local(a, i).wait() if stage == 1 else None

                @pl.when(jnp.logical_not(here))
                def _():
                    copy(a, i).start() if stage == 0 else copy(a, i).wait_send() if stage == 1 else None

                if stage == 2:

                    @pl.when(jnp.logical_not(same(frm(kinds[a], i))))
                    def _():
                        remote(
                            ins[a].at[i], outs[a].at[i], send.at[a, i], recv.at[a, i], to(kinds[a], i)
                        ).wait_recv()


def exchange(sizes, arrays, kinds, back, collective_id, after=()):
    n = len(arrays)
    return pl.pallas_call(
        ignoring(functools.partial(exchange_kernel, sizes, kinds, back), n, len(after)),
        out_shape=[jax.ShapeDtypeStruct(x.shape, x.dtype) for x in arrays],
        in_specs=[HBM] * (n + len(after)),
        out_specs=[HBM] * n,
        scratch_shapes=[
            pltpu.SemaphoreType.DMA((n, 4)),
            pltpu.SemaphoreType.DMA((n, 4)),
            pltpu.SemaphoreType.DMA((n,)),
        ],
        compiler_params=pltpu.CompilerParams(
            collective_id=collective_id, has_side_effects=True, vmem_limit_bytes=16 * MIB
        ),
        cost_estimate=lasting(35),
        name="exchange_back" if back else "exchange",
    )(*arrays, *after)


def swap_blocks(sizes):
    nu, nw, nv, nc, nf = sizes
    per = nw * nv * nc * nf
    pairs = []
    for j in range(nu):
        for r in range(per):
            u, rest = divmod(r, nw * nc)
            w, core = divmod(rest, nc)
            v, f = divmod(j, nf)
            pairs.append((j * per + r, (((u * nw + w) * nv + v) * nc + core) * nf + f))
    return pairs


def pad_columns(x, cols):
    return jnp.pad(x, [(0, 0)] * (x.ndim - 1) + [(0, cols - x.shape[-1])])


def body(sizes, tokens, cotangent, segment, position, gain_attn, w_query, w_key, w_value, w_output, gain_mlp, w_gate, w_up, w_down):
    del segment
    groups, block_rows, width = tokens.shape
    rows = groups * block_rows
    half = block_rows // 2
    hidden = w_gate.shape[1]
    slab = w_gate.shape[0]
    quarter = hidden // 4
    wide = -(-quarter // 256) * 256
    nkeys = sizes[1] * sizes[2] * sizes[3]
    group_rows = 4 * rows
    head_cols = width // 4
    qkv_cols = 1792
    here = (groups, 2, half)
    there = (groups, 8, half)

    swaps = swap_blocks(sizes)
    down_swapped = lax.ppermute(w_down, ALL, swaps)
    gain_one, gain_two = gain_attn.astype(f32)[:, None], gain_mlp.astype(f32)[:, None]

    def scaled(x, gain):
        return (x.astype(f32) * gain).astype(bf16).reshape(slab, 4, -1)

    def pairs(x):
        return x[:, :, :512].reshape(slab, 4, 4, LANES)

    q4, k4, v4 = scaled(w_query, gain_one), scaled(w_key, gain_one), scaled(w_value, gain_one)
    kv4 = jnp.stack([pairs(k4), pairs(v4)], 3).reshape(slab, 4, 1024)
    qkv_local = jnp.concatenate([kv4, k4[:, :, 512:], v4[:, :, 512:], q4], 2)
    qkv_local = jnp.transpose(pad_columns(qkv_local, qkv_cols), (1, 0, 2))
    gu_local = jnp.concatenate(
        [pad_columns(scaled(w_gate, gain_two), wide), pad_columns(scaled(w_up, gain_two), wide)], 2
    )
    gu_local = jnp.transpose(gu_local, (1, 0, 2))
    qkv_local, gu_local = exchange(sizes, [qkv_local, gu_local], ["heads", "hidden"], False, 6)
    qkv_whole = lax.all_gather(qkv_local, HEAD_SUM, axis=0, tiled=True).reshape(width, qkv_cols)
    qkv_whole = lax.all_gather(qkv_local, HEAD_SUM, axis=0, tiled=True).reshape(width, qkv_cols)
    out_whole = lax.all_gather(w_output, HEAD_SUM, axis=0, tiled=True)
    out_whole = jnp.concatenate([out_whole[:512], jnp.zeros((64, width), bf16), out_whole[512:]], 0)

    sequences = range(groups)
    nlocal = lax.axis_index(KEYS)
    block = jnp.arange(8, dtype=jnp.int32)
    block = nkeys * block + jnp.where(block < 4, nlocal, nkeys - 1 - nlocal)
    text = block[:, None] * half + jnp.arange(half, dtype=jnp.int32)[None, :]
    tiles = 8 // QUERY_BLOCKS
    nq = QUERY_BLOCKS * half
    rates = jnp.exp(jnp.arange(32, dtype=f32) * (-math.log(10000.0) / 32))
    inputs, inverse_one, normed_one = [], [], []
    for g in sequences:
        x = tokens[g].astype(f32)
        inverse = lax.rsqrt(jnp.mean(x * x, -1, keepdims=True) + EPSILON)
        inputs.append(x)
        inverse_one.append(inverse)
        normed_one.append(x * inverse)
    places = jnp.broadcast_to(pad_columns(position.reshape(here), LANES)[:, :, None], (groups, 2, 8, LANES))
    upstream = [cotangent[g].astype(f32) for g in sequences]
    held_one, tables, masks, query, kv, kv_own = ([] for _ in range(6))
    before = [qkv_local]
    for g in sequences:
        sent = [normed_one[g].astype(bf16).reshape(1, 2, half, width), places[g : g + 1]]
        rides = [("gather_keys", kv_own[0].reshape(8, half, 1152))] if g > 0 else []
        held, seen, *keys = gather_u(sent, (0, 8)[g], after=before, rides=rides)
        held_one.append(held.reshape(8 * half, width))
        seen = seen[0, :, 0, :half]
        lowest = text - jnp.minimum(seen, WINDOW - 1)
        lows, highs = lowest.reshape(tiles, nq), text.reshape(tiles, nq)
        klo, khi = lows[:, 0] // KEY_TILE, highs[:, -1] // KEY_TILE + 1
        lim = jnp.stack([jnp.tile(lows, (1, 2)), jnp.tile(highs, (1, 2))], 1)
        masks.append((jnp.pad(lim, ((0, 0), (0, 6), (0, 0))), klo, khi))
        angles = seen.reshape(8 * half, 1).astype(f32) * rates[None, :]
        cos, sin = jnp.cos(angles), jnp.sin(angles)
        tables.append((jnp.concatenate([cos, cos, cos, cos], 1), jnp.concatenate([-sin, sin, -sin, sin], 1)))
        own, q = rope(matmul(held_one[g], qkv_whole), *tables[g])
        kv_own.append(own)
        before = [own]
        query.append(q)

    third, rows_gu, rows_down = width // 3, 4 * slab, -(-w_down.shape[0] // 16) * 16
    slices = 2 * wide // third
    packed = jnp.concatenate(
        [
            jnp.transpose(gu_local.reshape(rows_gu, slices, third), (1, 0, 2)).reshape(slices * rows_gu, third),
            jnp.transpose(
                jnp.pad(down_swapped, ((0, rows_down - w_down.shape[0]), (0, 0))).reshape(rows_down, 3, third),
                (1, 0, 2),
            ).reshape(3 * rows_down, third),
        ],
        0,
    )
    (packed,) = tied([packed], held_one[1:])
    packed = lax.all_gather(packed, HIDDEN_SUM, axis=0)
    down_whole = packed[:, slices * rows_gu :].reshape(2 * nkeys, 3, rows_down, third)[:, :, : w_down.shape[0]]
    down_whole = jnp.transpose(down_whole, (0, 2, 1, 3)).reshape(quarter, width)
    down_whole = jnp.pad(down_whole, ((0, wide - quarter), (0, 0)))

    def key_arrays(g, others):
        own = kv_own[g].reshape(1, 8, half, 1152)
        kv.append([with_rings(own, sizes[1]), with_rings(others, sizes[1])])

    key_arrays(0, keys[0])
    (own_output,) = tied([w_output], held_one[:1])
    out_whole = lax.all_gather(own_output, HEAD_SUM, axis=0, tiled=True)
    out_whole = jnp.concatenate([out_whole[:512], jnp.zeros((64, width), bf16), out_whole[512:]], 0)
    attn, lse, parts = [], [], []
    rides = [("gather_keys", kv_own[1].reshape(8, half, 1152))]
    before = kv_own[1:]
    for g in sequences:
        out, sums, got_zero, *back_mlp = flash_forward(query[g], kv[g], *masks[g], after=before, rides=rides, ident=(9, 10)[g])
        attn.append(out)
        lse.append(sums)
        parts.append(matmul(out, out_whole).astype(bf16).reshape(8, half, width))
        if g == 0:
            key_arrays(1, got_zero)
        before, rides = [], [("scatter_u", parts[g])]
        rides += [("gather_hidden", (BRANCH_SCALE * x).astype(bf16)) for x in upstream]
    back_mlp = [x.reshape(4 * block_rows, width) for x in back_mlp]

    def own_u(x):
        me = lax.axis_index("u")
        return jnp.stack([lax.dynamic_index_in_dim(x, me, 0, False), lax.dynamic_index_in_dim(x, 7 - me, 0, False)], 0)

    def own_hidden(x):
        return lax.dynamic_index_in_dim(x, lax.axis_index(HIDDEN), 0, False)

    def total(own, got):
        return own.astype(f32) + jnp.sum(got.astype(f32), 0)

    middle, inverse_two, normed_two, held_two, activated, back_gu, back_held, mlp_part = ([] for _ in range(8))

    def to_feed_forward(g, got):
        x = inputs[g] + BRANCH_SCALE * total(own_u(parts[g]), got).reshape(block_rows, width)
        inverse = lax.rsqrt(jnp.mean(x * x, -1, keepdims=True) + EPSILON)
        middle.append(x)
        inverse_two.append(inverse)
        normed_two.append(x * inverse)
        held_two.append(gather_hidden(normed_two[g].astype(bf16)))

    def from_feed_forward(act, back_gate, back_up, back, part):
        activated.append(act)
        back_gu.append([back_gate, back_up])
        back_held.append(back.reshape(4, block_rows, width))
        mlp_part.append(part.reshape(4, block_rows, width))

    to_feed_forward(0, got_zero)
    *results, got_one = feed_forward(
        held_two[0], back_mlp[0], packed, down_whole, rides=[("scatter_u", parts[1])], ident=11
    )
    from_feed_forward(*results)
    back_middle, sent = [], []

    def to_attention(g, sums):
        x = upstream[g] + rms_back(sums, normed_two[g], inverse_two[g])
        back_middle.append(x)
        sent.append((BRANCH_SCALE * x).astype(bf16).reshape(2, half, width))

    to_attention(0, scatter_hidden(back_held[0].reshape(4 * block_rows, width)))
    to_feed_forward(1, got_one)
    *results, back_branch_zero, got_mlp = feed_forward(
        held_two[1],
        back_mlp[1],
        packed,
        down_whole,
        after=sent,
        rides=[("gather_u", sent[0]), ("scatter_hidden", mlp_part[0])],
        ident=12,
    )
    from_feed_forward(*results)
    layer_out = [(middle[0] + BRANCH_SCALE * total(own_hidden(mlp_part[0]), got_mlp)).astype(bf16)]
    gu_term, got_one = weight_gradient(held_two, back_gu, rides=[("scatter_hidden", back_held[1])], ident=13)
    to_attention(1, total(own_hidden(back_held[1]), got_one))
    back_branch = [back_branch_zero.reshape(8 * half, width)]
    dkv_own, dkv_along, dq = [], [], []
    rides = [("gather_u", sent[1]), ("scatter_hidden", mlp_part[1])]
    before = []
    for g in sequences:
        do = times_transposed(back_branch[g], out_whole).astype(bf16)
        lim, klo, khi = masks[g]
        dq_part, *rest = flash_backward(
            query[g], do, attn[g], kv[g], lim, lse[g], klo, khi, after=before, rides=rides, ident=14
        )
        if g == 0:
            back_branch.append(rest[4].reshape(8 * half, width))
            layer_out.append((middle[1] + BRANCH_SCALE * total(own_hidden(mlp_part[1]), rest[5])).astype(bf16))
            dq_part, gu_term = lax.optimization_barrier((dq_part, gu_term))
            gu_sum = lax.psum_scatter(gu_term, HIDDEN_SUM, scatter_dimension=0, tiled=True)
        dq.append(dq_part)
        own, along = scatter_keys_start(rest[:4], sizes[1])
        dkv_own.append(own)
        dkv_along.append(along)
        before, rides = [along], []
    (out_term,) = weight_gradient(attn, [[x] for x in back_branch], tile=LANES, after=[along])
    out_half = head_sum_start(jnp.concatenate([out_term[:512], out_term[576:]], 0), sizes)
    (down_term,) = weight_gradient(activated, [[back_mlp[i]] for i in sequences], after=[out_term])
    before = [down_term]
    back_qkv, late, grad_tokens = [], [], []
    for g in sequences:
        dkv = scatter_keys_end(dkv_own[g], dkv_along[g]).reshape(8 * half, 1152)
        back_qkv.append(unrope(dkv, dq[g], *tables[g], after=before))
        part = times_transposed(back_qkv[g], qkv_whole).astype(bf16)
        late.append(part.reshape(8, half, width))
        before = [part]
    qkv_term, got, out_got = weight_gradient(
        held_one,
        [[x] for x in back_qkv],
        after=before,
        rides=[("scatter_u", late[0]), ("scatter_hidden", out_half)],
        ident=15,
    )
    grad_output = total(own_hidden(out_half), out_got)
    down_term, gu_sum, qkv_term = lax.optimization_barrier((down_term, gu_sum, qkv_term))
    down_sum = down_term[:quarter].reshape(2 * nkeys, w_down.shape[0], width)
    down_sum = lax.psum_scatter(down_sum, HIDDEN_SUM, scatter_dimension=0, tiled=False)
    qkv_half = head_sum_start(qkv_term, sizes)
    late_one, qkv_got = scatter_u(late[1][None], rides=[("scatter_hidden", qkv_half)])
    qkv_sum = total(own_hidden(qkv_half), qkv_got).astype(bf16)
    for g, part in enumerate((total(own_u(late[0]), got), late_one)):
        part = part.reshape(block_rows, width)
        x = back_middle[g] + rms_back(part, normed_one[g], inverse_one[g])
        grad_tokens.append(x.astype(bf16))
    layer_out, grad_tokens = jnp.stack(layer_out, 0), jnp.stack(grad_tokens, 0)

    def along(weight, grad):
        return jnp.sum(weight.astype(f32) * grad, -1)

    qkv_sum, gu_sum = exchange(
        sizes,
        [qkv_sum.reshape(4, slab, qkv_cols), gu_sum.reshape(4, slab, 2 * wide)],
        ["heads", "hidden"],
        True,
        7,
        after=[grad_tokens],
    )
    gu_sum = jnp.transpose(gu_sum, (1, 0, 2)).astype(f32)
    grad_gate = gu_sum[:, :, :quarter].reshape(slab, hidden)
    grad_up = gu_sum[:, :, wide : wide + quarter].reshape(slab, hidden)
    grad_gain_mlp = along(w_gate, grad_gate) + along(w_up, grad_up)
    grad_gate, grad_up = grad_gate * gain_two, grad_up * gain_two
    grad_down = lax.ppermute(down_sum, ALL, [(b, a) for a, b in swaps]).astype(f32)

    qkv_sum = jnp.transpose(qkv_sum, (1, 0, 2)).astype(f32)
    kv_sum = qkv_sum[:, :, :1024].reshape(slab, 4, 4, 2, LANES)
    grad_key = jnp.concatenate(
        [kv_sum[:, :, :, 0].reshape(slab, 4, 512), qkv_sum[:, :, 1024:1088]], 2
    ).reshape(slab, width)
    grad_value = jnp.concatenate(
        [kv_sum[:, :, :, 1].reshape(slab, 4, 512), qkv_sum[:, :, 1088:1152]], 2
    ).reshape(slab, width)
    grad_query = qkv_sum[:, :, 1152:1728].reshape(slab, width)
    grad_gain_attn = along(w_query, grad_query) + along(w_key, grad_key) + along(w_value, grad_value)
    return (
        layer_out,
        grad_tokens,
        grad_gain_attn,
        grad_query * gain_one,
        grad_key * gain_one,
        grad_value * gain_one,
        grad_output,
        grad_gain_mlp,
        grad_gate,
        grad_up,
        grad_down,
    )


def solution(mesh):
    ctx, fsdp = mesh.shape["ctx"], mesh.shape["fsdp"]
    sizes = (4, ctx // 16, 2, 2, fsdp)
    fine = Mesh(mesh.devices.reshape(sizes), ALL)
    blocks = ("u", "w", "v", "core")
    act = P("f", blocks, None)
    ids = P("f", blocks)
    gain, weight = P(ALL), P(ALL, None)
    return jax.shard_map(
        functools.partial(body, sizes),
        mesh=fine,
        in_specs=(act, act, ids, ids, gain, weight, weight, weight, weight, gain, weight, weight, weight),
        out_specs=(act, act, gain, weight, weight, weight, weight, gain, weight, weight, weight),
        check_vma=False,
    )
```

```python
import functools
import math

import jax
import jax.numpy as jnp
from jax import lax
from jax.experimental import pallas as pl
from jax.experimental.pallas import tpu as pltpu
from jax.sharding import Mesh, PartitionSpec as P

HEADS = 36
HEAD_DIM = 64
WINDOW = 1024
EPSILON = 1e-05
BRANCH_SCALE = 1.4 / math.sqrt(40.0)
NEG_LARGE = -1e30
LANES = 128
PAIRS = 5
KEY_TILE = 256
QUERY_BLOCKS = 2
MIB = 1024 * 1024

f32, bf16 = jnp.float32, jnp.bfloat16


def matmul(left, right):
    return jnp.dot(left, right, preferred_element_type=f32)


def times_transposed(left, right):
    return lax.dot_general(left, right, (((1,), (1,)), ((), ())), preferred_element_type=f32)


def transposed_times(left, right):
    return lax.dot_general(left, right, (((0,), (0,)), ((), ())), preferred_element_type=f32)


def rms_back(upstream, normed, inverse):
    return inverse * (upstream - normed * jnp.mean(upstream * normed, -1, keepdims=True))


HBM = pl.BlockSpec(memory_space=pl.ANY)


def ignoring(kernel, args, extra):
    return lambda *refs: kernel(*refs[:args], *refs[args + extra :])


def lasting(micros):
    return pl.CostEstimate(flops=0, bytes_accessed=micros * 3_600_000, transcendentals=0)


MESH_IDS = pl.DeviceIdType.MESH
ALL = ("u", "w", "v", "core", "f")
KEYS = ("w", "v", "core")
HEAD_SUM = ("w", "v", "core", "f")
HIDDEN = ("v", "f")
HIDDEN_SUM = ("u", "w", "core")


def coords():
    return {axis: lax.axis_index(axis) for axis in ALL}


def device(place, **moved):
    return tuple(moved.get(axis, place[axis]) for axis in ALL)


def remote(src, dst, send, recv, where):
    return pltpu.make_async_remote_copy(
        src_ref=src, dst_ref=dst, send_sem=send, recv_sem=recv, device_id=where, device_id_type=MESH_IDS
    )


def ride_out(kind, x):
    shape = {
        "gather_u": (8,) + x.shape[1:],
        "scatter_u": (3, 2) + x.shape[1:],
        "gather_hidden": (4,) + x.shape,
        "scatter_hidden": (3,) + x.shape[1:],
        "gather_keys": (3,) + x.shape,
    }
    return jax.ShapeDtypeStruct(shape[kind], x.dtype)


def partner(kind, place, step):
    if kind in ("gather_u", "scatter_u"):
        k = place["u"] ^ step
        return k, device(place, u=k)
    if kind == "gather_keys":
        k = (2 * place["v"] + place["core"]) ^ step
        return k, device(place, v=k // 2, core=k % 2)
    k = (2 * place["v"] + place["f"]) ^ step
    return k, device(place, v=k // 2, f=k % 2)


def ride_slices(kind, src, dst, place, step):
    k, _ = partner(kind, place, step)
    u, t = place["u"], 2 * place["v"] + place["f"]
    if kind == "gather_u":
        return [(src.at[s], dst.at[7 - u if s else u], dst.at[7 - k if s else k]) for s in range(2)]
    if kind == "scatter_u":
        return [(src.at[7 - k if s else k], dst.at[step - 1, s], dst.at[step - 1, s]) for s in range(2)]
    if kind == "gather_hidden":
        return [(src, dst.at[t], dst.at[k])]
    if kind == "scatter_hidden":
        return [(src.at[k], dst.at[step - 1], dst.at[step - 1])]
    return [(src, dst.at[step - 1], dst.at[step - 1])]


def ride_copies(kind, src, dst, send, recv, keep, place, part):
    u, t = place["u"], 2 * place["v"] + place["f"]
    if part == "own":
        if kind == "gather_u":
            return [pltpu.make_async_copy(src.at[s], dst.at[7 - u if s else u], keep.at[s]) for s in range(2)]
        return [pltpu.make_async_copy(src, dst.at[t], keep.at[0])] if kind == "gather_hidden" else []
    copies = []
    if kind == "gather_keys" and part == "on":
        _, to = partner(kind, place, 1)
        return [remote(dst.at[1], dst.at[2], send.at[4], recv.at[4], to)]
    for step in (3, 2, 1):
        if kind == "gather_keys" and step == 3:
            continue
        _, to = partner(kind, place, step)
        for i, (here, there, landing) in enumerate(ride_slices(kind, src, dst, place, step)):
            at = 2 * step - 2 + i
            if part == "away":
                copies.append(remote(here, there, send.at[at], recv.at[at], to))
            else:
                copies.append(remote(landing, landing, send.at[at], recv.at[at], to))
    return copies


def ride_greet(kinds, place):
    barrier = pltpu.get_barrier_semaphore()
    for kind in kinds:
        for step in range(1, 4):
            _, to = partner(kind, place, step)
            pl.semaphore_signal(barrier, inc=1, device_id=to, device_id_type=MESH_IDS)


def ride_start(kinds, rides, arrived, sems, place):
    for a, kind in enumerate(kinds):
        for part in ("away", "own"):
            for copy in ride_copies(kind, rides[a], arrived[a], *(sem.at[a] for sem in sems), place, part):
                copy.start()


def ride_end(kinds, rides, arrived, sems, place):
    def copies(a, part):
        return ride_copies(kinds[a], rides[a], arrived[a], *(sem.at[a] for sem in sems), place, part)

    keys = [a for a, kind in enumerate(kinds) if kind == "gather_keys"]
    for a in keys:
        for copy in copies(a, "back"):
            copy.wait_recv()
        for copy in copies(a, "on"):
            copy.start()
    for a in range(len(kinds)):
        for copy in copies(a, "away"):
            copy.wait_send()
        for copy in copies(a, "own"):
            copy.wait()
        for copy in copies(a, "back") if a not in keys else ():
            copy.wait_recv()
    for a in keys:
        for copy in copies(a, "on"):
            copy.wait()


def ride_scratch(n):
    return [pltpu.SemaphoreType.DMA((n, 6)), pltpu.SemaphoreType.DMA((n, 6)), pltpu.SemaphoreType.DMA((n, 2))]


def riding(kernel, args, extra, outs, kinds, grid):
    n = len(kinds)

    def whole(*refs):
        ins, rides = refs[:args], refs[args : args + n]
        rest = refs[args + n + extra :]
        results, arrived, scratch = rest[:outs], rest[outs : outs + n], rest[outs + n : len(rest) - 3]
        sems = rest[len(rest) - 3 :]
        place = coords()
        ids = [pl.program_id(i) for i in range(len(grid))]
        first, last = ids[0] == 0, ids[0] == grid[0] - 1
        for i in range(1, len(grid)):
            first, last = first & (ids[i] == 0), last & (ids[i] == grid[i] - 1)

        @pl.when(first)
        def _():
            ride_greet(kinds, place)
            pl.semaphore_wait(pltpu.get_barrier_semaphore(), 3 * n)
            ride_start(kinds, rides, arrived, sems, place)

        kernel(*ins, *results, *scratch)

        @pl.when(last)
        def _():
            ride_end(kinds, rides, arrived, sems, place)

    return whole


def grid_call(kernel, grid, args, in_specs, out_specs, out_shape, scratch, name, micros, after=(), rides=(), ident=None):
    limit = 56 * MIB
    if not rides:
        return pl.pallas_call(
            ignoring(kernel, len(args), len(after)),
            grid=grid,
            in_specs=in_specs + [HBM] * len(after),
            out_specs=out_specs,
            out_shape=out_shape,
            scratch_shapes=scratch,
            compiler_params=pltpu.CompilerParams(vmem_limit_bytes=limit),
            cost_estimate=lasting(micros),
            name=name,
        )(*args, *after)
    kinds = [kind for kind, _ in rides]
    n = len(rides)
    return pl.pallas_call(
        riding(kernel, len(args), len(after), len(out_shape), kinds, grid),
        grid=grid,
        in_specs=in_specs + [HBM] * (n + len(after)),
        out_specs=out_specs + [HBM] * n,
        out_shape=out_shape + [ride_out(kind, x) for kind, x in rides],
        scratch_shapes=scratch + ride_scratch(n),
        compiler_params=pltpu.CompilerParams(vmem_limit_bytes=limit, collective_id=ident, has_side_effects=True),
        cost_estimate=lasting(max(micros, 50)),
        name=name + "_riding",
    )(*args, *[x for _, x in rides], *after)


def swap_halves(x):
    lane = lax.broadcasted_iota(jnp.int32, x.shape, 1)
    return jnp.where(lane % 64 < 32, pltpu.roll(x, LANES - 32, 1), pltpu.roll(x, 32, 1))


def rope_kernel(raw_ref, cos_ref, sin_ref, kv_ref, q_ref):
    cos, sin = cos_ref[...], sin_ref[...]

    def turn(x):
        return x * cos + swap_halves(x) * sin

    for p in range(4):
        kv_ref[:, 256 * p : 256 * p + 128] = turn(raw_ref[:, 256 * p : 256 * p + 128]).astype(bf16)
        kv_ref[:, 256 * p + 128 : 256 * p + 256] = raw_ref[:, 256 * p + 128 : 256 * p + 256].astype(bf16)
    last = raw_ref[:, 1024:1152]
    lane = lax.broadcasted_iota(jnp.int32, last.shape, 1)
    kv_ref[:, 1024:1152] = jnp.where(lane < 64, turn(last), last).astype(bf16)
    for p in range(5):
        q_ref[:, 128 * p : 128 * p + 128] = turn(raw_ref[:, 1152 + 128 * p : 1280 + 128 * p]).astype(bf16)


def rope(raw, cos, sin):
    rows = raw.shape[0]
    tile = min(256, rows)
    row = lambda cols: pl.BlockSpec((tile, cols), lambda i: (i, 0))
    return pl.pallas_call(
        rope_kernel,
        grid=(rows // tile,),
        in_specs=[row(1792), row(LANES), row(LANES)],
        out_specs=[row(1152), row(640)],
        out_shape=[jax.ShapeDtypeStruct((rows, 1152), bf16), jax.ShapeDtypeStruct((rows, 640), bf16)],
        compiler_params=pltpu.CompilerParams(vmem_limit_bytes=40 * MIB),
        name="rope",
    )(raw, cos, sin)


def unrope_kernel(dkv_ref, dq_ref, cos_ref, sin_ref, out_ref):
    cos, sin = cos_ref[...], sin_ref[...]

    def turn(x):
        return x * cos - swap_halves(x) * sin

    for p in range(4):
        a = 256 * p
        out_ref[:, a : a + 128] = turn(dkv_ref[:, a : a + 128].astype(f32)).astype(bf16)
        out_ref[:, a + 128 : a + 256] = dkv_ref[:, a + 128 : a + 256].astype(bf16)
    last = dkv_ref[:, 1024:1152].astype(f32)
    lane = lax.broadcasted_iota(jnp.int32, last.shape, 1)
    out_ref[:, 1024:1152] = jnp.where(lane < 64, turn(last), last).astype(bf16)
    for p in range(5):
        out_ref[:, 1152 + 128 * p : 1280 + 128 * p] = turn(
            dq_ref[:, 128 * p : 128 * p + 128].astype(f32)
        ).astype(bf16)


def unrope(dkv, dq, cos, sin, after=()):
    rows = dkv.shape[0]
    tile = min(256, rows)
    row = lambda cols: pl.BlockSpec((tile, cols), lambda i: (i, 0))
    return pl.pallas_call(
        ignoring(unrope_kernel, 4, len(after)),
        grid=(rows // tile,),
        in_specs=[row(1152), row(640), row(LANES), row(LANES)] + [HBM] * len(after),
        out_specs=row(1792),
        out_shape=jax.ShapeDtypeStruct((rows, 1792), bf16),
        compiler_params=pltpu.CompilerParams(vmem_limit_bytes=40 * MIB),
        name="unrope",
    )(dkv, dq, cos, sin, *after)


def hidden_blocks(sizes):
    nu, nw, nv, nc, nf = sizes
    out = []
    for i in range(nu * nw * nv * nc * nf):
        rest, f = divmod(i, nf)
        rest, core = divmod(rest, nc)
        uw, v = divmod(rest, nv)
        out.append((v * nf + f, uw * nc + core))
    return out


def pack_kernel(spots, block, q_ref, k_ref, v_ref, g_ref, u_ref, one_ref, two_ref, qkv_ref, gu_ref):
    slab = q_ref.shape[0]
    one, two = one_ref[...], two_ref[...]
    padded = 4 * gu_ref.shape[3] // 2 // len(spots) * gu_ref.shape[0]

    def scaled(ref, start, size, gain):
        return ref[:, start : start + size].astype(f32) * gain

    for t in range(4):
        cols = []
        at = 576 * t
        for p in range(4):
            cols.append(scaled(k_ref, at + 128 * p, 128, one))
            cols.append(scaled(v_ref, at + 128 * p, 128, one))
        cols.append(scaled(k_ref, at + 512, 64, one))
        cols.append(scaled(v_ref, at + 512, 64, one))
        cols.append(scaled(q_ref, at, 576, one))
        cols.append(jnp.zeros((slab, 64), f32))
        qkv_ref[t] = jnp.concatenate(cols, 1).astype(bf16)
        mine = sorted((place, i) for i, (owner, place) in enumerate(spots) if owner == t)
        for half, ref in enumerate((g_ref, u_ref)):
            cols = []
            for _, i in mine:
                cols.append(scaled(ref, i * block, block, two))
                cols.append(jnp.zeros((slab, padded - block), f32))
            whole = jnp.concatenate(cols, 1).astype(bf16)
            cut = gu_ref.shape[3]
            for s in range(2):
                gu_ref[t, 2 * half + s] = whole[:, s * cut : (s + 1) * cut]


def pack_weights(sizes, w_query, w_key, w_value, w_gate, w_up, gain_one, gain_two, block, padded):
    slab = w_query.shape[0]
    spots = hidden_blocks(sizes)
    cut = padded * len(spots) // 8
    return pl.pallas_call(
        functools.partial(pack_kernel, spots, block),
        out_shape=[jax.ShapeDtypeStruct((4, slab, 1792), bf16), jax.ShapeDtypeStruct((4, 4, slab, cut), bf16)],
        compiler_params=pltpu.CompilerParams(vmem_limit_bytes=48 * MIB),
        cost_estimate=lasting(10),
        name="pack_weights",
    )(w_query, w_key, w_value, w_gate, w_up, gain_one, gain_two)


def unpack_kernel(
    spots, block, padded, qkv_ref, gu_ref, q_ref, k_ref, v_ref, g_ref, u_ref, one_ref, two_ref,
    dq_ref, dk_ref, dv_ref, dg_ref, du_ref, done_ref, dtwo_ref,
):
    one, two = one_ref[...], two_ref[...]
    gains = jnp.zeros_like(one)
    wide = gu_ref.shape[2] // 2

    def part(t, start, size):
        return qkv_ref[t, :, start : start + size].astype(f32)

    for ref, out, first, last in ((k_ref, dk_ref, 0, 1024), (v_ref, dv_ref, 128, 1088)):
        cols = []
        for t in range(4):
            cols += [part(t, first + 256 * p, 128) for p in range(4)] + [part(t, last, 64)]
        grad = jnp.concatenate(cols, 1)
        gains = gains + jnp.sum(ref[...].astype(f32) * grad, 1, keepdims=True)
        out[...] = grad * one
    grad = jnp.concatenate([part(t, 1152, 576) for t in range(4)], 1)
    done_ref[...] = gains + jnp.sum(q_ref[...].astype(f32) * grad, 1, keepdims=True)
    dq_ref[...] = grad * one
    gains = jnp.zeros_like(two)
    for half, (ref, out) in enumerate(((g_ref, dg_ref), (u_ref, du_ref))):
        grad = jnp.concatenate(
            [
                gu_ref[t, :, half * wide + place * padded : half * wide + place * padded + block].astype(f32)
                for t, place in spots
            ],
            1,
        )
        gains = gains + jnp.sum(ref[...].astype(f32) * grad, 1, keepdims=True)
        out[...] = grad * two
    dtwo_ref[...] = gains


def unpack_gradients(sizes, qkv, gu, w_query, w_key, w_value, w_gate, w_up, gain_one, gain_two, block, padded):
    slab, width = w_query.shape
    hidden = w_gate.shape[1]
    shape = lambda cols: jax.ShapeDtypeStruct((slab, cols), f32)
    return pl.pallas_call(
        functools.partial(unpack_kernel, hidden_blocks(sizes), block, padded),
        out_shape=[shape(width)] * 3 + [shape(hidden)] * 2 + [shape(1)] * 2,
        compiler_params=pltpu.CompilerParams(vmem_limit_bytes=48 * MIB),
        cost_estimate=lasting(15),
        name="unpack_gradients",
    )(qkv, gu, w_query, w_key, w_value, w_gate, w_up, gain_one, gain_two)


def stack_heads(x, first, second):
    return jnp.concatenate([jnp.where(first, x, 0), jnp.where(second, x, 0)], 0)


def text_rows(source, ring, j, half, many):
    v, core = lax.axis_index("v"), lax.axis_index("core")
    v = 1 - v if source // 2 else v
    core = 1 - core if source % 2 else core
    at = (ring * 2 + v) * 2 + core
    block = many * j + (at if j < 4 else many - 1 - at)
    return pl.multiple_of(block * half, half)


def assemble(kv_refs, kv_s):
    rings, _, half, _ = kv_refs[0].shape
    for source, ref in enumerate(kv_refs):
        for ring in range(rings):
            for j in range(8):
                kv_s[pl.ds(text_rows(source, ring, j, half, 4 * rings), half), :] = ref[ring, j]


def flash_forward_kernel(
    bounds, q_ref, kv0, kv1, kv2, kv3, lim_ref, o_ref, lse_ref, kv_s, s_ref, vt_ref
):
    p, t = pl.program_id(0), pl.program_id(1)
    nq = q_ref.shape[0]
    tail = p == 4
    voff = pl.multiple_of(jnp.where(tail, 0, LANES), LANES)
    tiles = s_ref.shape[0]

    @pl.when(t == 0)
    def _():
        assemble((kv0, kv1, kv2, kv3), kv_s)
        for k in range(tiles):
            vt_ref[k] = kv_s[k * KEY_TILE : (k + 1) * KEY_TILE, pl.ds(voff, LANES)].T

    lane = lax.broadcasted_iota(jnp.int32, (nq, LANES), 1)
    qm = stack_heads(q_ref[...] * bf16(0.125), lane < 64, lane >= 64)
    lo, hi = lim_ref[0, 0:1, :], lim_ref[0, 1:2, :]
    row = lax.broadcasted_iota(jnp.int32, (KEY_TILE, 2 * nq), 0)
    klo, khi = bounds(t)

    def scores(k, high):
        base = pl.multiple_of(k * KEY_TILE, KEY_TILE)
        s = times_transposed(kv_s[pl.ds(base, KEY_TILE), 0:LANES], qm)
        s = jnp.where((row >= lo - base) & (row <= hi - base), s, NEG_LARGE)
        s_ref[k] = s
        return jnp.maximum(high, jnp.max(s.reshape(KEY_TILE // 8, 8, 2 * nq), 0))

    high = lax.fori_loop(klo, khi, scores, jnp.full((8, 2 * nq), NEG_LARGE, f32))
    high = jnp.max(high, 0, keepdims=True)

    def mix(k, carry):
        total, acc = carry
        w = jnp.exp(s_ref[k] - high)
        total = total + jnp.sum(w.reshape(KEY_TILE // 8, 8, 2 * nq), 0)
        acc = acc + matmul(vt_ref[k], w.astype(bf16))
        return total, acc

    total, acc = lax.fori_loop(
        klo, khi, mix, (jnp.zeros((8, 2 * nq), f32), jnp.zeros((LANES, 2 * nq), f32))
    )
    total = jnp.sum(total, 0, keepdims=True)
    out = (acc / total).T
    first, second = out[:nq], out[nq:]
    low = jnp.where(tail, 0.0, first)
    up = jnp.where(tail, first, second)
    o_ref[...] = jnp.where(lane < 64, low, up).astype(bf16)
    lse_ref[0, 0] = jnp.broadcast_to(high + jnp.log(total), (8, 2 * nq))


def flash_specs(rows, tiles, kv):
    nq = rows // tiles
    _, rings, _, half, _ = kv[0].shape
    part = pl.BlockSpec((nq, LANES), lambda p, t, *_: (t, p))
    keys = [
        pl.BlockSpec((None, rings, 8, half, 2 * LANES), lambda p, t, *_, i=i: (i, 0, 0, 0, p)) for i in (0, 0, 1, 2)
    ]
    lim = pl.BlockSpec((1, 8, 2 * nq), lambda p, t, *_: (t, 0, 0))
    lse = pl.BlockSpec((1, 1, 8, 2 * nq), lambda p, t, *_: (p, t, 0, 0))
    return nq, 32 * rings * half, part, keys, lim, lse


def window_bounds(rows, tiles, rings):
    half, many = rows // 8, 4 * rings

    def bounds(t):
        at = (lax.axis_index("w") * 2 + lax.axis_index("v")) * 2 + lax.axis_index("core")

        def first_row(j):
            return (many * j + jnp.where(j < 4, at, many - 1 - at)) * half

        low = jnp.maximum(first_row(t * QUERY_BLOCKS) - (WINDOW - 1), 0)
        high = first_row(t * QUERY_BLOCKS + QUERY_BLOCKS - 1) + half - 1
        return low // KEY_TILE, high // KEY_TILE + 1

    return bounds


def flash_call(kernel, name, args, klo, khi, in_specs, out_specs, out_shape, scratch, micros, after, rides, ident):
    tiles = klo.shape[0]
    grid = (PAIRS, tiles)
    if rides:
        bounds = window_bounds(args[0].shape[0], tiles, args[-3 if name == "flash_backward" else -2].shape[1])
        return grid_call(
            functools.partial(kernel, bounds), grid, args, in_specs, out_specs, out_shape, scratch, name, micros,
            after, rides, ident,
        )

    def bounded(klo_ref, khi_ref, *refs):
        kernel(lambda t: (klo_ref[t], khi_ref[t]), *refs)

    return pl.pallas_call(
        ignoring(bounded, 2 + len(args), len(after)),
        grid_spec=pltpu.PrefetchScalarGridSpec(
            num_scalar_prefetch=2,
            grid=grid,
            in_specs=in_specs + [HBM] * len(after),
            out_specs=out_specs,
            scratch_shapes=scratch,
        ),
        out_shape=out_shape,
        compiler_params=pltpu.CompilerParams(vmem_limit_bytes=56 * MIB),
        cost_estimate=lasting(micros),
        name=name,
    )(klo, khi, *args, *after)


def flash_forward(q, kv, lim, klo, khi, after=(), rides=(), ident=None):
    rows, tiles = q.shape[0], klo.shape[0]
    nq, keys, part, whole, limits, lses = flash_specs(rows, tiles, kv)
    return flash_call(
        flash_forward_kernel,
        "flash_forward",
        [q, kv[0], kv[1], kv[1], kv[1], lim],
        klo,
        khi,
        [part, *whole, limits],
        [part, lses],
        [jax.ShapeDtypeStruct((rows, 640), bf16), jax.ShapeDtypeStruct((PAIRS, tiles, 8, 2 * nq), f32)],
        [
            pltpu.VMEM((keys, 2 * LANES), bf16),
            pltpu.VMEM((keys // KEY_TILE, KEY_TILE, 2 * nq), f32),
            pltpu.VMEM((keys // KEY_TILE, LANES, KEY_TILE), bf16),
        ],
        40,
        after,
        rides,
        ident,
    )


def flash_backward_kernel(
    bounds, q_ref, do_ref, o_ref, kv0, kv1, kv2, kv3, lim_ref, lse_ref,
    dq_ref, dkv0, dkv1, dkv2, dkv3, kv_s, kt_ref, dk_ref, dv_ref,
):
    p, t = pl.program_id(0), pl.program_id(1)
    nq = q_ref.shape[0]
    tail = p == 4
    voff = pl.multiple_of(jnp.where(tail, 0, LANES), LANES)
    tiles = kt_ref.shape[0]

    @pl.when(t == 0)
    def _():
        assemble((kv0, kv1, kv2, kv3), kv_s)
        for k in range(tiles):
            kt_ref[k] = kv_s[k * KEY_TILE : (k + 1) * KEY_TILE, 0:LANES].T
        dk_ref[...] = jnp.zeros_like(dk_ref)
        dv_ref[...] = jnp.zeros_like(dv_ref)

    lane = lax.broadcasted_iota(jnp.int32, (nq, LANES), 1)
    qm = stack_heads(q_ref[...] * bf16(0.125), lane < 64, lane >= 64)
    side = jnp.where(tail, 1, 0)
    head = lane // 64
    dom = stack_heads(do_ref[...], head == side, head == 1 + side)
    back = do_ref[...].astype(f32) * o_ref[...].astype(f32)
    back = stack_heads(back, head == side, head == 1 + side)
    delta = jnp.sum(back.T, 0, keepdims=True)
    lo, hi = lim_ref[0, 0:1, :], lim_ref[0, 1:2, :]
    lse = lse_ref[0, 0, 0:1, :]
    row = lax.broadcasted_iota(jnp.int32, (KEY_TILE, 2 * nq), 0)

    def step(k, acc):
        base = pl.multiple_of(k * KEY_TILE, KEY_TILE)
        s = times_transposed(kv_s[pl.ds(base, KEY_TILE), 0:LANES], qm)
        w = jnp.exp(jnp.where((row >= lo - base) & (row <= hi - base), s - lse, NEG_LARGE))
        dp = times_transposed(kv_s[pl.ds(base, KEY_TILE), pl.ds(voff, LANES)], dom)
        ds = (w * (dp - delta)).astype(bf16)
        dv_ref[pl.ds(base, KEY_TILE), :] += matmul(w.astype(bf16), dom)
        dk_ref[pl.ds(base, KEY_TILE), :] += matmul(ds, qm)
        return acc + matmul(kt_ref[k], ds)

    acc = lax.fori_loop(*bounds(t), step, jnp.zeros((LANES, 2 * nq), f32))
    out = acc.T * 0.125
    dq_ref[...] = jnp.where(lane < 64, out[:nq], jnp.where(tail, 0.0, out[nq:]))

    @pl.when(t == pl.num_programs(1) - 1)
    def _():
        rings, _, half, _ = dkv0.shape
        for source, ref in enumerate((dkv0, dkv1, dkv2, dkv3)):
            for ring in range(rings):
                for j in range(8):
                    at = pl.ds(text_rows(source, ring, j, half, 4 * rings), half)
                    dk, dv = dk_ref[at, :], dv_ref[at, :]
                    ref[ring, j, :, 0:LANES] = jnp.where(tail, dk + dv, dk).astype(bf16)
                    ref[ring, j, :, LANES : 2 * LANES] = dv.astype(bf16)


def flash_backward(q, do, o, kv, lim, lse, klo, khi, after=(), rides=(), ident=None):
    rows, tiles = q.shape[0], klo.shape[0]
    nq, keys, part, whole, limits, lses = flash_specs(rows, tiles, kv)
    return flash_call(
        flash_backward_kernel,
        "flash_backward",
        [q, do, o, kv[0], kv[1], kv[1], kv[1], lim, lse],
        klo,
        khi,
        [part, part, part, *whole, limits, lses],
        [part] + [whole[0]] * 4,
        [jax.ShapeDtypeStruct((rows, 640), f32)] + [jax.ShapeDtypeStruct(kv[0].shape, bf16)] * 4,
        [
            pltpu.VMEM((keys, 2 * LANES), bf16),
            pltpu.VMEM((keys // KEY_TILE, LANES, KEY_TILE), bf16),
            pltpu.VMEM((keys, LANES), f32),
            pltpu.VMEM((keys, LANES), f32),
        ],
        48,
        after,
        rides,
        ident,
    )


def feed_forward_kernel(
    held_ref, back_ref, wg_ref, wu_ref, wd_ref, act_ref, bg_ref, bu_ref, bh_ref, br_ref, bh_acc, br_acc, wd_s
):
    t = pl.program_id(0)
    tile = wg_ref.shape[2]
    blocks, high, third = wd_ref.shape
    padded = high // 3

    @pl.when(t % (third // tile) == 0)
    def _():
        for b in range(blocks):
            for c in range(3):
                wd_s[b * padded : (b + 1) * padded, c * third : (c + 1) * third] = wd_ref[
                    b, c * padded : (c + 1) * padded, :
                ]

    wd = wd_s[pl.ds(pl.multiple_of(t % (third // tile) * tile, tile), tile), :]
    held = held_ref[...]
    width = held.shape[1]
    wg, wu = wg_ref[...].reshape(width, wg_ref.shape[2]), wu_ref[...].reshape(width, wu_ref.shape[2])
    gate, up = matmul(held, wg), matmul(held, wu)
    back_act = times_transposed(back_ref[...], wd)
    sig = jax.nn.sigmoid(gate)
    gs = gate * sig
    act = (gs * up).astype(bf16)
    bg = (back_act * up * sig * (1.0 + gate * (1.0 - sig))).astype(bf16)
    bu = (back_act * gs).astype(bf16)
    act_ref[...], bg_ref[...], bu_ref[...] = act, bg, bu
    bh = times_transposed(bg, wg) + times_transposed(bu, wu)
    br = matmul(act, wd)

    @pl.when(t == 0)
    def _():
        bh_acc[...] = bh
        br_acc[...] = br

    @pl.when(t > 0)
    def _():
        bh_acc[...] += bh
        br_acc[...] += br

    @pl.when(t == pl.num_programs(0) - 1)
    def _():
        bh_ref[...] = bh_acc[...].astype(bf16)
        br_ref[...] = br_acc[...].astype(bf16)


def feed_forward(held, back, packed, wide, after=(), rides=(), ident=None):
    rows, width = held.shape
    tile = 256
    tiles = wide // tile
    whole = pl.BlockSpec((rows, width), lambda t: (0, 0))
    part = pl.BlockSpec((rows, tile), lambda t: (0, t))
    many, third = packed.shape[0], packed.shape[2]
    per, blocks, high = third // tile, many * third // wide, packed.shape[1] - 4 * width // many
    first = 4 * width // many // high
    cols = lambda off: pl.BlockSpec((many, width // many, tile), lambda t: (0, (t + off) // per, (t + off) % per))
    return grid_call(
        feed_forward_kernel,
        (tiles,),
        [held, back, packed, packed, packed],
        [whole, whole, cols(0), cols(tiles), pl.BlockSpec((blocks, high, third), lambda t: (t // per, first, 0))],
        [part, part, part, whole, whole],
        [jax.ShapeDtypeStruct((rows, wide), bf16)] * 3 + [jax.ShapeDtypeStruct((rows, width), bf16)] * 2,
        [pltpu.VMEM((rows, width), f32)] * 2 + [pltpu.VMEM((third, width), bf16)],
        "feed_forward",
        42,
        after,
        rides,
        ident,
    )


def weight_gradient(lefts, rights, tile=256, after=(), rides=(), ident=None):
    many, per = len(lefts), len(rights[0])
    flat = [x for group in rights for x in group]
    rows, high = lefts[0].shape
    widths = [x.shape[1] for x in rights[0]]

    def kernel(*refs):
        ls, rs, out = refs[:many], refs[many : many + len(flat)], refs[many + len(flat)]
        start = 0
        for i, cols in enumerate(widths):
            total = transposed_times(ls[0][...], rs[i][...])
            for g in range(1, many):
                total = total + transposed_times(ls[g][...], rs[g * per + i][...])
            out[:, start : start + cols] = total.astype(bf16)
            start += cols

    return grid_call(
        kernel,
        (high // tile,),
        [*lefts, *flat],
        [pl.BlockSpec((rows, tile), lambda i: (0, i))] * many + [pl.BlockSpec(x.shape, lambda i: (0, 0)) for x in flat],
        [pl.BlockSpec((tile, sum(widths)), lambda i: (i, 0))],
        [jax.ShapeDtypeStruct((high, sum(widths)), bf16)],
        [],
        "weight_gradient",
        max(4, 2 * many * rows * high * sum(widths) // 10**9),
        after,
        rides,
        ident,
    )


def greet(places):
    barrier = pltpu.get_barrier_semaphore()
    for place in places:
        pl.semaphore_signal(barrier, inc=1, device_id=place, device_id_type=MESH_IDS)
    pl.semaphore_wait(barrier, len(places))


def greet_line(me, place, more=0):
    barrier = pltpu.get_barrier_semaphore()

    @pl.when(me > 0)
    def _():
        pl.semaphore_signal(barrier, inc=1, device_id=device(place, u=me - 1), device_id_type=MESH_IDS)

    @pl.when(me < 3)
    def _():
        pl.semaphore_signal(barrier, inc=1, device_id=device(place, u=me + 1), device_id_type=MESH_IDS)

    pl.semaphore_wait(barrier, 2 + more - jnp.where(me == 0, 1, 0) - jnp.where(me == 3, 1, 0))


def communicating(kernel, out, args, scratch, collective_id, name, vmem=40, after=(), micros=50):
    return pl.pallas_call(
        ignoring(kernel, len(args), len(after)),
        out_shape=out,
        in_specs=[HBM] * (len(args) + len(after)),
        out_specs=[HBM] * len(out) if isinstance(out, list) else HBM,
        scratch_shapes=scratch,
        compiler_params=pltpu.CompilerParams(
            collective_id=collective_id, has_side_effects=True, vmem_limit_bytes=vmem * MIB
        ),
        cost_estimate=lasting(micros),
        name=name,
    )(*args, *after)


def gather_u_kernel(n, kinds, *refs):
    r = len(kinds)
    ins, rides, outs, arrived = refs[:n], refs[n : n + r], refs[n + r : 2 * n + r], refs[2 * n + r : 2 * n + 2 * r]
    keep, send_r, send_l, recv_r, recv_l, *ride_sems = refs[2 * n + 2 * r :]
    place = coords()
    me = place["u"]
    if kinds:
        ride_greet(kinds, place)
    greet_line(me, place, 3 * r)
    right, left = device(place, u=jnp.minimum(me + 1, 3)), device(place, u=jnp.maximum(me - 1, 0))

    def spot(owner, slot, a):
        return outs[a].at[:, owner if slot == 0 else 7 - owner]

    def going(step, slot, a, rightward):
        owner = me - step if rightward else me + step
        owner = jnp.clip(owner, 0, 3)
        src = ins[a].at[:, slot] if step == 0 else spot(owner, slot, a)
        send, recv, to = (send_r, recv_l, right) if rightward else (send_l, recv_r, left)
        return remote(src, spot(owner, slot, a), send.at[step, slot, a], recv.at[step, slot, a], to)

    def coming(step, slot, a, from_left):
        owner = jnp.clip(me - 1 - step if from_left else me + 1 + step, 0, 3)
        send, recv, to = (send_r, recv_l, right) if from_left else (send_l, recv_r, left)
        there = spot(owner, slot, a)
        return remote(there, there, send.at[step, slot, a], recv.at[step, slot, a], to)

    parts = [(slot, a) for slot in range(2) for a in range(n)]
    own = [pltpu.make_async_copy(ins[a].at[:, s], spot(me, s, a), keep.at[s, a]) for s, a in parts]
    for step in range(3):
        for part in parts:
            if step > 0:

                @pl.when(me >= step)
                def _():
                    coming(step - 1, *part, True).wait_recv()

            @pl.when((me < 3) & (me >= step))
            def _():
                going(step, *part, True).start()

            if step > 0:

                @pl.when(me <= 3 - step)
                def _():
                    coming(step - 1, *part, False).wait_recv()

            @pl.when((me > 0) & (me <= 3 - step))
            def _():
                going(step, *part, False).start()

        if step == 0:
            for copy in own:
                copy.start()
            ride_start(kinds, rides, arrived, ride_sems, place)
    for part in parts:

        @pl.when(me == 3)
        def _():
            coming(2, *part, True).wait_recv()

        @pl.when(me == 0)
        def _():
            coming(2, *part, False).wait_recv()

    for step in range(3):
        for part in parts:

            @pl.when((me < 3) & (me >= step))
            def _():
                going(step, *part, True).wait_send()

            @pl.when((me > 0) & (me <= 3 - step))
            def _():
                going(step, *part, False).wait_send()

    for copy in own:
        copy.wait()
    ride_end(kinds, rides, arrived, ride_sems, place)


def gather_u(arrays, collective_id, after=(), rides=()):
    n = len(arrays)
    sems = pltpu.SemaphoreType.DMA((3, 2, n))
    return communicating(
        functools.partial(gather_u_kernel, n, [kind for kind, _ in rides]),
        [jax.ShapeDtypeStruct((x.shape[0], 8) + x.shape[2:], x.dtype) for x in arrays]
        + [ride_out(kind, x) for kind, x in rides],
        arrays + [x for _, x in rides],
        [pltpu.SemaphoreType.DMA((2, n)), sems, sems, sems, sems] + (ride_scratch(len(rides)) if rides else []),
        collective_id,
        "gather_u",
        after=after,
    )


def scatter_u_kernel(kinds, *refs):
    r = len(kinds)
    p_ref, *rides = refs[: 1 + r]
    out_ref, *arrived = refs[1 + r : 2 + 2 * r]
    own, from_l, from_r, total, load, send_r, send_l, recv_l, recv_r, store, *ride_sems = refs[2 + 2 * r :]
    place = coords()
    me = place["u"]
    if kinds:
        ride_greet(kinds, place)
    greet_line(me, place, 3 * r)
    ride_start(kinds, rides, arrived, ride_sems, place)
    right, left = device(place, u=jnp.minimum(me + 1, 3)), device(place, u=jnp.maximum(me - 1, 0))

    def mine(owner, slot):
        return p_ref.at[:, owner if slot == 0 else 7 - owner]

    loads = [
        pltpu.make_async_copy(mine(k, s), own.at[k, s], load.at[k, s]) for k in range(4) for s in range(2)
    ]
    order = [3, 0, 2, 1]

    def fetch(k, s):
        return loads[2 * k + s]

    for k in order:
        for s in range(2):
            fetch(k, s).start()

    def rightward(e, s):
        src = from_l.at[e, s]
        return remote(src, from_l.at[e, s], send_r.at[e, s], recv_l.at[e, s], right)

    def rightward_first(e, s):
        return remote(own.at[3 - e, s], from_l.at[e, s], send_r.at[e, s], recv_l.at[e, s], right)

    def leftward(k, s):
        return remote(from_r.at[k, s], from_r.at[k, s], send_l.at[k, s], recv_r.at[k, s], left)

    def leftward_first(k, s):
        return remote(own.at[k, s], from_r.at[k, s], send_l.at[k, s], recv_r.at[k, s], left)

    def add(into, other):
        into[...] = (into[...].astype(f32) + other[...].astype(f32)).astype(into.dtype)

    for s in range(2):
        for k in order:
            fetch(k, s).wait()
        for e in range(3):

            @pl.when(me == 0)
            def _():
                rightward_first(e, s).start()

            @pl.when(me == 3)
            def _():
                leftward_first(e, s).start()

    for e in range(3):
        for s in range(2):

            @pl.when((me > 0) & (me < 3 - e))
            def _():
                rightward(e, s).wait_recv()
                add(from_l.at[e, s], own.at[3 - e, s])
                rightward(e, s).start()

            @pl.when((me < 3) & (me > e))
            def _():
                leftward(e, s).wait_recv()
                add(from_r.at[e, s], own.at[e, s])
                leftward(e, s).start()

    stores = [pltpu.make_async_copy(total.at[s], out_ref.at[:, s], store.at[s]) for s in range(2)]
    for s in range(2):
        total[s] = own[me, s].astype(f32)

        @pl.when(me > 0)
        def _():
            e = jnp.minimum(3 - me, 2)
            rightward(e, s).wait_recv()
            total[s] += from_l[e, s].astype(f32)

        @pl.when(me < 3)
        def _():
            e = jnp.minimum(me, 2)
            leftward(e, s).wait_recv()
            total[s] += from_r[e, s].astype(f32)

        stores[s].start()
    for e in range(3):
        for s in range(2):

            @pl.when(me < 3 - e)
            def _():
                rightward(e, s).wait_send()

            @pl.when(me > e)
            def _():
                leftward(e, s).wait_send()

    for copy in stores:
        copy.wait()
    ride_end(kinds, rides, arrived, ride_sems, place)


def scatter_u(x, rides=(), after=()):
    groups, _, half, cols = x.shape
    piece = (groups, half, cols)
    sems = pltpu.SemaphoreType.DMA((3, 2))
    return communicating(
        functools.partial(scatter_u_kernel, [kind for kind, _ in rides]),
        [jax.ShapeDtypeStruct((groups, 2, half, cols), f32)] + [ride_out(kind, x) for kind, x in rides],
        [x] + [x for _, x in rides],
        [
            pltpu.VMEM((4, 2) + piece, x.dtype),
            pltpu.VMEM((3, 2) + piece, x.dtype),
            pltpu.VMEM((3, 2) + piece, x.dtype),
            pltpu.VMEM((2,) + piece, f32),
            pltpu.SemaphoreType.DMA((4, 2)),
            sems,
            sems,
            sems,
            sems,
            pltpu.SemaphoreType.DMA((2,)),
        ]
        + (ride_scratch(len(rides)) if rides else []),
        1,
        "scatter_u",
        after=after,
    )


def gather_hidden_kernel(x_ref, out_ref, keep, send_x, send_y, recv_x, recv_y):
    place = coords()
    v, f = place["v"], place["f"]
    x_to, y_to = device(place, v=1 - v), device(place, f=1 - f)
    greet([x_to, y_to])
    half = x_ref.shape[0] // 2

    def spot(row, col, h):
        start = pl.multiple_of((row * 2 + col) * 2 * half + h * half, half)
        return out_ref.at[pl.ds(start, half)]

    def own(h):
        return x_ref.at[pl.ds(h * half, half)]

    def via_x(src, dst, i):
        return remote(src, dst, send_x.at[i], recv_x.at[i], x_to)

    def via_y(src, dst, i):
        return remote(src, dst, send_y.at[i], recv_y.at[i], y_to)

    x_own = [via_x(own(h), spot(v, f, h), h) for h in range(2)]
    y_own = [via_y(own(h), spot(v, f, h), h) for h in range(2)]
    x_own[0].start()
    y_own[1].start()
    x_own[1].start()
    y_own[0].start()
    keeps = [pltpu.make_async_copy(own(h), spot(v, f, h), keep.at[h]) for h in range(2)]
    for copy in keeps:
        copy.start()
    via_x(own(0), spot(1 - v, f, 0), 0).wait_recv()
    y_on = via_y(spot(1 - v, f, 0), spot(1 - v, f, 0), 2)
    y_on.start()
    via_y(own(1), spot(v, 1 - f, 1), 1).wait_recv()
    x_on = via_x(spot(v, 1 - f, 1), spot(v, 1 - f, 1), 2)
    x_on.start()
    via_x(own(1), spot(1 - v, f, 1), 1).wait_recv()
    via_y(own(0), spot(v, 1 - f, 0), 0).wait_recv()
    via_x(own(1), spot(1 - v, 1 - f, 1), 2).wait_recv()
    via_y(own(0), spot(1 - v, 1 - f, 0), 2).wait_recv()
    for copy in x_own + y_own + [x_on, y_on]:
        copy.wait_send()
    for copy in keeps:
        copy.wait()


def gather_hidden(x, after=()):
    rows, cols = x.shape
    sems = pltpu.SemaphoreType.DMA((3,))
    return communicating(
        gather_hidden_kernel,
        jax.ShapeDtypeStruct((4 * rows, cols), x.dtype),
        [x],
        [pltpu.SemaphoreType.DMA((2,)), sems, sems, sems, sems],
        2,
        "gather_hidden",
        after=after,
        micros=20,
    )


def scatter_hidden_kernel(p_ref, out_ref, own, got_x, got_y, total, load, send_x, send_y, recv_x, recv_y, store):
    place = coords()
    v, f = place["v"], place["f"]
    x_to, y_to = device(place, v=1 - v), device(place, f=1 - f)
    greet([x_to, y_to])
    half = total.shape[1]

    def mine(row, col, h):
        start = pl.multiple_of((row * 2 + col) * 2 * half + h * half, half)
        return p_ref.at[pl.ds(start, half)]

    corners = [(v, f), (1 - v, f), (v, 1 - f), (1 - v, 1 - f)]
    loads = [
        [pltpu.make_async_copy(mine(*corners[i], h), own.at[i, h], load.at[i, h]) for h in range(2)]
        for i in range(4)
    ]
    for i in (3, 1, 2, 0):
        for h in range(2):
            loads[i][h].start()

    def via_x(src, i):
        return remote(src, got_x.at[i], send_x.at[i], recv_x.at[i], x_to)

    def via_y(src, i):
        return remote(src, got_y.at[i], send_y.at[i], recv_y.at[i], y_to)

    loads[3][0].wait()
    x_far = via_x(own.at[3, 0], 0)
    x_far.start()
    loads[3][1].wait()
    y_far = via_y(own.at[3, 1], 0)
    y_far.start()
    loads[1][0].wait()
    x_near = via_x(own.at[1, 0], 1)
    x_near.start()
    loads[2][1].wait()
    y_near = via_y(own.at[2, 1], 2)
    y_near.start()

    def add(into, other):
        into[...] = (into[...].astype(f32) + other[...].astype(f32)).astype(into.dtype)

    loads[2][0].wait()
    x_far.wait_recv()
    add(own.at[2, 0], got_x.at[0])
    y_sum = via_y(own.at[2, 0], 1)
    y_sum.start()
    loads[1][1].wait()
    y_far.wait_recv()
    add(own.at[1, 1], got_y.at[0])
    x_sum = via_x(own.at[1, 1], 2)
    x_sum.start()
    stores = [
        pltpu.make_async_copy(total.at[h], out_ref.at[pl.ds(h * half, half)], store.at[h]) for h in range(2)
    ]
    loads[0][0].wait()
    loads[0][1].wait()
    x_near.wait_recv()
    y_near.wait_recv()
    total[0] = own[0, 0].astype(f32) + got_x[1].astype(f32)
    total[1] = own[0, 1].astype(f32) + got_y[2].astype(f32)
    y_sum.wait_recv()
    total[0] += got_y[1].astype(f32)
    stores[0].start()
    x_sum.wait_recv()
    total[1] += got_x[2].astype(f32)
    stores[1].start()
    for copy in (x_far, y_far, x_near, y_near, x_sum, y_sum):
        copy.wait_send()
    for copy in stores:
        copy.wait()


def scatter_hidden(x):
    rows, cols = x.shape[0] // 4, x.shape[1]
    half = (rows // 2, cols)
    sems = pltpu.SemaphoreType.DMA((3,))
    return communicating(
        scatter_hidden_kernel,
        jax.ShapeDtypeStruct((rows, cols), f32),
        [x],
        [
            pltpu.VMEM((4, 2) + half, x.dtype),
            pltpu.VMEM((3,) + half, x.dtype),
            pltpu.VMEM((3,) + half, x.dtype),
            pltpu.VMEM((2,) + half, f32),
            pltpu.SemaphoreType.DMA((4, 2)),
            sems,
            sems,
            sems,
            sems,
            pltpu.SemaphoreType.DMA((2,)),
        ],
        3,
        "scatter_hidden",
    )


FLIP = [(0, 1), (1, 0)]


def head_sum_start(x, sizes, blocks=1):
    _, many, nv, nc, nf = sizes
    cols = x.shape[1]
    x = x.reshape(blocks, many, nv, nc, nf, x.shape[0] // (blocks * many * nv * nc * nf), cols)
    x = lax.psum_scatter(x, "w", scatter_dimension=1, tiled=False) if many > 1 else x[:, 0]
    core = lax.axis_index("core")
    mine, other = (
        jnp.transpose(lax.dynamic_index_in_dim(x, k, 2, False), (1, 2, 0, 3, 4)).reshape(nv * nf, -1, cols)
        for k in (core, 1 - core)
    )
    x = mine.astype(f32) + lax.ppermute(other, "core", FLIP).astype(f32)
    return x.astype(bf16)


def with_rings(x, many):
    return lax.all_gather(x, "w", axis=1) if many > 1 else x[:, None]


def scatter_keys_start(parts, many):
    parts = [x[0] for x in parts]
    if many > 1:
        parts = [lax.psum_scatter(x, "w", scatter_dimension=0, tiled=True) for x in parts]
    along = parts[2][0].astype(f32) + lax.ppermute(parts[3][0], "core", FLIP).astype(f32)
    own = parts[0][0].astype(f32) + lax.ppermute(parts[1][0], "core", FLIP).astype(f32)
    return own, along.astype(bf16)


def scatter_keys_end(own, along):
    return own + lax.ppermute(along, "v", FLIP).astype(f32)


def pieces_of(part, axes):
    me = lax.axis_index(axes)
    return [part(me ^ step) for step in (0, 3, 2, 1)]


def tied(xs, after):
    return lax.optimization_barrier((tuple(xs), tuple(after)))[0]


def scatter_pieces(pieces, axes, after=()):
    got = [
        lax.ppermute(piece, axes, [(i, i ^ step) for i in range(4)])
        for step, piece in zip((3, 2, 1), pieces[1:])
    ]
    total = pieces[0].astype(f32)
    for part in tied(got, after):
        total = total + part.astype(f32)
    return total


def pieces_u(x):
    def part(k):
        return jnp.stack(
            [lax.dynamic_index_in_dim(x, k, 0, False), lax.dynamic_index_in_dim(x, 7 - k, 0, False)], 0
        )

    return pieces_of(part, "u")


def pieces_hidden(x):
    blocks = x.reshape(4, x.shape[0] // 4, x.shape[1])
    return pieces_of(lambda k: lax.dynamic_index_in_dim(blocks, k, 0, False), HIDDEN)


def gather_hidden_async(x):
    me = lax.axis_index(HIDDEN)
    out = jnp.zeros((4,) + x.shape, x.dtype)
    for step in range(4):
        part = x if step == 0 else lax.ppermute(x, HIDDEN, [(i, i ^ step) for i in range(4)])
        out = lax.dynamic_update_index_in_dim(out, part, me ^ step, 0)
    return out.reshape(4 * x.shape[0], x.shape[1])


def gather_u_start(x):
    return [x] + [lax.ppermute(x, "u", [(i, i ^ step) for i in range(4)]) for step in (3, 2, 1)]


def gather_u_end(parts, after):
    me = lax.axis_index("u")
    out = jnp.zeros((8,) + parts[0].shape[1:], parts[0].dtype)
    for step, part in zip((0, 3, 2, 1), tied(parts, after)):
        k = me ^ step
        out = lax.dynamic_update_slice_in_dim(out, part[0:1], k, 0)
        out = lax.dynamic_update_slice_in_dim(out, part[1:2], 7 - k, 0)
    return out


def exchange_kernel(sizes, kinds, back, *refs):
    n = len(kinds)
    ins, outs = refs[:n], refs[n : 2 * n]
    send, recv, keep = refs[2 * n :]
    nu, nw, nv, nc, nf = sizes
    place = coords()
    u, w, v, core, f = (place[axis] for axis in ALL)

    def holder(kind, block):
        if kind == "along":
            return (block, w, v, core, f)
        if kind == "heads":
            at = (u * nw + w) * nv + v
            return (block, at // (nf * nc * nv), at // (nf * nc) % nv, at // nf % nc, at % nf)
        return (u, w, block // nf, v, block % nf)

    def owner(kind, slot):
        if kind == "along":
            return (slot, w, v, core, f)
        if kind == "heads":
            at = ((w * nv + v) * nc + core) * nf + f
            return (at // (nv * nw), at // nv % nw, at % nv, slot // nf, slot % nf)
        return (u, w, core, slot // nf, slot % nf)

    def same(other):
        equal = other[0] == u
        for a, b in zip(other[1:], (w, v, core, f)):
            equal = equal & (a == b)
        return equal

    def landing(kind):
        slot = core * nf + f
        block = v * nf + f if kind == "hidden" else u
        return block if back or kind == "along" else slot

    to, frm = (owner, holder) if back else (holder, owner)
    barrier = pltpu.get_barrier_semaphore()
    waits = jnp.int32(0)
    for kind in kinds:
        for i in range(4):
            other = frm(kind, i)

            @pl.when(jnp.logical_not(same(other)))
            def _():
                pl.semaphore_signal(barrier, inc=1, device_id=other, device_id_type=MESH_IDS)

            waits = waits + jnp.where(same(to(kind, i)), 0, 1)
    pl.semaphore_wait(barrier, waits)

    def land(a, at):
        return outs[a].at[at] if len(outs[a].shape) == 3 else outs[a].at[:, at]

    def copy(a, i):
        at = landing(kinds[a])
        return remote(ins[a].at[i], land(a, at), send.at[a, i], recv.at[a, at], to(kinds[a], i))

    def local(a, i):
        return pltpu.make_async_copy(ins[a].at[i], land(a, landing(kinds[a])), keep.at[a])

    for stage in range(3):
        for a in range(n):
            for i in range(4):
                here = same(to(kinds[a], i))

                @pl.when(here)
                def _():
                    local(a, i).start() if stage == 0 else local(a, i).wait() if stage == 1 else None

                @pl.when(jnp.logical_not(here))
                def _():
                    copy(a, i).start() if stage == 0 else copy(a, i).wait_send() if stage == 1 else None

                if stage == 2:

                    @pl.when(jnp.logical_not(same(frm(kinds[a], i))))
                    def _():
                        remote(
                            ins[a].at[i], land(a, i), send.at[a, i], recv.at[a, i], to(kinds[a], i)
                        ).wait_recv()


def exchange(sizes, arrays, kinds, back, collective_id, after=()):
    n = len(arrays)
    return pl.pallas_call(
        ignoring(functools.partial(exchange_kernel, sizes, kinds, back), n, len(after)),
        out_shape=[jax.ShapeDtypeStruct(x.shape, x.dtype) for x in arrays],
        in_specs=[HBM] * (n + len(after)),
        out_specs=[HBM] * n,
        scratch_shapes=[
            pltpu.SemaphoreType.DMA((n, 4)),
            pltpu.SemaphoreType.DMA((n, 4)),
            pltpu.SemaphoreType.DMA((n,)),
        ],
        compiler_params=pltpu.CompilerParams(
            collective_id=collective_id, has_side_effects=True, vmem_limit_bytes=16 * MIB
        ),
        cost_estimate=lasting(35),
        name="exchange_back" if back else "exchange",
    )(*arrays, *after)


def pad_columns(x, cols):
    return jnp.pad(x, [(0, 0)] * (x.ndim - 1) + [(0, cols - x.shape[-1])])


def body(sizes, tokens, cotangent, segment, position, gain_attn, w_query, w_key, w_value, w_output, gain_mlp, w_gate, w_up, w_down):
    del segment
    groups, block_rows, width = tokens.shape
    rows = groups * block_rows
    half = block_rows // 2
    hidden = w_gate.shape[1]
    slab = w_gate.shape[0]
    block = w_down.shape[0]
    padded = -(-block // 16) * 16
    nkeys = sizes[1] * sizes[2] * sizes[3]
    wide = 2 * nkeys * padded
    qkv_cols = 1792
    here = (groups, 2, half)
    there = (groups, 8, half)

    gain_one, gain_two = gain_attn.astype(f32)[:, None], gain_mlp.astype(f32)[:, None]
    qkv_local, gu_local = pack_weights(
        sizes, w_query, w_key, w_value, w_gate, w_up, gain_one, gain_two, block, padded
    )
    qkv_local, gu_local = exchange(sizes, [qkv_local, gu_local], ["heads", "hidden"], False, 6)
    out_whole = lax.all_gather(w_output, HEAD_SUM, axis=0, tiled=True)
    out_whole = jnp.concatenate([out_whole[:512], jnp.zeros((64, width), bf16), out_whole[512:]], 0)
    qkv_whole = lax.all_gather(qkv_local, HEAD_SUM, axis=0, tiled=True).reshape(width, qkv_cols)
    qkv_whole = lax.all_gather(qkv_local, HEAD_SUM, axis=0, tiled=True).reshape(width, qkv_cols)
    out_whole = lax.all_gather(w_output, HEAD_SUM, axis=0, tiled=True)
    out_whole = jnp.concatenate([out_whole[:512], jnp.zeros((64, width), bf16), out_whole[512:]], 0)

    sequences = range(groups)
    nlocal = lax.axis_index(KEYS)
    order = jnp.arange(8, dtype=jnp.int32)
    order = nkeys * order + jnp.where(order < 4, nlocal, nkeys - 1 - nlocal)
    text = order[:, None] * half + jnp.arange(half, dtype=jnp.int32)[None, :]
    tiles = 8 // QUERY_BLOCKS
    nq = QUERY_BLOCKS * half
    rates = jnp.exp(jnp.arange(32, dtype=f32) * (-math.log(10000.0) / 32))
    inputs, inverse_one, normed_one = [], [], []
    for g in sequences:
        x = tokens[g].astype(f32)
        inverse = lax.rsqrt(jnp.mean(x * x, -1, keepdims=True) + EPSILON)
        inputs.append(x)
        inverse_one.append(inverse)
        normed_one.append(x * inverse)
    places = jnp.broadcast_to(pad_columns(position.reshape(here), LANES)[:, :, None], (groups, 2, 8, LANES))
    upstream = [cotangent[g].astype(f32) for g in sequences]
    held_one, tables, masks, query, kv, kv_own = ([] for _ in range(6))
    before = [qkv_local, out_whole]
    for g in sequences:
        sent = [normed_one[g].astype(bf16).reshape(1, 2, half, width), places[g : g + 1]]
        rides = [("gather_keys", kv_own[0].reshape(8, half, 1152))] if g > 0 else []
        held, seen, *keys = gather_u(sent, (0, 8)[g], after=before, rides=rides)
        held_one.append(held.reshape(8 * half, width))
        seen = seen[0, :, 0, :half]
        lowest = text - jnp.minimum(seen, WINDOW - 1)
        lows, highs = lowest.reshape(tiles, nq), text.reshape(tiles, nq)
        klo, khi = lows[:, 0] // KEY_TILE, highs[:, -1] // KEY_TILE + 1
        lim = jnp.stack([jnp.tile(lows, (1, 2)), jnp.tile(highs, (1, 2))], 1)
        masks.append((jnp.pad(lim, ((0, 0), (0, 6), (0, 0))), klo, khi))
        angles = seen.reshape(8 * half, 1).astype(f32) * rates[None, :]
        cos, sin = jnp.cos(angles), jnp.sin(angles)
        tables.append((jnp.concatenate([cos, cos, cos, cos], 1), jnp.concatenate([-sin, sin, -sin, sin], 1)))
        own, q = rope(matmul(held_one[g], qkv_whole), *tables[g])
        kv_own.append(own)
        before = [own]
        query.append(q)

    third, rows_gu = width // 3, 4 * slab
    own_down = jnp.pad(w_down, ((0, padded - block), (0, 0))).reshape(padded, 3, third)
    packed = jnp.concatenate(
        [gu_local.reshape(4 * rows_gu, third), jnp.transpose(own_down, (1, 0, 2)).reshape(3 * padded, third)], 0
    )
    (packed,) = tied([packed], held_one[:1])
    packed = lax.all_gather(packed, HIDDEN_SUM, axis=0)

    def key_arrays(g, others):
        own = kv_own[g].reshape(1, 8, half, 1152)
        kv.append([with_rings(own, sizes[1]), with_rings(others, sizes[1])])

    key_arrays(0, keys[0])
    attn, lse, parts = [], [], []
    rides = [("gather_keys", kv_own[1].reshape(8, half, 1152))]
    before = kv_own[1:]
    for g in sequences:
        out, sums, got_zero, *back_mlp = flash_forward(query[g], kv[g], *masks[g], after=before, rides=rides, ident=(9, 10)[g])
        attn.append(out)
        lse.append(sums)
        parts.append(matmul(out, out_whole).astype(bf16).reshape(8, half, width))
        if g == 0:
            key_arrays(1, got_zero)
        before, rides = [], [("scatter_u", parts[g])]
        rides += [("gather_hidden", (BRANCH_SCALE * x).astype(bf16)) for x in upstream]
    back_mlp = [x.reshape(4 * block_rows, width) for x in back_mlp]

    def own_u(x):
        me = lax.axis_index("u")
        return jnp.stack([lax.dynamic_index_in_dim(x, me, 0, False), lax.dynamic_index_in_dim(x, 7 - me, 0, False)], 0)

    def own_hidden(x):
        return lax.dynamic_index_in_dim(x, lax.axis_index(HIDDEN), 0, False)

    def total(own, got):
        return own.astype(f32) + jnp.sum(got.astype(f32), 0)

    middle, inverse_two, normed_two, held_two, activated, back_gu, back_held, mlp_part = ([] for _ in range(8))

    def to_feed_forward(g, got):
        x = inputs[g] + BRANCH_SCALE * total(own_u(parts[g]), got).reshape(block_rows, width)
        inverse = lax.rsqrt(jnp.mean(x * x, -1, keepdims=True) + EPSILON)
        middle.append(x)
        inverse_two.append(inverse)
        normed_two.append(x * inverse)
        held_two.append(gather_hidden(normed_two[g].astype(bf16)))

    def from_feed_forward(act, back_gate, back_up, back, part):
        activated.append(act)
        back_gu.append([back_gate, back_up])
        back_held.append(back.reshape(4, block_rows, width))
        mlp_part.append(part.reshape(4, block_rows, width))

    to_feed_forward(0, got_zero)
    *results, got_one = feed_forward(
        held_two[0], back_mlp[0], packed, wide, rides=[("scatter_u", parts[1])], ident=11
    )
    from_feed_forward(*results)
    back_middle, sent = [], []

    def to_attention(g, sums):
        x = upstream[g] + rms_back(sums, normed_two[g], inverse_two[g])
        back_middle.append(x)
        sent.append((BRANCH_SCALE * x).astype(bf16).reshape(2, half, width))

    to_attention(0, scatter_hidden(back_held[0].reshape(4 * block_rows, width)))
    to_feed_forward(1, got_one)
    *results, back_branch_zero, got_mlp = feed_forward(
        held_two[1],
        back_mlp[1],
        packed,
        wide,
        after=sent,
        rides=[("gather_u", sent[0]), ("scatter_hidden", mlp_part[0])],
        ident=12,
    )
    from_feed_forward(*results)
    layer_out = [(middle[0] + BRANCH_SCALE * total(own_hidden(mlp_part[0]), got_mlp)).astype(bf16)]
    gu_term, got_one = weight_gradient(held_two, back_gu, rides=[("scatter_hidden", back_held[1])], ident=13)
    to_attention(1, total(own_hidden(back_held[1]), got_one))
    back_branch = [back_branch_zero.reshape(8 * half, width)]
    dkv_own, dkv_along, dq = [], [], []
    rides = [("gather_u", sent[1]), ("scatter_hidden", mlp_part[1])]
    before = []
    for g in sequences:
        do = times_transposed(back_branch[g], out_whole).astype(bf16)
        lim, klo, khi = masks[g]
        dq_part, *rest = flash_backward(
            query[g], do, attn[g], kv[g], lim, lse[g], klo, khi, after=before, rides=rides, ident=14
        )
        if g == 0:
            back_branch.append(rest[4].reshape(8 * half, width))
            layer_out.append((middle[1] + BRANCH_SCALE * total(own_hidden(mlp_part[1]), rest[5])).astype(bf16))
            dq_part, gu_term = lax.optimization_barrier((dq_part, gu_term))
            gu_sum = lax.psum_scatter(gu_term, HIDDEN_SUM, scatter_dimension=0, tiled=True)
        dq.append(dq_part)
        own, along = scatter_keys_start(rest[:4], sizes[1])
        dkv_own.append(own)
        dkv_along.append(along)
        before, rides = [along], []
    (out_term,) = weight_gradient(attn, [[x] for x in back_branch], tile=LANES, after=[along])
    out_half = head_sum_start(jnp.concatenate([out_term[:512], out_term[576:]], 0), sizes)
    (down_term,) = weight_gradient(activated, [[back_mlp[i]] for i in sequences], after=[out_term])
    before = [down_term]
    back_qkv, late, grad_tokens = [], [], []
    for g in sequences:
        dkv = scatter_keys_end(dkv_own[g], dkv_along[g]).reshape(8 * half, 1152)
        back_qkv.append(unrope(dkv, dq[g], *tables[g], after=before))
        part = times_transposed(back_qkv[g], qkv_whole).astype(bf16)
        late.append(part.reshape(8, half, width))
        before = [part]
    qkv_term, got, out_got = weight_gradient(
        held_one,
        [[x] for x in back_qkv],
        after=before,
        rides=[("scatter_u", late[0]), ("scatter_hidden", out_half)],
        ident=15,
    )
    grad_output = total(own_hidden(out_half), out_got)
    down_term, gu_sum, qkv_term = lax.optimization_barrier((down_term, gu_sum, qkv_term))
    down_sum = lax.psum_scatter(down_term, HIDDEN_SUM, scatter_dimension=0, tiled=True)
    qkv_half = head_sum_start(qkv_term, sizes, 4)
    late_one, qkv_got = scatter_u(late[1][None], rides=[("scatter_hidden", qkv_half)])
    qkv_sum = total(own_hidden(qkv_half), qkv_got).astype(bf16)
    for g, part in enumerate((total(own_u(late[0]), got), late_one)):
        part = part.reshape(block_rows, width)
        x = back_middle[g] + rms_back(part, normed_one[g], inverse_one[g])
        grad_tokens.append(x.astype(bf16))
    layer_out, grad_tokens = jnp.stack(layer_out, 0), jnp.stack(grad_tokens, 0)

    qkv_sum, gu_sum = exchange(
        sizes,
        [qkv_sum.reshape(4, slab, qkv_cols), gu_sum.reshape(4, slab, 2 * wide)],
        ["along", "hidden"],
        True,
        7,
        after=[grad_tokens],
    )
    grad_query, grad_key, grad_value, grad_gate, grad_up, grad_gain_attn, grad_gain_mlp = unpack_gradients(
        sizes, qkv_sum, gu_sum, w_query, w_key, w_value, w_gate, w_up, gain_one, gain_two, block, padded
    )
    grad_down = down_sum[:block].astype(f32)
    return (
        layer_out,
        grad_tokens,
        grad_gain_attn[:, 0],
        grad_query,
        grad_key,
        grad_value,
        grad_output,
        grad_gain_mlp[:, 0],
        grad_gate,
        grad_up,
        grad_down,
    )


def solution(mesh):
    ctx, fsdp = mesh.shape["ctx"], mesh.shape["fsdp"]
    sizes = (4, ctx // 16, 2, 2, fsdp)
    fine = Mesh(mesh.devices.reshape(sizes), ALL)
    blocks = ("u", "w", "v", "core")
    act = P("f", blocks, None)
    ids = P("f", blocks)
    gain, weight = P(ALL), P(ALL, None)
    return jax.shard_map(
        functools.partial(body, sizes),
        mesh=fine,
        in_specs=(act, act, ids, ids, gain, weight, weight, weight, weight, gain, weight, weight, weight),
        out_specs=(act, act, gain, weight, weight, weight, weight, gain, weight, weight, weight),
        check_vma=False,
    )
```

```python
import functools
import math

import jax
import jax.numpy as jnp
from jax import lax
from jax.experimental import pallas as pl
from jax.experimental.pallas import tpu as pltpu
from jax.sharding import Mesh, PartitionSpec as P

HEADS = 36
HEAD_DIM = 64
WINDOW = 1024
EPSILON = 1e-05
BRANCH_SCALE = 1.4 / math.sqrt(40.0)
NEG_LARGE = -1e30
LANES = 128
PAIRS = 5
KEY_TILE = 512
QUERY_BLOCKS = 2
MIB = 1024 * 1024

f32, bf16 = jnp.float32, jnp.bfloat16


def matmul(left, right):
    return jnp.dot(left, right, preferred_element_type=f32)


def times_transposed(left, right):
    return lax.dot_general(left, right, (((1,), (1,)), ((), ())), preferred_element_type=f32)


def transposed_times(left, right):
    return lax.dot_general(left, right, (((0,), (0,)), ((), ())), preferred_element_type=f32)


def rms_back(upstream, normed, inverse):
    return inverse * (upstream - normed * jnp.mean(upstream * normed, -1, keepdims=True))


HBM = pl.BlockSpec(memory_space=pl.ANY)


def ignoring(kernel, args, extra):
    return lambda *refs: kernel(*refs[:args], *refs[args + extra :])


def lasting(micros):
    return pl.CostEstimate(flops=0, bytes_accessed=micros * 3_600_000, transcendentals=0)


MESH_IDS = pl.DeviceIdType.MESH
ALL = ("u", "w", "v", "core", "f")
KEYS = ("w", "v", "core")
HEAD_SUM = ("w", "v", "core", "f")
HIDDEN = ("v", "f")
HIDDEN_SUM = ("u", "w", "core")


def coords():
    return {axis: lax.axis_index(axis) for axis in ALL}


def device(place, **moved):
    return tuple(moved.get(axis, place[axis]) for axis in ALL)


def remote(src, dst, send, recv, where):
    return pltpu.make_async_remote_copy(
        src_ref=src, dst_ref=dst, send_sem=send, recv_sem=recv, device_id=where, device_id_type=MESH_IDS
    )


def ride_out(kind, x):
    shape = {
        "gather_u": (8,) + x.shape[1:],
        "scatter_u": (3, 2) + x.shape[1:],
        "gather_hidden": (4,) + x.shape,
        "scatter_hidden": (3,) + x.shape[1:],
        "gather_keys": (3,) + x.shape,
        "swap_v": x.shape,
        "gather_heads": (8,) + x.shape,
    }
    return jax.ShapeDtypeStruct(shape[kind], x.dtype)


STEPS = {"gather_keys": (2, 1), "swap_v": (2,)}


def partner(kind, place, step):
    if kind in ("gather_u", "scatter_u"):
        k = place["u"] ^ step
        return k, device(place, u=k)
    if kind in ("gather_keys", "swap_v"):
        k = (2 * place["v"] + place["core"]) ^ step
        return k, device(place, v=k // 2, core=k % 2)
    k = (2 * place["v"] + place["f"]) ^ step
    return k, device(place, v=k // 2, f=k % 2)


def ride_slices(kind, src, dst, place, step):
    k, _ = partner(kind, place, step)
    t = 2 * place["v"] + place["f"]
    if kind == "scatter_u":
        return [(src.at[7 - k if s else k], dst.at[step - 1, s], dst.at[step - 1, s]) for s in range(2)]
    if kind == "gather_hidden":
        return [(src, dst.at[t], dst.at[k])]
    if kind == "scatter_hidden":
        return [(src.at[k], dst.at[step - 1], dst.at[step - 1])]
    if kind == "swap_v":
        return [(src, dst, dst)]
    return [(src, dst.at[step - 1], dst.at[step - 1])]


def ride_copies(kind, src, dst, send, recv, place, part):
    if kind == "gather_keys" and part == "on":
        _, to = partner(kind, place, 1)
        return [remote(dst.at[1], dst.at[2], send.at[4], recv.at[4], to)]
    copies = []
    for step in STEPS.get(kind, (3, 2, 1)):
        _, to = partner(kind, place, step)
        for i, (here, there, landing) in enumerate(ride_slices(kind, src, dst, place, step)):
            at = 2 * step - 2 + i
            if part == "away":
                copies.append(remote(here, there, send.at[at], recv.at[at], to))
            else:
                copies.append(remote(landing, landing, send.at[at], recv.at[at], to))
    return copies


def own_copies(kind, src, dst, keep, place):
    u, t = place["u"], 2 * place["v"] + place["f"]
    if kind == "gather_u":
        return [pltpu.make_async_copy(src.at[s], dst.at[7 - u if s else u], keep.at[s]) for s in range(2)]
    return [pltpu.make_async_copy(src, dst.at[t], keep.at[0])] if kind == "gather_hidden" else []


def chain_u(stage, src, dst, send, recv, place):
    me = place["u"]
    right, left = device(place, u=jnp.minimum(me + 1, 3)), device(place, u=jnp.maximum(me - 1, 0))

    def spot(owner, slot):
        return dst.at[7 - owner if slot else owner]

    def going(step, slot, side):
        owner = jnp.clip(me + step if side else me - step, 0, 3)
        here = src.at[slot] if step == 0 else spot(owner, slot)
        at = 6 * side + 2 * step + slot
        return remote(here, spot(owner, slot), send.at[at], recv.at[at], left if side else right)

    def coming(step, slot, side):
        there = spot(jnp.clip(me + 1 + step if side else me - 1 - step, 0, 3), slot)
        at = 6 * side + 2 * step + slot
        return remote(there, there, send.at[at], recv.at[at], right if side else left)

    def sends(step, side):
        return (me > 0) & (me <= 3 - step) if side else (me < 3) & (me >= step)

    def gets(step, side):
        return me <= 2 - step if side else me >= step + 1

    for slot in range(2):
        for side in range(2):
            if stage > 0:

                @pl.when(gets(stage - 1, side))
                def _():
                    coming(stage - 1, slot, side).wait_recv()

            if stage < 3:

                @pl.when(sends(stage, side))
                def _():
                    going(stage, slot, side).start()

    if stage == 3:
        for step in range(3):
            for slot in range(2):
                for side in range(2):

                    @pl.when(sends(step, side))
                    def _():
                        going(step, slot, side).wait_send()


def gather_heads(stage, src, dst, send, recv, keep, place):
    v, core, f = place["v"], place["core"], place["f"]
    mine = (2 * v + core) * 2 + f
    other = device(place, core=1 - core)

    def away(step):
        _, to = partner("gather_hidden", place, step)
        return remote(src, dst.at[mine], send.at[step], recv.at[step], to)

    def on(step):
        k = (2 * v + f) ^ step
        there = dst.at[(2 * (k // 2) + core) * 2 + k % 2]
        return remote(src if step == 0 else there, there, send.at[4 + step], recv.at[4 + step], other)

    def landed(step):
        k = (2 * v + f) ^ step
        there = dst.at[(2 * (k // 2) + core) * 2 + k % 2]
        return remote(there, there, send.at[step], recv.at[step], other)

    def passed(step):
        k = (2 * v + f) ^ step
        there = dst.at[(2 * (k // 2) + 1 - core) * 2 + k % 2]
        return remote(there, there, send.at[4 + step], recv.at[4 + step], other)

    local = pltpu.make_async_copy(src, dst.at[mine], keep.at[0]) if stage != 1 else None
    if stage == 0:
        local.start()
        for step in (3, 2, 1):
            away(step).start()
        on(0).start()
    elif stage == 1:
        for step in (1, 2, 3):
            landed(step).wait_recv()
            on(step).start()
    else:
        local.wait()
        for step in (1, 2, 3):
            away(step).wait_send()
        for step in range(4):
            on(step).wait_send()
            passed(step).wait_recv()


def ride_greet(kinds, place):
    barrier = pltpu.get_barrier_semaphore()
    count = 0
    for kind in kinds:
        if kind == "gather_heads":
            other = device(place, core=1 - place["core"])
            pl.semaphore_signal(barrier, inc=1, device_id=other, device_id_type=MESH_IDS)
            count = count + 1
        for step in STEPS.get(kind, (3, 2, 1)):
            _, to = partner(kind, place, step)
            pl.semaphore_signal(barrier, inc=1, device_id=to, device_id_type=MESH_IDS)
            count = count + 1
    return count


def ride_start(kinds, rides, arrived, sems, place):
    for a, kind in enumerate(kinds):
        send, recv, keep = (sem.at[a] for sem in sems)
        if kind == "gather_u":
            chain_u(0, rides[a], arrived[a], send, recv, place)
        elif kind == "gather_heads":
            gather_heads(0, rides[a], arrived[a], send, recv, keep, place)
        else:
            for copy in ride_copies(kind, rides[a], arrived[a], send, recv, place, "away"):
                copy.start()
        for copy in own_copies(kind, rides[a], arrived[a], keep, place):
            copy.start()


def ride_on(kinds, rides, arrived, sems, place, stage):
    for a, kind in enumerate(kinds):
        if kind == "gather_u":
            chain_u(stage, rides[a], arrived[a], sems[0].at[a], sems[1].at[a], place)


def ride_end(kinds, rides, arrived, sems, place):
    def copies(a, part):
        return ride_copies(kinds[a], rides[a], arrived[a], sems[0].at[a], sems[1].at[a], place, part)

    def heads(a, stage):
        gather_heads(stage, rides[a], arrived[a], *(sem.at[a] for sem in sems), place)

    keys = [a for a, kind in enumerate(kinds) if kind == "gather_keys"]
    for a, kind in enumerate(kinds):
        if kind == "gather_heads":
            heads(a, 1)
    for a in keys:
        for copy in copies(a, "back"):
            copy.wait_recv()
        for copy in copies(a, "on"):
            copy.start()
    for a, kind in enumerate(kinds):
        for copy in own_copies(kind, rides[a], arrived[a], sems[2].at[a], place):
            copy.wait()
        if kind == "gather_u":
            chain_u(3, rides[a], arrived[a], sems[0].at[a], sems[1].at[a], place)
            continue
        if kind == "gather_heads":
            heads(a, 2)
            continue
        for copy in copies(a, "away"):
            copy.wait_send()
        for copy in copies(a, "back") if a not in keys else ():
            copy.wait_recv()
    for a in keys:
        for copy in copies(a, "on"):
            copy.wait()


def ride_scratch(n):
    return [pltpu.SemaphoreType.DMA((n, 12)), pltpu.SemaphoreType.DMA((n, 12)), pltpu.SemaphoreType.DMA((n, 2))]


def riding(kernel, args, extra, outs, kinds, grid):
    n = len(kinds)

    def whole(*refs):
        ins, rides = refs[:args], refs[args : args + n]
        rest = refs[args + n + extra :]
        results, arrived, scratch = rest[:outs], rest[outs : outs + n], rest[outs + n : len(rest) - 3]
        sems = rest[len(rest) - 3 :]
        place = coords()
        ids = [pl.program_id(i) for i in range(len(grid))]
        first, last = ids[0] == 0, ids[0] == grid[0] - 1
        for i in range(1, len(grid)):
            first, last = first & (ids[i] == 0), last & (ids[i] == grid[i] - 1)

        @pl.when(first)
        def _():
            count = ride_greet(kinds, place)
            pl.semaphore_wait(pltpu.get_barrier_semaphore(), count)
            ride_start(kinds, rides, arrived, sems, place)

        kernel(*ins, *results, *scratch)

        if "gather_u" in kinds:
            total = math.prod(grid)
            at = ids[0]
            for i in range(1, len(grid)):
                at = at * grid[i] + ids[i]
            for stage in (1, 2):

                @pl.when(at == total * stage // 3 - 1)
                def _():
                    ride_on(kinds, rides, arrived, sems, place, stage)

        @pl.when(last)
        def _():
            ride_end(kinds, rides, arrived, sems, place)

    return whole


def grid_call(kernel, grid, args, in_specs, out_specs, out_shape, scratch, name, micros, after=(), rides=(), ident=None):
    limit = 56 * MIB
    if not rides:
        return pl.pallas_call(
            ignoring(kernel, len(args), len(after)),
            grid=grid,
            in_specs=in_specs + [HBM] * len(after),
            out_specs=out_specs,
            out_shape=out_shape,
            scratch_shapes=scratch,
            compiler_params=pltpu.CompilerParams(vmem_limit_bytes=limit),
            cost_estimate=lasting(micros),
            name=name,
        )(*args, *after)
    kinds = [kind for kind, _ in rides]
    n = len(rides)
    return pl.pallas_call(
        riding(kernel, len(args), len(after), len(out_shape), kinds, grid),
        grid=grid,
        in_specs=in_specs + [HBM] * (n + len(after)),
        out_specs=out_specs + [HBM] * n,
        out_shape=out_shape + [ride_out(kind, x) for kind, x in rides],
        scratch_shapes=scratch + ride_scratch(n),
        compiler_params=pltpu.CompilerParams(vmem_limit_bytes=limit, collective_id=ident, has_side_effects=True),
        cost_estimate=lasting(max(micros, 50)),
        name=name + "_riding",
    )(*args, *[x for _, x in rides], *after)


def swap_halves(x):
    lane = lax.broadcasted_iota(jnp.int32, x.shape, 1)
    return jnp.where(lane % 64 < 32, pltpu.roll(x, LANES - 32, 1), pltpu.roll(x, 32, 1))


def rope_kernel(raw_ref, cos_ref, sin_ref, kv_ref, q_ref):
    cos, sin = cos_ref[...], sin_ref[...]

    def turn(x):
        return x * cos + swap_halves(x) * sin

    for p in range(4):
        kv_ref[:, 256 * p : 256 * p + 128] = turn(raw_ref[:, 256 * p : 256 * p + 128]).astype(bf16)
        kv_ref[:, 256 * p + 128 : 256 * p + 256] = raw_ref[:, 256 * p + 128 : 256 * p + 256].astype(bf16)
    last = raw_ref[:, 1024:1152]
    lane = lax.broadcasted_iota(jnp.int32, last.shape, 1)
    kv_ref[:, 1024:1152] = jnp.where(lane < 64, turn(last), last).astype(bf16)
    for p in range(5):
        q_ref[:, 128 * p : 128 * p + 128] = turn(raw_ref[:, 1152 + 128 * p : 1280 + 128 * p]).astype(bf16)


def rope(raw, cos, sin):
    rows = raw.shape[0]
    tile = min(256, rows)
    row = lambda cols: pl.BlockSpec((tile, cols), lambda i: (i, 0))
    return pl.pallas_call(
        rope_kernel,
        grid=(rows // tile,),
        in_specs=[row(1792), row(LANES), row(LANES)],
        out_specs=[row(1152), row(640)],
        out_shape=[jax.ShapeDtypeStruct((rows, 1152), bf16), jax.ShapeDtypeStruct((rows, 640), bf16)],
        compiler_params=pltpu.CompilerParams(vmem_limit_bytes=40 * MIB),
        name="rope",
    )(raw, cos, sin)


def unrope_kernel(dkv_ref, dq_ref, cos_ref, sin_ref, out_ref):
    cos, sin = cos_ref[...], sin_ref[...]

    def turn(x):
        return x * cos - swap_halves(x) * sin

    for p in range(4):
        a = 256 * p
        out_ref[:, a : a + 128] = turn(dkv_ref[:, a : a + 128].astype(f32)).astype(bf16)
        out_ref[:, a + 128 : a + 256] = dkv_ref[:, a + 128 : a + 256].astype(bf16)
    last = dkv_ref[:, 1024:1152].astype(f32)
    lane = lax.broadcasted_iota(jnp.int32, last.shape, 1)
    out_ref[:, 1024:1152] = jnp.where(lane < 64, turn(last), last).astype(bf16)
    for p in range(5):
        out_ref[:, 1152 + 128 * p : 1280 + 128 * p] = turn(
            dq_ref[:, 128 * p : 128 * p + 128].astype(f32)
        ).astype(bf16)


def unrope(dkv, dq, cos, sin, after=()):
    rows = dkv.shape[0]
    tile = min(256, rows)
    row = lambda cols: pl.BlockSpec((tile, cols), lambda i: (i, 0))
    return pl.pallas_call(
        ignoring(unrope_kernel, 4, len(after)),
        grid=(rows // tile,),
        in_specs=[row(1152), row(640), row(LANES), row(LANES)] + [HBM] * len(after),
        out_specs=row(1792),
        out_shape=jax.ShapeDtypeStruct((rows, 1792), bf16),
        compiler_params=pltpu.CompilerParams(vmem_limit_bytes=40 * MIB),
        name="unrope",
    )(dkv, dq, cos, sin, *after)


def hidden_blocks(sizes):
    nu, nw, nv, nc, nf = sizes
    out = []
    for i in range(nu * nw * nv * nc * nf):
        rest, f = divmod(i, nf)
        rest, core = divmod(rest, nc)
        uw, v = divmod(rest, nv)
        out.append((v * nf + f, uw * nc + core))
    return out


def pack_kernel(spots, block, q_ref, k_ref, v_ref, g_ref, u_ref, one_ref, two_ref, qkv_ref, first_ref, second_ref):
    slab = q_ref.shape[0]
    one, two = one_ref[...], two_ref[...]
    padded = 8 * first_ref.shape[3] // len(spots)

    def scaled(ref, start, size, gain):
        return ref[:, start : start + size].astype(f32) * gain

    for t in range(4):
        cols = []
        at = 576 * t
        for p in range(4):
            cols.append(scaled(k_ref, at + 128 * p, 128, one))
            cols.append(scaled(v_ref, at + 128 * p, 128, one))
        cols.append(scaled(k_ref, at + 512, 64, one))
        cols.append(scaled(v_ref, at + 512, 64, one))
        cols.append(scaled(q_ref, at, 576, one))
        cols.append(jnp.zeros((slab, 64), f32))
        qkv_ref[t] = jnp.concatenate(cols, 1).astype(bf16)
        mine = sorted((place, i) for i, (owner, place) in enumerate(spots) if owner == t)
        for half, ref in enumerate((g_ref, u_ref)):
            cols = []
            for _, i in mine:
                cols.append(scaled(ref, i * block, block, two))
                cols.append(jnp.zeros((slab, padded - block), f32))
            whole = jnp.concatenate(cols, 1).astype(bf16)
            cut = first_ref.shape[3]
            first_ref[t, half] = whole[:, :cut]
            second_ref[t, half] = whole[:, cut:]


def pack_weights(sizes, w_query, w_key, w_value, w_gate, w_up, gain_one, gain_two, block, padded):
    slab = w_query.shape[0]
    spots = hidden_blocks(sizes)
    cut = padded * len(spots) // 8
    return pl.pallas_call(
        functools.partial(pack_kernel, spots, block),
        out_shape=[jax.ShapeDtypeStruct((4, slab, 1792), bf16)]
        + [jax.ShapeDtypeStruct((4, 2, slab, cut), bf16)] * 2,
        compiler_params=pltpu.CompilerParams(vmem_limit_bytes=48 * MIB),
        cost_estimate=lasting(10),
        name="pack_weights",
    )(w_query, w_key, w_value, w_gate, w_up, gain_one, gain_two)


def unpack_kernel(
    spots, block, padded, qkv_ref, gu_ref, q_ref, k_ref, v_ref, g_ref, u_ref, one_ref, two_ref,
    dq_ref, dk_ref, dv_ref, dg_ref, du_ref, done_ref, dtwo_ref,
):
    one, two = one_ref[...], two_ref[...]
    gains = jnp.zeros_like(one)
    wide = gu_ref.shape[2] // 2

    def part(t, start, size):
        return qkv_ref[t, :, start : start + size].astype(f32)

    for ref, out, first, last in ((k_ref, dk_ref, 0, 1024), (v_ref, dv_ref, 128, 1088)):
        cols = []
        for t in range(4):
            cols += [part(t, first + 256 * p, 128) for p in range(4)] + [part(t, last, 64)]
        grad = jnp.concatenate(cols, 1)
        gains = gains + jnp.sum(ref[...].astype(f32) * grad, 1, keepdims=True)
        out[...] = grad * one
    grad = jnp.concatenate([part(t, 1152, 576) for t in range(4)], 1)
    done_ref[...] = gains + jnp.sum(q_ref[...].astype(f32) * grad, 1, keepdims=True)
    dq_ref[...] = grad * one
    gains = jnp.zeros_like(two)
    for half, (ref, out) in enumerate(((g_ref, dg_ref), (u_ref, du_ref))):
        grad = jnp.concatenate(
            [
                gu_ref[t, :, half * wide + place * padded : half * wide + place * padded + block].astype(f32)
                for t, place in spots
            ],
            1,
        )
        gains = gains + jnp.sum(ref[...].astype(f32) * grad, 1, keepdims=True)
        out[...] = grad * two
    dtwo_ref[...] = gains


def unpack_gradients(sizes, qkv, gu, w_query, w_key, w_value, w_gate, w_up, gain_one, gain_two, block, padded):
    slab, width = w_query.shape
    hidden = w_gate.shape[1]
    shape = lambda cols: jax.ShapeDtypeStruct((slab, cols), f32)
    return pl.pallas_call(
        functools.partial(unpack_kernel, hidden_blocks(sizes), block, padded),
        out_shape=[shape(width)] * 3 + [shape(hidden)] * 2 + [shape(1)] * 2,
        compiler_params=pltpu.CompilerParams(vmem_limit_bytes=48 * MIB),
        cost_estimate=lasting(15),
        name="unpack_gradients",
    )(qkv, gu, w_query, w_key, w_value, w_gate, w_up, gain_one, gain_two)


def stack_heads(x, first, second):
    return jnp.concatenate([jnp.where(first, x, 0), jnp.where(second, x, 0)], 0)


def text_rows(source, ring, j, half, many):
    v, core = lax.axis_index("v"), lax.axis_index("core")
    v = 1 - v if source // 2 else v
    core = 1 - core if source % 2 else core
    at = (ring * 2 + v) * 2 + core
    block = many * j + (at if j < 4 else many - 1 - at)
    return pl.multiple_of(block * half, half)


def assemble(kv_refs, kv_s):
    rings, _, half, _ = kv_refs[0].shape
    for source, ref in enumerate(kv_refs):
        for ring in range(rings):
            for j in range(8):
                kv_s[pl.ds(text_rows(source, ring, j, half, 4 * rings), half), :] = ref[ring, j]


def flash_forward_kernel(
    bounds, q_ref, kv0, kv1, kv2, kv3, lim_ref, o_ref, lse_ref, kv_s, s_ref, vt_ref
):
    p, t = pl.program_id(0), pl.program_id(1)
    nq = q_ref.shape[0]
    tail = p == 4
    voff = pl.multiple_of(jnp.where(tail, 0, LANES), LANES)
    tiles = s_ref.shape[0]

    @pl.when(t == 0)
    def _():
        assemble((kv0, kv1, kv2, kv3), kv_s)
        for k in range(tiles):
            vt_ref[k] = kv_s[k * KEY_TILE : (k + 1) * KEY_TILE, pl.ds(voff, LANES)].T

    lane = lax.broadcasted_iota(jnp.int32, (nq, LANES), 1)
    qm = stack_heads(q_ref[...] * bf16(0.125), lane < 64, lane >= 64)
    lo, hi = lim_ref[0, 0:1, :], lim_ref[0, 1:2, :]
    row = lax.broadcasted_iota(jnp.int32, (KEY_TILE, 2 * nq), 0)
    klo, khi = bounds(t)

    def scores(k, high):
        base = pl.multiple_of(k * KEY_TILE, KEY_TILE)
        s = times_transposed(kv_s[pl.ds(base, KEY_TILE), 0:LANES], qm)
        s = jnp.where((row >= lo - base) & (row <= hi - base), s, NEG_LARGE)
        s_ref[k] = s
        return jnp.maximum(high, jnp.max(s.reshape(KEY_TILE // 8, 8, 2 * nq), 0))

    high = lax.fori_loop(klo, khi, scores, jnp.full((8, 2 * nq), NEG_LARGE, f32))
    high = jnp.max(high, 0, keepdims=True)

    def mix(k, carry):
        total, acc = carry
        w = jnp.exp(s_ref[k] - high)
        total = total + jnp.sum(w.reshape(KEY_TILE // 8, 8, 2 * nq), 0)
        acc = acc + matmul(vt_ref[k], w.astype(bf16))
        return total, acc

    total, acc = lax.fori_loop(
        klo, khi, mix, (jnp.zeros((8, 2 * nq), f32), jnp.zeros((LANES, 2 * nq), f32))
    )
    total = jnp.sum(total, 0, keepdims=True)
    out = (acc / total).T
    first, second = out[:nq], out[nq:]
    low = jnp.where(tail, 0.0, first)
    up = jnp.where(tail, first, second)
    o_ref[...] = jnp.where(lane < 64, low, up).astype(bf16)
    lse_ref[0, 0] = jnp.broadcast_to(high + jnp.log(total), (8, 2 * nq))


def flash_specs(rows, tiles, kv):
    nq = rows // tiles
    _, rings, _, half, _ = kv[0].shape
    part = pl.BlockSpec((nq, LANES), lambda p, t, *_: (t, p))
    keys = [
        pl.BlockSpec((None, rings, 8, half, 2 * LANES), lambda p, t, *_, i=i: (i, 0, 0, 0, p)) for i in (0, 0, 1, 2)
    ]
    lim = pl.BlockSpec((1, 8, 2 * nq), lambda p, t, *_: (t, 0, 0))
    lse = pl.BlockSpec((1, 1, 8, 2 * nq), lambda p, t, *_: (p, t, 0, 0))
    return nq, 32 * rings * half, part, keys, lim, lse


def window_bounds(rows, tiles, rings):
    half, many = rows // 8, 4 * rings

    def bounds(t):
        at = (lax.axis_index("w") * 2 + lax.axis_index("v")) * 2 + lax.axis_index("core")

        def first_row(j):
            return (many * j + jnp.where(j < 4, at, many - 1 - at)) * half

        low = jnp.maximum(first_row(t * QUERY_BLOCKS) - (WINDOW - 1), 0)
        high = first_row(t * QUERY_BLOCKS + QUERY_BLOCKS - 1) + half - 1
        return low // KEY_TILE, high // KEY_TILE + 1

    return bounds


def flash_call(kernel, name, args, klo, khi, in_specs, out_specs, out_shape, scratch, micros, after, rides, ident):
    tiles = klo.shape[0]
    grid = (PAIRS, tiles)
    if rides:
        bounds = window_bounds(args[0].shape[0], tiles, args[-3 if name == "flash_backward" else -2].shape[1])
        return grid_call(
            functools.partial(kernel, bounds), grid, args, in_specs, out_specs, out_shape, scratch, name, micros,
            after, rides, ident,
        )

    def bounded(klo_ref, khi_ref, *refs):
        kernel(lambda t: (klo_ref[t], khi_ref[t]), *refs)

    return pl.pallas_call(
        ignoring(bounded, 2 + len(args), len(after)),
        grid_spec=pltpu.PrefetchScalarGridSpec(
            num_scalar_prefetch=2,
            grid=grid,
            in_specs=in_specs + [HBM] * len(after),
            out_specs=out_specs,
            scratch_shapes=scratch,
        ),
        out_shape=out_shape,
        compiler_params=pltpu.CompilerParams(vmem_limit_bytes=56 * MIB),
        cost_estimate=lasting(micros),
        name=name,
    )(klo, khi, *args, *after)


def flash_forward(q, kv, lim, klo, khi, after=(), rides=(), ident=None):
    rows, tiles = q.shape[0], klo.shape[0]
    nq, keys, part, whole, limits, lses = flash_specs(rows, tiles, kv)
    return flash_call(
        flash_forward_kernel,
        "flash_forward",
        [q, kv[0], kv[1], kv[1], kv[1], lim],
        klo,
        khi,
        [part, *whole, limits],
        [part, lses],
        [jax.ShapeDtypeStruct((rows, 640), bf16), jax.ShapeDtypeStruct((PAIRS, tiles, 8, 2 * nq), f32)],
        [
            pltpu.VMEM((keys, 2 * LANES), bf16),
            pltpu.VMEM((keys // KEY_TILE, KEY_TILE, 2 * nq), f32),
            pltpu.VMEM((keys // KEY_TILE, LANES, KEY_TILE), bf16),
        ],
        40,
        after,
        rides,
        ident,
    )


def flash_backward_kernel(
    bounds, q_ref, do_ref, o_ref, kv0, kv1, kv2, kv3, lim_ref, lse_ref,
    dq_ref, dkv0, dkv1, dkv2, dkv3, kv_s, kt_ref, dk_ref, dv_ref,
):
    p, t = pl.program_id(0), pl.program_id(1)
    nq = q_ref.shape[0]
    tail = p == 4
    voff = pl.multiple_of(jnp.where(tail, 0, LANES), LANES)
    tiles = kt_ref.shape[0]

    @pl.when(t == 0)
    def _():
        assemble((kv0, kv1, kv2, kv3), kv_s)
        for k in range(tiles):
            kt_ref[k] = kv_s[k * KEY_TILE : (k + 1) * KEY_TILE, 0:LANES].T
        dk_ref[...] = jnp.zeros_like(dk_ref)
        dv_ref[...] = jnp.zeros_like(dv_ref)

    lane = lax.broadcasted_iota(jnp.int32, (nq, LANES), 1)
    qm = stack_heads(q_ref[...] * bf16(0.125), lane < 64, lane >= 64)
    side = jnp.where(tail, 1, 0)
    head = lane // 64
    dom = stack_heads(do_ref[...], head == side, head == 1 + side)
    back = do_ref[...].astype(f32) * o_ref[...].astype(f32)
    back = stack_heads(back, head == side, head == 1 + side)
    delta = jnp.sum(back.T, 0, keepdims=True)
    lo, hi = lim_ref[0, 0:1, :], lim_ref[0, 1:2, :]
    lse = lse_ref[0, 0, 0:1, :]
    row = lax.broadcasted_iota(jnp.int32, (KEY_TILE, 2 * nq), 0)

    def step(k, acc):
        base = pl.multiple_of(k * KEY_TILE, KEY_TILE)
        s = times_transposed(kv_s[pl.ds(base, KEY_TILE), 0:LANES], qm)
        w = jnp.exp(jnp.where((row >= lo - base) & (row <= hi - base), s - lse, NEG_LARGE))
        dp = times_transposed(kv_s[pl.ds(base, KEY_TILE), pl.ds(voff, LANES)], dom)
        ds = (w * (dp - delta)).astype(bf16)
        dv_ref[pl.ds(base, KEY_TILE), :] += matmul(w.astype(bf16), dom)
        dk_ref[pl.ds(base, KEY_TILE), :] += matmul(ds, qm)
        return acc + matmul(kt_ref[k], ds)

    acc = lax.fori_loop(*bounds(t), step, jnp.zeros((LANES, 2 * nq), f32))
    out = acc.T * 0.125
    dq_ref[...] = jnp.where(lane < 64, out[:nq], jnp.where(tail, 0.0, out[nq:]))

    @pl.when(t == pl.num_programs(1) - 1)
    def _():
        rings, _, half, _ = dkv0.shape
        for source, ref in enumerate((dkv0, dkv1, dkv2, dkv3)):
            for ring in range(rings):
                for j in range(8):
                    at = pl.ds(text_rows(source, ring, j, half, 4 * rings), half)
                    dk, dv = dk_ref[at, :], dv_ref[at, :]
                    ref[ring, j, :, 0:LANES] = jnp.where(tail, dk + dv, dk).astype(bf16)
                    ref[ring, j, :, LANES : 2 * LANES] = dv.astype(bf16)


def flash_backward(q, do, o, kv, lim, lse, klo, khi, after=(), rides=(), ident=None):
    rows, tiles = q.shape[0], klo.shape[0]
    nq, keys, part, whole, limits, lses = flash_specs(rows, tiles, kv)
    return flash_call(
        flash_backward_kernel,
        "flash_backward",
        [q, do, o, kv[0], kv[1], kv[1], kv[1], lim, lse],
        klo,
        khi,
        [part, part, part, *whole, limits, lses],
        [part] + [whole[0]] * 4,
        [jax.ShapeDtypeStruct((rows, 640), f32)] + [jax.ShapeDtypeStruct(kv[0].shape, bf16)] * 4,
        [
            pltpu.VMEM((keys, 2 * LANES), bf16),
            pltpu.VMEM((keys // KEY_TILE, LANES, KEY_TILE), bf16),
            pltpu.VMEM((keys, LANES), f32),
            pltpu.VMEM((keys, LANES), f32),
        ],
        48,
        after,
        rides,
        ident,
    )


def feed_forward_kernel(
    held_ref, back_ref, wg_ref, wu_ref, wd_ref, act_ref, bg_ref, bu_ref, bh_ref, br_ref, bh_acc, br_acc, wd_s
):
    t = pl.program_id(0)
    tile = wg_ref.shape[2]
    blocks, high, third = wd_ref.shape
    padded = high // 3

    @pl.when(t % (third // tile) == 0)
    def _():
        for b in range(blocks):
            for c in range(3):
                wd_s[b * padded : (b + 1) * padded, c * third : (c + 1) * third] = wd_ref[
                    b, c * padded : (c + 1) * padded, :
                ]

    wd = wd_s[pl.ds(pl.multiple_of(t % (third // tile) * tile, tile), tile), :]
    held = held_ref[...]
    width = held.shape[1]
    wg = wg_ref[...].reshape(width, tile)
    wu = wu_ref[...].reshape(width, tile)
    gate, up = matmul(held, wg), matmul(held, wu)
    back_act = times_transposed(back_ref[...], wd)
    sig = jax.nn.sigmoid(gate)
    gs = gate * sig
    act = (gs * up).astype(bf16)
    bg = (back_act * up * sig * (1.0 + gate * (1.0 - sig))).astype(bf16)
    bu = (back_act * gs).astype(bf16)
    act_ref[...], bg_ref[...], bu_ref[...] = act, bg, bu
    bh = times_transposed(bg, wg) + times_transposed(bu, wu)
    br = matmul(act, wd)

    @pl.when(t == 0)
    def _():
        bh_acc[...] = bh
        br_acc[...] = br

    @pl.when(t > 0)
    def _():
        bh_acc[...] += bh
        br_acc[...] += br

    @pl.when(t == pl.num_programs(0) - 1)
    def _():
        bh_ref[...] = bh_acc[...].astype(bf16)
        br_ref[...] = br_acc[...].astype(bf16)


def feed_forward(held, back, packed, wide, after=(), rides=(), ident=None):
    rows, width = held.shape
    tile = 256
    tiles = wide // tile
    whole = pl.BlockSpec((rows, width), lambda t: (0, 0))
    part = pl.BlockSpec((rows, tile), lambda t: (0, t))
    many, _, third = packed.shape
    per, blocks, slice_rows = third // tile, many * third // wide, width // many
    cols = lambda i: pl.BlockSpec((many, slice_rows, tile), lambda t: (0, t // per * 4 + i, t % per))
    down = pl.BlockSpec((blocks, 2 * slice_rows, third), lambda t: (t // per, 1, 0))
    return grid_call(
        feed_forward_kernel,
        (tiles,),
        [held, back, packed, packed, packed],
        [whole, whole, cols(0), cols(1), down],
        [part, part, part, whole, whole],
        [jax.ShapeDtypeStruct((rows, wide), bf16)] * 3 + [jax.ShapeDtypeStruct((rows, width), bf16)] * 2,
        [pltpu.VMEM((rows, width), f32)] * 2 + [pltpu.VMEM((third, width), bf16)],
        "feed_forward",
        42,
        after,
        rides,
        ident,
    )


def weight_gradient(lefts, rights, tile=256, after=(), rides=(), ident=None):
    many, per = len(lefts), len(rights[0])
    flat = [x for group in rights for x in group]
    rows, high = lefts[0].shape
    widths = [x.shape[1] for x in rights[0]]

    def kernel(*refs):
        ls, rs, out = refs[:many], refs[many : many + len(flat)], refs[many + len(flat)]
        start = 0
        for i, cols in enumerate(widths):
            total = transposed_times(ls[0][...], rs[i][...])
            for g in range(1, many):
                total = total + transposed_times(ls[g][...], rs[g * per + i][...])
            out[:, start : start + cols] = total.astype(bf16)
            start += cols

    return grid_call(
        kernel,
        (high // tile,),
        [*lefts, *flat],
        [pl.BlockSpec((rows, tile), lambda i: (0, i))] * many + [pl.BlockSpec(x.shape, lambda i: (0, 0)) for x in flat],
        [pl.BlockSpec((tile, sum(widths)), lambda i: (i, 0))],
        [jax.ShapeDtypeStruct((high, sum(widths)), bf16)],
        [],
        "weight_gradient",
        max(4, 2 * many * rows * high * sum(widths) // 10**9),
        after,
        rides,
        ident,
    )


def greet(places):
    barrier = pltpu.get_barrier_semaphore()
    for place in places:
        pl.semaphore_signal(barrier, inc=1, device_id=place, device_id_type=MESH_IDS)
    pl.semaphore_wait(barrier, len(places))


def greet_line(me, place, more=0):
    barrier = pltpu.get_barrier_semaphore()

    @pl.when(me > 0)
    def _():
        pl.semaphore_signal(barrier, inc=1, device_id=device(place, u=me - 1), device_id_type=MESH_IDS)

    @pl.when(me < 3)
    def _():
        pl.semaphore_signal(barrier, inc=1, device_id=device(place, u=me + 1), device_id_type=MESH_IDS)

    pl.semaphore_wait(barrier, 2 + more - jnp.where(me == 0, 1, 0) - jnp.where(me == 3, 1, 0))


def communicating(kernel, out, args, scratch, collective_id, name, vmem=40, after=(), micros=50):
    return pl.pallas_call(
        ignoring(kernel, len(args), len(after)),
        out_shape=out,
        in_specs=[HBM] * (len(args) + len(after)),
        out_specs=[HBM] * len(out) if isinstance(out, list) else HBM,
        scratch_shapes=scratch,
        compiler_params=pltpu.CompilerParams(
            collective_id=collective_id, has_side_effects=True, vmem_limit_bytes=vmem * MIB
        ),
        cost_estimate=lasting(micros),
        name=name,
    )(*args, *after)


def gather_u_kernel(n, kinds, *refs):
    r = len(kinds)
    ins, rides, outs, arrived = refs[:n], refs[n : n + r], refs[n + r : 2 * n + r], refs[2 * n + r : 2 * n + 2 * r]
    keep, send_r, send_l, recv_r, recv_l, *ride_sems = refs[2 * n + 2 * r :]
    place = coords()
    me = place["u"]
    greet_line(me, place, ride_greet(kinds, place))
    right, left = device(place, u=jnp.minimum(me + 1, 3)), device(place, u=jnp.maximum(me - 1, 0))

    def spot(owner, slot, a):
        return outs[a].at[:, owner if slot == 0 else 7 - owner]

    def going(step, slot, a, rightward):
        owner = me - step if rightward else me + step
        owner = jnp.clip(owner, 0, 3)
        src = ins[a].at[:, slot] if step == 0 else spot(owner, slot, a)
        send, recv, to = (send_r, recv_l, right) if rightward else (send_l, recv_r, left)
        return remote(src, spot(owner, slot, a), send.at[step, slot, a], recv.at[step, slot, a], to)

    def coming(step, slot, a, from_left):
        owner = jnp.clip(me - 1 - step if from_left else me + 1 + step, 0, 3)
        send, recv, to = (send_r, recv_l, right) if from_left else (send_l, recv_r, left)
        there = spot(owner, slot, a)
        return remote(there, there, send.at[step, slot, a], recv.at[step, slot, a], to)

    parts = [(slot, a) for slot in range(2) for a in range(n)]
    own = [pltpu.make_async_copy(ins[a].at[:, s], spot(me, s, a), keep.at[s, a]) for s, a in parts]
    for step in range(3):
        for part in parts:
            if step > 0:

                @pl.when(me >= step)
                def _():
                    coming(step - 1, *part, True).wait_recv()

            @pl.when((me < 3) & (me >= step))
            def _():
                going(step, *part, True).start()

            if step > 0:

                @pl.when(me <= 3 - step)
                def _():
                    coming(step - 1, *part, False).wait_recv()

            @pl.when((me > 0) & (me <= 3 - step))
            def _():
                going(step, *part, False).start()

        if step == 0:
            for copy in own:
                copy.start()
            ride_start(kinds, rides, arrived, ride_sems, place)
    for part in parts:

        @pl.when(me == 3)
        def _():
            coming(2, *part, True).wait_recv()

        @pl.when(me == 0)
        def _():
            coming(2, *part, False).wait_recv()

    for step in range(3):
        for part in parts:

            @pl.when((me < 3) & (me >= step))
            def _():
                going(step, *part, True).wait_send()

            @pl.when((me > 0) & (me <= 3 - step))
            def _():
                going(step, *part, False).wait_send()

    for copy in own:
        copy.wait()
    ride_end(kinds, rides, arrived, ride_sems, place)


def gather_u(arrays, collective_id, after=(), rides=()):
    n = len(arrays)
    sems = pltpu.SemaphoreType.DMA((3, 2, n))
    return communicating(
        functools.partial(gather_u_kernel, n, [kind for kind, _ in rides]),
        [jax.ShapeDtypeStruct((x.shape[0], 8) + x.shape[2:], x.dtype) for x in arrays]
        + [ride_out(kind, x) for kind, x in rides],
        arrays + [x for _, x in rides],
        [pltpu.SemaphoreType.DMA((2, n)), sems, sems, sems, sems] + (ride_scratch(len(rides)) if rides else []),
        collective_id,
        "gather_u",
        after=after,
    )


def scatter_u_kernel(kinds, *refs):
    r = len(kinds)
    p_ref, *rides = refs[: 1 + r]
    out_ref, *arrived = refs[1 + r : 2 + 2 * r]
    own, from_l, from_r, total, load, send_r, send_l, recv_l, recv_r, store, *ride_sems = refs[2 + 2 * r :]
    place = coords()
    me = place["u"]
    greet_line(me, place, ride_greet(kinds, place))
    ride_start(kinds, rides, arrived, ride_sems, place)
    right, left = device(place, u=jnp.minimum(me + 1, 3)), device(place, u=jnp.maximum(me - 1, 0))

    def mine(owner, slot):
        return p_ref.at[:, owner if slot == 0 else 7 - owner]

    loads = [
        pltpu.make_async_copy(mine(k, s), own.at[k, s], load.at[k, s]) for k in range(4) for s in range(2)
    ]
    order = [3, 0, 2, 1]

    def fetch(k, s):
        return loads[2 * k + s]

    for k in order:
        for s in range(2):
            fetch(k, s).start()

    def rightward(e, s):
        src = from_l.at[e, s]
        return remote(src, from_l.at[e, s], send_r.at[e, s], recv_l.at[e, s], right)

    def rightward_first(e, s):
        return remote(own.at[3 - e, s], from_l.at[e, s], send_r.at[e, s], recv_l.at[e, s], right)

    def leftward(k, s):
        return remote(from_r.at[k, s], from_r.at[k, s], send_l.at[k, s], recv_r.at[k, s], left)

    def leftward_first(k, s):
        return remote(own.at[k, s], from_r.at[k, s], send_l.at[k, s], recv_r.at[k, s], left)

    def add(into, other):
        into[...] = (into[...].astype(f32) + other[...].astype(f32)).astype(into.dtype)

    for s in range(2):
        for k in order:
            fetch(k, s).wait()
        for e in range(3):

            @pl.when(me == 0)
            def _():
                rightward_first(e, s).start()

            @pl.when(me == 3)
            def _():
                leftward_first(e, s).start()

    for e in range(3):
        for s in range(2):

            @pl.when((me > 0) & (me < 3 - e))
            def _():
                rightward(e, s).wait_recv()
                add(from_l.at[e, s], own.at[3 - e, s])
                rightward(e, s).start()

            @pl.when((me < 3) & (me > e))
            def _():
                leftward(e, s).wait_recv()
                add(from_r.at[e, s], own.at[e, s])
                leftward(e, s).start()

    stores = [pltpu.make_async_copy(total.at[s], out_ref.at[:, s], store.at[s]) for s in range(2)]
    for s in range(2):
        total[s] = own[me, s].astype(f32)

        @pl.when(me > 0)
        def _():
            e = jnp.minimum(3 - me, 2)
            rightward(e, s).wait_recv()
            total[s] += from_l[e, s].astype(f32)

        @pl.when(me < 3)
        def _():
            e = jnp.minimum(me, 2)
            leftward(e, s).wait_recv()
            total[s] += from_r[e, s].astype(f32)

        stores[s].start()
    for e in range(3):
        for s in range(2):

            @pl.when(me < 3 - e)
            def _():
                rightward(e, s).wait_send()

            @pl.when(me > e)
            def _():
                leftward(e, s).wait_send()

    for copy in stores:
        copy.wait()
    ride_end(kinds, rides, arrived, ride_sems, place)


def scatter_u(x, rides=(), after=()):
    groups, _, half, cols = x.shape
    piece = (groups, half, cols)
    sems = pltpu.SemaphoreType.DMA((3, 2))
    return communicating(
        functools.partial(scatter_u_kernel, [kind for kind, _ in rides]),
        [jax.ShapeDtypeStruct((groups, 2, half, cols), f32)] + [ride_out(kind, x) for kind, x in rides],
        [x] + [x for _, x in rides],
        [
            pltpu.VMEM((4, 2) + piece, x.dtype),
            pltpu.VMEM((3, 2) + piece, x.dtype),
            pltpu.VMEM((3, 2) + piece, x.dtype),
            pltpu.VMEM((2,) + piece, f32),
            pltpu.SemaphoreType.DMA((4, 2)),
            sems,
            sems,
            sems,
            sems,
            pltpu.SemaphoreType.DMA((2,)),
        ]
        + (ride_scratch(len(rides)) if rides else []),
        1,
        "scatter_u",
        after=after,
    )


def gather_hidden_kernel(x_ref, out_ref, keep, send_x, send_y, recv_x, recv_y):
    place = coords()
    v, f = place["v"], place["f"]
    x_to, y_to = device(place, v=1 - v), device(place, f=1 - f)
    greet([x_to, y_to])
    half = x_ref.shape[0] // 2

    def spot(row, col, h):
        start = pl.multiple_of((row * 2 + col) * 2 * half + h * half, half)
        return out_ref.at[pl.ds(start, half)]

    def own(h):
        return x_ref.at[pl.ds(h * half, half)]

    def via_x(src, dst, i):
        return remote(src, dst, send_x.at[i], recv_x.at[i], x_to)

    def via_y(src, dst, i):
        return remote(src, dst, send_y.at[i], recv_y.at[i], y_to)

    x_own = [via_x(own(h), spot(v, f, h), h) for h in range(2)]
    y_own = [via_y(own(h), spot(v, f, h), h) for h in range(2)]
    x_own[0].start()
    y_own[1].start()
    x_own[1].start()
    y_own[0].start()
    keeps = [pltpu.make_async_copy(own(h), spot(v, f, h), keep.at[h]) for h in range(2)]
    for copy in keeps:
        copy.start()
    via_x(own(0), spot(1 - v, f, 0), 0).wait_recv()
    y_on = via_y(spot(1 - v, f, 0), spot(1 - v, f, 0), 2)
    y_on.start()
    via_y(own(1), spot(v, 1 - f, 1), 1).wait_recv()
    x_on = via_x(spot(v, 1 - f, 1), spot(v, 1 - f, 1), 2)
    x_on.start()
    via_x(own(1), spot(1 - v, f, 1), 1).wait_recv()
    via_y(own(0), spot(v, 1 - f, 0), 0).wait_recv()
    via_x(own(1), spot(1 - v, 1 - f, 1), 2).wait_recv()
    via_y(own(0), spot(1 - v, 1 - f, 0), 2).wait_recv()
    for copy in x_own + y_own + [x_on, y_on]:
        copy.wait_send()
    for copy in keeps:
        copy.wait()


def gather_hidden(x, after=()):
    rows, cols = x.shape
    sems = pltpu.SemaphoreType.DMA((3,))
    return communicating(
        gather_hidden_kernel,
        jax.ShapeDtypeStruct((4 * rows, cols), x.dtype),
        [x],
        [pltpu.SemaphoreType.DMA((2,)), sems, sems, sems, sems],
        2,
        "gather_hidden",
        after=after,
        micros=20,
    )


def scatter_hidden_kernel(p_ref, out_ref, own, got_x, got_y, total, load, send_x, send_y, recv_x, recv_y, store):
    place = coords()
    v, f = place["v"], place["f"]
    x_to, y_to = device(place, v=1 - v), device(place, f=1 - f)
    greet([x_to, y_to])
    half = total.shape[1]

    def mine(row, col, h):
        start = pl.multiple_of((row * 2 + col) * 2 * half + h * half, half)
        return p_ref.at[pl.ds(start, half)]

    corners = [(v, f), (1 - v, f), (v, 1 - f), (1 - v, 1 - f)]
    loads = [
        [pltpu.make_async_copy(mine(*corners[i], h), own.at[i, h], load.at[i, h]) for h in range(2)]
        for i in range(4)
    ]
    for i in (3, 1, 2, 0):
        for h in range(2):
            loads[i][h].start()

    def via_x(src, i):
        return remote(src, got_x.at[i], send_x.at[i], recv_x.at[i], x_to)

    def via_y(src, i):
        return remote(src, got_y.at[i], send_y.at[i], recv_y.at[i], y_to)

    loads[3][0].wait()
    x_far = via_x(own.at[3, 0], 0)
    x_far.start()
    loads[3][1].wait()
    y_far = via_y(own.at[3, 1], 0)
    y_far.start()
    loads[1][0].wait()
    x_near = via_x(own.at[1, 0], 1)
    x_near.start()
    loads[2][1].wait()
    y_near = via_y(own.at[2, 1], 2)
    y_near.start()

    def add(into, other):
        into[...] = (into[...].astype(f32) + other[...].astype(f32)).astype(into.dtype)

    loads[2][0].wait()
    x_far.wait_recv()
    add(own.at[2, 0], got_x.at[0])
    y_sum = via_y(own.at[2, 0], 1)
    y_sum.start()
    loads[1][1].wait()
    y_far.wait_recv()
    add(own.at[1, 1], got_y.at[0])
    x_sum = via_x(own.at[1, 1], 2)
    x_sum.start()
    stores = [
        pltpu.make_async_copy(total.at[h], out_ref.at[pl.ds(h * half, half)], store.at[h]) for h in range(2)
    ]
    loads[0][0].wait()
    loads[0][1].wait()
    x_near.wait_recv()
    y_near.wait_recv()
    total[0] = own[0, 0].astype(f32) + got_x[1].astype(f32)
    total[1] = own[0, 1].astype(f32) + got_y[2].astype(f32)
    y_sum.wait_recv()
    total[0] += got_y[1].astype(f32)
    stores[0].start()
    x_sum.wait_recv()
    total[1] += got_x[2].astype(f32)
    stores[1].start()
    for copy in (x_far, y_far, x_near, y_near, x_sum, y_sum):
        copy.wait_send()
    for copy in stores:
        copy.wait()


def scatter_hidden(x):
    rows, cols = x.shape[0] // 4, x.shape[1]
    half = (rows // 2, cols)
    sems = pltpu.SemaphoreType.DMA((3,))
    return communicating(
        scatter_hidden_kernel,
        jax.ShapeDtypeStruct((rows, cols), f32),
        [x],
        [
            pltpu.VMEM((4, 2) + half, x.dtype),
            pltpu.VMEM((3,) + half, x.dtype),
            pltpu.VMEM((3,) + half, x.dtype),
            pltpu.VMEM((2,) + half, f32),
            pltpu.SemaphoreType.DMA((4, 2)),
            sems,
            sems,
            sems,
            sems,
            pltpu.SemaphoreType.DMA((2,)),
        ],
        3,
        "scatter_hidden",
    )


FLIP = [(0, 1), (1, 0)]


def core_sum_kernel(x_ref, out_ref, mine, got, load, send, recv, store):
    place = coords()
    core = place["core"]
    other = device(place, core=1 - core)
    barrier = pltpu.get_barrier_semaphore()
    pl.semaphore_signal(barrier, inc=1, device_id=other, device_id_type=MESH_IDS)
    pl.semaphore_wait(barrier, 1)
    blocks = x_ref.shape[0]
    order = [(v, f) for v in range(2) for f in range(2)]

    def sending(k):
        v, f = order[k]
        return remote(x_ref.at[:, v, 1 - core, f], got.at[k], send.at[k], recv.at[k], other)

    def loading(k):
        v, f = order[k]
        return pltpu.make_async_copy(x_ref.at[:, v, core, f], mine.at[k], load.at[k])

    def storing(k):
        return pltpu.make_async_copy(mine.at[k], out_ref.at[k], store.at[k])

    for k in range(4):
        sending(k).start()
        loading(k).start()
    for k in range(4):
        loading(k).wait()
        sending(k).wait_recv()
        for i in range(blocks):
            mine[k, i] = (mine[k, i].astype(f32) + got[k, i].astype(f32)).astype(mine.dtype)
        storing(k).start()
    for k in range(4):
        sending(k).wait_send()
        storing(k).wait()


def head_sum_start(x, sizes, collective_id, blocks=1):
    _, many, nv, nc, nf = sizes
    rows, cols = x.shape[0] // (blocks * many * nv * nc * nf), x.shape[1]
    x = x.reshape(blocks, many, nv, nc, nf, rows, cols)
    x = lax.psum_scatter(x, "w", scatter_dimension=1, tiled=False) if many > 1 else x[:, 0]
    sems = pltpu.SemaphoreType.DMA((4,))
    out = communicating(
        core_sum_kernel,
        jax.ShapeDtypeStruct((4, blocks, rows, cols), x.dtype),
        [x],
        [pltpu.VMEM((4, blocks, rows, cols), x.dtype)] * 2 + [sems] * 4,
        collective_id,
        "core_sum",
        micros=12,
    )
    return out.reshape(4, blocks * rows, cols)


def with_rings(x, many):
    return lax.all_gather(x, "w", axis=1) if many > 1 else x[:, None]


def scatter_keys_start(parts, many):
    parts = [x[0] for x in parts]
    if many > 1:
        parts = [lax.psum_scatter(x, "w", scatter_dimension=0, tiled=True) for x in parts]
    along = parts[2][0].astype(f32) + lax.ppermute(parts[3][0], "core", FLIP).astype(f32)
    own = parts[0][0].astype(f32) + lax.ppermute(parts[1][0], "core", FLIP).astype(f32)
    return own, along.astype(bf16)


def scatter_keys_end(own, along, after):
    (along,) = tied([lax.ppermute(along, "v", FLIP)], after)
    return own + along.astype(f32)


def pieces_of(part, axes):
    me = lax.axis_index(axes)
    return [part(me ^ step) for step in (0, 3, 2, 1)]


def tied(xs, after):
    return lax.optimization_barrier((tuple(xs), tuple(after)))[0]


def scatter_pieces(pieces, axes, after=()):
    got = [
        lax.ppermute(piece, axes, [(i, i ^ step) for i in range(4)])
        for step, piece in zip((3, 2, 1), pieces[1:])
    ]
    total = pieces[0].astype(f32)
    for part in tied(got, after):
        total = total + part.astype(f32)
    return total


def pieces_u(x):
    def part(k):
        return jnp.stack(
            [lax.dynamic_index_in_dim(x, k, 0, False), lax.dynamic_index_in_dim(x, 7 - k, 0, False)], 0
        )

    return pieces_of(part, "u")


def pieces_hidden(x):
    blocks = x.reshape(4, x.shape[0] // 4, x.shape[1])
    return pieces_of(lambda k: lax.dynamic_index_in_dim(blocks, k, 0, False), HIDDEN)


def gather_hidden_async(x):
    me = lax.axis_index(HIDDEN)
    out = jnp.zeros((4,) + x.shape, x.dtype)
    for step in range(4):
        part = x if step == 0 else lax.ppermute(x, HIDDEN, [(i, i ^ step) for i in range(4)])
        out = lax.dynamic_update_index_in_dim(out, part, me ^ step, 0)
    return out.reshape(4 * x.shape[0], x.shape[1])


def gather_u_start(x):
    return [x] + [lax.ppermute(x, "u", [(i, i ^ step) for i in range(4)]) for step in (3, 2, 1)]


def gather_u_end(parts, after):
    me = lax.axis_index("u")
    out = jnp.zeros((8,) + parts[0].shape[1:], parts[0].dtype)
    for step, part in zip((0, 3, 2, 1), tied(parts, after)):
        k = me ^ step
        out = lax.dynamic_update_slice_in_dim(out, part[0:1], k, 0)
        out = lax.dynamic_update_slice_in_dim(out, part[1:2], 7 - k, 0)
    return out


def exchange_kernel(sizes, kinds, back, spots, *refs):
    n, more = len(kinds), len(spots) - len(kinds)
    ins, outs = refs[:n], refs[n + more : len(refs) - 3]
    send, recv, keep = refs[len(refs) - 3 :]
    nu, nw, nv, nc, nf = sizes
    place = coords()
    u, w, v, core, f = (place[axis] for axis in ALL)

    def holder(kind, block):
        if kind == "along":
            return (block, w, v, core, f)
        if kind == "heads":
            at = (u * nw + w) * nv + v
            return (block, at // (nf * nc * nv), at // (nf * nc) % nv, at // nf % nc, at % nf)
        return (u, w, block // nf, v, block % nf)

    def owner(kind, slot):
        if kind == "along":
            return (slot, w, v, core, f)
        if kind == "heads":
            at = ((w * nv + v) * nc + core) * nf + f
            return (at // (nv * nw), at // nv % nw, at % nv, slot // nf, slot % nf)
        return (u, w, core, slot // nf, slot % nf)

    def same(other):
        equal = other[0] == u
        for a, b in zip(other[1:], (w, v, core, f)):
            equal = equal & (a == b)
        return equal

    def landing(kind):
        slot = core * nf + f
        block = v * nf + f if kind == "hidden" else u
        return block if back or kind == "along" else slot

    to, frm = (owner, holder) if back else (holder, owner)
    barrier = pltpu.get_barrier_semaphore()
    waits = jnp.int32(0)
    for kind in kinds:
        for i in range(4):
            other = frm(kind, i)

            @pl.when(jnp.logical_not(same(other)))
            def _():
                pl.semaphore_signal(barrier, inc=1, device_id=other, device_id_type=MESH_IDS)

            waits = waits + jnp.where(same(to(kind, i)), 0, 1)
    pl.semaphore_wait(barrier, waits)

    def land(a, at):
        out, first = spots[a]
        return outs[out].at[at] if first is None else outs[out].at[first : first + ins[a].shape[1], at]

    def copy(a, i):
        at = landing(kinds[a])
        return remote(ins[a].at[i], land(a, at), send.at[a, i], recv.at[a, at], to(kinds[a], i))

    def local(a, i):
        return pltpu.make_async_copy(ins[a].at[i], land(a, landing(kinds[a])), keep.at[a])

    own = []
    if more:
        out, first = spots[n]
        own = [pltpu.make_async_copy(refs[n], outs[out].at[first : first + refs[n].shape[0]], keep.at[n])]
    for stage in range(3):
        for rest in own:
            rest.start() if stage == 0 else rest.wait() if stage == 1 else None
        for a in range(n):
            for i in range(4):
                here = same(to(kinds[a], i))

                @pl.when(here)
                def _():
                    local(a, i).start() if stage == 0 else local(a, i).wait() if stage == 1 else None

                @pl.when(jnp.logical_not(here))
                def _():
                    copy(a, i).start() if stage == 0 else copy(a, i).wait_send() if stage == 1 else None

                if stage == 2:

                    @pl.when(jnp.logical_not(same(frm(kinds[a], i))))
                    def _():
                        remote(
                            ins[a].at[i], land(a, i), send.at[a, i], recv.at[a, i], to(kinds[a], i)
                        ).wait_recv()


def exchange(sizes, arrays, kinds, back, collective_id, shapes, spots, after=()):
    n = len(kinds)
    return pl.pallas_call(
        ignoring(functools.partial(exchange_kernel, sizes, kinds, back, spots), len(arrays), len(after)),
        out_shape=[jax.ShapeDtypeStruct(shape, arrays[0].dtype) for shape in shapes],
        in_specs=[HBM] * (len(arrays) + len(after)),
        out_specs=[HBM] * len(shapes),
        scratch_shapes=[
            pltpu.SemaphoreType.DMA((n, 4)),
            pltpu.SemaphoreType.DMA((n, 4)),
            pltpu.SemaphoreType.DMA((n + 1,)),
        ],
        compiler_params=pltpu.CompilerParams(
            collective_id=collective_id, has_side_effects=True, vmem_limit_bytes=16 * MIB
        ),
        cost_estimate=lasting(35),
        name="exchange_back" if back else "exchange",
    )(*arrays, *after)


def pad_columns(x, cols):
    return jnp.pad(x, [(0, 0)] * (x.ndim - 1) + [(0, cols - x.shape[-1])])


def body(sizes, tokens, cotangent, segment, position, gain_attn, w_query, w_key, w_value, w_output, gain_mlp, w_gate, w_up, w_down):
    del segment
    groups, block_rows, width = tokens.shape
    rows = groups * block_rows
    half = block_rows // 2
    hidden = w_gate.shape[1]
    slab = w_gate.shape[0]
    block = w_down.shape[0]
    padded = -(-block // 16) * 16
    nkeys = sizes[1] * sizes[2] * sizes[3]
    wide = 2 * nkeys * padded
    qkv_cols = 1792
    here = (groups, 2, half)
    there = (groups, 8, half)

    gain_one, gain_two = gain_attn.astype(f32)[:, None], gain_mlp.astype(f32)[:, None]
    qkv_local, first_local, second_local = pack_weights(
        sizes, w_query, w_key, w_value, w_gate, w_up, gain_one, gain_two, block, padded
    )
    third = width // 3
    own_down = jnp.pad(w_down, ((0, padded - block), (0, 0))).reshape(padded, 3, third)
    own_down = jnp.transpose(own_down, (1, 0, 2)).reshape(-1, 4, slab, third)
    qkv_local, packed = exchange(
        sizes,
        [qkv_local, first_local, second_local, own_down],
        ["heads", "hidden", "hidden"],
        False,
        6,
        [qkv_local.shape, (6, 4, slab, third)],
        [(0, None), (1, 0), (1, 4), (1, 2)],
    )

    def all_heads(x):
        if sizes[1] > 1:
            x = lax.all_gather(x, "w", axis=0)
        return x.reshape(-1, x.shape[-1])

    sequences = range(groups)
    nlocal = lax.axis_index(KEYS)
    order = jnp.arange(8, dtype=jnp.int32)
    order = nkeys * order + jnp.where(order < 4, nlocal, nkeys - 1 - nlocal)
    text = order[:, None] * half + jnp.arange(half, dtype=jnp.int32)[None, :]
    tiles = 8 // QUERY_BLOCKS
    nq = QUERY_BLOCKS * half
    rates = jnp.exp(jnp.arange(32, dtype=f32) * (-math.log(10000.0) / 32))
    inputs, inverse_one, normed_one = [], [], []
    for g in sequences:
        x = tokens[g].astype(f32)
        inverse = lax.rsqrt(jnp.mean(x * x, -1, keepdims=True) + EPSILON)
        inputs.append(x)
        inverse_one.append(inverse)
        normed_one.append(x * inverse)
    places = jnp.broadcast_to(pad_columns(position.reshape(here), LANES)[:, :, None], (groups, 2, 8, LANES))
    upstream = [cotangent[g].astype(f32) for g in sequences]
    held_one, tables, masks, query, kv, kv_own = ([] for _ in range(6))
    before = []
    for g in sequences:
        sent = [normed_one[g].astype(bf16).reshape(1, 2, half, width), places[g : g + 1]]
        rides = [("gather_keys", kv_own[0].reshape(8, half, 1152)) if g > 0 else ("gather_heads", qkv_local)]
        if g > 0:
            rides.append(("gather_heads", w_output))
        held, seen, got, *out_rows = gather_u(sent, (0, 8)[g], after=before, rides=rides)
        held_one.append(held.reshape(8 * half, width))
        if g == 0:
            qkv_whole = all_heads(got)
        seen = seen[0, :, 0, :half]
        lowest = text - jnp.minimum(seen, WINDOW - 1)
        lows, highs = lowest.reshape(tiles, nq), text.reshape(tiles, nq)
        klo, khi = lows[:, 0] // KEY_TILE, highs[:, -1] // KEY_TILE + 1
        lim = jnp.stack([jnp.tile(lows, (1, 2)), jnp.tile(highs, (1, 2))], 1)
        masks.append((jnp.pad(lim, ((0, 0), (0, 6), (0, 0))), klo, khi))
        angles = seen.reshape(8 * half, 1).astype(f32) * rates[None, :]
        cos, sin = jnp.cos(angles), jnp.sin(angles)
        tables.append((jnp.concatenate([cos, cos, cos, cos], 1), jnp.concatenate([-sin, sin, -sin, sin], 1)))
        own, q = rope(matmul(held_one[g], qkv_whole), *tables[g])
        kv_own.append(own)
        before = [own]
        query.append(q)

    (packed,) = tied([packed], held_one[1:])
    packed = lax.all_gather(packed.reshape(-1, third), HIDDEN_SUM, axis=0)

    def key_arrays(g, others):
        own = kv_own[g].reshape(1, 8, half, 1152)
        kv.append([with_rings(own, sizes[1]), with_rings(others, sizes[1])])

    key_arrays(0, got)
    attn, lse, parts = [], [], []
    out_whole = all_heads(out_rows[0])
    out_whole = jnp.concatenate([out_whole[:512], jnp.zeros((64, width), bf16), out_whole[512:]], 0)
    rides = [("gather_keys", kv_own[1].reshape(8, half, 1152))]
    before = kv_own[1:]
    for g in sequences:
        out, sums, got_zero, *got = flash_forward(query[g], kv[g], *masks[g], after=before, rides=rides, ident=(9, 10)[g])
        attn.append(out)
        lse.append(sums)
        if g == 0:
            key_arrays(1, got_zero)
        parts.append(matmul(out, out_whole).astype(bf16).reshape(8, half, width))
        before, rides = [], [("scatter_u", parts[g])]
        rides += [("gather_hidden", (BRANCH_SCALE * x).astype(bf16)) for x in upstream]
    back_mlp = [x.reshape(4 * block_rows, width) for x in got]

    def own_u(x):
        me = lax.axis_index("u")
        return jnp.stack([lax.dynamic_index_in_dim(x, me, 0, False), lax.dynamic_index_in_dim(x, 7 - me, 0, False)], 0)

    def own_hidden(x):
        return lax.dynamic_index_in_dim(x, lax.axis_index(HIDDEN), 0, False)

    def total(own, got):
        return own.astype(f32) + jnp.sum(got.astype(f32), 0)

    middle, inverse_two, normed_two, held_two, activated, back_gu, back_held, mlp_part = ([] for _ in range(8))

    def to_feed_forward(g, got):
        x = inputs[g] + BRANCH_SCALE * total(own_u(parts[g]), got).reshape(block_rows, width)
        inverse = lax.rsqrt(jnp.mean(x * x, -1, keepdims=True) + EPSILON)
        middle.append(x)
        inverse_two.append(inverse)
        normed_two.append(x * inverse)
        held_two.append(gather_hidden(normed_two[g].astype(bf16)))

    def from_feed_forward(act, back_gate, back_up, back, part):
        activated.append(act)
        back_gu.append([back_gate, back_up])
        back_held.append(back.reshape(4, block_rows, width))
        mlp_part.append(part.reshape(4, block_rows, width))

    to_feed_forward(0, got_zero)
    *results, got_one = feed_forward(
        held_two[0], back_mlp[0], packed, wide, rides=[("scatter_u", parts[1])], ident=11
    )
    from_feed_forward(*results)
    back_middle, sent = [], []

    def to_attention(g, sums):
        x = upstream[g] + rms_back(sums, normed_two[g], inverse_two[g])
        back_middle.append(x)
        sent.append((BRANCH_SCALE * x).astype(bf16).reshape(2, half, width))

    to_attention(0, scatter_hidden(back_held[0].reshape(4 * block_rows, width)))
    to_feed_forward(1, got_one)
    *results, back_branch_zero, got_mlp = feed_forward(
        held_two[1],
        back_mlp[1],
        packed,
        wide,
        after=sent,
        rides=[("gather_u", sent[0]), ("scatter_hidden", mlp_part[0])],
        ident=12,
    )
    from_feed_forward(*results)
    layer_out = [(middle[0] + BRANCH_SCALE * total(own_hidden(mlp_part[0]), got_mlp)).astype(bf16)]
    (down_term,) = weight_gradient(activated, [[back_mlp[i]] for i in sequences])
    down_sum = lax.psum_scatter(down_term, HIDDEN_SUM, scatter_dimension=0, tiled=True)
    gu_term, got_one = weight_gradient(
        held_two, back_gu, after=[down_term], rides=[("scatter_hidden", back_held[1])], ident=13
    )
    to_attention(1, total(own_hidden(back_held[1]), got_one))
    back_branch = [back_branch_zero.reshape(8 * half, width)]
    dkv_own, dkv_along, dq = [], [], []
    rides = [("gather_u", sent[1]), ("scatter_hidden", mlp_part[1])]
    for g in sequences:
        do = times_transposed(back_branch[g], out_whole).astype(bf16)
        lim, klo, khi = masks[g]
        dq_part, *rest = flash_backward(
            query[g], do, attn[g], kv[g], lim, lse[g], klo, khi, rides=rides, ident=(14, 17)[g]
        )
        if g == 0:
            back_branch.append(rest[4].reshape(8 * half, width))
            layer_out.append((middle[1] + BRANCH_SCALE * total(own_hidden(mlp_part[1]), rest[5])).astype(bf16))
            dq_part, gu_term, down_sum = lax.optimization_barrier((dq_part, gu_term, down_sum))
            gu_sum = lax.psum_scatter(gu_term, HIDDEN_SUM, scatter_dimension=0, tiled=True)
        dq.append(dq_part)
        own, along = scatter_keys_start(rest[:4], sizes[1])
        dkv_own.append(own)
        dkv_along.append(along)
        rides = [("swap_v", along)]
    (out_term,) = weight_gradient(attn, [[x] for x in back_branch], tile=LANES, after=[along])
    out_half = head_sum_start(jnp.concatenate([out_term[:512], out_term[576:]], 0), sizes, 18)
    before = [out_term]
    back_qkv, late, grad_tokens = [], [], []
    for g in sequences:
        dkv = dkv_own[0] + rest[4].astype(f32) if g == 0 else scatter_keys_end(dkv_own[1], dkv_along[1], before)
        dkv = dkv.reshape(8 * half, 1152)
        back_qkv.append(unrope(dkv, dq[g], *tables[g], after=before))
        part = times_transposed(back_qkv[g], qkv_whole).astype(bf16)
        late.append(part.reshape(8, half, width))
        before = [part]
    qkv_term, got, out_got = weight_gradient(
        held_one,
        [[x] for x in back_qkv],
        after=before,
        rides=[("scatter_u", late[0]), ("scatter_hidden", out_half)],
        ident=15,
    )
    grad_output = total(own_hidden(out_half), out_got)
    qkv_half = head_sum_start(qkv_term, sizes, 19, 4)
    late_one, qkv_got = scatter_u(late[1][None], rides=[("scatter_hidden", qkv_half)])
    qkv_sum = total(own_hidden(qkv_half), qkv_got).astype(bf16)
    for g, part in enumerate((total(own_u(late[0]), got), late_one)):
        part = part.reshape(block_rows, width)
        x = back_middle[g] + rms_back(part, normed_one[g], inverse_one[g])
        grad_tokens.append(x.astype(bf16))
    layer_out, grad_tokens = jnp.stack(layer_out, 0), jnp.stack(grad_tokens, 0)

    qkv_sum, gu_sum = exchange(
        sizes,
        [qkv_sum.reshape(4, slab, qkv_cols), gu_sum.reshape(4, slab, 2 * wide)],
        ["along", "hidden"],
        True,
        7,
        [(4, slab, qkv_cols), (4, slab, 2 * wide)],
        [(0, None), (1, None)],
        after=[grad_tokens],
    )
    grad_query, grad_key, grad_value, grad_gate, grad_up, grad_gain_attn, grad_gain_mlp = unpack_gradients(
        sizes, qkv_sum, gu_sum, w_query, w_key, w_value, w_gate, w_up, gain_one, gain_two, block, padded
    )
    grad_down = down_sum[:block].astype(f32)
    return (
        layer_out,
        grad_tokens,
        grad_gain_attn[:, 0],
        grad_query,
        grad_key,
        grad_value,
        grad_output,
        grad_gain_mlp[:, 0],
        grad_gate,
        grad_up,
        grad_down,
    )


def solution(mesh):
    ctx, fsdp = mesh.shape["ctx"], mesh.shape["fsdp"]
    sizes = (4, ctx // 16, 2, 2, fsdp)
    fine = Mesh(mesh.devices.reshape(sizes), ALL)
    blocks = ("u", "w", "v", "core")
    act = P("f", blocks, None)
    ids = P("f", blocks)
    gain, weight = P(ALL), P(ALL, None)
    return jax.shard_map(
        functools.partial(body, sizes),
        mesh=fine,
        in_specs=(act, act, ids, ids, gain, weight, weight, weight, weight, gain, weight, weight, weight),
        out_specs=(act, act, gain, weight, weight, weight, weight, gain, weight, weight, weight),
        check_vma=False,
    )
```

```python
import functools
import math

import jax
import jax.numpy as jnp
from jax import lax
from jax.experimental import pallas as pl
from jax.experimental.pallas import tpu as pltpu
from jax.sharding import Mesh, PartitionSpec as P

HEADS = 36
HEAD_DIM = 64
WINDOW = 1024
EPSILON = 1e-05
BRANCH_SCALE = 1.4 / math.sqrt(40.0)
NEG_LARGE = -1e30
LANES = 128
PAIRS = 5
KEY_TILE = 512
QUERY_BLOCKS = 2
MIB = 1024 * 1024

f32, bf16 = jnp.float32, jnp.bfloat16


def matmul(left, right):
    return jnp.dot(left, right, preferred_element_type=f32)


def times_transposed(left, right):
    return lax.dot_general(left, right, (((1,), (1,)), ((), ())), preferred_element_type=f32)


def transposed_times(left, right):
    return lax.dot_general(left, right, (((0,), (0,)), ((), ())), preferred_element_type=f32)


def rms_back(upstream, normed, inverse):
    return inverse * (upstream - normed * jnp.mean(upstream * normed, -1, keepdims=True))


HBM = pl.BlockSpec(memory_space=pl.ANY)


def ignoring(kernel, args, extra):
    return lambda *refs: kernel(*refs[:args], *refs[args + extra :])


def lasting(micros):
    return pl.CostEstimate(flops=0, bytes_accessed=micros * 3_600_000, transcendentals=0)


MESH_IDS = pl.DeviceIdType.MESH
ALL = ("u", "w", "v", "core", "f")
KEYS = ("w", "v", "core")
HEAD_SUM = ("w", "v", "core", "f")
HIDDEN = ("v", "f")
HIDDEN_SUM = ("u", "w", "core")


def coords():
    return {axis: lax.axis_index(axis) for axis in ALL}


def device(place, **moved):
    return tuple(moved.get(axis, place[axis]) for axis in ALL)


def remote(src, dst, send, recv, where):
    return pltpu.make_async_remote_copy(
        src_ref=src, dst_ref=dst, send_sem=send, recv_sem=recv, device_id=where, device_id_type=MESH_IDS
    )


def ride_out(kind, x):
    shape = {
        "gather_u": (8,) + x.shape[1:],
        "scatter_u": (3, 2) + x.shape[1:],
        "gather_hidden": (4,) + x.shape,
        "scatter_hidden": (3,) + x.shape[1:],
        "gather_keys": (3,) + x.shape,
        "swap_v": x.shape,
        "gather_heads": (8,) + x.shape,
    }
    return jax.ShapeDtypeStruct(shape[kind], x.dtype)


STEPS = {"gather_keys": (2, 1), "swap_v": (2,)}


def partner(kind, place, step):
    if kind in ("gather_u", "scatter_u"):
        k = place["u"] ^ step
        return k, device(place, u=k)
    if kind in ("gather_keys", "swap_v"):
        k = (2 * place["v"] + place["core"]) ^ step
        return k, device(place, v=k // 2, core=k % 2)
    k = (2 * place["v"] + place["f"]) ^ step
    return k, device(place, v=k // 2, f=k % 2)


def ride_slices(kind, src, dst, place, step):
    k, _ = partner(kind, place, step)
    t = 2 * place["v"] + place["f"]
    if kind == "scatter_u":
        return [(src.at[7 - k if s else k], dst.at[step - 1, s], dst.at[step - 1, s]) for s in range(2)]
    if kind == "gather_hidden":
        return [(src, dst.at[t], dst.at[k])]
    if kind == "scatter_hidden":
        return [(src.at[k], dst.at[step - 1], dst.at[step - 1])]
    if kind == "swap_v":
        return [(src, dst, dst)]
    return [(src, dst.at[step - 1], dst.at[step - 1])]


def ride_copies(kind, src, dst, send, recv, place, part):
    if kind == "gather_keys" and part == "on":
        _, to = partner(kind, place, 1)
        return [remote(dst.at[1], dst.at[2], send.at[4], recv.at[4], to)]
    copies = []
    for step in STEPS.get(kind, (3, 2, 1)):
        _, to = partner(kind, place, step)
        for i, (here, there, landing) in enumerate(ride_slices(kind, src, dst, place, step)):
            at = 2 * step - 2 + i
            if part == "away":
                copies.append(remote(here, there, send.at[at], recv.at[at], to))
            else:
                copies.append(remote(landing, landing, send.at[at], recv.at[at], to))
    return copies


def own_copies(kind, src, dst, keep, place):
    u, t = place["u"], 2 * place["v"] + place["f"]
    if kind == "gather_u":
        return [pltpu.make_async_copy(src.at[s], dst.at[7 - u if s else u], keep.at[s]) for s in range(2)]
    return [pltpu.make_async_copy(src, dst.at[t], keep.at[0])] if kind == "gather_hidden" else []


def chain_u(stage, src, dst, send, recv, place):
    me = place["u"]
    right, left = device(place, u=jnp.minimum(me + 1, 3)), device(place, u=jnp.maximum(me - 1, 0))

    def spot(owner, slot):
        return dst.at[7 - owner if slot else owner]

    def going(step, slot, side):
        owner = jnp.clip(me + step if side else me - step, 0, 3)
        here = src.at[slot] if step == 0 else spot(owner, slot)
        at = 6 * side + 2 * step + slot
        return remote(here, spot(owner, slot), send.at[at], recv.at[at], left if side else right)

    def coming(step, slot, side):
        there = spot(jnp.clip(me + 1 + step if side else me - 1 - step, 0, 3), slot)
        at = 6 * side + 2 * step + slot
        return remote(there, there, send.at[at], recv.at[at], right if side else left)

    def sends(step, side):
        return (me > 0) & (me <= 3 - step) if side else (me < 3) & (me >= step)

    def gets(step, side):
        return me <= 2 - step if side else me >= step + 1

    for slot in range(2):
        for side in range(2):
            if stage > 0:

                @pl.when(gets(stage - 1, side))
                def _():
                    coming(stage - 1, slot, side).wait_recv()

            if stage < 3:

                @pl.when(sends(stage, side))
                def _():
                    going(stage, slot, side).start()

    if stage == 3:
        for step in range(3):
            for slot in range(2):
                for side in range(2):

                    @pl.when(sends(step, side))
                    def _():
                        going(step, slot, side).wait_send()


def gather_heads(stage, src, dst, send, recv, keep, place):
    v, core, f = place["v"], place["core"], place["f"]
    mine = (2 * v + core) * 2 + f
    other = device(place, core=1 - core)

    def away(step):
        _, to = partner("gather_hidden", place, step)
        return remote(src, dst.at[mine], send.at[step], recv.at[step], to)

    def on(step):
        k = (2 * v + f) ^ step
        there = dst.at[(2 * (k // 2) + core) * 2 + k % 2]
        return remote(src if step == 0 else there, there, send.at[4 + step], recv.at[4 + step], other)

    def landed(step):
        k = (2 * v + f) ^ step
        there = dst.at[(2 * (k // 2) + core) * 2 + k % 2]
        return remote(there, there, send.at[step], recv.at[step], other)

    def passed(step):
        k = (2 * v + f) ^ step
        there = dst.at[(2 * (k // 2) + 1 - core) * 2 + k % 2]
        return remote(there, there, send.at[4 + step], recv.at[4 + step], other)

    local = pltpu.make_async_copy(src, dst.at[mine], keep.at[0]) if stage != 1 else None
    if stage == 0:
        local.start()
        for step in (3, 2, 1):
            away(step).start()
        on(0).start()
    elif stage == 1:
        for step in (1, 2, 3):
            landed(step).wait_recv()
            on(step).start()
    else:
        local.wait()
        for step in (1, 2, 3):
            away(step).wait_send()
        for step in range(4):
            on(step).wait_send()
            passed(step).wait_recv()


def ride_greet(kinds, place):
    barrier = pltpu.get_barrier_semaphore()
    count = 0
    for kind in kinds:
        if kind == "gather_heads":
            other = device(place, core=1 - place["core"])
            pl.semaphore_signal(barrier, inc=1, device_id=other, device_id_type=MESH_IDS)
            count = count + 1
        for step in STEPS.get(kind, (3, 2, 1)):
            _, to = partner(kind, place, step)
            pl.semaphore_signal(barrier, inc=1, device_id=to, device_id_type=MESH_IDS)
            count = count + 1
    return count


def ride_start(kinds, rides, arrived, sems, place):
    for a, kind in enumerate(kinds):
        send, recv, keep = (sem.at[a] for sem in sems)
        if kind == "gather_u":
            chain_u(0, rides[a], arrived[a], send, recv, place)
        elif kind == "gather_heads":
            gather_heads(0, rides[a], arrived[a], send, recv, keep, place)
        else:
            for copy in ride_copies(kind, rides[a], arrived[a], send, recv, place, "away"):
                copy.start()
        for copy in own_copies(kind, rides[a], arrived[a], keep, place):
            copy.start()


def ride_on(kinds, rides, arrived, sems, place, stage):
    for a, kind in enumerate(kinds):
        if kind == "gather_u":
            chain_u(stage, rides[a], arrived[a], sems[0].at[a], sems[1].at[a], place)


def ride_end(kinds, rides, arrived, sems, place):
    def copies(a, part):
        return ride_copies(kinds[a], rides[a], arrived[a], sems[0].at[a], sems[1].at[a], place, part)

    def heads(a, stage):
        gather_heads(stage, rides[a], arrived[a], *(sem.at[a] for sem in sems), place)

    keys = [a for a, kind in enumerate(kinds) if kind == "gather_keys"]
    for a, kind in enumerate(kinds):
        if kind == "gather_heads":
            heads(a, 1)
    for a in keys:
        for copy in copies(a, "back"):
            copy.wait_recv()
        for copy in copies(a, "on"):
            copy.start()
    for a, kind in enumerate(kinds):
        for copy in own_copies(kind, rides[a], arrived[a], sems[2].at[a], place):
            copy.wait()
        if kind == "gather_u":
            chain_u(3, rides[a], arrived[a], sems[0].at[a], sems[1].at[a], place)
            continue
        if kind == "gather_heads":
            heads(a, 2)
            continue
        for copy in copies(a, "away"):
            copy.wait_send()
        for copy in copies(a, "back") if a not in keys else ():
            copy.wait_recv()
    for a in keys:
        for copy in copies(a, "on"):
            copy.wait()


def ride_scratch(n):
    return [pltpu.SemaphoreType.DMA((n, 12)), pltpu.SemaphoreType.DMA((n, 12)), pltpu.SemaphoreType.DMA((n, 2))]


def riding(kernel, args, extra, outs, kinds, grid):
    n = len(kinds)

    def whole(*refs):
        ins, rides = refs[:args], refs[args : args + n]
        rest = refs[args + n + extra :]
        results, arrived, scratch = rest[:outs], rest[outs : outs + n], rest[outs + n : len(rest) - 3]
        sems = rest[len(rest) - 3 :]
        place = coords()
        ids = [pl.program_id(i) for i in range(len(grid))]
        first, last = ids[0] == 0, ids[0] == grid[0] - 1
        for i in range(1, len(grid)):
            first, last = first & (ids[i] == 0), last & (ids[i] == grid[i] - 1)

        @pl.when(first)
        def _():
            count = ride_greet(kinds, place)
            pl.semaphore_wait(pltpu.get_barrier_semaphore(), count)
            ride_start(kinds, rides, arrived, sems, place)

        kernel(*ins, *results, *scratch)

        if "gather_u" in kinds:
            total = math.prod(grid)
            at = ids[0]
            for i in range(1, len(grid)):
                at = at * grid[i] + ids[i]
            for stage in (1, 2):

                @pl.when(at == total * stage // 3 - 1)
                def _():
                    ride_on(kinds, rides, arrived, sems, place, stage)

        @pl.when(last)
        def _():
            ride_end(kinds, rides, arrived, sems, place)

    return whole


def grid_call(kernel, grid, args, in_specs, out_specs, out_shape, scratch, name, micros, after=(), rides=(), ident=None):
    limit = 56 * MIB
    if not rides:
        return pl.pallas_call(
            ignoring(kernel, len(args), len(after)),
            grid=grid,
            in_specs=in_specs + [HBM] * len(after),
            out_specs=out_specs,
            out_shape=out_shape,
            scratch_shapes=scratch,
            compiler_params=pltpu.CompilerParams(vmem_limit_bytes=limit),
            cost_estimate=lasting(micros),
            name=name,
        )(*args, *after)
    kinds = [kind for kind, _ in rides]
    n = len(rides)
    return pl.pallas_call(
        riding(kernel, len(args), len(after), len(out_shape), kinds, grid),
        grid=grid,
        in_specs=in_specs + [HBM] * (n + len(after)),
        out_specs=out_specs + [HBM] * n,
        out_shape=out_shape + [ride_out(kind, x) for kind, x in rides],
        scratch_shapes=scratch + ride_scratch(n),
        compiler_params=pltpu.CompilerParams(vmem_limit_bytes=limit, collective_id=ident, has_side_effects=True),
        cost_estimate=lasting(max(micros, 50)),
        name=name + "_riding",
    )(*args, *[x for _, x in rides], *after)


def swap_halves(x):
    lane = lax.broadcasted_iota(jnp.int32, x.shape, 1)
    return jnp.where(lane % 64 < 32, pltpu.roll(x, LANES - 32, 1), pltpu.roll(x, 32, 1))


def rope_kernel(raw_ref, cos_ref, sin_ref, kv_ref, q_ref):
    cos, sin = cos_ref[...], sin_ref[...]

    def turn(x):
        return x * cos + swap_halves(x) * sin

    for p in range(4):
        kv_ref[:, 256 * p : 256 * p + 128] = turn(raw_ref[:, 256 * p : 256 * p + 128]).astype(bf16)
        kv_ref[:, 256 * p + 128 : 256 * p + 256] = raw_ref[:, 256 * p + 128 : 256 * p + 256].astype(bf16)
    last = raw_ref[:, 1024:1152]
    lane = lax.broadcasted_iota(jnp.int32, last.shape, 1)
    kv_ref[:, 1024:1152] = jnp.where(lane < 64, turn(last), last).astype(bf16)
    for p in range(5):
        q_ref[:, 128 * p : 128 * p + 128] = turn(raw_ref[:, 1152 + 128 * p : 1280 + 128 * p]).astype(bf16)


def rope(raw, cos, sin):
    rows = raw.shape[0]
    tile = min(256, rows)
    row = lambda cols: pl.BlockSpec((tile, cols), lambda i: (i, 0))
    return pl.pallas_call(
        rope_kernel,
        grid=(rows // tile,),
        in_specs=[row(1792), row(LANES), row(LANES)],
        out_specs=[row(1152), row(640)],
        out_shape=[jax.ShapeDtypeStruct((rows, 1152), bf16), jax.ShapeDtypeStruct((rows, 640), bf16)],
        compiler_params=pltpu.CompilerParams(vmem_limit_bytes=40 * MIB),
        name="rope",
    )(raw, cos, sin)


def unrope_kernel(dkv_ref, dq_ref, cos_ref, sin_ref, out_ref):
    cos, sin = cos_ref[...], sin_ref[...]

    def turn(x):
        return x * cos - swap_halves(x) * sin

    for p in range(4):
        a = 256 * p
        out_ref[:, a : a + 128] = turn(dkv_ref[:, a : a + 128].astype(f32)).astype(bf16)
        out_ref[:, a + 128 : a + 256] = dkv_ref[:, a + 128 : a + 256].astype(bf16)
    last = dkv_ref[:, 1024:1152].astype(f32)
    lane = lax.broadcasted_iota(jnp.int32, last.shape, 1)
    out_ref[:, 1024:1152] = jnp.where(lane < 64, turn(last), last).astype(bf16)
    for p in range(5):
        out_ref[:, 1152 + 128 * p : 1280 + 128 * p] = turn(
            dq_ref[:, 128 * p : 128 * p + 128].astype(f32)
        ).astype(bf16)


def unrope(dkv, dq, cos, sin, after=()):
    rows = dkv.shape[0]
    tile = min(256, rows)
    row = lambda cols: pl.BlockSpec((tile, cols), lambda i: (i, 0))
    return pl.pallas_call(
        ignoring(unrope_kernel, 4, len(after)),
        grid=(rows // tile,),
        in_specs=[row(1152), row(640), row(LANES), row(LANES)] + [HBM] * len(after),
        out_specs=row(1792),
        out_shape=jax.ShapeDtypeStruct((rows, 1792), bf16),
        compiler_params=pltpu.CompilerParams(vmem_limit_bytes=40 * MIB),
        name="unrope",
    )(dkv, dq, cos, sin, *after)


def hidden_blocks(sizes):
    nu, nw, nv, nc, nf = sizes
    out = []
    for i in range(nu * nw * nv * nc * nf):
        rest, f = divmod(i, nf)
        rest, core = divmod(rest, nc)
        uw, v = divmod(rest, nv)
        out.append((v * nf + f, uw * nc + core))
    return out


def pack_kernel(spots, block, q_ref, k_ref, v_ref, g_ref, u_ref, one_ref, two_ref, qkv_ref, first_ref, second_ref):
    slab = q_ref.shape[0]
    one, two = one_ref[...], two_ref[...]
    padded = 8 * first_ref.shape[3] // len(spots)

    def scaled(ref, start, size, gain):
        return ref[:, start : start + size].astype(f32) * gain

    for t in range(4):
        cols = []
        at = 576 * t
        for p in range(4):
            cols.append(scaled(k_ref, at + 128 * p, 128, one))
            cols.append(scaled(v_ref, at + 128 * p, 128, one))
        cols.append(scaled(k_ref, at + 512, 64, one))
        cols.append(scaled(v_ref, at + 512, 64, one))
        cols.append(scaled(q_ref, at, 576, one))
        cols.append(jnp.zeros((slab, 64), f32))
        qkv_ref[t] = jnp.concatenate(cols, 1).astype(bf16)
        mine = sorted((place, i) for i, (owner, place) in enumerate(spots) if owner == t)
        for half, ref in enumerate((g_ref, u_ref)):
            cols = []
            for _, i in mine:
                cols.append(scaled(ref, i * block, block, two))
                cols.append(jnp.zeros((slab, padded - block), f32))
            whole = jnp.concatenate(cols, 1).astype(bf16)
            cut = first_ref.shape[3]
            first_ref[t, half] = whole[:, :cut]
            second_ref[t, half] = whole[:, cut:]


def pack_weights(sizes, w_query, w_key, w_value, w_gate, w_up, gain_one, gain_two, block, padded):
    slab = w_query.shape[0]
    spots = hidden_blocks(sizes)
    cut = padded * len(spots) // 8
    return pl.pallas_call(
        functools.partial(pack_kernel, spots, block),
        out_shape=[jax.ShapeDtypeStruct((4, slab, 1792), bf16)]
        + [jax.ShapeDtypeStruct((4, 2, slab, cut), bf16)] * 2,
        compiler_params=pltpu.CompilerParams(vmem_limit_bytes=48 * MIB),
        cost_estimate=lasting(10),
        name="pack_weights",
    )(w_query, w_key, w_value, w_gate, w_up, gain_one, gain_two)


def unpack_kernel(
    spots, block, padded, qkv_ref, gu_ref, q_ref, k_ref, v_ref, g_ref, u_ref, one_ref, two_ref,
    dq_ref, dk_ref, dv_ref, dg_ref, du_ref, done_ref, dtwo_ref,
):
    one, two = one_ref[...], two_ref[...]
    gains = jnp.zeros_like(one)
    wide = gu_ref.shape[2] // 2

    def part(t, start, size):
        return qkv_ref[t, :, start : start + size].astype(f32)

    for ref, out, first, last in ((k_ref, dk_ref, 0, 1024), (v_ref, dv_ref, 128, 1088)):
        cols = []
        for t in range(4):
            cols += [part(t, first + 256 * p, 128) for p in range(4)] + [part(t, last, 64)]
        grad = jnp.concatenate(cols, 1)
        gains = gains + jnp.sum(ref[...].astype(f32) * grad, 1, keepdims=True)
        out[...] = grad * one
    grad = jnp.concatenate([part(t, 1152, 576) for t in range(4)], 1)
    done_ref[...] = gains + jnp.sum(q_ref[...].astype(f32) * grad, 1, keepdims=True)
    dq_ref[...] = grad * one
    gains = jnp.zeros_like(two)
    for half, (ref, out) in enumerate(((g_ref, dg_ref), (u_ref, du_ref))):
        grad = jnp.concatenate(
            [
                gu_ref[t, :, half * wide + place * padded : half * wide + place * padded + block].astype(f32)
                for t, place in spots
            ],
            1,
        )
        gains = gains + jnp.sum(ref[...].astype(f32) * grad, 1, keepdims=True)
        out[...] = grad * two
    dtwo_ref[...] = gains


def unpack_gradients(sizes, qkv, gu, w_query, w_key, w_value, w_gate, w_up, gain_one, gain_two, block, padded):
    slab, width = w_query.shape
    hidden = w_gate.shape[1]
    shape = lambda cols: jax.ShapeDtypeStruct((slab, cols), f32)
    return pl.pallas_call(
        functools.partial(unpack_kernel, hidden_blocks(sizes), block, padded),
        out_shape=[shape(width)] * 3 + [shape(hidden)] * 2 + [shape(1)] * 2,
        compiler_params=pltpu.CompilerParams(vmem_limit_bytes=48 * MIB),
        cost_estimate=lasting(15),
        name="unpack_gradients",
    )(qkv, gu, w_query, w_key, w_value, w_gate, w_up, gain_one, gain_two)


def stack_heads(x, first, second):
    return jnp.concatenate([jnp.where(first, x, 0), jnp.where(second, x, 0)], 0)


def text_rows(source, ring, j, half, many):
    v, core = lax.axis_index("v"), lax.axis_index("core")
    v = 1 - v if source // 2 else v
    core = 1 - core if source % 2 else core
    at = (ring * 2 + v) * 2 + core
    block = many * j + (at if j < 4 else many - 1 - at)
    return pl.multiple_of(block * half, half)


def assemble(kv_refs, kv_s):
    rings, _, half, _ = kv_refs[0].shape
    for source, ref in enumerate(kv_refs):
        for ring in range(rings):
            for j in range(8):
                kv_s[pl.ds(text_rows(source, ring, j, half, 4 * rings), half), :] = ref[ring, j]


def flash_forward_kernel(
    bounds, q_ref, kv0, kv1, kv2, kv3, lim_ref, o_ref, lse_ref, kv_s, s_ref, vt_ref
):
    p, t = pl.program_id(0), pl.program_id(1)
    nq = q_ref.shape[0]
    tail = p == 4
    voff = pl.multiple_of(jnp.where(tail, 0, LANES), LANES)
    tiles = s_ref.shape[0]

    @pl.when(t == 0)
    def _():
        assemble((kv0, kv1, kv2, kv3), kv_s)
        for k in range(tiles):
            vt_ref[k] = kv_s[k * KEY_TILE : (k + 1) * KEY_TILE, pl.ds(voff, LANES)].T

    lane = lax.broadcasted_iota(jnp.int32, (nq, LANES), 1)
    qm = stack_heads(q_ref[...] * bf16(0.125), lane < 64, lane >= 64)
    lo, hi = lim_ref[0, 0:1, :], lim_ref[0, 1:2, :]
    row = lax.broadcasted_iota(jnp.int32, (KEY_TILE, 2 * nq), 0)
    klo, khi = bounds(t)

    def scores(k, high):
        base = pl.multiple_of(k * KEY_TILE, KEY_TILE)
        s = times_transposed(kv_s[pl.ds(base, KEY_TILE), 0:LANES], qm)
        s = jnp.where((row >= lo - base) & (row <= hi - base), s, NEG_LARGE)
        s_ref[k] = s
        return jnp.maximum(high, jnp.max(s.reshape(KEY_TILE // 8, 8, 2 * nq), 0))

    high = lax.fori_loop(klo, khi, scores, jnp.full((8, 2 * nq), NEG_LARGE, f32))
    high = jnp.max(high, 0, keepdims=True)

    def mix(k, carry):
        total, acc = carry
        w = jnp.exp(s_ref[k] - high)
        total = total + jnp.sum(w.reshape(KEY_TILE // 8, 8, 2 * nq), 0)
        acc = acc + matmul(vt_ref[k], w.astype(bf16))
        return total, acc

    total, acc = lax.fori_loop(
        klo, khi, mix, (jnp.zeros((8, 2 * nq), f32), jnp.zeros((LANES, 2 * nq), f32))
    )
    total = jnp.sum(total, 0, keepdims=True)
    out = (acc / total).T
    first, second = out[:nq], out[nq:]
    low = jnp.where(tail, 0.0, first)
    up = jnp.where(tail, first, second)
    o_ref[...] = jnp.where(lane < 64, low, up).astype(bf16)
    lse_ref[0, 0] = jnp.broadcast_to(high + jnp.log(total), (8, 2 * nq))


def flash_specs(rows, tiles, kv):
    nq = rows // tiles
    _, rings, _, half, _ = kv[0].shape
    part = pl.BlockSpec((nq, LANES), lambda p, t, *_: (t, p))
    keys = [
        pl.BlockSpec((None, rings, 8, half, 2 * LANES), lambda p, t, *_, i=i: (i, 0, 0, 0, p)) for i in (0, 0, 1, 2)
    ]
    lim = pl.BlockSpec((1, 8, 2 * nq), lambda p, t, *_: (t, 0, 0))
    lse = pl.BlockSpec((1, 1, 8, 2 * nq), lambda p, t, *_: (p, t, 0, 0))
    return nq, 32 * rings * half, part, keys, lim, lse


def window_bounds(rows, tiles, rings):
    half, many = rows // 8, 4 * rings

    def bounds(t):
        at = (lax.axis_index("w") * 2 + lax.axis_index("v")) * 2 + lax.axis_index("core")

        def first_row(j):
            return (many * j + jnp.where(j < 4, at, many - 1 - at)) * half

        low = jnp.maximum(first_row(t * QUERY_BLOCKS) - (WINDOW - 1), 0)
        high = first_row(t * QUERY_BLOCKS + QUERY_BLOCKS - 1) + half - 1
        return low // KEY_TILE, high // KEY_TILE + 1

    return bounds


def flash_call(kernel, name, args, klo, khi, in_specs, out_specs, out_shape, scratch, micros, after, rides, ident):
    tiles = klo.shape[0]
    grid = (PAIRS, tiles)
    if rides:
        bounds = window_bounds(args[0].shape[0], tiles, args[-3 if name == "flash_backward" else -2].shape[1])
        return grid_call(
            functools.partial(kernel, bounds), grid, args, in_specs, out_specs, out_shape, scratch, name, micros,
            after, rides, ident,
        )

    def bounded(klo_ref, khi_ref, *refs):
        kernel(lambda t: (klo_ref[t], khi_ref[t]), *refs)

    return pl.pallas_call(
        ignoring(bounded, 2 + len(args), len(after)),
        grid_spec=pltpu.PrefetchScalarGridSpec(
            num_scalar_prefetch=2,
            grid=grid,
            in_specs=in_specs + [HBM] * len(after),
            out_specs=out_specs,
            scratch_shapes=scratch,
        ),
        out_shape=out_shape,
        compiler_params=pltpu.CompilerParams(vmem_limit_bytes=56 * MIB),
        cost_estimate=lasting(micros),
        name=name,
    )(klo, khi, *args, *after)


def flash_forward(q, kv, lim, klo, khi, after=(), rides=(), ident=None):
    rows, tiles = q.shape[0], klo.shape[0]
    nq, keys, part, whole, limits, lses = flash_specs(rows, tiles, kv)
    return flash_call(
        flash_forward_kernel,
        "flash_forward",
        [q, kv[0], kv[1], kv[1], kv[1], lim],
        klo,
        khi,
        [part, *whole, limits],
        [part, lses],
        [jax.ShapeDtypeStruct((rows, 640), bf16), jax.ShapeDtypeStruct((PAIRS, tiles, 8, 2 * nq), f32)],
        [
            pltpu.VMEM((keys, 2 * LANES), bf16),
            pltpu.VMEM((keys // KEY_TILE, KEY_TILE, 2 * nq), f32),
            pltpu.VMEM((keys // KEY_TILE, LANES, KEY_TILE), bf16),
        ],
        40,
        after,
        rides,
        ident,
    )


def flash_backward_kernel(
    bounds, q_ref, do_ref, o_ref, kv0, kv1, kv2, kv3, lim_ref, lse_ref,
    dq_ref, dkv0, dkv1, dkv2, dkv3, kv_s, kt_ref, dk_ref, dv_ref,
):
    p, t = pl.program_id(0), pl.program_id(1)
    nq = q_ref.shape[0]
    tail = p == 4
    voff = pl.multiple_of(jnp.where(tail, 0, LANES), LANES)
    tiles = kt_ref.shape[0]

    @pl.when(t == 0)
    def _():
        assemble((kv0, kv1, kv2, kv3), kv_s)
        for k in range(tiles):
            kt_ref[k] = kv_s[k * KEY_TILE : (k + 1) * KEY_TILE, 0:LANES].T
        dk_ref[...] = jnp.zeros_like(dk_ref)
        dv_ref[...] = jnp.zeros_like(dv_ref)

    lane = lax.broadcasted_iota(jnp.int32, (nq, LANES), 1)
    qm = stack_heads(q_ref[...] * bf16(0.125), lane < 64, lane >= 64)
    side = jnp.where(tail, 1, 0)
    head = lane // 64
    dom = stack_heads(do_ref[...], head == side, head == 1 + side)
    back = do_ref[...].astype(f32) * o_ref[...].astype(f32)
    back = stack_heads(back, head == side, head == 1 + side)
    delta = jnp.sum(back.T, 0, keepdims=True)
    lo, hi = lim_ref[0, 0:1, :], lim_ref[0, 1:2, :]
    lse = lse_ref[0, 0, 0:1, :]
    row = lax.broadcasted_iota(jnp.int32, (KEY_TILE, 2 * nq), 0)

    def step(k, acc):
        base = pl.multiple_of(k * KEY_TILE, KEY_TILE)
        s = times_transposed(kv_s[pl.ds(base, KEY_TILE), 0:LANES], qm)
        w = jnp.exp(jnp.where((row >= lo - base) & (row <= hi - base), s - lse, NEG_LARGE))
        dp = times_transposed(kv_s[pl.ds(base, KEY_TILE), pl.ds(voff, LANES)], dom)
        ds = (w * (dp - delta)).astype(bf16)
        dv_ref[pl.ds(base, KEY_TILE), :] += matmul(w.astype(bf16), dom)
        dk_ref[pl.ds(base, KEY_TILE), :] += matmul(ds, qm)
        return acc + matmul(kt_ref[k], ds)

    acc = lax.fori_loop(*bounds(t), step, jnp.zeros((LANES, 2 * nq), f32))
    out = acc.T * 0.125
    dq_ref[...] = jnp.where(lane < 64, out[:nq], jnp.where(tail, 0.0, out[nq:]))

    @pl.when(t == pl.num_programs(1) - 1)
    def _():
        rings, _, half, _ = dkv0.shape
        for source, ref in enumerate((dkv0, dkv1, dkv2, dkv3)):
            for ring in range(rings):
                for j in range(8):
                    at = pl.ds(text_rows(source, ring, j, half, 4 * rings), half)
                    dk, dv = dk_ref[at, :], dv_ref[at, :]
                    ref[ring, j, :, 0:LANES] = jnp.where(tail, dk + dv, dk).astype(bf16)
                    ref[ring, j, :, LANES : 2 * LANES] = dv.astype(bf16)


def flash_backward(q, do, o, kv, lim, lse, klo, khi, after=(), rides=(), ident=None):
    rows, tiles = q.shape[0], klo.shape[0]
    nq, keys, part, whole, limits, lses = flash_specs(rows, tiles, kv)
    return flash_call(
        flash_backward_kernel,
        "flash_backward",
        [q, do, o, kv[0], kv[1], kv[1], kv[1], lim, lse],
        klo,
        khi,
        [part, part, part, *whole, limits, lses],
        [part] + [whole[0]] * 4,
        [jax.ShapeDtypeStruct((rows, 640), f32)] + [jax.ShapeDtypeStruct(kv[0].shape, bf16)] * 4,
        [
            pltpu.VMEM((keys, 2 * LANES), bf16),
            pltpu.VMEM((keys // KEY_TILE, LANES, KEY_TILE), bf16),
            pltpu.VMEM((keys, LANES), f32),
            pltpu.VMEM((keys, LANES), f32),
        ],
        48,
        after,
        rides,
        ident,
    )


def feed_forward_kernel(
    held_ref, back_ref, wg_ref, wu_ref, wd_ref, act_ref, bg_ref, bu_ref, bh_ref, br_ref, bh_acc, br_acc, wd_s
):
    t = pl.program_id(0)
    tile = wg_ref.shape[2]
    blocks, high, third = wd_ref.shape
    padded = high // 3

    @pl.when(t % (third // tile) == 0)
    def _():
        for b in range(blocks):
            for c in range(3):
                wd_s[b * padded : (b + 1) * padded, c * third : (c + 1) * third] = wd_ref[
                    b, c * padded : (c + 1) * padded, :
                ]

    wd = wd_s[pl.ds(pl.multiple_of(t % (third // tile) * tile, tile), tile), :]
    held = held_ref[...]
    width = held.shape[1]
    wg = wg_ref[...].reshape(width, tile)
    wu = wu_ref[...].reshape(width, tile)
    gate, up = matmul(held, wg), matmul(held, wu)
    back_act = times_transposed(back_ref[...], wd)
    sig = jax.nn.sigmoid(gate)
    gs = gate * sig
    act = (gs * up).astype(bf16)
    bg = (back_act * up * sig * (1.0 + gate * (1.0 - sig))).astype(bf16)
    bu = (back_act * gs).astype(bf16)
    act_ref[...], bg_ref[...], bu_ref[...] = act, bg, bu
    bh = times_transposed(bg, wg) + times_transposed(bu, wu)
    br = matmul(act, wd)

    @pl.when(t == 0)
    def _():
        bh_acc[...] = bh
        br_acc[...] = br

    @pl.when(t > 0)
    def _():
        bh_acc[...] += bh
        br_acc[...] += br

    @pl.when(t == pl.num_programs(0) - 1)
    def _():
        bh_ref[...] = bh_acc[...].astype(bf16)
        br_ref[...] = br_acc[...].astype(bf16)


def feed_forward(held, back, packed, wide, after=(), rides=(), ident=None):
    rows, width = held.shape
    tile = 256
    tiles = wide // tile
    whole = pl.BlockSpec((rows, width), lambda t: (0, 0))
    part = pl.BlockSpec((rows, tile), lambda t: (0, t))
    many, _, third = packed.shape
    per, blocks, slice_rows = third // tile, many * third // wide, width // many
    cols = lambda i: pl.BlockSpec((many, slice_rows, tile), lambda t: (0, t // per * 4 + i, t % per))
    down = pl.BlockSpec((blocks, 2 * slice_rows, third), lambda t: (t // per, 1, 0))
    return grid_call(
        feed_forward_kernel,
        (tiles,),
        [held, back, packed, packed, packed],
        [whole, whole, cols(0), cols(1), down],
        [part, part, part, whole, whole],
        [jax.ShapeDtypeStruct((rows, wide), bf16)] * 3 + [jax.ShapeDtypeStruct((rows, width), bf16)] * 2,
        [pltpu.VMEM((rows, width), f32)] * 2 + [pltpu.VMEM((third, width), bf16)],
        "feed_forward",
        42,
        after,
        rides,
        ident,
    )


def weight_gradient(lefts, rights, tile=256, after=(), rides=(), ident=None):
    many, per = len(lefts), len(rights[0])
    flat = [x for group in rights for x in group]
    rows, high = lefts[0].shape
    widths = [x.shape[1] for x in rights[0]]

    def kernel(*refs):
        ls, rs, out = refs[:many], refs[many : many + len(flat)], refs[many + len(flat)]
        start = 0
        for i, cols in enumerate(widths):
            total = transposed_times(ls[0][...], rs[i][...])
            for g in range(1, many):
                total = total + transposed_times(ls[g][...], rs[g * per + i][...])
            out[:, start : start + cols] = total.astype(bf16)
            start += cols

    return grid_call(
        kernel,
        (high // tile,),
        [*lefts, *flat],
        [pl.BlockSpec((rows, tile), lambda i: (0, i))] * many + [pl.BlockSpec(x.shape, lambda i: (0, 0)) for x in flat],
        [pl.BlockSpec((tile, sum(widths)), lambda i: (i, 0))],
        [jax.ShapeDtypeStruct((high, sum(widths)), bf16)],
        [],
        "weight_gradient",
        max(4, 2 * many * rows * high * sum(widths) // 10**9),
        after,
        rides,
        ident,
    )


def greet(places):
    barrier = pltpu.get_barrier_semaphore()
    for place in places:
        pl.semaphore_signal(barrier, inc=1, device_id=place, device_id_type=MESH_IDS)
    pl.semaphore_wait(barrier, len(places))


def greet_line(me, place, more=0):
    barrier = pltpu.get_barrier_semaphore()

    @pl.when(me > 0)
    def _():
        pl.semaphore_signal(barrier, inc=1, device_id=device(place, u=me - 1), device_id_type=MESH_IDS)

    @pl.when(me < 3)
    def _():
        pl.semaphore_signal(barrier, inc=1, device_id=device(place, u=me + 1), device_id_type=MESH_IDS)

    pl.semaphore_wait(barrier, 2 + more - jnp.where(me == 0, 1, 0) - jnp.where(me == 3, 1, 0))


def communicating(kernel, out, args, scratch, collective_id, name, vmem=40, after=(), micros=50):
    return pl.pallas_call(
        ignoring(kernel, len(args), len(after)),
        out_shape=out,
        in_specs=[HBM] * (len(args) + len(after)),
        out_specs=[HBM] * len(out) if isinstance(out, list) else HBM,
        scratch_shapes=scratch,
        compiler_params=pltpu.CompilerParams(
            collective_id=collective_id, has_side_effects=True, vmem_limit_bytes=vmem * MIB
        ),
        cost_estimate=lasting(micros),
        name=name,
    )(*args, *after)


def gather_u_kernel(n, kinds, *refs):
    r = len(kinds)
    ins, rides, outs, arrived = refs[:n], refs[n : n + r], refs[n + r : 2 * n + r], refs[2 * n + r : 2 * n + 2 * r]
    keep, send_r, send_l, recv_r, recv_l, *ride_sems = refs[2 * n + 2 * r :]
    place = coords()
    me = place["u"]
    greet_line(me, place, ride_greet(kinds, place))
    right, left = device(place, u=jnp.minimum(me + 1, 3)), device(place, u=jnp.maximum(me - 1, 0))

    def spot(owner, slot, a):
        return outs[a].at[:, owner if slot == 0 else 7 - owner]

    def going(step, slot, a, rightward):
        owner = me - step if rightward else me + step
        owner = jnp.clip(owner, 0, 3)
        src = ins[a].at[:, slot] if step == 0 else spot(owner, slot, a)
        send, recv, to = (send_r, recv_l, right) if rightward else (send_l, recv_r, left)
        return remote(src, spot(owner, slot, a), send.at[step, slot, a], recv.at[step, slot, a], to)

    def coming(step, slot, a, from_left):
        owner = jnp.clip(me - 1 - step if from_left else me + 1 + step, 0, 3)
        send, recv, to = (send_r, recv_l, right) if from_left else (send_l, recv_r, left)
        there = spot(owner, slot, a)
        return remote(there, there, send.at[step, slot, a], recv.at[step, slot, a], to)

    parts = [(slot, a) for slot in range(2) for a in range(n)]
    own = [pltpu.make_async_copy(ins[a].at[:, s], spot(me, s, a), keep.at[s, a]) for s, a in parts]
    for step in range(3):
        for part in parts:
            if step > 0:

                @pl.when(me >= step)
                def _():
                    coming(step - 1, *part, True).wait_recv()

            @pl.when((me < 3) & (me >= step))
            def _():
                going(step, *part, True).start()

            if step > 0:

                @pl.when(me <= 3 - step)
                def _():
                    coming(step - 1, *part, False).wait_recv()

            @pl.when((me > 0) & (me <= 3 - step))
            def _():
                going(step, *part, False).start()

        if step == 0:
            for copy in own:
                copy.start()
            ride_start(kinds, rides, arrived, ride_sems, place)
    for part in parts:

        @pl.when(me == 3)
        def _():
            coming(2, *part, True).wait_recv()

        @pl.when(me == 0)
        def _():
            coming(2, *part, False).wait_recv()

    for step in range(3):
        for part in parts:

            @pl.when((me < 3) & (me >= step))
            def _():
                going(step, *part, True).wait_send()

            @pl.when((me > 0) & (me <= 3 - step))
            def _():
                going(step, *part, False).wait_send()

    for copy in own:
        copy.wait()
    ride_end(kinds, rides, arrived, ride_sems, place)


def gather_u(arrays, collective_id, after=(), rides=()):
    n = len(arrays)
    sems = pltpu.SemaphoreType.DMA((3, 2, n))
    return communicating(
        functools.partial(gather_u_kernel, n, [kind for kind, _ in rides]),
        [jax.ShapeDtypeStruct((x.shape[0], 8) + x.shape[2:], x.dtype) for x in arrays]
        + [ride_out(kind, x) for kind, x in rides],
        arrays + [x for _, x in rides],
        [pltpu.SemaphoreType.DMA((2, n)), sems, sems, sems, sems] + (ride_scratch(len(rides)) if rides else []),
        collective_id,
        "gather_u",
        after=after,
    )


def scatter_u_kernel(kinds, *refs):
    r = len(kinds)
    p_ref, *rides = refs[: 1 + r]
    out_ref, *arrived = refs[1 + r : 2 + 2 * r]
    own, from_l, from_r, total, load, send_r, send_l, recv_l, recv_r, store, *ride_sems = refs[2 + 2 * r :]
    place = coords()
    me = place["u"]
    greet_line(me, place, ride_greet(kinds, place))
    ride_start(kinds, rides, arrived, ride_sems, place)
    right, left = device(place, u=jnp.minimum(me + 1, 3)), device(place, u=jnp.maximum(me - 1, 0))

    def mine(owner, slot):
        return p_ref.at[:, owner if slot == 0 else 7 - owner]

    loads = [
        pltpu.make_async_copy(mine(k, s), own.at[k, s], load.at[k, s]) for k in range(4) for s in range(2)
    ]
    order = [3, 0, 2, 1]

    def fetch(k, s):
        return loads[2 * k + s]

    for k in order:
        for s in range(2):
            fetch(k, s).start()

    def rightward(e, s):
        src = from_l.at[e, s]
        return remote(src, from_l.at[e, s], send_r.at[e, s], recv_l.at[e, s], right)

    def rightward_first(e, s):
        return remote(own.at[3 - e, s], from_l.at[e, s], send_r.at[e, s], recv_l.at[e, s], right)

    def leftward(k, s):
        return remote(from_r.at[k, s], from_r.at[k, s], send_l.at[k, s], recv_r.at[k, s], left)

    def leftward_first(k, s):
        return remote(own.at[k, s], from_r.at[k, s], send_l.at[k, s], recv_r.at[k, s], left)

    def add(into, other):
        into[...] = (into[...].astype(f32) + other[...].astype(f32)).astype(into.dtype)

    for s in range(2):
        for k in order:
            fetch(k, s).wait()
        for e in range(3):

            @pl.when(me == 0)
            def _():
                rightward_first(e, s).start()

            @pl.when(me == 3)
            def _():
                leftward_first(e, s).start()

    for e in range(3):
        for s in range(2):

            @pl.when((me > 0) & (me < 3 - e))
            def _():
                rightward(e, s).wait_recv()
                add(from_l.at[e, s], own.at[3 - e, s])
                rightward(e, s).start()

            @pl.when((me < 3) & (me > e))
            def _():
                leftward(e, s).wait_recv()
                add(from_r.at[e, s], own.at[e, s])
                leftward(e, s).start()

    stores = [pltpu.make_async_copy(total.at[s], out_ref.at[:, s], store.at[s]) for s in range(2)]
    for s in range(2):
        total[s] = own[me, s].astype(f32)

        @pl.when(me > 0)
        def _():
            e = jnp.minimum(3 - me, 2)
            rightward(e, s).wait_recv()
            total[s] += from_l[e, s].astype(f32)

        @pl.when(me < 3)
        def _():
            e = jnp.minimum(me, 2)
            leftward(e, s).wait_recv()
            total[s] += from_r[e, s].astype(f32)

        stores[s].start()
    for e in range(3):
        for s in range(2):

            @pl.when(me < 3 - e)
            def _():
                rightward(e, s).wait_send()

            @pl.when(me > e)
            def _():
                leftward(e, s).wait_send()

    for copy in stores:
        copy.wait()
    ride_end(kinds, rides, arrived, ride_sems, place)


def scatter_u(x, rides=(), after=()):
    groups, _, half, cols = x.shape
    piece = (groups, half, cols)
    sems = pltpu.SemaphoreType.DMA((3, 2))
    return communicating(
        functools.partial(scatter_u_kernel, [kind for kind, _ in rides]),
        [jax.ShapeDtypeStruct((groups, 2, half, cols), f32)] + [ride_out(kind, x) for kind, x in rides],
        [x] + [x for _, x in rides],
        [
            pltpu.VMEM((4, 2) + piece, x.dtype),
            pltpu.VMEM((3, 2) + piece, x.dtype),
            pltpu.VMEM((3, 2) + piece, x.dtype),
            pltpu.VMEM((2,) + piece, f32),
            pltpu.SemaphoreType.DMA((4, 2)),
            sems,
            sems,
            sems,
            sems,
            pltpu.SemaphoreType.DMA((2,)),
        ]
        + (ride_scratch(len(rides)) if rides else []),
        1,
        "scatter_u",
        after=after,
    )


def gather_hidden_kernel(x_ref, out_ref, keep, send_x, send_y, recv_x, recv_y):
    place = coords()
    v, f = place["v"], place["f"]
    x_to, y_to = device(place, v=1 - v), device(place, f=1 - f)
    greet([x_to, y_to])
    half = x_ref.shape[0] // 2

    def spot(row, col, h):
        start = pl.multiple_of((row * 2 + col) * 2 * half + h * half, half)
        return out_ref.at[pl.ds(start, half)]

    def own(h):
        return x_ref.at[pl.ds(h * half, half)]

    def via_x(src, dst, i):
        return remote(src, dst, send_x.at[i], recv_x.at[i], x_to)

    def via_y(src, dst, i):
        return remote(src, dst, send_y.at[i], recv_y.at[i], y_to)

    x_own = [via_x(own(h), spot(v, f, h), h) for h in range(2)]
    y_own = [via_y(own(h), spot(v, f, h), h) for h in range(2)]
    x_own[0].start()
    y_own[1].start()
    x_own[1].start()
    y_own[0].start()
    keeps = [pltpu.make_async_copy(own(h), spot(v, f, h), keep.at[h]) for h in range(2)]
    for copy in keeps:
        copy.start()
    via_x(own(0), spot(1 - v, f, 0), 0).wait_recv()
    y_on = via_y(spot(1 - v, f, 0), spot(1 - v, f, 0), 2)
    y_on.start()
    via_y(own(1), spot(v, 1 - f, 1), 1).wait_recv()
    x_on = via_x(spot(v, 1 - f, 1), spot(v, 1 - f, 1), 2)
    x_on.start()
    via_x(own(1), spot(1 - v, f, 1), 1).wait_recv()
    via_y(own(0), spot(v, 1 - f, 0), 0).wait_recv()
    via_x(own(1), spot(1 - v, 1 - f, 1), 2).wait_recv()
    via_y(own(0), spot(1 - v, 1 - f, 0), 2).wait_recv()
    for copy in x_own + y_own + [x_on, y_on]:
        copy.wait_send()
    for copy in keeps:
        copy.wait()


def gather_hidden(x, after=()):
    rows, cols = x.shape
    sems = pltpu.SemaphoreType.DMA((3,))
    return communicating(
        gather_hidden_kernel,
        jax.ShapeDtypeStruct((4 * rows, cols), x.dtype),
        [x],
        [pltpu.SemaphoreType.DMA((2,)), sems, sems, sems, sems],
        2,
        "gather_hidden",
        after=after,
        micros=20,
    )


def scatter_hidden_kernel(p_ref, out_ref, own, got_x, got_y, total, load, send_x, send_y, recv_x, recv_y, store):
    place = coords()
    v, f = place["v"], place["f"]
    x_to, y_to = device(place, v=1 - v), device(place, f=1 - f)
    greet([x_to, y_to])
    half = total.shape[1]

    def mine(row, col, h):
        start = pl.multiple_of((row * 2 + col) * 2 * half + h * half, half)
        return p_ref.at[pl.ds(start, half)]

    corners = [(v, f), (1 - v, f), (v, 1 - f), (1 - v, 1 - f)]
    loads = [
        [pltpu.make_async_copy(mine(*corners[i], h), own.at[i, h], load.at[i, h]) for h in range(2)]
        for i in range(4)
    ]
    for i in (3, 1, 2, 0):
        for h in range(2):
            loads[i][h].start()

    def via_x(src, i):
        return remote(src, got_x.at[i], send_x.at[i], recv_x.at[i], x_to)

    def via_y(src, i):
        return remote(src, got_y.at[i], send_y.at[i], recv_y.at[i], y_to)

    loads[3][0].wait()
    x_far = via_x(own.at[3, 0], 0)
    x_far.start()
    loads[3][1].wait()
    y_far = via_y(own.at[3, 1], 0)
    y_far.start()
    loads[1][0].wait()
    x_near = via_x(own.at[1, 0], 1)
    x_near.start()
    loads[2][1].wait()
    y_near = via_y(own.at[2, 1], 2)
    y_near.start()

    def add(into, other):
        into[...] = (into[...].astype(f32) + other[...].astype(f32)).astype(into.dtype)

    loads[2][0].wait()
    x_far.wait_recv()
    add(own.at[2, 0], got_x.at[0])
    y_sum = via_y(own.at[2, 0], 1)
    y_sum.start()
    loads[1][1].wait()
    y_far.wait_recv()
    add(own.at[1, 1], got_y.at[0])
    x_sum = via_x(own.at[1, 1], 2)
    x_sum.start()
    stores = [
        pltpu.make_async_copy(total.at[h], out_ref.at[pl.ds(h * half, half)], store.at[h]) for h in range(2)
    ]
    loads[0][0].wait()
    loads[0][1].wait()
    x_near.wait_recv()
    y_near.wait_recv()
    total[0] = own[0, 0].astype(f32) + got_x[1].astype(f32)
    total[1] = own[0, 1].astype(f32) + got_y[2].astype(f32)
    y_sum.wait_recv()
    total[0] += got_y[1].astype(f32)
    stores[0].start()
    x_sum.wait_recv()
    total[1] += got_x[2].astype(f32)
    stores[1].start()
    for copy in (x_far, y_far, x_near, y_near, x_sum, y_sum):
        copy.wait_send()
    for copy in stores:
        copy.wait()


def scatter_hidden(x):
    rows, cols = x.shape[0] // 4, x.shape[1]
    half = (rows // 2, cols)
    sems = pltpu.SemaphoreType.DMA((3,))
    return communicating(
        scatter_hidden_kernel,
        jax.ShapeDtypeStruct((rows, cols), f32),
        [x],
        [
            pltpu.VMEM((4, 2) + half, x.dtype),
            pltpu.VMEM((3,) + half, x.dtype),
            pltpu.VMEM((3,) + half, x.dtype),
            pltpu.VMEM((2,) + half, f32),
            pltpu.SemaphoreType.DMA((4, 2)),
            sems,
            sems,
            sems,
            sems,
            pltpu.SemaphoreType.DMA((2,)),
        ],
        3,
        "scatter_hidden",
    )


FLIP = [(0, 1), (1, 0)]


def core_sum_kernel(x_ref, out_ref, mine, got, load, send, recv, store):
    place = coords()
    core = place["core"]
    other = device(place, core=1 - core)
    barrier = pltpu.get_barrier_semaphore()
    pl.semaphore_signal(barrier, inc=1, device_id=other, device_id_type=MESH_IDS)
    pl.semaphore_wait(barrier, 1)
    blocks = x_ref.shape[0]
    order = [(v, f) for v in range(2) for f in range(2)]

    def sending(k):
        v, f = order[k]
        return remote(x_ref.at[:, v, 1 - core, f], got.at[k], send.at[k], recv.at[k], other)

    def loading(k):
        v, f = order[k]
        return pltpu.make_async_copy(x_ref.at[:, v, core, f], mine.at[k], load.at[k])

    def storing(k):
        return pltpu.make_async_copy(mine.at[k], out_ref.at[k], store.at[k])

    for k in range(4):
        sending(k).start()
        loading(k).start()
    for k in range(4):
        loading(k).wait()
        sending(k).wait_recv()
        for i in range(blocks):
            mine[k, i] = (mine[k, i].astype(f32) + got[k, i].astype(f32)).astype(mine.dtype)
        storing(k).start()
    for k in range(4):
        sending(k).wait_send()
        storing(k).wait()


def head_sum_start(x, sizes, collective_id, blocks=1):
    _, many, nv, nc, nf = sizes
    rows, cols = x.shape[0] // (blocks * many * nv * nc * nf), x.shape[1]
    x = x.reshape(blocks, many, nv, nc, nf, rows, cols)
    x = lax.psum_scatter(x, "w", scatter_dimension=1, tiled=False) if many > 1 else x[:, 0]
    sems = pltpu.SemaphoreType.DMA((4,))
    out = communicating(
        core_sum_kernel,
        jax.ShapeDtypeStruct((4, blocks, rows, cols), x.dtype),
        [x],
        [pltpu.VMEM((4, blocks, rows, cols), x.dtype)] * 2 + [sems] * 4,
        collective_id,
        "core_sum",
        micros=12,
    )
    return out.reshape(4, blocks * rows, cols)


def with_rings(x, many):
    return lax.all_gather(x, "w", axis=1) if many > 1 else x[:, None]


def scatter_keys_start(parts, many):
    parts = [x[0] for x in parts]
    if many > 1:
        parts = [lax.psum_scatter(x, "w", scatter_dimension=0, tiled=True) for x in parts]
    along = parts[2][0].astype(f32) + lax.ppermute(parts[3][0], "core", FLIP).astype(f32)
    own = parts[0][0].astype(f32) + lax.ppermute(parts[1][0], "core", FLIP).astype(f32)
    return own, along.astype(bf16)


def pieces_of(part, axes):
    me = lax.axis_index(axes)
    return [part(me ^ step) for step in (0, 3, 2, 1)]


def tied(xs, after):
    return lax.optimization_barrier((tuple(xs), tuple(after)))[0]


def scatter_pieces(pieces, axes, after=()):
    got = [
        lax.ppermute(piece, axes, [(i, i ^ step) for i in range(4)])
        for step, piece in zip((3, 2, 1), pieces[1:])
    ]
    total = pieces[0].astype(f32)
    for part in tied(got, after):
        total = total + part.astype(f32)
    return total


def pieces_u(x):
    def part(k):
        return jnp.stack(
            [lax.dynamic_index_in_dim(x, k, 0, False), lax.dynamic_index_in_dim(x, 7 - k, 0, False)], 0
        )

    return pieces_of(part, "u")


def pieces_hidden(x):
    blocks = x.reshape(4, x.shape[0] // 4, x.shape[1])
    return pieces_of(lambda k: lax.dynamic_index_in_dim(blocks, k, 0, False), HIDDEN)


def gather_hidden_async(x):
    me = lax.axis_index(HIDDEN)
    out = jnp.zeros((4,) + x.shape, x.dtype)
    for step in range(4):
        part = x if step == 0 else lax.ppermute(x, HIDDEN, [(i, i ^ step) for i in range(4)])
        out = lax.dynamic_update_index_in_dim(out, part, me ^ step, 0)
    return out.reshape(4 * x.shape[0], x.shape[1])


def gather_u_start(x):
    return [x] + [lax.ppermute(x, "u", [(i, i ^ step) for i in range(4)]) for step in (3, 2, 1)]


def gather_u_end(parts, after):
    me = lax.axis_index("u")
    out = jnp.zeros((8,) + parts[0].shape[1:], parts[0].dtype)
    for step, part in zip((0, 3, 2, 1), tied(parts, after)):
        k = me ^ step
        out = lax.dynamic_update_slice_in_dim(out, part[0:1], k, 0)
        out = lax.dynamic_update_slice_in_dim(out, part[1:2], 7 - k, 0)
    return out


def exchange_kernel(sizes, kinds, back, spots, *refs):
    n, more = len(kinds), len(spots) - len(kinds)
    ins, outs = refs[:n], refs[n + more : len(refs) - 3]
    send, recv, keep = refs[len(refs) - 3 :]
    nu, nw, nv, nc, nf = sizes
    place = coords()
    u, w, v, core, f = (place[axis] for axis in ALL)

    def holder(kind, block):
        if kind == "along":
            return (block, w, v, core, f)
        if kind == "heads":
            at = (u * nw + w) * nv + v
            return (block, at // (nf * nc * nv), at // (nf * nc) % nv, at // nf % nc, at % nf)
        return (u, w, block // nf, v, block % nf)

    def owner(kind, slot):
        if kind == "along":
            return (slot, w, v, core, f)
        if kind == "heads":
            at = ((w * nv + v) * nc + core) * nf + f
            return (at // (nv * nw), at // nv % nw, at % nv, slot // nf, slot % nf)
        return (u, w, core, slot // nf, slot % nf)

    def same(other):
        equal = other[0] == u
        for a, b in zip(other[1:], (w, v, core, f)):
            equal = equal & (a == b)
        return equal

    def landing(kind):
        slot = core * nf + f
        block = v * nf + f if kind == "hidden" else u
        return block if back or kind == "along" else slot

    to, frm = (owner, holder) if back else (holder, owner)
    barrier = pltpu.get_barrier_semaphore()
    waits = jnp.int32(0)
    for kind in kinds:
        for i in range(4):
            other = frm(kind, i)

            @pl.when(jnp.logical_not(same(other)))
            def _():
                pl.semaphore_signal(barrier, inc=1, device_id=other, device_id_type=MESH_IDS)

            waits = waits + jnp.where(same(to(kind, i)), 0, 1)
    pl.semaphore_wait(barrier, waits)

    def land(a, at):
        out, first = spots[a]
        return outs[out].at[at] if first is None else outs[out].at[first : first + ins[a].shape[1], at]

    def copy(a, i):
        at = landing(kinds[a])
        return remote(ins[a].at[i], land(a, at), send.at[a, i], recv.at[a, at], to(kinds[a], i))

    def local(a, i):
        return pltpu.make_async_copy(ins[a].at[i], land(a, landing(kinds[a])), keep.at[a])

    own = []
    if more:
        out, first = spots[n]
        own = [pltpu.make_async_copy(refs[n], outs[out].at[first : first + refs[n].shape[0]], keep.at[n])]
    for stage in range(3):
        for rest in own:
            rest.start() if stage == 0 else rest.wait() if stage == 1 else None
        for a in range(n):
            for i in range(4):
                here = same(to(kinds[a], i))

                @pl.when(here)
                def _():
                    local(a, i).start() if stage == 0 else local(a, i).wait() if stage == 1 else None

                @pl.when(jnp.logical_not(here))
                def _():
                    copy(a, i).start() if stage == 0 else copy(a, i).wait_send() if stage == 1 else None

                if stage == 2:

                    @pl.when(jnp.logical_not(same(frm(kinds[a], i))))
                    def _():
                        remote(
                            ins[a].at[i], land(a, i), send.at[a, i], recv.at[a, i], to(kinds[a], i)
                        ).wait_recv()


def exchange(sizes, arrays, kinds, back, collective_id, shapes, spots, after=()):
    n = len(kinds)
    return pl.pallas_call(
        ignoring(functools.partial(exchange_kernel, sizes, kinds, back, spots), len(arrays), len(after)),
        out_shape=[jax.ShapeDtypeStruct(shape, arrays[0].dtype) for shape in shapes],
        in_specs=[HBM] * (len(arrays) + len(after)),
        out_specs=[HBM] * len(shapes),
        scratch_shapes=[
            pltpu.SemaphoreType.DMA((n, 4)),
            pltpu.SemaphoreType.DMA((n, 4)),
            pltpu.SemaphoreType.DMA((n + 1,)),
        ],
        compiler_params=pltpu.CompilerParams(
            collective_id=collective_id, has_side_effects=True, vmem_limit_bytes=16 * MIB
        ),
        cost_estimate=lasting(35),
        name="exchange_back" if back else "exchange",
    )(*arrays, *after)


def pad_columns(x, cols):
    return jnp.pad(x, [(0, 0)] * (x.ndim - 1) + [(0, cols - x.shape[-1])])


def body(sizes, tokens, cotangent, segment, position, gain_attn, w_query, w_key, w_value, w_output, gain_mlp, w_gate, w_up, w_down):
    del segment
    groups, block_rows, width = tokens.shape
    rows = groups * block_rows
    half = block_rows // 2
    hidden = w_gate.shape[1]
    slab = w_gate.shape[0]
    block = w_down.shape[0]
    padded = -(-block // 16) * 16
    nkeys = sizes[1] * sizes[2] * sizes[3]
    wide = 2 * nkeys * padded
    qkv_cols = 1792
    here = (groups, 2, half)
    there = (groups, 8, half)

    gain_one, gain_two = gain_attn.astype(f32)[:, None], gain_mlp.astype(f32)[:, None]
    qkv_local, first_local, second_local = pack_weights(
        sizes, w_query, w_key, w_value, w_gate, w_up, gain_one, gain_two, block, padded
    )
    third = width // 3
    own_down = jnp.pad(w_down, ((0, padded - block), (0, 0))).reshape(padded, 3, third)
    own_down = jnp.transpose(own_down, (1, 0, 2)).reshape(-1, 4, slab, third)
    qkv_local, packed = exchange(
        sizes,
        [qkv_local, first_local, second_local, own_down],
        ["heads", "hidden", "hidden"],
        False,
        6,
        [qkv_local.shape, (6, 4, slab, third)],
        [(0, None), (1, 0), (1, 4), (1, 2)],
    )

    def all_heads(x):
        if sizes[1] > 1:
            x = lax.all_gather(x, "w", axis=0)
        return x.reshape(-1, x.shape[-1])

    sequences = range(groups)
    nlocal = lax.axis_index(KEYS)
    order = jnp.arange(8, dtype=jnp.int32)
    order = nkeys * order + jnp.where(order < 4, nlocal, nkeys - 1 - nlocal)
    text = order[:, None] * half + jnp.arange(half, dtype=jnp.int32)[None, :]
    tiles = 8 // QUERY_BLOCKS
    nq = QUERY_BLOCKS * half
    rates = jnp.exp(jnp.arange(32, dtype=f32) * (-math.log(10000.0) / 32))
    inputs, inverse_one, normed_one = [], [], []
    for g in sequences:
        x = tokens[g].astype(f32)
        inverse = lax.rsqrt(jnp.mean(x * x, -1, keepdims=True) + EPSILON)
        inputs.append(x)
        inverse_one.append(inverse)
        normed_one.append(x * inverse)
    places = jnp.broadcast_to(pad_columns(position.reshape(here), LANES)[:, :, None], (groups, 2, 8, LANES))
    upstream = [cotangent[g].astype(f32) for g in sequences]
    held_one, tables, masks, query, kv, kv_own = ([] for _ in range(6))
    before = []
    for g in sequences:
        sent = [normed_one[g].astype(bf16).reshape(1, 2, half, width), places[g : g + 1]]
        rides = [("gather_keys", kv_own[0].reshape(8, half, 1152)) if g > 0 else ("gather_heads", qkv_local)]
        if g > 0:
            rides.append(("gather_heads", w_output))
        held, seen, got, *out_rows = gather_u(sent, (0, 8)[g], after=before, rides=rides)
        held_one.append(held.reshape(8 * half, width))
        if g == 0:
            qkv_whole = all_heads(got)
        seen = seen[0, :, 0, :half]
        lowest = text - jnp.minimum(seen, WINDOW - 1)
        lows, highs = lowest.reshape(tiles, nq), text.reshape(tiles, nq)
        klo, khi = lows[:, 0] // KEY_TILE, highs[:, -1] // KEY_TILE + 1
        lim = jnp.stack([jnp.tile(lows, (1, 2)), jnp.tile(highs, (1, 2))], 1)
        masks.append((jnp.pad(lim, ((0, 0), (0, 6), (0, 0))), klo, khi))
        angles = seen.reshape(8 * half, 1).astype(f32) * rates[None, :]
        cos, sin = jnp.cos(angles), jnp.sin(angles)
        tables.append((jnp.concatenate([cos, cos, cos, cos], 1), jnp.concatenate([-sin, sin, -sin, sin], 1)))
        own, q = rope(matmul(held_one[g], qkv_whole), *tables[g])
        kv_own.append(own)
        before = [own]
        query.append(q)

    (packed,) = tied([packed], held_one[:1])
    packed = lax.all_gather(packed.reshape(-1, third), HIDDEN_SUM, axis=0)

    def key_arrays(g, others):
        own = kv_own[g].reshape(1, 8, half, 1152)
        kv.append([with_rings(own, sizes[1]), with_rings(others, sizes[1])])

    key_arrays(0, got)
    attn, lse, parts = [], [], []
    out_whole = all_heads(out_rows[0])
    out_whole = jnp.concatenate([out_whole[:512], jnp.zeros((64, width), bf16), out_whole[512:]], 0)
    rides = [("gather_keys", kv_own[1].reshape(8, half, 1152))]
    before = kv_own[1:]
    for g in sequences:
        out, sums, got_zero, *got = flash_forward(query[g], kv[g], *masks[g], after=before, rides=rides, ident=(9, 10)[g])
        attn.append(out)
        lse.append(sums)
        if g == 0:
            key_arrays(1, got_zero)
        parts.append(matmul(out, out_whole).astype(bf16).reshape(8, half, width))
        before, rides = [], [("scatter_u", parts[g])]
        rides += [("gather_hidden", (BRANCH_SCALE * x).astype(bf16)) for x in upstream]
    back_mlp = [x.reshape(4 * block_rows, width) for x in got]

    def own_u(x):
        me = lax.axis_index("u")
        return jnp.stack([lax.dynamic_index_in_dim(x, me, 0, False), lax.dynamic_index_in_dim(x, 7 - me, 0, False)], 0)

    def own_hidden(x):
        return lax.dynamic_index_in_dim(x, lax.axis_index(HIDDEN), 0, False)

    def total(own, got):
        return own.astype(f32) + jnp.sum(got.astype(f32), 0)

    middle, inverse_two, normed_two, held_two, activated, back_gu, back_held, mlp_part = ([] for _ in range(8))

    def to_feed_forward(g, got):
        x = inputs[g] + BRANCH_SCALE * total(own_u(parts[g]), got).reshape(block_rows, width)
        inverse = lax.rsqrt(jnp.mean(x * x, -1, keepdims=True) + EPSILON)
        middle.append(x)
        inverse_two.append(inverse)
        normed_two.append(x * inverse)
        held_two.append(gather_hidden(normed_two[g].astype(bf16)))

    def from_feed_forward(act, back_gate, back_up, back, part):
        activated.append(act)
        back_gu.append([back_gate, back_up])
        back_held.append(back.reshape(4, block_rows, width))
        mlp_part.append(part.reshape(4, block_rows, width))

    to_feed_forward(0, got_zero)
    *results, got_one = feed_forward(
        held_two[0], back_mlp[0], packed, wide, rides=[("scatter_u", parts[1])], ident=11
    )
    from_feed_forward(*results)
    back_middle, sent = [], []

    def to_attention(g, sums):
        x = upstream[g] + rms_back(sums, normed_two[g], inverse_two[g])
        back_middle.append(x)
        sent.append((BRANCH_SCALE * x).astype(bf16).reshape(2, half, width))

    to_attention(0, scatter_hidden(back_held[0].reshape(4 * block_rows, width)))
    to_feed_forward(1, got_one)
    *results, back_branch_zero, got_mlp = feed_forward(
        held_two[1],
        back_mlp[1],
        packed,
        wide,
        after=sent,
        rides=[("gather_u", sent[0]), ("scatter_hidden", mlp_part[0])],
        ident=12,
    )
    from_feed_forward(*results)
    layer_out = [(middle[0] + BRANCH_SCALE * total(own_hidden(mlp_part[0]), got_mlp)).astype(bf16)]
    (down_term,) = weight_gradient(activated, [[back_mlp[i]] for i in sequences])
    down_sum = lax.psum_scatter(down_term, HIDDEN_SUM, scatter_dimension=0, tiled=True)
    gu_term, got_one = weight_gradient(
        held_two, back_gu, after=[down_term], rides=[("scatter_hidden", back_held[1])], ident=13
    )
    to_attention(1, total(own_hidden(back_held[1]), got_one))
    back_branch = [back_branch_zero.reshape(8 * half, width)]
    dkv_own, dkv_along, dq = [], [], []
    rides = [("gather_u", sent[1]), ("scatter_hidden", mlp_part[1])]
    for g in sequences:
        do = times_transposed(back_branch[g], out_whole).astype(bf16)
        lim, klo, khi = masks[g]
        dq_part, *rest = flash_backward(
            query[g], do, attn[g], kv[g], lim, lse[g], klo, khi, rides=rides, ident=(14, 17)[g]
        )
        if g == 0:
            back_branch.append(rest[4].reshape(8 * half, width))
            layer_out.append((middle[1] + BRANCH_SCALE * total(own_hidden(mlp_part[1]), rest[5])).astype(bf16))
            dq_part, gu_term, down_sum = lax.optimization_barrier((dq_part, gu_term, down_sum))
            gu_sum = lax.psum_scatter(gu_term, HIDDEN_SUM, scatter_dimension=0, tiled=True)
        dq.append(dq_part)
        own, along = scatter_keys_start(rest[:4], sizes[1])
        dkv_own.append(own)
        dkv_along.append(along)
        rides = [("swap_v", along)]
    def to_tokens(g, dkv):
        back_qkv.append(unrope(dkv.reshape(8 * half, 1152), dq[g], *tables[g], after=[along]))
        part = times_transposed(back_qkv[g], qkv_whole).astype(bf16)
        late.append(part.reshape(8, half, width))

    back_qkv, late, grad_tokens = [], [], []
    to_tokens(0, dkv_own[0] + rest[4].astype(f32))
    out_term, along = weight_gradient(
        attn, [[x] for x in back_branch], tile=LANES, after=late[:1], rides=[("swap_v", along)], ident=15
    )
    out_half = head_sum_start(jnp.concatenate([out_term[:512], out_term[576:]], 0), sizes, 18)
    to_tokens(1, dkv_own[1] + along.astype(f32))
    (qkv_term,) = weight_gradient(held_one, [[x] for x in back_qkv])
    qkv_half = head_sum_start(qkv_term, sizes, 19, 4)
    sums, qkv_got, out_got = scatter_u(
        jnp.stack(late, 0), rides=[("scatter_hidden", qkv_half), ("scatter_hidden", out_half)]
    )
    grad_output = total(own_hidden(out_half), out_got)
    qkv_sum = total(own_hidden(qkv_half), qkv_got).astype(bf16)
    for g in sequences:
        part = sums[g].reshape(block_rows, width)
        x = back_middle[g] + rms_back(part, normed_one[g], inverse_one[g])
        grad_tokens.append(x.astype(bf16))
    layer_out, grad_tokens = jnp.stack(layer_out, 0), jnp.stack(grad_tokens, 0)

    qkv_sum, gu_sum = exchange(
        sizes,
        [qkv_sum.reshape(4, slab, qkv_cols), gu_sum.reshape(4, slab, 2 * wide)],
        ["along", "hidden"],
        True,
        7,
        [(4, slab, qkv_cols), (4, slab, 2 * wide)],
        [(0, None), (1, None)],
        after=[grad_tokens],
    )
    grad_query, grad_key, grad_value, grad_gate, grad_up, grad_gain_attn, grad_gain_mlp = unpack_gradients(
        sizes, qkv_sum, gu_sum, w_query, w_key, w_value, w_gate, w_up, gain_one, gain_two, block, padded
    )
    grad_down = down_sum[:block].astype(f32)
    return (
        layer_out,
        grad_tokens,
        grad_gain_attn[:, 0],
        grad_query,
        grad_key,
        grad_value,
        grad_output,
        grad_gain_mlp[:, 0],
        grad_gate,
        grad_up,
        grad_down,
    )


def solution(mesh):
    ctx, fsdp = mesh.shape["ctx"], mesh.shape["fsdp"]
    sizes = (4, ctx // 16, 2, 2, fsdp)
    fine = Mesh(mesh.devices.reshape(sizes), ALL)
    blocks = ("u", "w", "v", "core")
    act = P("f", blocks, None)
    ids = P("f", blocks)
    gain, weight = P(ALL), P(ALL, None)
    return jax.shard_map(
        functools.partial(body, sizes),
        mesh=fine,
        in_specs=(act, act, ids, ids, gain, weight, weight, weight, weight, gain, weight, weight, weight),
        out_specs=(act, act, gain, weight, weight, weight, weight, gain, weight, weight, weight),
        check_vma=False,
    )
```

```python
import functools
import math

import jax
import jax.numpy as jnp
from jax import lax
from jax.experimental import pallas as pl
from jax.experimental.pallas import tpu as pltpu
from jax.sharding import Mesh, PartitionSpec as P

HEADS = 36
HEAD_DIM = 64
WINDOW = 1024
EPSILON = 1e-05
BRANCH_SCALE = 1.4 / math.sqrt(40.0)
NEG_LARGE = -1e30
LANES = 128
PAIRS = 5
KEY_TILE = 512
QUERY_BLOCKS = 2
MIB = 1024 * 1024

f32, bf16 = jnp.float32, jnp.bfloat16


def matmul(left, right):
    return jnp.dot(left, right, preferred_element_type=f32)


def times_transposed(left, right):
    return lax.dot_general(left, right, (((1,), (1,)), ((), ())), preferred_element_type=f32)


def transposed_times(left, right):
    return lax.dot_general(left, right, (((0,), (0,)), ((), ())), preferred_element_type=f32)


def rms_back(upstream, normed, inverse):
    return inverse * (upstream - normed * jnp.mean(upstream * normed, -1, keepdims=True))


HBM = pl.BlockSpec(memory_space=pl.ANY)


def ignoring(kernel, args, extra):
    return lambda *refs: kernel(*refs[:args], *refs[args + extra :])


def lasting(micros):
    return pl.CostEstimate(flops=0, bytes_accessed=micros * 3_600_000, transcendentals=0)


MESH_IDS = pl.DeviceIdType.MESH
ALL = ("u", "w", "v", "core", "f")
KEYS = ("w", "v", "core")
HEAD_SUM = ("w", "v", "core", "f")
HIDDEN = ("v", "f")
HIDDEN_SUM = ("u", "w", "core")


def coords():
    return {axis: lax.axis_index(axis) for axis in ALL}


def device(place, **moved):
    return tuple(moved.get(axis, place[axis]) for axis in ALL)


def remote(src, dst, send, recv, where):
    return pltpu.make_async_remote_copy(
        src_ref=src, dst_ref=dst, send_sem=send, recv_sem=recv, device_id=where, device_id_type=MESH_IDS
    )


def ride_out(kind, x):
    shape = {
        "gather_u": (8,) + x.shape[1:],
        "scatter_u": (3, 2) + x.shape[1:],
        "gather_hidden": (4,) + x.shape,
        "scatter_hidden": (3,) + x.shape[1:],
        "gather_keys": (3,) + x.shape,
        "swap_v": x.shape,
        "gather_heads": (8,) + x.shape,
        "gather_halves": (8,) + x.shape,
    }
    return jax.ShapeDtypeStruct(shape[kind], x.dtype)


STEPS = {"gather_keys": (2, 1), "swap_v": (2,)}


def partner(kind, place, step):
    if kind in ("gather_u", "scatter_u"):
        k = place["u"] ^ step
        return k, device(place, u=k)
    if kind in ("gather_keys", "swap_v"):
        k = (2 * place["v"] + place["core"]) ^ step
        return k, device(place, v=k // 2, core=k % 2)
    k = (2 * place["v"] + place["f"]) ^ step
    return k, device(place, v=k // 2, f=k % 2)


def ride_slices(kind, src, dst, place, step):
    k, _ = partner(kind, place, step)
    t = 2 * place["v"] + place["f"]
    if kind == "scatter_u":
        return [(src.at[7 - k if s else k], dst.at[step - 1, s], dst.at[step - 1, s]) for s in range(2)]
    if kind == "gather_hidden":
        return [(src, dst.at[t], dst.at[k])]
    if kind == "scatter_hidden":
        return [(src.at[k], dst.at[step - 1], dst.at[step - 1])]
    if kind == "swap_v":
        return [(src, dst, dst)]
    return [(src, dst.at[step - 1], dst.at[step - 1])]


def ride_copies(kind, src, dst, send, recv, place, part):
    if kind == "gather_keys" and part == "on":
        _, to = partner(kind, place, 1)
        return [remote(dst.at[1], dst.at[2], send.at[4], recv.at[4], to)]
    copies = []
    for step in STEPS.get(kind, (3, 2, 1)):
        _, to = partner(kind, place, step)
        for i, (here, there, landing) in enumerate(ride_slices(kind, src, dst, place, step)):
            at = 2 * step - 2 + i
            if part == "away":
                copies.append(remote(here, there, send.at[at], recv.at[at], to))
            else:
                copies.append(remote(landing, landing, send.at[at], recv.at[at], to))
    return copies


def own_copies(kind, src, dst, keep, place):
    u, t = place["u"], 2 * place["v"] + place["f"]
    if kind == "gather_u":
        return [pltpu.make_async_copy(src.at[s], dst.at[7 - u if s else u], keep.at[s]) for s in range(2)]
    return [pltpu.make_async_copy(src, dst.at[t], keep.at[0])] if kind == "gather_hidden" else []


def chain_u(stage, src, dst, send, recv, place):
    me = place["u"]
    right, left = device(place, u=jnp.minimum(me + 1, 3)), device(place, u=jnp.maximum(me - 1, 0))

    def spot(owner, slot):
        return dst.at[7 - owner if slot else owner]

    def going(step, slot, side):
        owner = jnp.clip(me + step if side else me - step, 0, 3)
        here = src.at[slot] if step == 0 else spot(owner, slot)
        at = 6 * side + 2 * step + slot
        return remote(here, spot(owner, slot), send.at[at], recv.at[at], left if side else right)

    def coming(step, slot, side):
        there = spot(jnp.clip(me + 1 + step if side else me - 1 - step, 0, 3), slot)
        at = 6 * side + 2 * step + slot
        return remote(there, there, send.at[at], recv.at[at], right if side else left)

    def sends(step, side):
        return (me > 0) & (me <= 3 - step) if side else (me < 3) & (me >= step)

    def gets(step, side):
        return me <= 2 - step if side else me >= step + 1

    for slot in range(2):
        for side in range(2):
            if stage > 0:

                @pl.when(gets(stage - 1, side))
                def _():
                    coming(stage - 1, slot, side).wait_recv()

            if stage < 3:

                @pl.when(sends(stage, side))
                def _():
                    going(stage, slot, side).start()

    if stage == 3:
        for step in range(3):
            for slot in range(2):
                for side in range(2):

                    @pl.when(sends(step, side))
                    def _():
                        going(step, slot, side).wait_send()


def gather_heads(stage, src, dst, send, recv, keep, place):
    v, core, f = place["v"], place["core"], place["f"]
    mine = (2 * v + core) * 2 + f
    other = device(place, core=1 - core)

    def away(step):
        _, to = partner("gather_hidden", place, step)
        return remote(src, dst.at[mine], send.at[step], recv.at[step], to)

    def on(step):
        k = (2 * v + f) ^ step
        there = dst.at[(2 * (k // 2) + core) * 2 + k % 2]
        return remote(src if step == 0 else there, there, send.at[4 + step], recv.at[4 + step], other)

    def landed(step):
        k = (2 * v + f) ^ step
        there = dst.at[(2 * (k // 2) + core) * 2 + k % 2]
        return remote(there, there, send.at[step], recv.at[step], other)

    def passed(step):
        k = (2 * v + f) ^ step
        there = dst.at[(2 * (k // 2) + 1 - core) * 2 + k % 2]
        return remote(there, there, send.at[4 + step], recv.at[4 + step], other)

    local = pltpu.make_async_copy(src, dst.at[mine], keep.at[0]) if stage != 1 else None
    if stage == 0:
        local.start()
        for step in (3, 2, 1):
            away(step).start()
        on(0).start()
    elif stage == 1:
        for step in (1, 2, 3):
            landed(step).wait_recv()
            on(step).start()
    else:
        local.wait()
        for step in (1, 2, 3):
            away(step).wait_send()
        for step in range(4):
            on(step).wait_send()
            passed(step).wait_recv()


def gather_halves(stage, src, dst, send, recv, keep, place):
    v, core, f = place["v"], place["core"], place["f"]
    x_to, y_to, other = device(place, v=1 - v), device(place, f=1 - f), device(place, core=1 - core)
    many = src.shape[0] // 2

    def spot(row, core_, col):
        return dst.at[(2 * row + core_) * 2 + col]

    def half(ref, h):
        return ref.at[many * h : many * h + many]

    def going(here, there, at, to):
        return remote(here, there, send.at[at], recv.at[at], to)

    corners = [(v, f), (1 - v, f), (v, 1 - f), (1 - v, 1 - f)]
    own = [(0, 0, x_to), (3, 1, y_to), (1, 1, x_to), (2, 0, y_to)]

    def sends():
        return [going(half(src, h), half(spot(v, core, f), h), at, to) for at, h, to in own]

    def passing():
        y_on, x_on = half(spot(1 - v, core, f), 0), half(spot(v, core, 1 - f), 1)
        return [going(y_on, y_on, 5, y_to), going(x_on, x_on, 4, x_to)]

    def across(k, core_):
        there = spot(corners[k][0], core_, corners[k][1])
        return going(src if k == 0 and core_ is core else there, there, 6 + k, other)

    def landing(ref, h, at):
        return going(half(ref, h), half(ref, h), at, other)

    if stage == 0:
        pltpu.make_async_copy(src, spot(v, core, f), keep.at[0]).start()
        for copy in sends():
            copy.start()
        across(0, core).start()
    elif stage == 1:
        landing(spot(1 - v, core, f), 0, 0).wait_recv()
        landing(spot(v, core, 1 - f), 1, 3).wait_recv()
        for copy in passing():
            copy.start()
    elif stage == 2:
        landing(spot(1 - v, core, f), 1, 1).wait_recv()
        across(1, core).start()
        landing(spot(v, core, 1 - f), 0, 2).wait_recv()
        across(2, core).start()
        landing(spot(1 - v, core, 1 - f), 0, 5).wait_recv()
        landing(spot(1 - v, core, 1 - f), 1, 4).wait_recv()
        across(3, core).start()
    else:
        pltpu.make_async_copy(src, spot(v, core, f), keep.at[0]).wait()
        for copy in sends() + passing():
            copy.wait_send()
        for k in range(4):
            across(k, core).wait_send()
            across(k, 1 - core).wait_recv()


def ride_greet(kinds, place):
    barrier = pltpu.get_barrier_semaphore()
    count = 0
    for kind in kinds:
        if kind == "gather_heads":
            other = device(place, core=1 - place["core"])
            pl.semaphore_signal(barrier, inc=1, device_id=other, device_id_type=MESH_IDS)
            count = count + 1
        if kind == "gather_halves":
            for axis in ("v", "f", "core"):
                to = device(place, **{axis: 1 - place[axis]})
                pl.semaphore_signal(barrier, inc=1, device_id=to, device_id_type=MESH_IDS)
            count = count + 3
            continue
        for step in STEPS.get(kind, (3, 2, 1)):
            _, to = partner(kind, place, step)
            pl.semaphore_signal(barrier, inc=1, device_id=to, device_id_type=MESH_IDS)
            count = count + 1
    return count


def ride_start(kinds, rides, arrived, sems, place):
    for a, kind in enumerate(kinds):
        send, recv, keep = (sem.at[a] for sem in sems)
        if kind == "gather_u":
            chain_u(0, rides[a], arrived[a], send, recv, place)
        elif kind == "gather_halves":
            gather_halves(0, rides[a], arrived[a], send, recv, keep, place)
        elif kind == "gather_heads":
            gather_heads(0, rides[a], arrived[a], send, recv, keep, place)
        else:
            for copy in ride_copies(kind, rides[a], arrived[a], send, recv, place, "away"):
                copy.start()
        for copy in own_copies(kind, rides[a], arrived[a], keep, place):
            copy.start()


def ride_on(kinds, rides, arrived, sems, place, stage):
    for a, kind in enumerate(kinds):
        if kind == "gather_halves":
            gather_halves(1, rides[a], arrived[a], *(sem.at[a] for sem in sems), place)
        if kind == "gather_u":
            chain_u(stage, rides[a], arrived[a], sems[0].at[a], sems[1].at[a], place)


def ride_end(kinds, rides, arrived, sems, place):
    def copies(a, part):
        return ride_copies(kinds[a], rides[a], arrived[a], sems[0].at[a], sems[1].at[a], place, part)

    def heads(a, stage):
        gather_heads(stage, rides[a], arrived[a], *(sem.at[a] for sem in sems), place)

    keys = [a for a, kind in enumerate(kinds) if kind == "gather_keys"]
    for a, kind in enumerate(kinds):
        if kind == "gather_heads":
            heads(a, 1)
        if kind == "gather_halves":
            gather_halves(2, rides[a], arrived[a], *(sem.at[a] for sem in sems), place)
    for a in keys:
        for copy in copies(a, "back"):
            copy.wait_recv()
        for copy in copies(a, "on"):
            copy.start()
    for a, kind in enumerate(kinds):
        for copy in own_copies(kind, rides[a], arrived[a], sems[2].at[a], place):
            copy.wait()
        if kind == "gather_u":
            chain_u(3, rides[a], arrived[a], sems[0].at[a], sems[1].at[a], place)
            continue
        if kind == "gather_heads":
            heads(a, 2)
            continue
        if kind == "gather_halves":
            gather_halves(3, rides[a], arrived[a], *(sem.at[a] for sem in sems), place)
            continue
        for copy in copies(a, "away"):
            copy.wait_send()
        for copy in copies(a, "back") if a not in keys else ():
            copy.wait_recv()
    for a in keys:
        for copy in copies(a, "on"):
            copy.wait()


def ride_scratch(n):
    return [pltpu.SemaphoreType.DMA((n, 12)), pltpu.SemaphoreType.DMA((n, 12)), pltpu.SemaphoreType.DMA((n, 2))]


def riding(kernel, args, extra, outs, kinds, grid):
    n = len(kinds)

    def whole(*refs):
        ins, rides = refs[:args], refs[args : args + n]
        rest = refs[args + n + extra :]
        results, arrived, scratch = rest[:outs], rest[outs : outs + n], rest[outs + n : len(rest) - 3]
        sems = rest[len(rest) - 3 :]
        place = coords()
        ids = [pl.program_id(i) for i in range(len(grid))]
        first, last = ids[0] == 0, ids[0] == grid[0] - 1
        for i in range(1, len(grid)):
            first, last = first & (ids[i] == 0), last & (ids[i] == grid[i] - 1)

        @pl.when(first)
        def _():
            count = ride_greet(kinds, place)
            pl.semaphore_wait(pltpu.get_barrier_semaphore(), count)
            ride_start(kinds, rides, arrived, sems, place)

        kernel(*ins, *results, *scratch)

        if "gather_u" in kinds:
            total = math.prod(grid)
            at = ids[0]
            for i in range(1, len(grid)):
                at = at * grid[i] + ids[i]
            for stage in (1, 2):

                @pl.when(at == total * stage // 3 - 1)
                def _():
                    ride_on(kinds, rides, arrived, sems, place, stage)

        @pl.when(last)
        def _():
            ride_end(kinds, rides, arrived, sems, place)

    return whole


def grid_call(kernel, grid, args, in_specs, out_specs, out_shape, scratch, name, micros, after=(), rides=(), ident=None):
    limit = 56 * MIB
    if not rides:
        return pl.pallas_call(
            ignoring(kernel, len(args), len(after)),
            grid=grid,
            in_specs=in_specs + [HBM] * len(after),
            out_specs=out_specs,
            out_shape=out_shape,
            scratch_shapes=scratch,
            compiler_params=pltpu.CompilerParams(vmem_limit_bytes=limit),
            cost_estimate=lasting(micros),
            name=name,
        )(*args, *after)
    kinds = [kind for kind, _ in rides]
    n = len(rides)
    return pl.pallas_call(
        riding(kernel, len(args), len(after), len(out_shape), kinds, grid),
        grid=grid,
        in_specs=in_specs + [HBM] * (n + len(after)),
        out_specs=out_specs + [HBM] * n,
        out_shape=out_shape + [ride_out(kind, x) for kind, x in rides],
        scratch_shapes=scratch + ride_scratch(n),
        compiler_params=pltpu.CompilerParams(vmem_limit_bytes=limit, collective_id=ident, has_side_effects=True),
        cost_estimate=lasting(max(micros, 50)),
        name=name + "_riding",
    )(*args, *[x for _, x in rides], *after)


def swap_halves(x):
    lane = lax.broadcasted_iota(jnp.int32, x.shape, 1)
    return jnp.where(lane % 64 < 32, pltpu.roll(x, LANES - 32, 1), pltpu.roll(x, 32, 1))


def rope_kernel(raw_ref, cos_ref, sin_ref, kv_ref, q_ref):
    cos, sin = cos_ref[...], sin_ref[...]

    def turn(x):
        return x * cos + swap_halves(x) * sin

    for p in range(4):
        kv_ref[:, 256 * p : 256 * p + 128] = turn(raw_ref[:, 256 * p : 256 * p + 128]).astype(bf16)
        kv_ref[:, 256 * p + 128 : 256 * p + 256] = raw_ref[:, 256 * p + 128 : 256 * p + 256].astype(bf16)
    last = raw_ref[:, 1024:1152]
    lane = lax.broadcasted_iota(jnp.int32, last.shape, 1)
    kv_ref[:, 1024:1152] = jnp.where(lane < 64, turn(last), last).astype(bf16)
    for p in range(5):
        q_ref[:, 128 * p : 128 * p + 128] = turn(raw_ref[:, 1152 + 128 * p : 1280 + 128 * p]).astype(bf16)


def rope(raw, cos, sin):
    rows = raw.shape[0]
    tile = min(256, rows)
    row = lambda cols: pl.BlockSpec((tile, cols), lambda i: (i, 0))
    return pl.pallas_call(
        rope_kernel,
        grid=(rows // tile,),
        in_specs=[row(1792), row(LANES), row(LANES)],
        out_specs=[row(1152), row(640)],
        out_shape=[jax.ShapeDtypeStruct((rows, 1152), bf16), jax.ShapeDtypeStruct((rows, 640), bf16)],
        compiler_params=pltpu.CompilerParams(vmem_limit_bytes=40 * MIB),
        name="rope",
    )(raw, cos, sin)


def unrope_kernel(dkv_ref, dq_ref, cos_ref, sin_ref, out_ref):
    cos, sin = cos_ref[...], sin_ref[...]

    def turn(x):
        return x * cos - swap_halves(x) * sin

    for p in range(4):
        a = 256 * p
        out_ref[:, a : a + 128] = turn(dkv_ref[:, a : a + 128].astype(f32)).astype(bf16)
        out_ref[:, a + 128 : a + 256] = dkv_ref[:, a + 128 : a + 256].astype(bf16)
    last = dkv_ref[:, 1024:1152].astype(f32)
    lane = lax.broadcasted_iota(jnp.int32, last.shape, 1)
    out_ref[:, 1024:1152] = jnp.where(lane < 64, turn(last), last).astype(bf16)
    for p in range(5):
        out_ref[:, 1152 + 128 * p : 1280 + 128 * p] = turn(
            dq_ref[:, 128 * p : 128 * p + 128].astype(f32)
        ).astype(bf16)


def unrope(dkv, dq, cos, sin, after=()):
    rows = dkv.shape[0]
    tile = min(256, rows)
    row = lambda cols: pl.BlockSpec((tile, cols), lambda i: (i, 0))
    return pl.pallas_call(
        ignoring(unrope_kernel, 4, len(after)),
        grid=(rows // tile,),
        in_specs=[row(1152), row(640), row(LANES), row(LANES)] + [HBM] * len(after),
        out_specs=row(1792),
        out_shape=jax.ShapeDtypeStruct((rows, 1792), bf16),
        compiler_params=pltpu.CompilerParams(vmem_limit_bytes=40 * MIB),
        name="unrope",
    )(dkv, dq, cos, sin, *after)


def hidden_blocks(sizes):
    nu, nw, nv, nc, nf = sizes
    out = []
    for i in range(nu * nw * nv * nc * nf):
        rest, f = divmod(i, nf)
        rest, core = divmod(rest, nc)
        uw, v = divmod(rest, nv)
        out.append((v * nf + f, uw * nc + core))
    return out


def pack_kernel(spots, block, q_ref, k_ref, v_ref, g_ref, u_ref, one_ref, two_ref, qkv_ref, first_ref, second_ref):
    slab = q_ref.shape[0]
    one, two = one_ref[...], two_ref[...]
    padded = 8 * first_ref.shape[3] // len(spots)

    def scaled(ref, start, size, gain):
        return ref[:, start : start + size].astype(f32) * gain

    for t in range(4):
        cols = []
        at = 576 * t
        for p in range(4):
            cols.append(scaled(k_ref, at + 128 * p, 128, one))
            cols.append(scaled(v_ref, at + 128 * p, 128, one))
        cols.append(scaled(k_ref, at + 512, 64, one))
        cols.append(scaled(v_ref, at + 512, 64, one))
        cols.append(scaled(q_ref, at, 576, one))
        cols.append(jnp.zeros((slab, 64), f32))
        qkv_ref[t] = jnp.concatenate(cols, 1).astype(bf16)
        mine = sorted((place, i) for i, (owner, place) in enumerate(spots) if owner == t)
        for half, ref in enumerate((g_ref, u_ref)):
            cols = []
            for _, i in mine:
                cols.append(scaled(ref, i * block, block, two))
                cols.append(jnp.zeros((slab, padded - block), f32))
            whole = jnp.concatenate(cols, 1).astype(bf16)
            cut = first_ref.shape[3]
            first_ref[t, half] = whole[:, :cut]
            second_ref[t, half] = whole[:, cut:]


def pack_weights(sizes, w_query, w_key, w_value, w_gate, w_up, gain_one, gain_two, block, padded):
    slab = w_query.shape[0]
    spots = hidden_blocks(sizes)
    cut = padded * len(spots) // 8
    return pl.pallas_call(
        functools.partial(pack_kernel, spots, block),
        out_shape=[jax.ShapeDtypeStruct((4, slab, 1792), bf16)]
        + [jax.ShapeDtypeStruct((4, 2, slab, cut), bf16)] * 2,
        compiler_params=pltpu.CompilerParams(vmem_limit_bytes=48 * MIB),
        cost_estimate=lasting(10),
        name="pack_weights",
    )(w_query, w_key, w_value, w_gate, w_up, gain_one, gain_two)


def unpack_kernel(
    spots, block, padded, qkv_ref, gu_ref, q_ref, k_ref, v_ref, g_ref, u_ref, one_ref, two_ref,
    dq_ref, dk_ref, dv_ref, dg_ref, du_ref, done_ref, dtwo_ref,
):
    one, two = one_ref[...], two_ref[...]
    gains = jnp.zeros_like(one)
    wide = gu_ref.shape[2] // 2

    def part(t, start, size):
        return qkv_ref[t, :, start : start + size].astype(f32)

    for ref, out, first, last in ((k_ref, dk_ref, 0, 1024), (v_ref, dv_ref, 128, 1088)):
        cols = []
        for t in range(4):
            cols += [part(t, first + 256 * p, 128) for p in range(4)] + [part(t, last, 64)]
        grad = jnp.concatenate(cols, 1)
        gains = gains + jnp.sum(ref[...].astype(f32) * grad, 1, keepdims=True)
        out[...] = grad * one
    grad = jnp.concatenate([part(t, 1152, 576) for t in range(4)], 1)
    done_ref[...] = gains + jnp.sum(q_ref[...].astype(f32) * grad, 1, keepdims=True)
    dq_ref[...] = grad * one
    gains = jnp.zeros_like(two)
    for half, (ref, out) in enumerate(((g_ref, dg_ref), (u_ref, du_ref))):
        grad = jnp.concatenate(
            [
                gu_ref[t, :, half * wide + place * padded : half * wide + place * padded + block].astype(f32)
                for t, place in spots
            ],
            1,
        )
        gains = gains + jnp.sum(ref[...].astype(f32) * grad, 1, keepdims=True)
        out[...] = grad * two
    dtwo_ref[...] = gains


def unpack_gradients(sizes, qkv, gu, w_query, w_key, w_value, w_gate, w_up, gain_one, gain_two, block, padded):
    slab, width = w_query.shape
    hidden = w_gate.shape[1]
    shape = lambda cols: jax.ShapeDtypeStruct((slab, cols), f32)
    return pl.pallas_call(
        functools.partial(unpack_kernel, hidden_blocks(sizes), block, padded),
        out_shape=[shape(width)] * 3 + [shape(hidden)] * 2 + [shape(1)] * 2,
        compiler_params=pltpu.CompilerParams(vmem_limit_bytes=48 * MIB),
        cost_estimate=lasting(15),
        name="unpack_gradients",
    )(qkv, gu, w_query, w_key, w_value, w_gate, w_up, gain_one, gain_two)


def stack_heads(x, first, second):
    return jnp.concatenate([jnp.where(first, x, 0), jnp.where(second, x, 0)], 0)


def text_rows(source, ring, j, half, many):
    v, core = lax.axis_index("v"), lax.axis_index("core")
    v = 1 - v if source // 2 else v
    core = 1 - core if source % 2 else core
    at = (ring * 2 + v) * 2 + core
    block = many * j + (at if j < 4 else many - 1 - at)
    return pl.multiple_of(block * half, half)


def assemble(kv_refs, kv_s):
    rings, _, half, _ = kv_refs[0].shape
    for source, ref in enumerate(kv_refs):
        for ring in range(rings):
            for j in range(8):
                kv_s[pl.ds(text_rows(source, ring, j, half, 4 * rings), half), :] = ref[ring, j]


def flash_forward_kernel(
    bounds, q_ref, kv0, kv1, kv2, kv3, lim_ref, o_ref, lse_ref, kv_s, s_ref, vt_ref
):
    p, t = pl.program_id(0), pl.program_id(1)
    nq = q_ref.shape[0]
    tail = p == 4
    voff = pl.multiple_of(jnp.where(tail, 0, LANES), LANES)
    tiles = s_ref.shape[0]

    @pl.when(t == 0)
    def _():
        assemble((kv0, kv1, kv2, kv3), kv_s)
        for k in range(tiles):
            vt_ref[k] = kv_s[k * KEY_TILE : (k + 1) * KEY_TILE, pl.ds(voff, LANES)].T

    lane = lax.broadcasted_iota(jnp.int32, (nq, LANES), 1)
    qm = stack_heads(q_ref[...] * bf16(0.125), lane < 64, lane >= 64)
    lo, hi = lim_ref[0, 0:1, :], lim_ref[0, 1:2, :]
    row = lax.broadcasted_iota(jnp.int32, (KEY_TILE, 2 * nq), 0)
    klo, khi = bounds(t)

    def scores(k, high):
        base = pl.multiple_of(k * KEY_TILE, KEY_TILE)
        s = times_transposed(kv_s[pl.ds(base, KEY_TILE), 0:LANES], qm)
        s = jnp.where((row >= lo - base) & (row <= hi - base), s, NEG_LARGE)
        s_ref[k] = s
        return jnp.maximum(high, jnp.max(s.reshape(KEY_TILE // 8, 8, 2 * nq), 0))

    high = lax.fori_loop(klo, khi, scores, jnp.full((8, 2 * nq), NEG_LARGE, f32))
    high = jnp.max(high, 0, keepdims=True)

    def mix(k, carry):
        total, acc = carry
        w = jnp.exp(s_ref[k] - high)
        total = total + jnp.sum(w.reshape(KEY_TILE // 8, 8, 2 * nq), 0)
        acc = acc + matmul(vt_ref[k], w.astype(bf16))
        return total, acc

    total, acc = lax.fori_loop(
        klo, khi, mix, (jnp.zeros((8, 2 * nq), f32), jnp.zeros((LANES, 2 * nq), f32))
    )
    total = jnp.sum(total, 0, keepdims=True)
    out = (acc / total).T
    first, second = out[:nq], out[nq:]
    low = jnp.where(tail, 0.0, first)
    up = jnp.where(tail, first, second)
    o_ref[...] = jnp.where(lane < 64, low, up).astype(bf16)
    lse_ref[0, 0] = jnp.broadcast_to(high + jnp.log(total), (8, 2 * nq))


def flash_specs(rows, tiles, kv):
    nq = rows // tiles
    _, rings, _, half, _ = kv[0].shape
    part = pl.BlockSpec((nq, LANES), lambda p, t, *_: (t, p))
    keys = [
        pl.BlockSpec((None, rings, 8, half, 2 * LANES), lambda p, t, *_, i=i: (i, 0, 0, 0, p)) for i in (0, 0, 1, 2)
    ]
    lim = pl.BlockSpec((1, 8, 2 * nq), lambda p, t, *_: (t, 0, 0))
    lse = pl.BlockSpec((1, 1, 8, 2 * nq), lambda p, t, *_: (p, t, 0, 0))
    return nq, 32 * rings * half, part, keys, lim, lse


def window_bounds(rows, tiles, rings):
    half, many = rows // 8, 4 * rings

    def bounds(t):
        at = (lax.axis_index("w") * 2 + lax.axis_index("v")) * 2 + lax.axis_index("core")

        def first_row(j):
            return (many * j + jnp.where(j < 4, at, many - 1 - at)) * half

        low = jnp.maximum(first_row(t * QUERY_BLOCKS) - (WINDOW - 1), 0)
        high = first_row(t * QUERY_BLOCKS + QUERY_BLOCKS - 1) + half - 1
        return low // KEY_TILE, high // KEY_TILE + 1

    return bounds


def flash_call(kernel, name, args, klo, khi, in_specs, out_specs, out_shape, scratch, micros, after, rides, ident):
    tiles = klo.shape[0]
    grid = (PAIRS, tiles)
    if rides:
        bounds = window_bounds(args[0].shape[0], tiles, args[-3 if name == "flash_backward" else -2].shape[1])
        return grid_call(
            functools.partial(kernel, bounds), grid, args, in_specs, out_specs, out_shape, scratch, name, micros,
            after, rides, ident,
        )

    def bounded(klo_ref, khi_ref, *refs):
        kernel(lambda t: (klo_ref[t], khi_ref[t]), *refs)

    return pl.pallas_call(
        ignoring(bounded, 2 + len(args), len(after)),
        grid_spec=pltpu.PrefetchScalarGridSpec(
            num_scalar_prefetch=2,
            grid=grid,
            in_specs=in_specs + [HBM] * len(after),
            out_specs=out_specs,
            scratch_shapes=scratch,
        ),
        out_shape=out_shape,
        compiler_params=pltpu.CompilerParams(vmem_limit_bytes=56 * MIB),
        cost_estimate=lasting(micros),
        name=name,
    )(klo, khi, *args, *after)


def flash_forward(q, kv, lim, klo, khi, after=(), rides=(), ident=None):
    rows, tiles = q.shape[0], klo.shape[0]
    nq, keys, part, whole, limits, lses = flash_specs(rows, tiles, kv)
    return flash_call(
        flash_forward_kernel,
        "flash_forward",
        [q, kv[0], kv[1], kv[1], kv[1], lim],
        klo,
        khi,
        [part, *whole, limits],
        [part, lses],
        [jax.ShapeDtypeStruct((rows, 640), bf16), jax.ShapeDtypeStruct((PAIRS, tiles, 8, 2 * nq), f32)],
        [
            pltpu.VMEM((keys, 2 * LANES), bf16),
            pltpu.VMEM((keys // KEY_TILE, KEY_TILE, 2 * nq), f32),
            pltpu.VMEM((keys // KEY_TILE, LANES, KEY_TILE), bf16),
        ],
        40,
        after,
        rides,
        ident,
    )


def flash_backward_kernel(
    bounds, q_ref, do_ref, o_ref, kv0, kv1, kv2, kv3, lim_ref, lse_ref,
    dq_ref, dkv0, dkv1, dkv2, dkv3, kv_s, kt_ref, dk_ref, dv_ref,
):
    p, t = pl.program_id(0), pl.program_id(1)
    nq = q_ref.shape[0]
    tail = p == 4
    voff = pl.multiple_of(jnp.where(tail, 0, LANES), LANES)
    tiles = kt_ref.shape[0]

    @pl.when(t == 0)
    def _():
        assemble((kv0, kv1, kv2, kv3), kv_s)
        for k in range(tiles):
            kt_ref[k] = kv_s[k * KEY_TILE : (k + 1) * KEY_TILE, 0:LANES].T
        dk_ref[...] = jnp.zeros_like(dk_ref)
        dv_ref[...] = jnp.zeros_like(dv_ref)

    lane = lax.broadcasted_iota(jnp.int32, (nq, LANES), 1)
    qm = stack_heads(q_ref[...] * bf16(0.125), lane < 64, lane >= 64)
    side = jnp.where(tail, 1, 0)
    head = lane // 64
    dom = stack_heads(do_ref[...], head == side, head == 1 + side)
    back = do_ref[...].astype(f32) * o_ref[...].astype(f32)
    back = stack_heads(back, head == side, head == 1 + side)
    delta = jnp.sum(back.T, 0, keepdims=True)
    lo, hi = lim_ref[0, 0:1, :], lim_ref[0, 1:2, :]
    lse = lse_ref[0, 0, 0:1, :]
    row = lax.broadcasted_iota(jnp.int32, (KEY_TILE, 2 * nq), 0)

    def step(k, acc):
        base = pl.multiple_of(k * KEY_TILE, KEY_TILE)
        s = times_transposed(kv_s[pl.ds(base, KEY_TILE), 0:LANES], qm)
        w = jnp.exp(jnp.where((row >= lo - base) & (row <= hi - base), s - lse, NEG_LARGE))
        dp = times_transposed(kv_s[pl.ds(base, KEY_TILE), pl.ds(voff, LANES)], dom)
        ds = (w * (dp - delta)).astype(bf16)
        dv_ref[pl.ds(base, KEY_TILE), :] += matmul(w.astype(bf16), dom)
        dk_ref[pl.ds(base, KEY_TILE), :] += matmul(ds, qm)
        return acc + matmul(kt_ref[k], ds)

    acc = lax.fori_loop(*bounds(t), step, jnp.zeros((LANES, 2 * nq), f32))
    out = acc.T * 0.125
    dq_ref[...] = jnp.where(lane < 64, out[:nq], jnp.where(tail, 0.0, out[nq:]))

    @pl.when(t == pl.num_programs(1) - 1)
    def _():
        rings, _, half, _ = dkv0.shape
        for source, ref in enumerate((dkv0, dkv1, dkv2, dkv3)):
            for ring in range(rings):
                for j in range(8):
                    at = pl.ds(text_rows(source, ring, j, half, 4 * rings), half)
                    dk, dv = dk_ref[at, :], dv_ref[at, :]
                    ref[ring, j, :, 0:LANES] = jnp.where(tail, dk + dv, dk).astype(bf16)
                    ref[ring, j, :, LANES : 2 * LANES] = dv.astype(bf16)


def flash_backward(q, do, o, kv, lim, lse, klo, khi, after=(), rides=(), ident=None):
    rows, tiles = q.shape[0], klo.shape[0]
    nq, keys, part, whole, limits, lses = flash_specs(rows, tiles, kv)
    return flash_call(
        flash_backward_kernel,
        "flash_backward",
        [q, do, o, kv[0], kv[1], kv[1], kv[1], lim, lse],
        klo,
        khi,
        [part, part, part, *whole, limits, lses],
        [part] + [whole[0]] * 4,
        [jax.ShapeDtypeStruct((rows, 640), f32)] + [jax.ShapeDtypeStruct(kv[0].shape, bf16)] * 4,
        [
            pltpu.VMEM((keys, 2 * LANES), bf16),
            pltpu.VMEM((keys // KEY_TILE, LANES, KEY_TILE), bf16),
            pltpu.VMEM((keys, LANES), f32),
            pltpu.VMEM((keys, LANES), f32),
        ],
        48,
        after,
        rides,
        ident,
    )


def feed_forward_kernel(
    held_ref, back_ref, wg_ref, wu_ref, wd_ref, act_ref, bg_ref, bu_ref, bh_ref, br_ref, bh_acc, br_acc, wd_s
):
    t = pl.program_id(0)
    tile = wg_ref.shape[2]
    blocks, high, third = wd_ref.shape
    padded = high // 3

    @pl.when(t % (third // tile) == 0)
    def _():
        for b in range(blocks):
            for c in range(3):
                wd_s[b * padded : (b + 1) * padded, c * third : (c + 1) * third] = wd_ref[
                    b, c * padded : (c + 1) * padded, :
                ]

    wd = wd_s[pl.ds(pl.multiple_of(t % (third // tile) * tile, tile), tile), :]
    held = held_ref[...]
    width = held.shape[1]
    wg = wg_ref[...].reshape(width, tile)
    wu = wu_ref[...].reshape(width, tile)
    gate, up = matmul(held, wg), matmul(held, wu)
    back_act = times_transposed(back_ref[...], wd)
    sig = jax.nn.sigmoid(gate)
    gs = gate * sig
    act = (gs * up).astype(bf16)
    bg = (back_act * up * sig * (1.0 + gate * (1.0 - sig))).astype(bf16)
    bu = (back_act * gs).astype(bf16)
    act_ref[...], bg_ref[...], bu_ref[...] = act, bg, bu
    bh = times_transposed(bg, wg) + times_transposed(bu, wu)
    br = matmul(act, wd)

    @pl.when(t == 0)
    def _():
        bh_acc[...] = bh
        br_acc[...] = br

    @pl.when(t > 0)
    def _():
        bh_acc[...] += bh
        br_acc[...] += br

    @pl.when(t == pl.num_programs(0) - 1)
    def _():
        bh_ref[...] = bh_acc[...].astype(bf16)
        br_ref[...] = br_acc[...].astype(bf16)


def feed_forward(held, back, packed, wide, after=(), rides=(), ident=None):
    rows, width = held.shape
    tile = 256
    tiles = wide // tile
    whole = pl.BlockSpec((rows, width), lambda t: (0, 0))
    part = pl.BlockSpec((rows, tile), lambda t: (0, t))
    many, _, third = packed.shape
    per, blocks, slice_rows = third // tile, many * third // wide, width // many
    cols = lambda i: pl.BlockSpec((many, slice_rows, tile), lambda t: (0, t // per * 4 + i, t % per))
    down = pl.BlockSpec((blocks, 2 * slice_rows, third), lambda t: (t // per, 1, 0))
    return grid_call(
        feed_forward_kernel,
        (tiles,),
        [held, back, packed, packed, packed],
        [whole, whole, cols(0), cols(1), down],
        [part, part, part, whole, whole],
        [jax.ShapeDtypeStruct((rows, wide), bf16)] * 3 + [jax.ShapeDtypeStruct((rows, width), bf16)] * 2,
        [pltpu.VMEM((rows, width), f32)] * 2 + [pltpu.VMEM((third, width), bf16)],
        "feed_forward",
        42,
        after,
        rides,
        ident,
    )


def weight_gradient(lefts, rights, tile=256, after=(), rides=(), ident=None):
    many, per = len(lefts), len(rights[0])
    flat = [x for group in rights for x in group]
    rows, high = lefts[0].shape
    widths = [x.shape[1] for x in rights[0]]

    def kernel(*refs):
        ls, rs, out = refs[:many], refs[many : many + len(flat)], refs[many + len(flat)]
        start = 0
        for i, cols in enumerate(widths):
            total = transposed_times(ls[0][...], rs[i][...])
            for g in range(1, many):
                total = total + transposed_times(ls[g][...], rs[g * per + i][...])
            out[:, start : start + cols] = total.astype(bf16)
            start += cols

    return grid_call(
        kernel,
        (high // tile,),
        [*lefts, *flat],
        [pl.BlockSpec((rows, tile), lambda i: (0, i))] * many + [pl.BlockSpec(x.shape, lambda i: (0, 0)) for x in flat],
        [pl.BlockSpec((tile, sum(widths)), lambda i: (i, 0))],
        [jax.ShapeDtypeStruct((high, sum(widths)), bf16)],
        [],
        "weight_gradient",
        max(4, 2 * many * rows * high * sum(widths) // 10**9),
        after,
        rides,
        ident,
    )


def greet(places):
    barrier = pltpu.get_barrier_semaphore()
    for place in places:
        pl.semaphore_signal(barrier, inc=1, device_id=place, device_id_type=MESH_IDS)
    pl.semaphore_wait(barrier, len(places))


def greet_line(me, place, more=0):
    barrier = pltpu.get_barrier_semaphore()

    @pl.when(me > 0)
    def _():
        pl.semaphore_signal(barrier, inc=1, device_id=device(place, u=me - 1), device_id_type=MESH_IDS)

    @pl.when(me < 3)
    def _():
        pl.semaphore_signal(barrier, inc=1, device_id=device(place, u=me + 1), device_id_type=MESH_IDS)

    pl.semaphore_wait(barrier, 2 + more - jnp.where(me == 0, 1, 0) - jnp.where(me == 3, 1, 0))


def communicating(kernel, out, args, scratch, collective_id, name, vmem=40, after=(), micros=50):
    return pl.pallas_call(
        ignoring(kernel, len(args), len(after)),
        out_shape=out,
        in_specs=[HBM] * (len(args) + len(after)),
        out_specs=[HBM] * len(out) if isinstance(out, list) else HBM,
        scratch_shapes=scratch,
        compiler_params=pltpu.CompilerParams(
            collective_id=collective_id, has_side_effects=True, vmem_limit_bytes=vmem * MIB
        ),
        cost_estimate=lasting(micros),
        name=name,
    )(*args, *after)


def gather_u_kernel(n, kinds, *refs):
    r = len(kinds)
    ins, rides, outs, arrived = refs[:n], refs[n : n + r], refs[n + r : 2 * n + r], refs[2 * n + r : 2 * n + 2 * r]
    keep, send_r, send_l, recv_r, recv_l, *ride_sems = refs[2 * n + 2 * r :]
    place = coords()
    me = place["u"]
    greet_line(me, place, ride_greet(kinds, place))
    right, left = device(place, u=jnp.minimum(me + 1, 3)), device(place, u=jnp.maximum(me - 1, 0))

    def spot(owner, slot, a):
        return outs[a].at[:, owner if slot == 0 else 7 - owner]

    def going(step, slot, a, rightward):
        owner = me - step if rightward else me + step
        owner = jnp.clip(owner, 0, 3)
        src = ins[a].at[:, slot] if step == 0 else spot(owner, slot, a)
        send, recv, to = (send_r, recv_l, right) if rightward else (send_l, recv_r, left)
        return remote(src, spot(owner, slot, a), send.at[step, slot, a], recv.at[step, slot, a], to)

    def coming(step, slot, a, from_left):
        owner = jnp.clip(me - 1 - step if from_left else me + 1 + step, 0, 3)
        send, recv, to = (send_r, recv_l, right) if from_left else (send_l, recv_r, left)
        there = spot(owner, slot, a)
        return remote(there, there, send.at[step, slot, a], recv.at[step, slot, a], to)

    parts = [(slot, a) for slot in range(2) for a in range(n)]
    own = [pltpu.make_async_copy(ins[a].at[:, s], spot(me, s, a), keep.at[s, a]) for s, a in parts]
    for step in range(3):
        for part in parts:
            if step > 0:

                @pl.when(me >= step)
                def _():
                    coming(step - 1, *part, True).wait_recv()

            @pl.when((me < 3) & (me >= step))
            def _():
                going(step, *part, True).start()

            if step > 0:

                @pl.when(me <= 3 - step)
                def _():
                    coming(step - 1, *part, False).wait_recv()

            @pl.when((me > 0) & (me <= 3 - step))
            def _():
                going(step, *part, False).start()

        if step == 0:
            for copy in own:
                copy.start()
            ride_start(kinds, rides, arrived, ride_sems, place)
        if step == 1:
            ride_on(kinds, rides, arrived, ride_sems, place, 1)
    for part in parts:

        @pl.when(me == 3)
        def _():
            coming(2, *part, True).wait_recv()

        @pl.when(me == 0)
        def _():
            coming(2, *part, False).wait_recv()

    for step in range(3):
        for part in parts:

            @pl.when((me < 3) & (me >= step))
            def _():
                going(step, *part, True).wait_send()

            @pl.when((me > 0) & (me <= 3 - step))
            def _():
                going(step, *part, False).wait_send()

    for copy in own:
        copy.wait()
    ride_end(kinds, rides, arrived, ride_sems, place)


def gather_u(arrays, collective_id, after=(), rides=()):
    n = len(arrays)
    sems = pltpu.SemaphoreType.DMA((3, 2, n))
    return communicating(
        functools.partial(gather_u_kernel, n, [kind for kind, _ in rides]),
        [jax.ShapeDtypeStruct((x.shape[0], 8) + x.shape[2:], x.dtype) for x in arrays]
        + [ride_out(kind, x) for kind, x in rides],
        arrays + [x for _, x in rides],
        [pltpu.SemaphoreType.DMA((2, n)), sems, sems, sems, sems] + (ride_scratch(len(rides)) if rides else []),
        collective_id,
        "gather_u",
        after=after,
    )


def scatter_u_kernel(kinds, *refs):
    r = len(kinds)
    p_ref, *rides = refs[: 1 + r]
    out_ref, *arrived = refs[1 + r : 2 + 2 * r]
    own, from_l, from_r, total, load, send_r, send_l, recv_l, recv_r, store, *ride_sems = refs[2 + 2 * r :]
    place = coords()
    me = place["u"]
    greet_line(me, place, ride_greet(kinds, place))
    ride_start(kinds, rides, arrived, ride_sems, place)
    right, left = device(place, u=jnp.minimum(me + 1, 3)), device(place, u=jnp.maximum(me - 1, 0))

    def mine(owner, slot):
        return p_ref.at[:, owner if slot == 0 else 7 - owner]

    loads = [
        pltpu.make_async_copy(mine(k, s), own.at[k, s], load.at[k, s]) for k in range(4) for s in range(2)
    ]
    order = [3, 0, 2, 1]

    def fetch(k, s):
        return loads[2 * k + s]

    for k in order:
        for s in range(2):
            fetch(k, s).start()

    def rightward(e, s):
        src = from_l.at[e, s]
        return remote(src, from_l.at[e, s], send_r.at[e, s], recv_l.at[e, s], right)

    def rightward_first(e, s):
        return remote(own.at[3 - e, s], from_l.at[e, s], send_r.at[e, s], recv_l.at[e, s], right)

    def leftward(k, s):
        return remote(from_r.at[k, s], from_r.at[k, s], send_l.at[k, s], recv_r.at[k, s], left)

    def leftward_first(k, s):
        return remote(own.at[k, s], from_r.at[k, s], send_l.at[k, s], recv_r.at[k, s], left)

    def add(into, other):
        into[...] = (into[...].astype(f32) + other[...].astype(f32)).astype(into.dtype)

    for s in range(2):
        for k in order:
            fetch(k, s).wait()
        for e in range(3):

            @pl.when(me == 0)
            def _():
                rightward_first(e, s).start()

            @pl.when(me == 3)
            def _():
                leftward_first(e, s).start()

    for e in range(3):
        for s in range(2):

            @pl.when((me > 0) & (me < 3 - e))
            def _():
                rightward(e, s).wait_recv()
                add(from_l.at[e, s], own.at[3 - e, s])
                rightward(e, s).start()

            @pl.when((me < 3) & (me > e))
            def _():
                leftward(e, s).wait_recv()
                add(from_r.at[e, s], own.at[e, s])
                leftward(e, s).start()

    stores = [pltpu.make_async_copy(total.at[s], out_ref.at[:, s], store.at[s]) for s in range(2)]
    for s in range(2):
        total[s] = own[me, s].astype(f32)

        @pl.when(me > 0)
        def _():
            e = jnp.minimum(3 - me, 2)
            rightward(e, s).wait_recv()
            total[s] += from_l[e, s].astype(f32)

        @pl.when(me < 3)
        def _():
            e = jnp.minimum(me, 2)
            leftward(e, s).wait_recv()
            total[s] += from_r[e, s].astype(f32)

        stores[s].start()
    for e in range(3):
        for s in range(2):

            @pl.when(me < 3 - e)
            def _():
                rightward(e, s).wait_send()

            @pl.when(me > e)
            def _():
                leftward(e, s).wait_send()

    for copy in stores:
        copy.wait()
    ride_end(kinds, rides, arrived, ride_sems, place)


def scatter_u(x, rides=(), after=()):
    groups, _, half, cols = x.shape
    piece = (groups, half, cols)
    sems = pltpu.SemaphoreType.DMA((3, 2))
    return communicating(
        functools.partial(scatter_u_kernel, [kind for kind, _ in rides]),
        [jax.ShapeDtypeStruct((groups, 2, half, cols), f32)] + [ride_out(kind, x) for kind, x in rides],
        [x] + [x for _, x in rides],
        [
            pltpu.VMEM((4, 2) + piece, x.dtype),
            pltpu.VMEM((3, 2) + piece, x.dtype),
            pltpu.VMEM((3, 2) + piece, x.dtype),
            pltpu.VMEM((2,) + piece, f32),
            pltpu.SemaphoreType.DMA((4, 2)),
            sems,
            sems,
            sems,
            sems,
            pltpu.SemaphoreType.DMA((2,)),
        ]
        + (ride_scratch(len(rides)) if rides else []),
        1,
        "scatter_u",
        after=after,
    )


def gather_hidden_kernel(x_ref, out_ref, keep, send_x, send_y, recv_x, recv_y):
    place = coords()
    v, f = place["v"], place["f"]
    x_to, y_to = device(place, v=1 - v), device(place, f=1 - f)
    greet([x_to, y_to])
    half = x_ref.shape[0] // 2

    def spot(row, col, h):
        start = pl.multiple_of((row * 2 + col) * 2 * half + h * half, half)
        return out_ref.at[pl.ds(start, half)]

    def own(h):
        return x_ref.at[pl.ds(h * half, half)]

    def via_x(src, dst, i):
        return remote(src, dst, send_x.at[i], recv_x.at[i], x_to)

    def via_y(src, dst, i):
        return remote(src, dst, send_y.at[i], recv_y.at[i], y_to)

    x_own = [via_x(own(h), spot(v, f, h), h) for h in range(2)]
    y_own = [via_y(own(h), spot(v, f, h), h) for h in range(2)]
    x_own[0].start()
    y_own[1].start()
    x_own[1].start()
    y_own[0].start()
    keeps = [pltpu.make_async_copy(own(h), spot(v, f, h), keep.at[h]) for h in range(2)]
    for copy in keeps:
        copy.start()
    via_x(own(0), spot(1 - v, f, 0), 0).wait_recv()
    y_on = via_y(spot(1 - v, f, 0), spot(1 - v, f, 0), 2)
    y_on.start()
    via_y(own(1), spot(v, 1 - f, 1), 1).wait_recv()
    x_on = via_x(spot(v, 1 - f, 1), spot(v, 1 - f, 1), 2)
    x_on.start()
    via_x(own(1), spot(1 - v, f, 1), 1).wait_recv()
    via_y(own(0), spot(v, 1 - f, 0), 0).wait_recv()
    via_x(own(1), spot(1 - v, 1 - f, 1), 2).wait_recv()
    via_y(own(0), spot(1 - v, 1 - f, 0), 2).wait_recv()
    for copy in x_own + y_own + [x_on, y_on]:
        copy.wait_send()
    for copy in keeps:
        copy.wait()


def gather_hidden(x, after=()):
    rows, cols = x.shape
    sems = pltpu.SemaphoreType.DMA((3,))
    return communicating(
        gather_hidden_kernel,
        jax.ShapeDtypeStruct((4 * rows, cols), x.dtype),
        [x],
        [pltpu.SemaphoreType.DMA((2,)), sems, sems, sems, sems],
        2,
        "gather_hidden",
        after=after,
        micros=20,
    )


def scatter_hidden_kernel(p_ref, out_ref, own, got_x, got_y, total, load, send_x, send_y, recv_x, recv_y, store):
    place = coords()
    v, f = place["v"], place["f"]
    x_to, y_to = device(place, v=1 - v), device(place, f=1 - f)
    greet([x_to, y_to])
    half = total.shape[1]

    def mine(row, col, h):
        start = pl.multiple_of((row * 2 + col) * 2 * half + h * half, half)
        return p_ref.at[pl.ds(start, half)]

    corners = [(v, f), (1 - v, f), (v, 1 - f), (1 - v, 1 - f)]
    loads = [
        [pltpu.make_async_copy(mine(*corners[i], h), own.at[i, h], load.at[i, h]) for h in range(2)]
        for i in range(4)
    ]
    for i in (3, 1, 2, 0):
        for h in range(2):
            loads[i][h].start()

    def via_x(src, i):
        return remote(src, got_x.at[i], send_x.at[i], recv_x.at[i], x_to)

    def via_y(src, i):
        return remote(src, got_y.at[i], send_y.at[i], recv_y.at[i], y_to)

    loads[3][0].wait()
    x_far = via_x(own.at[3, 0], 0)
    x_far.start()
    loads[3][1].wait()
    y_far = via_y(own.at[3, 1], 0)
    y_far.start()
    loads[1][0].wait()
    x_near = via_x(own.at[1, 0], 1)
    x_near.start()
    loads[2][1].wait()
    y_near = via_y(own.at[2, 1], 2)
    y_near.start()

    def add(into, other):
        into[...] = (into[...].astype(f32) + other[...].astype(f32)).astype(into.dtype)

    loads[2][0].wait()
    x_far.wait_recv()
    add(own.at[2, 0], got_x.at[0])
    y_sum = via_y(own.at[2, 0], 1)
    y_sum.start()
    loads[1][1].wait()
    y_far.wait_recv()
    add(own.at[1, 1], got_y.at[0])
    x_sum = via_x(own.at[1, 1], 2)
    x_sum.start()
    stores = [
        pltpu.make_async_copy(total.at[h], out_ref.at[pl.ds(h * half, half)], store.at[h]) for h in range(2)
    ]
    loads[0][0].wait()
    loads[0][1].wait()
    x_near.wait_recv()
    y_near.wait_recv()
    total[0] = own[0, 0].astype(f32) + got_x[1].astype(f32)
    total[1] = own[0, 1].astype(f32) + got_y[2].astype(f32)
    y_sum.wait_recv()
    total[0] += got_y[1].astype(f32)
    stores[0].start()
    x_sum.wait_recv()
    total[1] += got_x[2].astype(f32)
    stores[1].start()
    for copy in (x_far, y_far, x_near, y_near, x_sum, y_sum):
        copy.wait_send()
    for copy in stores:
        copy.wait()


def scatter_hidden(x):
    rows, cols = x.shape[0] // 4, x.shape[1]
    half = (rows // 2, cols)
    sems = pltpu.SemaphoreType.DMA((3,))
    return communicating(
        scatter_hidden_kernel,
        jax.ShapeDtypeStruct((rows, cols), f32),
        [x],
        [
            pltpu.VMEM((4, 2) + half, x.dtype),
            pltpu.VMEM((3,) + half, x.dtype),
            pltpu.VMEM((3,) + half, x.dtype),
            pltpu.VMEM((2,) + half, f32),
            pltpu.SemaphoreType.DMA((4, 2)),
            sems,
            sems,
            sems,
            sems,
            pltpu.SemaphoreType.DMA((2,)),
        ],
        3,
        "scatter_hidden",
    )


FLIP = [(0, 1), (1, 0)]


def core_sum_kernel(x_ref, out_ref, mine, got, load, send, recv, store):
    place = coords()
    core = place["core"]
    other = device(place, core=1 - core)
    barrier = pltpu.get_barrier_semaphore()
    pl.semaphore_signal(barrier, inc=1, device_id=other, device_id_type=MESH_IDS)
    pl.semaphore_wait(barrier, 1)
    blocks = x_ref.shape[0]
    order = [(v, f) for v in range(2) for f in range(2)]

    def sending(k):
        v, f = order[k]
        return remote(x_ref.at[:, v, 1 - core, f], got.at[k], send.at[k], recv.at[k], other)

    def loading(k):
        v, f = order[k]
        return pltpu.make_async_copy(x_ref.at[:, v, core, f], mine.at[k], load.at[k])

    def storing(k):
        return pltpu.make_async_copy(mine.at[k], out_ref.at[k], store.at[k])

    for k in range(4):
        sending(k).start()
        loading(k).start()
    for k in range(4):
        loading(k).wait()
        sending(k).wait_recv()
        for i in range(blocks):
            mine[k, i] = (mine[k, i].astype(f32) + got[k, i].astype(f32)).astype(mine.dtype)
        storing(k).start()
    for k in range(4):
        sending(k).wait_send()
        storing(k).wait()


def head_sum_start(x, sizes, collective_id, blocks=1):
    _, many, nv, nc, nf = sizes
    rows, cols = x.shape[0] // (blocks * many * nv * nc * nf), x.shape[1]
    x = x.reshape(blocks, many, nv, nc, nf, rows, cols)
    x = lax.psum_scatter(x, "w", scatter_dimension=1, tiled=False) if many > 1 else x[:, 0]
    sems = pltpu.SemaphoreType.DMA((4,))
    out = communicating(
        core_sum_kernel,
        jax.ShapeDtypeStruct((4, blocks, rows, cols), x.dtype),
        [x],
        [pltpu.VMEM((4, blocks, rows, cols), x.dtype)] * 2 + [sems] * 4,
        collective_id,
        "core_sum",
        micros=12,
    )
    return out.reshape(4, blocks * rows, cols)


def with_rings(x, many):
    return lax.all_gather(x, "w", axis=1) if many > 1 else x[:, None]


def scatter_keys_start(parts, many):
    parts = [x[0] for x in parts]
    if many > 1:
        parts = [lax.psum_scatter(x, "w", scatter_dimension=0, tiled=True) for x in parts]
    along = parts[2][0].astype(f32) + lax.ppermute(parts[3][0], "core", FLIP).astype(f32)
    own = parts[0][0].astype(f32) + lax.ppermute(parts[1][0], "core", FLIP).astype(f32)
    return own, along.astype(bf16)


def pieces_of(part, axes):
    me = lax.axis_index(axes)
    return [part(me ^ step) for step in (0, 3, 2, 1)]


def tied(xs, after):
    return lax.optimization_barrier((tuple(xs), tuple(after)))[0]


def scatter_pieces(pieces, axes, after=()):
    got = [
        lax.ppermute(piece, axes, [(i, i ^ step) for i in range(4)])
        for step, piece in zip((3, 2, 1), pieces[1:])
    ]
    total = pieces[0].astype(f32)
    for part in tied(got, after):
        total = total + part.astype(f32)
    return total


def pieces_u(x):
    def part(k):
        return jnp.stack(
            [lax.dynamic_index_in_dim(x, k, 0, False), lax.dynamic_index_in_dim(x, 7 - k, 0, False)], 0
        )

    return pieces_of(part, "u")


def pieces_hidden(x):
    blocks = x.reshape(4, x.shape[0] // 4, x.shape[1])
    return pieces_of(lambda k: lax.dynamic_index_in_dim(blocks, k, 0, False), HIDDEN)


def gather_hidden_async(x):
    me = lax.axis_index(HIDDEN)
    out = jnp.zeros((4,) + x.shape, x.dtype)
    for step in range(4):
        part = x if step == 0 else lax.ppermute(x, HIDDEN, [(i, i ^ step) for i in range(4)])
        out = lax.dynamic_update_index_in_dim(out, part, me ^ step, 0)
    return out.reshape(4 * x.shape[0], x.shape[1])


def gather_u_start(x):
    return [x] + [lax.ppermute(x, "u", [(i, i ^ step) for i in range(4)]) for step in (3, 2, 1)]


def gather_u_end(parts, after):
    me = lax.axis_index("u")
    out = jnp.zeros((8,) + parts[0].shape[1:], parts[0].dtype)
    for step, part in zip((0, 3, 2, 1), tied(parts, after)):
        k = me ^ step
        out = lax.dynamic_update_slice_in_dim(out, part[0:1], k, 0)
        out = lax.dynamic_update_slice_in_dim(out, part[1:2], 7 - k, 0)
    return out


def exchange_kernel(sizes, kinds, back, spots, *refs):
    n, more = len(kinds), len(spots) - len(kinds)
    ins, outs = refs[:n], refs[n + more : len(refs) - 3]
    send, recv, keep = refs[len(refs) - 3 :]
    nu, nw, nv, nc, nf = sizes
    place = coords()
    u, w, v, core, f = (place[axis] for axis in ALL)

    def holder(kind, block):
        if kind == "along":
            return (block, w, v, core, f)
        if kind == "heads":
            at = (u * nw + w) * nv + v
            return (block, at // (nf * nc * nv), at // (nf * nc) % nv, at // nf % nc, at % nf)
        return (u, w, block // nf, v, block % nf)

    def owner(kind, slot):
        if kind == "along":
            return (slot, w, v, core, f)
        if kind == "heads":
            at = ((w * nv + v) * nc + core) * nf + f
            return (at // (nv * nw), at // nv % nw, at % nv, slot // nf, slot % nf)
        return (u, w, core, slot // nf, slot % nf)

    def same(other):
        equal = other[0] == u
        for a, b in zip(other[1:], (w, v, core, f)):
            equal = equal & (a == b)
        return equal

    def landing(kind):
        slot = core * nf + f
        block = v * nf + f if kind == "hidden" else u
        return block if back or kind == "along" else slot

    to, frm = (owner, holder) if back else (holder, owner)
    barrier = pltpu.get_barrier_semaphore()
    waits = jnp.int32(0)
    for kind in kinds:
        for i in range(4):
            other = frm(kind, i)

            @pl.when(jnp.logical_not(same(other)))
            def _():
                pl.semaphore_signal(barrier, inc=1, device_id=other, device_id_type=MESH_IDS)

            waits = waits + jnp.where(same(to(kind, i)), 0, 1)
    pl.semaphore_wait(barrier, waits)

    def land(a, at):
        out, first = spots[a]
        return outs[out].at[at] if first is None else outs[out].at[first : first + ins[a].shape[1], at]

    def copy(a, i):
        at = landing(kinds[a])
        return remote(ins[a].at[i], land(a, at), send.at[a, i], recv.at[a, at], to(kinds[a], i))

    def local(a, i):
        return pltpu.make_async_copy(ins[a].at[i], land(a, landing(kinds[a])), keep.at[a])

    own = []
    if more:
        out, first = spots[n]
        own = [pltpu.make_async_copy(refs[n], outs[out].at[first : first + refs[n].shape[0]], keep.at[n])]
    for stage in range(3):
        for rest in own:
            rest.start() if stage == 0 else rest.wait() if stage == 1 else None
        for a in range(n):
            for i in range(4):
                here = same(to(kinds[a], i))

                @pl.when(here)
                def _():
                    local(a, i).start() if stage == 0 else local(a, i).wait() if stage == 1 else None

                @pl.when(jnp.logical_not(here))
                def _():
                    copy(a, i).start() if stage == 0 else copy(a, i).wait_send() if stage == 1 else None

                if stage == 2:

                    @pl.when(jnp.logical_not(same(frm(kinds[a], i))))
                    def _():
                        remote(
                            ins[a].at[i], land(a, i), send.at[a, i], recv.at[a, i], to(kinds[a], i)
                        ).wait_recv()


def exchange(sizes, arrays, kinds, back, collective_id, shapes, spots, after=()):
    n = len(kinds)
    return pl.pallas_call(
        ignoring(functools.partial(exchange_kernel, sizes, kinds, back, spots), len(arrays), len(after)),
        out_shape=[jax.ShapeDtypeStruct(shape, arrays[0].dtype) for shape in shapes],
        in_specs=[HBM] * (len(arrays) + len(after)),
        out_specs=[HBM] * len(shapes),
        scratch_shapes=[
            pltpu.SemaphoreType.DMA((n, 4)),
            pltpu.SemaphoreType.DMA((n, 4)),
            pltpu.SemaphoreType.DMA((n + 1,)),
        ],
        compiler_params=pltpu.CompilerParams(
            collective_id=collective_id, has_side_effects=True, vmem_limit_bytes=16 * MIB
        ),
        cost_estimate=lasting(35),
        name="exchange_back" if back else "exchange",
    )(*arrays, *after)


def pad_columns(x, cols):
    return jnp.pad(x, [(0, 0)] * (x.ndim - 1) + [(0, cols - x.shape[-1])])


def body(sizes, tokens, cotangent, segment, position, gain_attn, w_query, w_key, w_value, w_output, gain_mlp, w_gate, w_up, w_down):
    del segment
    groups, block_rows, width = tokens.shape
    rows = groups * block_rows
    half = block_rows // 2
    hidden = w_gate.shape[1]
    slab = w_gate.shape[0]
    block = w_down.shape[0]
    padded = -(-block // 16) * 16
    nkeys = sizes[1] * sizes[2] * sizes[3]
    wide = 2 * nkeys * padded
    qkv_cols = 1792
    here = (groups, 2, half)
    there = (groups, 8, half)

    gain_one, gain_two = gain_attn.astype(f32)[:, None], gain_mlp.astype(f32)[:, None]
    qkv_local, first_local, second_local = pack_weights(
        sizes, w_query, w_key, w_value, w_gate, w_up, gain_one, gain_two, block, padded
    )
    third = width // 3
    own_down = jnp.pad(w_down, ((0, padded - block), (0, 0))).reshape(padded, 3, third)
    own_down = jnp.transpose(own_down, (1, 0, 2)).reshape(-1, 4, slab, third)
    qkv_local, packed = exchange(
        sizes,
        [qkv_local, first_local, second_local, own_down],
        ["heads", "hidden", "hidden"],
        False,
        6,
        [qkv_local.shape, (6, 4, slab, third)],
        [(0, None), (1, 0), (1, 4), (1, 2)],
    )

    def all_heads(x):
        if sizes[1] > 1:
            x = lax.all_gather(x, "w", axis=0)
        return x.reshape(-1, x.shape[-1])

    sequences = range(groups)
    nlocal = lax.axis_index(KEYS)
    order = jnp.arange(8, dtype=jnp.int32)
    order = nkeys * order + jnp.where(order < 4, nlocal, nkeys - 1 - nlocal)
    text = order[:, None] * half + jnp.arange(half, dtype=jnp.int32)[None, :]
    tiles = 8 // QUERY_BLOCKS
    nq = QUERY_BLOCKS * half
    rates = jnp.exp(jnp.arange(32, dtype=f32) * (-math.log(10000.0) / 32))
    inputs, inverse_one, normed_one = [], [], []
    for g in sequences:
        x = tokens[g].astype(f32)
        inverse = lax.rsqrt(jnp.mean(x * x, -1, keepdims=True) + EPSILON)
        inputs.append(x)
        inverse_one.append(inverse)
        normed_one.append(x * inverse)
    places = jnp.broadcast_to(pad_columns(position.reshape(here), LANES)[:, :, None], (groups, 2, 8, LANES))
    upstream = [cotangent[g].astype(f32) for g in sequences]
    held_one, tables, masks, query, kv, kv_own = ([] for _ in range(6))
    before = []
    for g in sequences:
        sent = [normed_one[g].astype(bf16).reshape(1, 2, half, width), places[g : g + 1]]
        rides = [("gather_keys", kv_own[0].reshape(8, half, 1152)) if g > 0 else ("gather_halves", qkv_local)]
        if g > 0:
            rides.append(("gather_heads", w_output))
        held, seen, got, *out_rows = gather_u(sent, (0, 8)[g], after=before, rides=rides)
        held_one.append(held.reshape(8 * half, width))
        if g == 0:
            qkv_whole = all_heads(got)
        seen = seen[0, :, 0, :half]
        lowest = text - jnp.minimum(seen, WINDOW - 1)
        lows, highs = lowest.reshape(tiles, nq), text.reshape(tiles, nq)
        klo, khi = lows[:, 0] // KEY_TILE, highs[:, -1] // KEY_TILE + 1
        lim = jnp.stack([jnp.tile(lows, (1, 2)), jnp.tile(highs, (1, 2))], 1)
        masks.append((jnp.pad(lim, ((0, 0), (0, 6), (0, 0))), klo, khi))
        angles = seen.reshape(8 * half, 1).astype(f32) * rates[None, :]
        cos, sin = jnp.cos(angles), jnp.sin(angles)
        tables.append((jnp.concatenate([cos, cos, cos, cos], 1), jnp.concatenate([-sin, sin, -sin, sin], 1)))
        own, q = rope(matmul(held_one[g], qkv_whole), *tables[g])
        kv_own.append(own)
        before = [own]
        query.append(q)

    (packed,) = tied([packed], held_one[:1])
    packed = lax.all_gather(packed.reshape(-1, third), HIDDEN_SUM, axis=0)

    def key_arrays(g, others):
        own = kv_own[g].reshape(1, 8, half, 1152)
        kv.append([with_rings(own, sizes[1]), with_rings(others, sizes[1])])

    key_arrays(0, got)
    attn, lse, parts = [], [], []
    out_whole = all_heads(out_rows[0])
    out_whole = jnp.concatenate([out_whole[:512], jnp.zeros((64, width), bf16), out_whole[512:]], 0)
    rides = [("gather_keys", kv_own[1].reshape(8, half, 1152))]
    before = kv_own[1:]
    for g in sequences:
        out, sums, got_zero, *got = flash_forward(query[g], kv[g], *masks[g], after=before, rides=rides, ident=(9, 10)[g])
        attn.append(out)
        lse.append(sums)
        if g == 0:
            key_arrays(1, got_zero)
        parts.append(matmul(out, out_whole).astype(bf16).reshape(8, half, width))
        before, rides = [], [("scatter_u", parts[g])]
        rides += [("gather_hidden", (BRANCH_SCALE * x).astype(bf16)) for x in upstream]
    back_mlp = [x.reshape(4 * block_rows, width) for x in got]

    def own_u(x):
        me = lax.axis_index("u")
        return jnp.stack([lax.dynamic_index_in_dim(x, me, 0, False), lax.dynamic_index_in_dim(x, 7 - me, 0, False)], 0)

    def own_hidden(x):
        return lax.dynamic_index_in_dim(x, lax.axis_index(HIDDEN), 0, False)

    def total(own, got):
        return own.astype(f32) + jnp.sum(got.astype(f32), 0)

    middle, inverse_two, normed_two, held_two, activated, back_gu, back_held, mlp_part = ([] for _ in range(8))

    def to_feed_forward(g, got):
        x = inputs[g] + BRANCH_SCALE * total(own_u(parts[g]), got).reshape(block_rows, width)
        inverse = lax.rsqrt(jnp.mean(x * x, -1, keepdims=True) + EPSILON)
        middle.append(x)
        inverse_two.append(inverse)
        normed_two.append(x * inverse)
        held_two.append(gather_hidden(normed_two[g].astype(bf16)))

    def from_feed_forward(act, back_gate, back_up, back, part):
        activated.append(act)
        back_gu.append([back_gate, back_up])
        back_held.append(back.reshape(4, block_rows, width))
        mlp_part.append(part.reshape(4, block_rows, width))

    to_feed_forward(0, got_zero)
    *results, got_one = feed_forward(
        held_two[0], back_mlp[0], packed, wide, rides=[("scatter_u", parts[1])], ident=11
    )
    from_feed_forward(*results)
    back_middle, sent = [], []

    def to_attention(g, sums):
        x = upstream[g] + rms_back(sums, normed_two[g], inverse_two[g])
        back_middle.append(x)
        sent.append((BRANCH_SCALE * x).astype(bf16).reshape(2, half, width))

    to_attention(0, scatter_hidden(back_held[0].reshape(4 * block_rows, width)))
    to_feed_forward(1, got_one)
    *results, back_branch_zero, got_mlp = feed_forward(
        held_two[1],
        back_mlp[1],
        packed,
        wide,
        after=sent,
        rides=[("gather_u", sent[0]), ("scatter_hidden", mlp_part[0])],
        ident=12,
    )
    from_feed_forward(*results)
    layer_out = [(middle[0] + BRANCH_SCALE * total(own_hidden(mlp_part[0]), got_mlp)).astype(bf16)]
    (down_term,) = weight_gradient(activated, [[back_mlp[i]] for i in sequences])
    down_sum = lax.psum_scatter(down_term, HIDDEN_SUM, scatter_dimension=0, tiled=True)
    gu_term, got_one = weight_gradient(
        held_two, back_gu, after=[down_term], rides=[("scatter_hidden", back_held[1])], ident=13
    )
    to_attention(1, total(own_hidden(back_held[1]), got_one))
    back_branch = [back_branch_zero.reshape(8 * half, width)]
    dkv_own, dkv_along, dq = [], [], []
    rides = [("gather_u", sent[1]), ("scatter_hidden", mlp_part[1])]
    for g in sequences:
        do = times_transposed(back_branch[g], out_whole).astype(bf16)
        lim, klo, khi = masks[g]
        dq_part, *rest = flash_backward(
            query[g], do, attn[g], kv[g], lim, lse[g], klo, khi, rides=rides, ident=(14, 17)[g]
        )
        if g == 0:
            back_branch.append(rest[4].reshape(8 * half, width))
            layer_out.append((middle[1] + BRANCH_SCALE * total(own_hidden(mlp_part[1]), rest[5])).astype(bf16))
            dq_part, gu_term, down_sum = lax.optimization_barrier((dq_part, gu_term, down_sum))
            gu_sum = lax.psum_scatter(gu_term, HIDDEN_SUM, scatter_dimension=0, tiled=True)
        dq.append(dq_part)
        own, along = scatter_keys_start(rest[:4], sizes[1])
        dkv_own.append(own)
        dkv_along.append(along)
        rides = [("swap_v", along)]
    def to_tokens(g, dkv):
        back_qkv.append(unrope(dkv.reshape(8 * half, 1152), dq[g], *tables[g], after=[along]))
        part = times_transposed(back_qkv[g], qkv_whole).astype(bf16)
        late.append(part.reshape(8, half, width))

    back_qkv, late, grad_tokens = [], [], []
    to_tokens(0, dkv_own[0] + rest[4].astype(f32))
    out_term, along = weight_gradient(
        attn, [[x] for x in back_branch], tile=LANES, after=late[:1], rides=[("swap_v", along)], ident=15
    )
    out_half = head_sum_start(jnp.concatenate([out_term[:512], out_term[576:]], 0), sizes, 18)
    to_tokens(1, dkv_own[1] + along.astype(f32))
    (qkv_term,) = weight_gradient(held_one, [[x] for x in back_qkv])
    qkv_half = head_sum_start(qkv_term, sizes, 19, 4)
    sums, qkv_got, out_got = scatter_u(
        jnp.stack(late, 0), rides=[("scatter_hidden", qkv_half), ("scatter_hidden", out_half)]
    )
    grad_output = total(own_hidden(out_half), out_got)
    qkv_sum = total(own_hidden(qkv_half), qkv_got).astype(bf16)
    for g in sequences:
        part = sums[g].reshape(block_rows, width)
        x = back_middle[g] + rms_back(part, normed_one[g], inverse_one[g])
        grad_tokens.append(x.astype(bf16))
    layer_out, grad_tokens = jnp.stack(layer_out, 0), jnp.stack(grad_tokens, 0)

    qkv_sum, gu_sum = exchange(
        sizes,
        [qkv_sum.reshape(4, slab, qkv_cols), gu_sum.reshape(4, slab, 2 * wide)],
        ["along", "hidden"],
        True,
        7,
        [(4, slab, qkv_cols), (4, slab, 2 * wide)],
        [(0, None), (1, None)],
        after=[grad_tokens],
    )
    grad_query, grad_key, grad_value, grad_gate, grad_up, grad_gain_attn, grad_gain_mlp = unpack_gradients(
        sizes, qkv_sum, gu_sum, w_query, w_key, w_value, w_gate, w_up, gain_one, gain_two, block, padded
    )
    grad_down = down_sum[:block].astype(f32)
    return (
        layer_out,
        grad_tokens,
        grad_gain_attn[:, 0],
        grad_query,
        grad_key,
        grad_value,
        grad_output,
        grad_gain_mlp[:, 0],
        grad_gate,
        grad_up,
        grad_down,
    )


def solution(mesh):
    ctx, fsdp = mesh.shape["ctx"], mesh.shape["fsdp"]
    sizes = (4, ctx // 16, 2, 2, fsdp)
    fine = Mesh(mesh.devices.reshape(sizes), ALL)
    blocks = ("u", "w", "v", "core")
    act = P("f", blocks, None)
    ids = P("f", blocks)
    gain, weight = P(ALL), P(ALL, None)
    return jax.shard_map(
        functools.partial(body, sizes),
        mesh=fine,
        in_specs=(act, act, ids, ids, gain, weight, weight, weight, weight, gain, weight, weight, weight),
        out_specs=(act, act, gain, weight, weight, weight, weight, gain, weight, weight, weight),
        check_vma=False,
    )
```

```python
import functools
import math

import jax
import jax.numpy as jnp
from jax import lax
from jax.experimental import pallas as pl
from jax.experimental.pallas import tpu as pltpu
from jax.sharding import Mesh, PartitionSpec as P

HEADS = 36
HEAD_DIM = 64
WINDOW = 1024
EPSILON = 1e-05
BRANCH_SCALE = 1.4 / math.sqrt(40.0)
NEG_LARGE = -1e30
LANES = 128
PAIRS = 5
KEY_TILE = 512
QUERY_BLOCKS = 2
MIB = 1024 * 1024

f32, bf16 = jnp.float32, jnp.bfloat16


def matmul(left, right):
    return jnp.dot(left, right, preferred_element_type=f32)


def times_transposed(left, right):
    return lax.dot_general(left, right, (((1,), (1,)), ((), ())), preferred_element_type=f32)


def transposed_times(left, right):
    return lax.dot_general(left, right, (((0,), (0,)), ((), ())), preferred_element_type=f32)


def rms_back(upstream, normed, inverse):
    return inverse * (upstream - normed * jnp.mean(upstream * normed, -1, keepdims=True))


HBM = pl.BlockSpec(memory_space=pl.ANY)


def ignoring(kernel, args, extra):
    return lambda *refs: kernel(*refs[:args], *refs[args + extra :])


def lasting(micros):
    return pl.CostEstimate(flops=0, bytes_accessed=micros * 3_600_000, transcendentals=0)


MESH_IDS = pl.DeviceIdType.MESH
ALL = ("u", "w", "v", "core", "f")
KEYS = ("w", "v", "core")
HEAD_SUM = ("w", "v", "core", "f")
HIDDEN = ("v", "f")
HIDDEN_SUM = ("u", "w", "core")


def coords():
    return {axis: lax.axis_index(axis) for axis in ALL}


def device(place, **moved):
    return tuple(moved.get(axis, place[axis]) for axis in ALL)


def remote(src, dst, send, recv, where):
    return pltpu.make_async_remote_copy(
        src_ref=src, dst_ref=dst, send_sem=send, recv_sem=recv, device_id=where, device_id_type=MESH_IDS
    )


def ride_out(kind, x):
    shape = {
        "gather_u": (8,) + x.shape[1:],
        "scatter_u": (3, 2) + x.shape[1:],
        "gather_hidden": (4,) + x.shape,
        "scatter_hidden": (3,) + x.shape[1:],
        "gather_keys": (3,) + x.shape,
        "swap_v": x.shape,
        "gather_heads": (8,) + x.shape,
        "gather_halves": (8,) + x.shape,
    }
    return jax.ShapeDtypeStruct(shape[kind], x.dtype)


STEPS = {"gather_keys": (2, 1), "swap_v": (2,)}


def partner(kind, place, step):
    if kind in ("gather_u", "scatter_u"):
        k = place["u"] ^ step
        return k, device(place, u=k)
    if kind in ("gather_keys", "swap_v"):
        k = (2 * place["v"] + place["core"]) ^ step
        return k, device(place, v=k // 2, core=k % 2)
    k = (2 * place["v"] + place["f"]) ^ step
    return k, device(place, v=k // 2, f=k % 2)


def ride_slices(kind, src, dst, place, step):
    k, _ = partner(kind, place, step)
    t = 2 * place["v"] + place["f"]
    if kind == "scatter_u":
        return [(src.at[7 - k if s else k], dst.at[step - 1, s], dst.at[step - 1, s]) for s in range(2)]
    if kind == "gather_hidden":
        return [(src, dst.at[t], dst.at[k])]
    if kind == "scatter_hidden":
        return [(src.at[k], dst.at[step - 1], dst.at[step - 1])]
    if kind == "swap_v":
        return [(src, dst, dst)]
    return [(src, dst.at[step - 1], dst.at[step - 1])]


def ride_copies(kind, src, dst, send, recv, place, part):
    if kind == "gather_keys" and part == "on":
        _, to = partner(kind, place, 1)
        return [remote(dst.at[1], dst.at[2], send.at[4], recv.at[4], to)]
    copies = []
    for step in STEPS.get(kind, (3, 2, 1)):
        _, to = partner(kind, place, step)
        for i, (here, there, landing) in enumerate(ride_slices(kind, src, dst, place, step)):
            at = 2 * step - 2 + i
            if part == "away":
                copies.append(remote(here, there, send.at[at], recv.at[at], to))
            else:
                copies.append(remote(landing, landing, send.at[at], recv.at[at], to))
    return copies


def own_copies(kind, src, dst, keep, place):
    u, t = place["u"], 2 * place["v"] + place["f"]
    if kind == "gather_u":
        return [pltpu.make_async_copy(src.at[s], dst.at[7 - u if s else u], keep.at[s]) for s in range(2)]
    return [pltpu.make_async_copy(src, dst.at[t], keep.at[0])] if kind == "gather_hidden" else []


def chain_u(stage, src, dst, send, recv, place):
    me = place["u"]
    right, left = device(place, u=jnp.minimum(me + 1, 3)), device(place, u=jnp.maximum(me - 1, 0))

    def spot(owner, slot):
        return dst.at[7 - owner if slot else owner]

    def going(step, slot, side):
        owner = jnp.clip(me + step if side else me - step, 0, 3)
        here = src.at[slot] if step == 0 else spot(owner, slot)
        at = 6 * side + 2 * step + slot
        return remote(here, spot(owner, slot), send.at[at], recv.at[at], left if side else right)

    def coming(step, slot, side):
        there = spot(jnp.clip(me + 1 + step if side else me - 1 - step, 0, 3), slot)
        at = 6 * side + 2 * step + slot
        return remote(there, there, send.at[at], recv.at[at], right if side else left)

    def sends(step, side):
        return (me > 0) & (me <= 3 - step) if side else (me < 3) & (me >= step)

    def gets(step, side):
        return me <= 2 - step if side else me >= step + 1

    for slot in range(2):
        for side in range(2):
            if stage > 0:

                @pl.when(gets(stage - 1, side))
                def _():
                    coming(stage - 1, slot, side).wait_recv()

            if stage < 3:

                @pl.when(sends(stage, side))
                def _():
                    going(stage, slot, side).start()

    if stage == 3:
        for step in range(3):
            for slot in range(2):
                for side in range(2):

                    @pl.when(sends(step, side))
                    def _():
                        going(step, slot, side).wait_send()


def gather_heads(stage, src, dst, send, recv, keep, place):
    v, core, f = place["v"], place["core"], place["f"]
    mine = (2 * v + core) * 2 + f
    other = device(place, core=1 - core)

    def away(step):
        _, to = partner("gather_hidden", place, step)
        return remote(src, dst.at[mine], send.at[step], recv.at[step], to)

    def on(step):
        k = (2 * v + f) ^ step
        there = dst.at[(2 * (k // 2) + core) * 2 + k % 2]
        return remote(src if step == 0 else there, there, send.at[4 + step], recv.at[4 + step], other)

    def landed(step):
        k = (2 * v + f) ^ step
        there = dst.at[(2 * (k // 2) + core) * 2 + k % 2]
        return remote(there, there, send.at[step], recv.at[step], other)

    def passed(step):
        k = (2 * v + f) ^ step
        there = dst.at[(2 * (k // 2) + 1 - core) * 2 + k % 2]
        return remote(there, there, send.at[4 + step], recv.at[4 + step], other)

    local = pltpu.make_async_copy(src, dst.at[mine], keep.at[0]) if stage != 1 else None
    if stage == 0:
        local.start()
        for step in (3, 2, 1):
            away(step).start()
        on(0).start()
    elif stage == 1:
        for step in (1, 2, 3):
            landed(step).wait_recv()
            on(step).start()
    else:
        local.wait()
        for step in (1, 2, 3):
            away(step).wait_send()
        for step in range(4):
            on(step).wait_send()
            passed(step).wait_recv()


def gather_halves(stage, src, dst, send, recv, keep, place):
    v, core, f = place["v"], place["core"], place["f"]
    x_to, y_to, other = device(place, v=1 - v), device(place, f=1 - f), device(place, core=1 - core)
    many = src.shape[0] // 2

    def spot(row, core_, col):
        return dst.at[(2 * row + core_) * 2 + col]

    def half(ref, h):
        return ref.at[many * h : many * h + many]

    def going(here, there, at, to):
        return remote(here, there, send.at[at], recv.at[at], to)

    corners = [(v, f), (1 - v, f), (v, 1 - f), (1 - v, 1 - f)]
    own = [(0, 0, x_to), (3, 1, y_to), (1, 1, x_to), (2, 0, y_to)]

    def sends():
        return [going(half(src, h), half(spot(v, core, f), h), at, to) for at, h, to in own]

    def passing():
        y_on, x_on = half(spot(1 - v, core, f), 0), half(spot(v, core, 1 - f), 1)
        return [going(y_on, y_on, 5, y_to), going(x_on, x_on, 4, x_to)]

    def across(k, core_):
        there = spot(corners[k][0], core_, corners[k][1])
        return going(src if k == 0 and core_ is core else there, there, 6 + k, other)

    def landing(ref, h, at):
        return going(half(ref, h), half(ref, h), at, other)

    if stage == 0:
        pltpu.make_async_copy(src, spot(v, core, f), keep.at[0]).start()
        for copy in sends():
            copy.start()
        across(0, core).start()
    elif stage == 1:
        landing(spot(1 - v, core, f), 0, 0).wait_recv()
        landing(spot(v, core, 1 - f), 1, 3).wait_recv()
        for copy in passing():
            copy.start()
    elif stage == 2:
        landing(spot(1 - v, core, f), 1, 1).wait_recv()
        across(1, core).start()
        landing(spot(v, core, 1 - f), 0, 2).wait_recv()
        across(2, core).start()
        landing(spot(1 - v, core, 1 - f), 0, 5).wait_recv()
        landing(spot(1 - v, core, 1 - f), 1, 4).wait_recv()
        across(3, core).start()
    else:
        pltpu.make_async_copy(src, spot(v, core, f), keep.at[0]).wait()
        for copy in sends() + passing():
            copy.wait_send()
        for k in range(4):
            across(k, core).wait_send()
            across(k, 1 - core).wait_recv()


def ride_greet(kinds, place):
    barrier = pltpu.get_barrier_semaphore()
    count = 0
    for kind in kinds:
        if kind == "gather_heads":
            other = device(place, core=1 - place["core"])
            pl.semaphore_signal(barrier, inc=1, device_id=other, device_id_type=MESH_IDS)
            count = count + 1
        if kind == "gather_halves":
            for axis in ("v", "f", "core"):
                to = device(place, **{axis: 1 - place[axis]})
                pl.semaphore_signal(barrier, inc=1, device_id=to, device_id_type=MESH_IDS)
            count = count + 3
            continue
        for step in STEPS.get(kind, (3, 2, 1)):
            _, to = partner(kind, place, step)
            pl.semaphore_signal(barrier, inc=1, device_id=to, device_id_type=MESH_IDS)
            count = count + 1
    return count


def ride_start(kinds, rides, arrived, sems, place):
    for a, kind in enumerate(kinds):
        send, recv, keep = (sem.at[a] for sem in sems)
        if kind == "gather_u":
            chain_u(0, rides[a], arrived[a], send, recv, place)
        elif kind == "gather_halves":
            gather_halves(0, rides[a], arrived[a], send, recv, keep, place)
        elif kind == "gather_heads":
            gather_heads(0, rides[a], arrived[a], send, recv, keep, place)
        else:
            for copy in ride_copies(kind, rides[a], arrived[a], send, recv, place, "away"):
                copy.start()
        for copy in own_copies(kind, rides[a], arrived[a], keep, place):
            copy.start()


def ride_on(kinds, rides, arrived, sems, place, stage):
    for a, kind in enumerate(kinds):
        if kind == "gather_halves":
            gather_halves(1, rides[a], arrived[a], *(sem.at[a] for sem in sems), place)
        if kind == "gather_u":
            chain_u(stage, rides[a], arrived[a], sems[0].at[a], sems[1].at[a], place)


def ride_end(kinds, rides, arrived, sems, place):
    def copies(a, part):
        return ride_copies(kinds[a], rides[a], arrived[a], sems[0].at[a], sems[1].at[a], place, part)

    def heads(a, stage):
        gather_heads(stage, rides[a], arrived[a], *(sem.at[a] for sem in sems), place)

    keys = [a for a, kind in enumerate(kinds) if kind == "gather_keys"]
    for a, kind in enumerate(kinds):
        if kind == "gather_heads":
            heads(a, 1)
        if kind == "gather_halves":
            gather_halves(2, rides[a], arrived[a], *(sem.at[a] for sem in sems), place)
    for a in keys:
        for copy in copies(a, "back"):
            copy.wait_recv()
        for copy in copies(a, "on"):
            copy.start()
    for a, kind in enumerate(kinds):
        for copy in own_copies(kind, rides[a], arrived[a], sems[2].at[a], place):
            copy.wait()
        if kind == "gather_u":
            chain_u(3, rides[a], arrived[a], sems[0].at[a], sems[1].at[a], place)
            continue
        if kind == "gather_heads":
            heads(a, 2)
            continue
        if kind == "gather_halves":
            gather_halves(3, rides[a], arrived[a], *(sem.at[a] for sem in sems), place)
            continue
        for copy in copies(a, "away"):
            copy.wait_send()
        for copy in copies(a, "back") if a not in keys else ():
            copy.wait_recv()
    for a in keys:
        for copy in copies(a, "on"):
            copy.wait()


def ride_scratch(n):
    return [pltpu.SemaphoreType.DMA((n, 12)), pltpu.SemaphoreType.DMA((n, 12)), pltpu.SemaphoreType.DMA((n, 2))]


def riding(kernel, args, extra, outs, kinds, grid):
    n = len(kinds)

    def whole(*refs):
        ins, rides = refs[:args], refs[args : args + n]
        rest = refs[args + n + extra :]
        results, arrived, scratch = rest[:outs], rest[outs : outs + n], rest[outs + n : len(rest) - 3]
        sems = rest[len(rest) - 3 :]
        place = coords()
        ids = [pl.program_id(i) for i in range(len(grid))]
        first, last = ids[0] == 0, ids[0] == grid[0] - 1
        for i in range(1, len(grid)):
            first, last = first & (ids[i] == 0), last & (ids[i] == grid[i] - 1)

        @pl.when(first)
        def _():
            count = ride_greet(kinds, place)
            pl.semaphore_wait(pltpu.get_barrier_semaphore(), count)
            ride_start(kinds, rides, arrived, sems, place)

        kernel(*ins, *results, *scratch)

        if "gather_u" in kinds:
            total = math.prod(grid)
            at = ids[0]
            for i in range(1, len(grid)):
                at = at * grid[i] + ids[i]
            for stage in (1, 2):

                @pl.when(at == total * stage // 3 - 1)
                def _():
                    ride_on(kinds, rides, arrived, sems, place, stage)

        @pl.when(last)
        def _():
            ride_end(kinds, rides, arrived, sems, place)

    return whole


def grid_call(kernel, grid, args, in_specs, out_specs, out_shape, scratch, name, micros, after=(), rides=(), ident=None):
    limit = 56 * MIB
    if not rides:
        return pl.pallas_call(
            ignoring(kernel, len(args), len(after)),
            grid=grid,
            in_specs=in_specs + [HBM] * len(after),
            out_specs=out_specs,
            out_shape=out_shape,
            scratch_shapes=scratch,
            compiler_params=pltpu.CompilerParams(vmem_limit_bytes=limit),
            cost_estimate=lasting(micros),
            name=name,
        )(*args, *after)
    kinds = [kind for kind, _ in rides]
    n = len(rides)
    return pl.pallas_call(
        riding(kernel, len(args), len(after), len(out_shape), kinds, grid),
        grid=grid,
        in_specs=in_specs + [HBM] * (n + len(after)),
        out_specs=out_specs + [HBM] * n,
        out_shape=out_shape + [ride_out(kind, x) for kind, x in rides],
        scratch_shapes=scratch + ride_scratch(n),
        compiler_params=pltpu.CompilerParams(vmem_limit_bytes=limit, collective_id=ident, has_side_effects=True),
        cost_estimate=lasting(max(micros, 50)),
        name=name + "_riding",
    )(*args, *[x for _, x in rides], *after)


def swap_halves(x):
    lane = lax.broadcasted_iota(jnp.int32, x.shape, 1)
    return jnp.where(lane % 64 < 32, pltpu.roll(x, LANES - 32, 1), pltpu.roll(x, 32, 1))


def rope_kernel(raw_ref, cos_ref, sin_ref, kv_ref, q_ref):
    cos, sin = cos_ref[...], sin_ref[...]

    def turn(x):
        return x * cos + swap_halves(x) * sin

    for p in range(4):
        kv_ref[:, 256 * p : 256 * p + 128] = turn(raw_ref[:, 256 * p : 256 * p + 128]).astype(bf16)
        kv_ref[:, 256 * p + 128 : 256 * p + 256] = raw_ref[:, 256 * p + 128 : 256 * p + 256].astype(bf16)
    last = raw_ref[:, 1024:1152]
    lane = lax.broadcasted_iota(jnp.int32, last.shape, 1)
    kv_ref[:, 1024:1152] = jnp.where(lane < 64, turn(last), last).astype(bf16)
    for p in range(5):
        q_ref[:, 128 * p : 128 * p + 128] = turn(raw_ref[:, 1152 + 128 * p : 1280 + 128 * p]).astype(bf16)


def rope(raw, cos, sin):
    rows = raw.shape[0]
    tile = min(256, rows)
    row = lambda cols: pl.BlockSpec((tile, cols), lambda i: (i, 0))
    return pl.pallas_call(
        rope_kernel,
        grid=(rows // tile,),
        in_specs=[row(1792), row(LANES), row(LANES)],
        out_specs=[row(1152), row(640)],
        out_shape=[jax.ShapeDtypeStruct((rows, 1152), bf16), jax.ShapeDtypeStruct((rows, 640), bf16)],
        compiler_params=pltpu.CompilerParams(vmem_limit_bytes=40 * MIB),
        name="rope",
    )(raw, cos, sin)


def unrope_kernel(dkv_ref, dq_ref, cos_ref, sin_ref, out_ref):
    cos, sin = cos_ref[...], sin_ref[...]

    def turn(x):
        return x * cos - swap_halves(x) * sin

    for p in range(4):
        a = 256 * p
        out_ref[:, a : a + 128] = turn(dkv_ref[:, a : a + 128].astype(f32)).astype(bf16)
        out_ref[:, a + 128 : a + 256] = dkv_ref[:, a + 128 : a + 256].astype(bf16)
    last = dkv_ref[:, 1024:1152].astype(f32)
    lane = lax.broadcasted_iota(jnp.int32, last.shape, 1)
    out_ref[:, 1024:1152] = jnp.where(lane < 64, turn(last), last).astype(bf16)
    for p in range(5):
        out_ref[:, 1152 + 128 * p : 1280 + 128 * p] = turn(
            dq_ref[:, 128 * p : 128 * p + 128].astype(f32)
        ).astype(bf16)


def unrope(dkv, dq, cos, sin, after=()):
    rows = dkv.shape[0]
    tile = min(256, rows)
    row = lambda cols: pl.BlockSpec((tile, cols), lambda i: (i, 0))
    return pl.pallas_call(
        ignoring(unrope_kernel, 4, len(after)),
        grid=(rows // tile,),
        in_specs=[row(1152), row(640), row(LANES), row(LANES)] + [HBM] * len(after),
        out_specs=row(1792),
        out_shape=jax.ShapeDtypeStruct((rows, 1792), bf16),
        compiler_params=pltpu.CompilerParams(vmem_limit_bytes=40 * MIB),
        name="unrope",
    )(dkv, dq, cos, sin, *after)


def hidden_blocks(sizes):
    nu, nw, nv, nc, nf = sizes
    out = []
    for i in range(nu * nw * nv * nc * nf):
        rest, f = divmod(i, nf)
        rest, core = divmod(rest, nc)
        uw, v = divmod(rest, nv)
        out.append((v * nf + f, uw * nc + core))
    return out


def pack_kernel(spots, block, q_ref, k_ref, v_ref, g_ref, u_ref, one_ref, two_ref, qkv_ref, first_ref, second_ref):
    slab = q_ref.shape[0]
    one, two = one_ref[...], two_ref[...]
    padded = 8 * first_ref.shape[3] // len(spots)

    def scaled(ref, start, size, gain):
        return ref[:, start : start + size].astype(f32) * gain

    for t in range(4):
        cols = []
        at = 576 * t
        for p in range(4):
            cols.append(scaled(k_ref, at + 128 * p, 128, one))
            cols.append(scaled(v_ref, at + 128 * p, 128, one))
        cols.append(scaled(k_ref, at + 512, 64, one))
        cols.append(scaled(v_ref, at + 512, 64, one))
        cols.append(scaled(q_ref, at, 576, one))
        cols.append(jnp.zeros((slab, 64), f32))
        qkv_ref[t] = jnp.concatenate(cols, 1).astype(bf16)
        mine = sorted((place, i) for i, (owner, place) in enumerate(spots) if owner == t)
        for half, ref in enumerate((g_ref, u_ref)):
            cols = []
            for _, i in mine:
                cols.append(scaled(ref, i * block, block, two))
                cols.append(jnp.zeros((slab, padded - block), f32))
            whole = jnp.concatenate(cols, 1).astype(bf16)
            cut = first_ref.shape[3]
            first_ref[t, half] = whole[:, :cut]
            second_ref[t, half] = whole[:, cut:]


def pack_weights(sizes, w_query, w_key, w_value, w_gate, w_up, gain_one, gain_two, block, padded):
    slab = w_query.shape[0]
    spots = hidden_blocks(sizes)
    cut = padded * len(spots) // 8
    return pl.pallas_call(
        functools.partial(pack_kernel, spots, block),
        out_shape=[jax.ShapeDtypeStruct((4, slab, 1792), bf16)]
        + [jax.ShapeDtypeStruct((4, 2, slab, cut), bf16)] * 2,
        compiler_params=pltpu.CompilerParams(vmem_limit_bytes=48 * MIB),
        cost_estimate=lasting(10),
        name="pack_weights",
    )(w_query, w_key, w_value, w_gate, w_up, gain_one, gain_two)


def unpack_kernel(
    spots, block, padded, qkv_ref, gu_ref, q_ref, k_ref, v_ref, g_ref, u_ref, one_ref, two_ref,
    dq_ref, dk_ref, dv_ref, dg_ref, du_ref, done_ref, dtwo_ref,
):
    one, two = one_ref[...], two_ref[...]
    gains = jnp.zeros_like(one)
    wide = gu_ref.shape[2] // 2

    def part(t, start, size):
        return qkv_ref[t, :, start : start + size].astype(f32)

    for ref, out, first, last in ((k_ref, dk_ref, 0, 1024), (v_ref, dv_ref, 128, 1088)):
        cols = []
        for t in range(4):
            cols += [part(t, first + 256 * p, 128) for p in range(4)] + [part(t, last, 64)]
        grad = jnp.concatenate(cols, 1)
        gains = gains + jnp.sum(ref[...].astype(f32) * grad, 1, keepdims=True)
        out[...] = grad * one
    grad = jnp.concatenate([part(t, 1152, 576) for t in range(4)], 1)
    done_ref[...] = gains + jnp.sum(q_ref[...].astype(f32) * grad, 1, keepdims=True)
    dq_ref[...] = grad * one
    gains = jnp.zeros_like(two)
    for half, (ref, out) in enumerate(((g_ref, dg_ref), (u_ref, du_ref))):
        grad = jnp.concatenate(
            [
                gu_ref[t, :, half * wide + place * padded : half * wide + place * padded + block].astype(f32)
                for t, place in spots
            ],
            1,
        )
        gains = gains + jnp.sum(ref[...].astype(f32) * grad, 1, keepdims=True)
        out[...] = grad * two
    dtwo_ref[...] = gains


def unpack_gradients(sizes, qkv, gu, w_query, w_key, w_value, w_gate, w_up, gain_one, gain_two, block, padded):
    slab, width = w_query.shape
    hidden = w_gate.shape[1]
    shape = lambda cols: jax.ShapeDtypeStruct((slab, cols), f32)
    return pl.pallas_call(
        functools.partial(unpack_kernel, hidden_blocks(sizes), block, padded),
        out_shape=[shape(width)] * 3 + [shape(hidden)] * 2 + [shape(1)] * 2,
        compiler_params=pltpu.CompilerParams(vmem_limit_bytes=48 * MIB),
        cost_estimate=lasting(15),
        name="unpack_gradients",
    )(qkv, gu, w_query, w_key, w_value, w_gate, w_up, gain_one, gain_two)


def stack_heads(x, first, second):
    return jnp.concatenate([jnp.where(first, x, 0), jnp.where(second, x, 0)], 0)


def text_rows(source, ring, j, half, many):
    v, core = lax.axis_index("v"), lax.axis_index("core")
    v = 1 - v if source // 2 else v
    core = 1 - core if source % 2 else core
    at = (ring * 2 + v) * 2 + core
    block = many * j + (at if j < 4 else many - 1 - at)
    return pl.multiple_of(block * half, half)


def assemble(kv_refs, kv_s):
    rings, _, half, _ = kv_refs[0].shape
    for source, ref in enumerate(kv_refs):
        for ring in range(rings):
            for j in range(8):
                kv_s[pl.ds(text_rows(source, ring, j, half, 4 * rings), half), :] = ref[ring, j]


def flash_forward_kernel(
    bounds, q_ref, kv0, kv1, kv2, kv3, lim_ref, o_ref, lse_ref, kv_s, s_ref, vt_ref
):
    p, t = pl.program_id(0), pl.program_id(1)
    nq = q_ref.shape[0]
    tail = p == 4
    voff = pl.multiple_of(jnp.where(tail, 0, LANES), LANES)
    tiles = s_ref.shape[0]

    @pl.when(t == 0)
    def _():
        assemble((kv0, kv1, kv2, kv3), kv_s)
        for k in range(tiles):
            vt_ref[k] = kv_s[k * KEY_TILE : (k + 1) * KEY_TILE, pl.ds(voff, LANES)].T

    lane = lax.broadcasted_iota(jnp.int32, (nq, LANES), 1)
    qm = stack_heads(q_ref[...] * bf16(0.125), lane < 64, lane >= 64)
    lo, hi = lim_ref[0, 0:1, :], lim_ref[0, 1:2, :]
    row = lax.broadcasted_iota(jnp.int32, (KEY_TILE, 2 * nq), 0)
    klo, khi = bounds(t)

    def scores(k, high):
        base = pl.multiple_of(k * KEY_TILE, KEY_TILE)
        s = times_transposed(kv_s[pl.ds(base, KEY_TILE), 0:LANES], qm)
        s = jnp.where((row >= lo - base) & (row <= hi - base), s, NEG_LARGE)
        s_ref[k] = s
        return jnp.maximum(high, jnp.max(s.reshape(KEY_TILE // 8, 8, 2 * nq), 0))

    high = lax.fori_loop(klo, khi, scores, jnp.full((8, 2 * nq), NEG_LARGE, f32))
    high = jnp.max(high, 0, keepdims=True)

    def mix(k, carry):
        total, acc = carry
        w = jnp.exp(s_ref[k] - high)
        total = total + jnp.sum(w.reshape(KEY_TILE // 8, 8, 2 * nq), 0)
        acc = acc + matmul(vt_ref[k], w.astype(bf16))
        return total, acc

    total, acc = lax.fori_loop(
        klo, khi, mix, (jnp.zeros((8, 2 * nq), f32), jnp.zeros((LANES, 2 * nq), f32))
    )
    total = jnp.sum(total, 0, keepdims=True)
    out = (acc / total).T
    first, second = out[:nq], out[nq:]
    low = jnp.where(tail, 0.0, first)
    up = jnp.where(tail, first, second)
    o_ref[...] = jnp.where(lane < 64, low, up).astype(bf16)
    lse_ref[0, 0] = jnp.broadcast_to(high + jnp.log(total), (8, 2 * nq))


def flash_specs(rows, tiles, kv):
    nq = rows // tiles
    _, rings, _, half, _ = kv[0].shape
    part = pl.BlockSpec((nq, LANES), lambda p, t, *_: (t, p))
    keys = [
        pl.BlockSpec((None, rings, 8, half, 2 * LANES), lambda p, t, *_, i=i: (i, 0, 0, 0, p)) for i in (0, 0, 1, 2)
    ]
    lim = pl.BlockSpec((1, 8, 2 * nq), lambda p, t, *_: (t, 0, 0))
    lse = pl.BlockSpec((1, 1, 8, 2 * nq), lambda p, t, *_: (p, t, 0, 0))
    return nq, 32 * rings * half, part, keys, lim, lse


def window_bounds(rows, tiles, rings):
    half, many = rows // 8, 4 * rings

    def bounds(t):
        at = (lax.axis_index("w") * 2 + lax.axis_index("v")) * 2 + lax.axis_index("core")

        def first_row(j):
            return (many * j + jnp.where(j < 4, at, many - 1 - at)) * half

        low = jnp.maximum(first_row(t * QUERY_BLOCKS) - (WINDOW - 1), 0)
        high = first_row(t * QUERY_BLOCKS + QUERY_BLOCKS - 1) + half - 1
        return low // KEY_TILE, high // KEY_TILE + 1

    return bounds


def flash_call(kernel, name, args, klo, khi, in_specs, out_specs, out_shape, scratch, micros, after, rides, ident):
    tiles = klo.shape[0]
    grid = (PAIRS, tiles)
    if rides:
        bounds = window_bounds(args[0].shape[0], tiles, args[-3 if name == "flash_backward" else -2].shape[1])
        return grid_call(
            functools.partial(kernel, bounds), grid, args, in_specs, out_specs, out_shape, scratch, name, micros,
            after, rides, ident,
        )

    def bounded(klo_ref, khi_ref, *refs):
        kernel(lambda t: (klo_ref[t], khi_ref[t]), *refs)

    return pl.pallas_call(
        ignoring(bounded, 2 + len(args), len(after)),
        grid_spec=pltpu.PrefetchScalarGridSpec(
            num_scalar_prefetch=2,
            grid=grid,
            in_specs=in_specs + [HBM] * len(after),
            out_specs=out_specs,
            scratch_shapes=scratch,
        ),
        out_shape=out_shape,
        compiler_params=pltpu.CompilerParams(vmem_limit_bytes=56 * MIB),
        cost_estimate=lasting(micros),
        name=name,
    )(klo, khi, *args, *after)


def flash_forward(q, kv, lim, klo, khi, after=(), rides=(), ident=None):
    rows, tiles = q.shape[0], klo.shape[0]
    nq, keys, part, whole, limits, lses = flash_specs(rows, tiles, kv)
    return flash_call(
        flash_forward_kernel,
        "flash_forward",
        [q, kv[0], kv[1], kv[1], kv[1], lim],
        klo,
        khi,
        [part, *whole, limits],
        [part, lses],
        [jax.ShapeDtypeStruct((rows, 640), bf16), jax.ShapeDtypeStruct((PAIRS, tiles, 8, 2 * nq), f32)],
        [
            pltpu.VMEM((keys, 2 * LANES), bf16),
            pltpu.VMEM((keys // KEY_TILE, KEY_TILE, 2 * nq), f32),
            pltpu.VMEM((keys // KEY_TILE, LANES, KEY_TILE), bf16),
        ],
        40,
        after,
        rides,
        ident,
    )


def flash_backward_kernel(
    bounds, q_ref, do_ref, o_ref, kv0, kv1, kv2, kv3, lim_ref, lse_ref,
    dq_ref, dkv0, dkv1, dkv2, dkv3, kv_s, kt_ref, dk_ref, dv_ref,
):
    p, t = pl.program_id(0), pl.program_id(1)
    nq = q_ref.shape[0]
    tail = p == 4
    voff = pl.multiple_of(jnp.where(tail, 0, LANES), LANES)
    tiles = kt_ref.shape[0]

    @pl.when(t == 0)
    def _():
        assemble((kv0, kv1, kv2, kv3), kv_s)
        for k in range(tiles):
            kt_ref[k] = kv_s[k * KEY_TILE : (k + 1) * KEY_TILE, 0:LANES].T
        dk_ref[...] = jnp.zeros_like(dk_ref)
        dv_ref[...] = jnp.zeros_like(dv_ref)

    lane = lax.broadcasted_iota(jnp.int32, (nq, LANES), 1)
    qm = stack_heads(q_ref[...] * bf16(0.125), lane < 64, lane >= 64)
    side = jnp.where(tail, 1, 0)
    head = lane // 64
    dom = stack_heads(do_ref[...], head == side, head == 1 + side)
    back = do_ref[...].astype(f32) * o_ref[...].astype(f32)
    back = stack_heads(back, head == side, head == 1 + side)
    delta = jnp.sum(back.T, 0, keepdims=True)
    lo, hi = lim_ref[0, 0:1, :], lim_ref[0, 1:2, :]
    lse = lse_ref[0, 0, 0:1, :]
    row = lax.broadcasted_iota(jnp.int32, (KEY_TILE, 2 * nq), 0)

    def step(k, acc):
        base = pl.multiple_of(k * KEY_TILE, KEY_TILE)
        s = times_transposed(kv_s[pl.ds(base, KEY_TILE), 0:LANES], qm)
        w = jnp.exp(jnp.where((row >= lo - base) & (row <= hi - base), s - lse, NEG_LARGE))
        dp = times_transposed(kv_s[pl.ds(base, KEY_TILE), pl.ds(voff, LANES)], dom)
        ds = (w * (dp - delta)).astype(bf16)
        dv_ref[pl.ds(base, KEY_TILE), :] += matmul(w.astype(bf16), dom)
        dk_ref[pl.ds(base, KEY_TILE), :] += matmul(ds, qm)
        return acc + matmul(kt_ref[k], ds)

    acc = lax.fori_loop(*bounds(t), step, jnp.zeros((LANES, 2 * nq), f32))
    out = acc.T * 0.125
    dq_ref[...] = jnp.where(lane < 64, out[:nq], jnp.where(tail, 0.0, out[nq:]))

    @pl.when(t == pl.num_programs(1) - 1)
    def _():
        rings, _, half, _ = dkv0.shape
        for source, ref in enumerate((dkv0, dkv1, dkv2, dkv3)):
            for ring in range(rings):
                for j in range(8):
                    at = pl.ds(text_rows(source, ring, j, half, 4 * rings), half)
                    dk, dv = dk_ref[at, :], dv_ref[at, :]
                    ref[ring, j, :, 0:LANES] = jnp.where(tail, dk + dv, dk).astype(bf16)
                    ref[ring, j, :, LANES : 2 * LANES] = dv.astype(bf16)


def flash_backward(q, do, o, kv, lim, lse, klo, khi, after=(), rides=(), ident=None):
    rows, tiles = q.shape[0], klo.shape[0]
    nq, keys, part, whole, limits, lses = flash_specs(rows, tiles, kv)
    return flash_call(
        flash_backward_kernel,
        "flash_backward",
        [q, do, o, kv[0], kv[1], kv[1], kv[1], lim, lse],
        klo,
        khi,
        [part, part, part, *whole, limits, lses],
        [part] + [whole[0]] * 4,
        [jax.ShapeDtypeStruct((rows, 640), f32)] + [jax.ShapeDtypeStruct(kv[0].shape, bf16)] * 4,
        [
            pltpu.VMEM((keys, 2 * LANES), bf16),
            pltpu.VMEM((keys // KEY_TILE, LANES, KEY_TILE), bf16),
            pltpu.VMEM((keys, LANES), f32),
            pltpu.VMEM((keys, LANES), f32),
        ],
        48,
        after,
        rides,
        ident,
    )


def feed_forward_kernel(
    held_ref, back_ref, wg_ref, wu_ref, wd_ref, act_ref, bg_ref, bu_ref, bh_ref, br_ref, bh_acc, br_acc, wd_s
):
    t = pl.program_id(0)
    tile = wg_ref.shape[2]
    blocks, high, third = wd_ref.shape
    padded = high // 3

    @pl.when(t % (third // tile) == 0)
    def _():
        for b in range(blocks):
            for c in range(3):
                wd_s[b * padded : (b + 1) * padded, c * third : (c + 1) * third] = wd_ref[
                    b, c * padded : (c + 1) * padded, :
                ]

    wd = wd_s[pl.ds(pl.multiple_of(t % (third // tile) * tile, tile), tile), :]
    held = held_ref[...]
    width = held.shape[1]
    wg = wg_ref[...].reshape(width, tile)
    wu = wu_ref[...].reshape(width, tile)
    gate, up = matmul(held, wg), matmul(held, wu)
    back_act = times_transposed(back_ref[...], wd)
    sig = jax.nn.sigmoid(gate)
    gs = gate * sig
    act = (gs * up).astype(bf16)
    bg = (back_act * up * sig * (1.0 + gate * (1.0 - sig))).astype(bf16)
    bu = (back_act * gs).astype(bf16)
    act_ref[...], bg_ref[...], bu_ref[...] = act, bg, bu
    bh = times_transposed(bg, wg) + times_transposed(bu, wu)
    br = matmul(act, wd)

    @pl.when(t == 0)
    def _():
        bh_acc[...] = bh
        br_acc[...] = br

    @pl.when(t > 0)
    def _():
        bh_acc[...] += bh
        br_acc[...] += br

    @pl.when(t == pl.num_programs(0) - 1)
    def _():
        bh_ref[...] = bh_acc[...].astype(bf16)
        br_ref[...] = br_acc[...].astype(bf16)


def feed_forward(held, back, packed, wide, after=(), rides=(), ident=None):
    rows, width = held.shape
    tile = 256
    tiles = wide // tile
    whole = pl.BlockSpec((rows, width), lambda t: (0, 0))
    part = pl.BlockSpec((rows, tile), lambda t: (0, t))
    many, _, third = packed.shape
    per, blocks, slice_rows = third // tile, many * third // wide, width // many
    cols = lambda i: pl.BlockSpec((many, slice_rows, tile), lambda t: (0, t // per * 4 + i, t % per))
    down = pl.BlockSpec((blocks, 2 * slice_rows, third), lambda t: (t // per, 1, 0))
    return grid_call(
        feed_forward_kernel,
        (tiles,),
        [held, back, packed, packed, packed],
        [whole, whole, cols(0), cols(1), down],
        [part, part, part, whole, whole],
        [jax.ShapeDtypeStruct((rows, wide), bf16)] * 3 + [jax.ShapeDtypeStruct((rows, width), bf16)] * 2,
        [pltpu.VMEM((rows, width), f32)] * 2 + [pltpu.VMEM((third, width), bf16)],
        "feed_forward",
        42,
        after,
        rides,
        ident,
    )


def weight_gradient(lefts, rights, tile=256, after=(), rides=(), ident=None):
    many, per = len(lefts), len(rights[0])
    flat = [x for group in rights for x in group]
    rows, high = lefts[0].shape
    widths = [x.shape[1] for x in rights[0]]

    def kernel(*refs):
        ls, rs, out = refs[:many], refs[many : many + len(flat)], refs[many + len(flat)]
        start = 0
        for i, cols in enumerate(widths):
            total = transposed_times(ls[0][...], rs[i][...])
            for g in range(1, many):
                total = total + transposed_times(ls[g][...], rs[g * per + i][...])
            out[:, start : start + cols] = total.astype(bf16)
            start += cols

    return grid_call(
        kernel,
        (high // tile,),
        [*lefts, *flat],
        [pl.BlockSpec((rows, tile), lambda i: (0, i))] * many + [pl.BlockSpec(x.shape, lambda i: (0, 0)) for x in flat],
        [pl.BlockSpec((tile, sum(widths)), lambda i: (i, 0))],
        [jax.ShapeDtypeStruct((high, sum(widths)), bf16)],
        [],
        "weight_gradient",
        max(4, 2 * many * rows * high * sum(widths) // 10**9),
        after,
        rides,
        ident,
    )


def greet(places):
    barrier = pltpu.get_barrier_semaphore()
    for place in places:
        pl.semaphore_signal(barrier, inc=1, device_id=place, device_id_type=MESH_IDS)
    pl.semaphore_wait(barrier, len(places))


def greet_line(me, place, more=0):
    barrier = pltpu.get_barrier_semaphore()

    @pl.when(me > 0)
    def _():
        pl.semaphore_signal(barrier, inc=1, device_id=device(place, u=me - 1), device_id_type=MESH_IDS)

    @pl.when(me < 3)
    def _():
        pl.semaphore_signal(barrier, inc=1, device_id=device(place, u=me + 1), device_id_type=MESH_IDS)

    pl.semaphore_wait(barrier, 2 + more - jnp.where(me == 0, 1, 0) - jnp.where(me == 3, 1, 0))


def communicating(kernel, out, args, scratch, collective_id, name, vmem=40, after=(), micros=50):
    return pl.pallas_call(
        ignoring(kernel, len(args), len(after)),
        out_shape=out,
        in_specs=[HBM] * (len(args) + len(after)),
        out_specs=[HBM] * len(out) if isinstance(out, list) else HBM,
        scratch_shapes=scratch,
        compiler_params=pltpu.CompilerParams(
            collective_id=collective_id, has_side_effects=True, vmem_limit_bytes=vmem * MIB
        ),
        cost_estimate=lasting(micros),
        name=name,
    )(*args, *after)


def gather_u_kernel(n, kinds, *refs):
    r = len(kinds)
    ins, rides, outs, arrived = refs[:n], refs[n : n + r], refs[n + r : 2 * n + r], refs[2 * n + r : 2 * n + 2 * r]
    keep, send_r, send_l, recv_r, recv_l, *ride_sems = refs[2 * n + 2 * r :]
    place = coords()
    me = place["u"]
    greet_line(me, place, ride_greet(kinds, place))
    right, left = device(place, u=jnp.minimum(me + 1, 3)), device(place, u=jnp.maximum(me - 1, 0))

    def spot(owner, slot, a):
        return outs[a].at[:, owner if slot == 0 else 7 - owner]

    def going(step, slot, a, rightward):
        owner = me - step if rightward else me + step
        owner = jnp.clip(owner, 0, 3)
        src = ins[a].at[:, slot] if step == 0 else spot(owner, slot, a)
        send, recv, to = (send_r, recv_l, right) if rightward else (send_l, recv_r, left)
        return remote(src, spot(owner, slot, a), send.at[step, slot, a], recv.at[step, slot, a], to)

    def coming(step, slot, a, from_left):
        owner = jnp.clip(me - 1 - step if from_left else me + 1 + step, 0, 3)
        send, recv, to = (send_r, recv_l, right) if from_left else (send_l, recv_r, left)
        there = spot(owner, slot, a)
        return remote(there, there, send.at[step, slot, a], recv.at[step, slot, a], to)

    parts = [(slot, a) for slot in range(2) for a in range(n)]
    own = [pltpu.make_async_copy(ins[a].at[:, s], spot(me, s, a), keep.at[s, a]) for s, a in parts]
    for step in range(3):
        for part in parts:
            if step > 0:

                @pl.when(me >= step)
                def _():
                    coming(step - 1, *part, True).wait_recv()

            @pl.when((me < 3) & (me >= step))
            def _():
                going(step, *part, True).start()

            if step > 0:

                @pl.when(me <= 3 - step)
                def _():
                    coming(step - 1, *part, False).wait_recv()

            @pl.when((me > 0) & (me <= 3 - step))
            def _():
                going(step, *part, False).start()

        if step == 0:
            for copy in own:
                copy.start()
            ride_start(kinds, rides, arrived, ride_sems, place)
        if step == 1:
            ride_on(kinds, rides, arrived, ride_sems, place, 1)
    for part in parts:

        @pl.when(me == 3)
        def _():
            coming(2, *part, True).wait_recv()

        @pl.when(me == 0)
        def _():
            coming(2, *part, False).wait_recv()

    for step in range(3):
        for part in parts:

            @pl.when((me < 3) & (me >= step))
            def _():
                going(step, *part, True).wait_send()

            @pl.when((me > 0) & (me <= 3 - step))
            def _():
                going(step, *part, False).wait_send()

    for copy in own:
        copy.wait()
    ride_end(kinds, rides, arrived, ride_sems, place)


def gather_u(arrays, collective_id, after=(), rides=()):
    n = len(arrays)
    sems = pltpu.SemaphoreType.DMA((3, 2, n))
    return communicating(
        functools.partial(gather_u_kernel, n, [kind for kind, _ in rides]),
        [jax.ShapeDtypeStruct((x.shape[0], 8) + x.shape[2:], x.dtype) for x in arrays]
        + [ride_out(kind, x) for kind, x in rides],
        arrays + [x for _, x in rides],
        [pltpu.SemaphoreType.DMA((2, n)), sems, sems, sems, sems] + (ride_scratch(len(rides)) if rides else []),
        collective_id,
        "gather_u",
        after=after,
    )


def scatter_u_kernel(kinds, *refs):
    r = len(kinds)
    p_ref, *rides = refs[: 1 + r]
    out_ref, *arrived = refs[1 + r : 2 + 2 * r]
    own, from_l, from_r, total, load, send_r, send_l, recv_l, recv_r, store, *ride_sems = refs[2 + 2 * r :]
    place = coords()
    me = place["u"]
    greet_line(me, place, ride_greet(kinds, place))
    ride_start(kinds, rides, arrived, ride_sems, place)
    right, left = device(place, u=jnp.minimum(me + 1, 3)), device(place, u=jnp.maximum(me - 1, 0))

    def mine(owner, slot):
        return p_ref.at[:, owner if slot == 0 else 7 - owner]

    loads = [
        pltpu.make_async_copy(mine(k, s), own.at[k, s], load.at[k, s]) for k in range(4) for s in range(2)
    ]
    order = [3, 0, 2, 1]

    def fetch(k, s):
        return loads[2 * k + s]

    for k in order:
        for s in range(2):
            fetch(k, s).start()

    def rightward(e, s):
        src = from_l.at[e, s]
        return remote(src, from_l.at[e, s], send_r.at[e, s], recv_l.at[e, s], right)

    def rightward_first(e, s):
        return remote(own.at[3 - e, s], from_l.at[e, s], send_r.at[e, s], recv_l.at[e, s], right)

    def leftward(k, s):
        return remote(from_r.at[k, s], from_r.at[k, s], send_l.at[k, s], recv_r.at[k, s], left)

    def leftward_first(k, s):
        return remote(own.at[k, s], from_r.at[k, s], send_l.at[k, s], recv_r.at[k, s], left)

    def add(into, other):
        into[...] = (into[...].astype(f32) + other[...].astype(f32)).astype(into.dtype)

    for s in range(2):
        for k in order:
            fetch(k, s).wait()
        for e in range(3):

            @pl.when(me == 0)
            def _():
                rightward_first(e, s).start()

            @pl.when(me == 3)
            def _():
                leftward_first(e, s).start()

    for e in range(3):
        for s in range(2):

            @pl.when((me > 0) & (me < 3 - e))
            def _():
                rightward(e, s).wait_recv()
                add(from_l.at[e, s], own.at[3 - e, s])
                rightward(e, s).start()

            @pl.when((me < 3) & (me > e))
            def _():
                leftward(e, s).wait_recv()
                add(from_r.at[e, s], own.at[e, s])
                leftward(e, s).start()

    stores = [pltpu.make_async_copy(total.at[s], out_ref.at[:, s], store.at[s]) for s in range(2)]
    for s in range(2):
        total[s] = own[me, s].astype(f32)

        @pl.when(me > 0)
        def _():
            e = jnp.minimum(3 - me, 2)
            rightward(e, s).wait_recv()
            total[s] += from_l[e, s].astype(f32)

        @pl.when(me < 3)
        def _():
            e = jnp.minimum(me, 2)
            leftward(e, s).wait_recv()
            total[s] += from_r[e, s].astype(f32)

        stores[s].start()
    for e in range(3):
        for s in range(2):

            @pl.when(me < 3 - e)
            def _():
                rightward(e, s).wait_send()

            @pl.when(me > e)
            def _():
                leftward(e, s).wait_send()

    for copy in stores:
        copy.wait()
    ride_end(kinds, rides, arrived, ride_sems, place)


def scatter_u(x, rides=(), after=()):
    groups, _, half, cols = x.shape
    piece = (groups, half, cols)
    sems = pltpu.SemaphoreType.DMA((3, 2))
    return communicating(
        functools.partial(scatter_u_kernel, [kind for kind, _ in rides]),
        [jax.ShapeDtypeStruct((groups, 2, half, cols), f32)] + [ride_out(kind, x) for kind, x in rides],
        [x] + [x for _, x in rides],
        [
            pltpu.VMEM((4, 2) + piece, x.dtype),
            pltpu.VMEM((3, 2) + piece, x.dtype),
            pltpu.VMEM((3, 2) + piece, x.dtype),
            pltpu.VMEM((2,) + piece, f32),
            pltpu.SemaphoreType.DMA((4, 2)),
            sems,
            sems,
            sems,
            sems,
            pltpu.SemaphoreType.DMA((2,)),
        ]
        + (ride_scratch(len(rides)) if rides else []),
        1,
        "scatter_u",
        after=after,
    )


def gather_hidden_kernel(x_ref, out_ref, keep, send_x, send_y, recv_x, recv_y):
    place = coords()
    v, f = place["v"], place["f"]
    x_to, y_to = device(place, v=1 - v), device(place, f=1 - f)
    greet([x_to, y_to])
    half = x_ref.shape[0] // 2

    def spot(row, col, h):
        start = pl.multiple_of((row * 2 + col) * 2 * half + h * half, half)
        return out_ref.at[pl.ds(start, half)]

    def own(h):
        return x_ref.at[pl.ds(h * half, half)]

    def via_x(src, dst, i):
        return remote(src, dst, send_x.at[i], recv_x.at[i], x_to)

    def via_y(src, dst, i):
        return remote(src, dst, send_y.at[i], recv_y.at[i], y_to)

    x_own = [via_x(own(h), spot(v, f, h), h) for h in range(2)]
    y_own = [via_y(own(h), spot(v, f, h), h) for h in range(2)]
    x_own[0].start()
    y_own[1].start()
    x_own[1].start()
    y_own[0].start()
    keeps = [pltpu.make_async_copy(own(h), spot(v, f, h), keep.at[h]) for h in range(2)]
    for copy in keeps:
        copy.start()
    via_x(own(0), spot(1 - v, f, 0), 0).wait_recv()
    y_on = via_y(spot(1 - v, f, 0), spot(1 - v, f, 0), 2)
    y_on.start()
    via_y(own(1), spot(v, 1 - f, 1), 1).wait_recv()
    x_on = via_x(spot(v, 1 - f, 1), spot(v, 1 - f, 1), 2)
    x_on.start()
    via_x(own(1), spot(1 - v, f, 1), 1).wait_recv()
    via_y(own(0), spot(v, 1 - f, 0), 0).wait_recv()
    via_x(own(1), spot(1 - v, 1 - f, 1), 2).wait_recv()
    via_y(own(0), spot(1 - v, 1 - f, 0), 2).wait_recv()
    for copy in x_own + y_own + [x_on, y_on]:
        copy.wait_send()
    for copy in keeps:
        copy.wait()


def gather_hidden(x, after=()):
    rows, cols = x.shape
    sems = pltpu.SemaphoreType.DMA((3,))
    return communicating(
        gather_hidden_kernel,
        jax.ShapeDtypeStruct((4 * rows, cols), x.dtype),
        [x],
        [pltpu.SemaphoreType.DMA((2,)), sems, sems, sems, sems],
        2,
        "gather_hidden",
        after=after,
        micros=20,
    )


def scatter_hidden_kernel(p_ref, out_ref, own, got_x, got_y, total, load, send_x, send_y, recv_x, recv_y, store):
    place = coords()
    v, f = place["v"], place["f"]
    x_to, y_to = device(place, v=1 - v), device(place, f=1 - f)
    greet([x_to, y_to])
    half = total.shape[1]

    def mine(row, col, h):
        start = pl.multiple_of((row * 2 + col) * 2 * half + h * half, half)
        return p_ref.at[pl.ds(start, half)]

    corners = [(v, f), (1 - v, f), (v, 1 - f), (1 - v, 1 - f)]
    loads = [
        [pltpu.make_async_copy(mine(*corners[i], h), own.at[i, h], load.at[i, h]) for h in range(2)]
        for i in range(4)
    ]
    for i in (3, 1, 2, 0):
        for h in range(2):
            loads[i][h].start()

    def via_x(src, i):
        return remote(src, got_x.at[i], send_x.at[i], recv_x.at[i], x_to)

    def via_y(src, i):
        return remote(src, got_y.at[i], send_y.at[i], recv_y.at[i], y_to)

    loads[3][0].wait()
    x_far = via_x(own.at[3, 0], 0)
    x_far.start()
    loads[3][1].wait()
    y_far = via_y(own.at[3, 1], 0)
    y_far.start()
    loads[1][0].wait()
    x_near = via_x(own.at[1, 0], 1)
    x_near.start()
    loads[2][1].wait()
    y_near = via_y(own.at[2, 1], 2)
    y_near.start()

    def add(into, other):
        into[...] = (into[...].astype(f32) + other[...].astype(f32)).astype(into.dtype)

    loads[2][0].wait()
    x_far.wait_recv()
    add(own.at[2, 0], got_x.at[0])
    y_sum = via_y(own.at[2, 0], 1)
    y_sum.start()
    loads[1][1].wait()
    y_far.wait_recv()
    add(own.at[1, 1], got_y.at[0])
    x_sum = via_x(own.at[1, 1], 2)
    x_sum.start()
    stores = [
        pltpu.make_async_copy(total.at[h], out_ref.at[pl.ds(h * half, half)], store.at[h]) for h in range(2)
    ]
    loads[0][0].wait()
    loads[0][1].wait()
    x_near.wait_recv()
    y_near.wait_recv()
    total[0] = own[0, 0].astype(f32) + got_x[1].astype(f32)
    total[1] = own[0, 1].astype(f32) + got_y[2].astype(f32)
    y_sum.wait_recv()
    total[0] += got_y[1].astype(f32)
    stores[0].start()
    x_sum.wait_recv()
    total[1] += got_x[2].astype(f32)
    stores[1].start()
    for copy in (x_far, y_far, x_near, y_near, x_sum, y_sum):
        copy.wait_send()
    for copy in stores:
        copy.wait()


def scatter_hidden(x):
    rows, cols = x.shape[0] // 4, x.shape[1]
    half = (rows // 2, cols)
    sems = pltpu.SemaphoreType.DMA((3,))
    return communicating(
        scatter_hidden_kernel,
        jax.ShapeDtypeStruct((rows, cols), f32),
        [x],
        [
            pltpu.VMEM((4, 2) + half, x.dtype),
            pltpu.VMEM((3,) + half, x.dtype),
            pltpu.VMEM((3,) + half, x.dtype),
            pltpu.VMEM((2,) + half, f32),
            pltpu.SemaphoreType.DMA((4, 2)),
            sems,
            sems,
            sems,
            sems,
            pltpu.SemaphoreType.DMA((2,)),
        ],
        3,
        "scatter_hidden",
    )


FLIP = [(0, 1), (1, 0)]


def core_sum_kernel(x_ref, out_ref, mine, got, load, send, recv, store):
    place = coords()
    core = place["core"]
    other = device(place, core=1 - core)
    barrier = pltpu.get_barrier_semaphore()
    pl.semaphore_signal(barrier, inc=1, device_id=other, device_id_type=MESH_IDS)
    pl.semaphore_wait(barrier, 1)
    blocks = x_ref.shape[0]
    order = [(v, f) for v in range(2) for f in range(2)]

    def sending(k):
        v, f = order[k]
        return remote(x_ref.at[:, v, 1 - core, f], got.at[k], send.at[k], recv.at[k], other)

    def loading(k):
        v, f = order[k]
        return pltpu.make_async_copy(x_ref.at[:, v, core, f], mine.at[k], load.at[k])

    def storing(k):
        return pltpu.make_async_copy(mine.at[k], out_ref.at[k], store.at[k])

    for k in range(4):
        sending(k).start()
        loading(k).start()
    for k in range(4):
        loading(k).wait()
        sending(k).wait_recv()
        for i in range(blocks):
            mine[k, i] = (mine[k, i].astype(f32) + got[k, i].astype(f32)).astype(mine.dtype)
        storing(k).start()
    for k in range(4):
        sending(k).wait_send()
        storing(k).wait()


def head_sum_start(x, sizes, collective_id, blocks=1):
    _, many, nv, nc, nf = sizes
    rows, cols = x.shape[0] // (blocks * many * nv * nc * nf), x.shape[1]
    x = x.reshape(blocks, many, nv, nc, nf, rows, cols)
    x = lax.psum_scatter(x, "w", scatter_dimension=1, tiled=False) if many > 1 else x[:, 0]
    sems = pltpu.SemaphoreType.DMA((4,))
    out = communicating(
        core_sum_kernel,
        jax.ShapeDtypeStruct((4, blocks, rows, cols), x.dtype),
        [x],
        [pltpu.VMEM((4, blocks, rows, cols), x.dtype)] * 2 + [sems] * 4,
        collective_id,
        "core_sum",
        micros=12,
    )
    return out.reshape(4, blocks * rows, cols)


def with_rings(x, many):
    return lax.all_gather(x, "w", axis=1) if many > 1 else x[:, None]


def scatter_keys_start(parts, many):
    parts = [x[0] for x in parts]
    if many > 1:
        parts = [lax.psum_scatter(x, "w", scatter_dimension=0, tiled=True) for x in parts]
    along = parts[2][0].astype(f32) + lax.ppermute(parts[3][0], "core", FLIP).astype(f32)
    own = parts[0][0].astype(f32) + lax.ppermute(parts[1][0], "core", FLIP).astype(f32)
    return own, along.astype(bf16)


def pieces_of(part, axes):
    me = lax.axis_index(axes)
    return [part(me ^ step) for step in (0, 3, 2, 1)]


def tied(xs, after):
    return lax.optimization_barrier((tuple(xs), tuple(after)))[0]


def scatter_pieces(pieces, axes, after=()):
    got = [
        lax.ppermute(piece, axes, [(i, i ^ step) for i in range(4)])
        for step, piece in zip((3, 2, 1), pieces[1:])
    ]
    total = pieces[0].astype(f32)
    for part in tied(got, after):
        total = total + part.astype(f32)
    return total


def pieces_u(x):
    def part(k):
        return jnp.stack(
            [lax.dynamic_index_in_dim(x, k, 0, False), lax.dynamic_index_in_dim(x, 7 - k, 0, False)], 0
        )

    return pieces_of(part, "u")


def pieces_hidden(x):
    blocks = x.reshape(4, x.shape[0] // 4, x.shape[1])
    return pieces_of(lambda k: lax.dynamic_index_in_dim(blocks, k, 0, False), HIDDEN)


def gather_hidden_async(x):
    me = lax.axis_index(HIDDEN)
    out = jnp.zeros((4,) + x.shape, x.dtype)
    for step in range(4):
        part = x if step == 0 else lax.ppermute(x, HIDDEN, [(i, i ^ step) for i in range(4)])
        out = lax.dynamic_update_index_in_dim(out, part, me ^ step, 0)
    return out.reshape(4 * x.shape[0], x.shape[1])


def gather_u_start(x):
    return [x] + [lax.ppermute(x, "u", [(i, i ^ step) for i in range(4)]) for step in (3, 2, 1)]


def gather_u_end(parts, after):
    me = lax.axis_index("u")
    out = jnp.zeros((8,) + parts[0].shape[1:], parts[0].dtype)
    for step, part in zip((0, 3, 2, 1), tied(parts, after)):
        k = me ^ step
        out = lax.dynamic_update_slice_in_dim(out, part[0:1], k, 0)
        out = lax.dynamic_update_slice_in_dim(out, part[1:2], 7 - k, 0)
    return out


def exchange_kernel(sizes, kinds, back, spots, *refs):
    n, more = len(kinds), len(spots) - len(kinds)
    ins, outs = refs[:n], refs[n + more : len(refs) - 3]
    send, recv, keep = refs[len(refs) - 3 :]
    nu, nw, nv, nc, nf = sizes
    place = coords()
    u, w, v, core, f = (place[axis] for axis in ALL)

    def holder(kind, block):
        if kind == "along":
            return (block, w, v, core, f)
        if kind == "heads":
            at = (u * nw + w) * nv + v
            return (block, at // (nf * nc * nv), at // (nf * nc) % nv, at // nf % nc, at % nf)
        return (u, w, block // nf, v, block % nf)

    def owner(kind, slot):
        if kind == "along":
            return (slot, w, v, core, f)
        if kind == "heads":
            at = ((w * nv + v) * nc + core) * nf + f
            return (at // (nv * nw), at // nv % nw, at % nv, slot // nf, slot % nf)
        return (u, w, core, slot // nf, slot % nf)

    def same(other):
        equal = other[0] == u
        for a, b in zip(other[1:], (w, v, core, f)):
            equal = equal & (a == b)
        return equal

    def landing(kind):
        slot = core * nf + f
        block = v * nf + f if kind == "hidden" else u
        return block if back or kind == "along" else slot

    to, frm = (owner, holder) if back else (holder, owner)
    barrier = pltpu.get_barrier_semaphore()
    waits = jnp.int32(0)
    for kind in kinds:
        for i in range(4):
            other = frm(kind, i)

            @pl.when(jnp.logical_not(same(other)))
            def _():
                pl.semaphore_signal(barrier, inc=1, device_id=other, device_id_type=MESH_IDS)

            waits = waits + jnp.where(same(to(kind, i)), 0, 1)
    pl.semaphore_wait(barrier, waits)

    def land(a, at):
        out, first = spots[a]
        return outs[out].at[at] if first is None else outs[out].at[first : first + ins[a].shape[1], at]

    def copy(a, i):
        at = landing(kinds[a])
        return remote(ins[a].at[i], land(a, at), send.at[a, i], recv.at[a, at], to(kinds[a], i))

    def local(a, i):
        return pltpu.make_async_copy(ins[a].at[i], land(a, landing(kinds[a])), keep.at[a])

    own = []
    if more:
        out, first = spots[n]
        own = [pltpu.make_async_copy(refs[n], outs[out].at[first : first + refs[n].shape[0]], keep.at[n])]
    for stage in range(3):
        for rest in own:
            rest.start() if stage == 0 else rest.wait() if stage == 1 else None
        for a in range(n):
            for i in range(4):
                here = same(to(kinds[a], i))

                @pl.when(here)
                def _():
                    local(a, i).start() if stage == 0 else local(a, i).wait() if stage == 1 else None

                @pl.when(jnp.logical_not(here))
                def _():
                    copy(a, i).start() if stage == 0 else copy(a, i).wait_send() if stage == 1 else None

                if stage == 2:

                    @pl.when(jnp.logical_not(same(frm(kinds[a], i))))
                    def _():
                        remote(
                            ins[a].at[i], land(a, i), send.at[a, i], recv.at[a, i], to(kinds[a], i)
                        ).wait_recv()


def exchange(sizes, arrays, kinds, back, collective_id, shapes, spots, after=()):
    n = len(kinds)
    return pl.pallas_call(
        ignoring(functools.partial(exchange_kernel, sizes, kinds, back, spots), len(arrays), len(after)),
        out_shape=[jax.ShapeDtypeStruct(shape, arrays[0].dtype) for shape in shapes],
        in_specs=[HBM] * (len(arrays) + len(after)),
        out_specs=[HBM] * len(shapes),
        scratch_shapes=[
            pltpu.SemaphoreType.DMA((n, 4)),
            pltpu.SemaphoreType.DMA((n, 4)),
            pltpu.SemaphoreType.DMA((n + 1,)),
        ],
        compiler_params=pltpu.CompilerParams(
            collective_id=collective_id, has_side_effects=True, vmem_limit_bytes=16 * MIB
        ),
        cost_estimate=lasting(35),
        name="exchange_back" if back else "exchange",
    )(*arrays, *after)


def pad_columns(x, cols):
    return jnp.pad(x, [(0, 0)] * (x.ndim - 1) + [(0, cols - x.shape[-1])])


def body(sizes, tokens, cotangent, segment, position, gain_attn, w_query, w_key, w_value, w_output, gain_mlp, w_gate, w_up, w_down):
    del segment
    groups, block_rows, width = tokens.shape
    rows = groups * block_rows
    half = block_rows // 2
    hidden = w_gate.shape[1]
    slab = w_gate.shape[0]
    block = w_down.shape[0]
    padded = -(-block // 16) * 16
    nkeys = sizes[1] * sizes[2] * sizes[3]
    wide = 2 * nkeys * padded
    qkv_cols = 1792
    here = (groups, 2, half)
    there = (groups, 8, half)

    gain_one, gain_two = gain_attn.astype(f32)[:, None], gain_mlp.astype(f32)[:, None]
    qkv_local, first_local, second_local = pack_weights(
        sizes, w_query, w_key, w_value, w_gate, w_up, gain_one, gain_two, block, padded
    )
    third = width // 3
    own_down = jnp.pad(w_down, ((0, padded - block), (0, 0))).reshape(padded, 3, third)
    own_down = jnp.transpose(own_down, (1, 0, 2)).reshape(-1, 4, slab, third)
    qkv_local, packed = exchange(
        sizes,
        [qkv_local, first_local, second_local, own_down],
        ["heads", "hidden", "hidden"],
        False,
        6,
        [qkv_local.shape, (6, 4, slab, third)],
        [(0, None), (1, 0), (1, 4), (1, 2)],
    )

    def all_heads(x):
        if sizes[1] > 1:
            x = lax.all_gather(x, "w", axis=0)
        return x.reshape(-1, x.shape[-1])

    sequences = range(groups)
    nlocal = lax.axis_index(KEYS)
    order = jnp.arange(8, dtype=jnp.int32)
    order = nkeys * order + jnp.where(order < 4, nlocal, nkeys - 1 - nlocal)
    text = order[:, None] * half + jnp.arange(half, dtype=jnp.int32)[None, :]
    tiles = 8 // QUERY_BLOCKS
    nq = QUERY_BLOCKS * half
    rates = jnp.exp(jnp.arange(32, dtype=f32) * (-math.log(10000.0) / 32))
    inputs, inverse_one, normed_one = [], [], []
    for g in sequences:
        x = tokens[g].astype(f32)
        inverse = lax.rsqrt(jnp.mean(x * x, -1, keepdims=True) + EPSILON)
        inputs.append(x)
        inverse_one.append(inverse)
        normed_one.append(x * inverse)
    places = jnp.broadcast_to(pad_columns(position.reshape(here), LANES)[:, :, None], (groups, 2, 8, LANES))
    upstream = [cotangent[g].astype(f32) for g in sequences]
    held_one, tables, masks, query, kv, kv_own = ([] for _ in range(6))
    before = []
    for g in sequences:
        sent = [normed_one[g].astype(bf16).reshape(1, 2, half, width), places[g : g + 1]]
        rides = [("gather_keys", kv_own[0].reshape(8, half, 1152)) if g > 0 else ("gather_halves", qkv_local)]
        if g > 0:
            rides.append(("gather_heads", w_output))
        held, seen, got, *out_rows = gather_u(sent, (0, 8)[g], after=before, rides=rides)
        held_one.append(held.reshape(8 * half, width))
        if g == 0:
            qkv_whole = all_heads(got)
        seen = seen[0, :, 0, :half]
        lowest = text - jnp.minimum(seen, WINDOW - 1)
        lows, highs = lowest.reshape(tiles, nq), text.reshape(tiles, nq)
        klo, khi = lows[:, 0] // KEY_TILE, highs[:, -1] // KEY_TILE + 1
        lim = jnp.stack([jnp.tile(lows, (1, 2)), jnp.tile(highs, (1, 2))], 1)
        masks.append((jnp.pad(lim, ((0, 0), (0, 6), (0, 0))), klo, khi))
        angles = seen.reshape(8 * half, 1).astype(f32) * rates[None, :]
        cos, sin = jnp.cos(angles), jnp.sin(angles)
        tables.append((jnp.concatenate([cos, cos, cos, cos], 1), jnp.concatenate([-sin, sin, -sin, sin], 1)))
        own, q = rope(matmul(held_one[g], qkv_whole), *tables[g])
        kv_own.append(own)
        before = [own]
        query.append(q)

    (packed,) = tied([packed], held_one[:1])
    packed = lax.all_gather(packed.reshape(-1, third), HIDDEN_SUM, axis=0)

    def key_arrays(g, others):
        own = kv_own[g].reshape(1, 8, half, 1152)
        kv.append([with_rings(own, sizes[1]), with_rings(others, sizes[1])])

    key_arrays(0, got)
    attn, lse, parts = [], [], []
    out_whole = all_heads(out_rows[0])
    out_whole = jnp.concatenate([out_whole[:512], jnp.zeros((64, width), bf16), out_whole[512:]], 0)
    rides = [("gather_keys", kv_own[1].reshape(8, half, 1152))]
    before = kv_own[1:]
    for g in sequences:
        out, sums, got_zero, *got = flash_forward(query[g], kv[g], *masks[g], after=before, rides=rides, ident=(9, 10)[g])
        attn.append(out)
        lse.append(sums)
        if g == 0:
            key_arrays(1, got_zero)
        parts.append(matmul(out, out_whole).astype(bf16).reshape(8, half, width))
        before, rides = [], [("scatter_u", parts[g])]
        rides += [("gather_hidden", (BRANCH_SCALE * x).astype(bf16)) for x in upstream]
    back_mlp = [x.reshape(4 * block_rows, width) for x in got]

    def own_u(x):
        me = lax.axis_index("u")
        return jnp.stack([lax.dynamic_index_in_dim(x, me, 0, False), lax.dynamic_index_in_dim(x, 7 - me, 0, False)], 0)

    def own_hidden(x):
        return lax.dynamic_index_in_dim(x, lax.axis_index(HIDDEN), 0, False)

    def total(own, got):
        return own.astype(f32) + jnp.sum(got.astype(f32), 0)

    middle, inverse_two, normed_two, held_two, activated, back_gu, back_held, mlp_part = ([] for _ in range(8))

    def to_feed_forward(g, got):
        x = inputs[g] + BRANCH_SCALE * total(own_u(parts[g]), got).reshape(block_rows, width)
        inverse = lax.rsqrt(jnp.mean(x * x, -1, keepdims=True) + EPSILON)
        middle.append(x)
        inverse_two.append(inverse)
        normed_two.append(x * inverse)
        held_two.append(gather_hidden(normed_two[g].astype(bf16)))

    def from_feed_forward(act, back_gate, back_up, back, part):
        activated.append(act)
        back_gu.append([back_gate, back_up])
        back_held.append(back.reshape(4, block_rows, width))
        mlp_part.append(part.reshape(4, block_rows, width))

    to_feed_forward(0, got_zero)
    *results, got_one = feed_forward(
        held_two[0], back_mlp[0], packed, wide, rides=[("scatter_u", parts[1])], ident=11
    )
    from_feed_forward(*results)
    back_middle, sent = [], []

    def to_attention(g, sums):
        x = upstream[g] + rms_back(sums, normed_two[g], inverse_two[g])
        back_middle.append(x)
        sent.append((BRANCH_SCALE * x).astype(bf16).reshape(2, half, width))

    to_feed_forward(1, got_one)
    *results, got_zero = feed_forward(
        held_two[1],
        back_mlp[1],
        packed,
        wide,
        rides=[("scatter_hidden", back_held[0])],
        ident=12,
    )
    from_feed_forward(*results)
    to_attention(0, total(own_hidden(back_held[0]), got_zero))
    layer_out = []
    (down_term,) = weight_gradient(activated, [[back_mlp[i]] for i in sequences])
    down_sum = lax.psum_scatter(down_term, HIDDEN_SUM, scatter_dimension=0, tiled=True)
    gu_term, got_one, back_branch_zero = weight_gradient(
        held_two,
        back_gu,
        after=[down_term],
        rides=[("scatter_hidden", back_held[1]), ("gather_u", sent[0])],
        ident=13,
    )
    to_attention(1, total(own_hidden(back_held[1]), got_one))
    back_branch = [back_branch_zero.reshape(8 * half, width)]
    dkv_own, dkv_along, dq = [], [], []
    rides = [("gather_u", sent[1])] + [("scatter_hidden", x) for x in mlp_part]
    for g in sequences:
        do = times_transposed(back_branch[g], out_whole).astype(bf16)
        lim, klo, khi = masks[g]
        dq_part, *rest = flash_backward(
            query[g], do, attn[g], kv[g], lim, lse[g], klo, khi, rides=rides, ident=(14, 17)[g]
        )
        if g == 0:
            back_branch.append(rest[4].reshape(8 * half, width))
            for i in sequences:
                x = total(own_hidden(mlp_part[i]), rest[5 + i])
                layer_out.append((middle[i] + BRANCH_SCALE * x).astype(bf16))
            dq_part, gu_term, down_sum = lax.optimization_barrier((dq_part, gu_term, down_sum))
            gu_sum = lax.psum_scatter(gu_term, HIDDEN_SUM, scatter_dimension=0, tiled=True)
        dq.append(dq_part)
        own, along = scatter_keys_start(rest[:4], sizes[1])
        dkv_own.append(own)
        dkv_along.append(along)
        rides = [("swap_v", along)]
    def to_tokens(g, dkv):
        back_qkv.append(unrope(dkv.reshape(8 * half, 1152), dq[g], *tables[g], after=[along]))
        part = times_transposed(back_qkv[g], qkv_whole).astype(bf16)
        late.append(part.reshape(8, half, width))

    back_qkv, late, grad_tokens = [], [], []
    to_tokens(0, dkv_own[0] + rest[4].astype(f32))
    out_term, along = weight_gradient(
        attn, [[x] for x in back_branch], tile=LANES, after=late[:1], rides=[("swap_v", along)], ident=15
    )
    out_half = head_sum_start(jnp.concatenate([out_term[:512], out_term[576:]], 0), sizes, 18)
    to_tokens(1, dkv_own[1] + along.astype(f32))
    (qkv_term,) = weight_gradient(held_one, [[x] for x in back_qkv])
    qkv_half = head_sum_start(qkv_term, sizes, 19, 4)
    sums, qkv_got, out_got = scatter_u(
        jnp.stack(late, 0), rides=[("scatter_hidden", qkv_half), ("scatter_hidden", out_half)]
    )
    grad_output = total(own_hidden(out_half), out_got)
    qkv_sum = total(own_hidden(qkv_half), qkv_got).astype(bf16)
    for g in sequences:
        part = sums[g].reshape(block_rows, width)
        x = back_middle[g] + rms_back(part, normed_one[g], inverse_one[g])
        grad_tokens.append(x.astype(bf16))
    layer_out, grad_tokens = jnp.stack(layer_out, 0), jnp.stack(grad_tokens, 0)

    qkv_sum, gu_sum = exchange(
        sizes,
        [qkv_sum.reshape(4, slab, qkv_cols), gu_sum.reshape(4, slab, 2 * wide)],
        ["along", "hidden"],
        True,
        7,
        [(4, slab, qkv_cols), (4, slab, 2 * wide)],
        [(0, None), (1, None)],
        after=[grad_tokens],
    )
    grad_query, grad_key, grad_value, grad_gate, grad_up, grad_gain_attn, grad_gain_mlp = unpack_gradients(
        sizes, qkv_sum, gu_sum, w_query, w_key, w_value, w_gate, w_up, gain_one, gain_two, block, padded
    )
    grad_down = down_sum[:block].astype(f32)
    return (
        layer_out,
        grad_tokens,
        grad_gain_attn[:, 0],
        grad_query,
        grad_key,
        grad_value,
        grad_output,
        grad_gain_mlp[:, 0],
        grad_gate,
        grad_up,
        grad_down,
    )


def solution(mesh):
    ctx, fsdp = mesh.shape["ctx"], mesh.shape["fsdp"]
    sizes = (4, ctx // 16, 2, 2, fsdp)
    fine = Mesh(mesh.devices.reshape(sizes), ALL)
    blocks = ("u", "w", "v", "core")
    act = P("f", blocks, None)
    ids = P("f", blocks)
    gain, weight = P(ALL), P(ALL, None)
    return jax.shard_map(
        functools.partial(body, sizes),
        mesh=fine,
        in_specs=(act, act, ids, ids, gain, weight, weight, weight, weight, gain, weight, weight, weight),
        out_specs=(act, act, gain, weight, weight, weight, weight, gain, weight, weight, weight),
        check_vma=False,
    )
```
